32 devices in a mesh: dp: 4 (over x, core), wide: 4 (over z), row: 2 (over y).
Axes of the slice: x: 2, y: 2, z: 4, core: 2. Of those that a mesh axis runs over, the one named last changes fastest.
Arguments:
- patches: bfloat16 [64, 24, 24, 1024], P(('dp', 'wide'), 'row'), may hold values from -6 to 6
- grid_sizes: int32 [64], P(('dp', 'wide')), may hold values from 16 to 24, as said below
- conv_in: bfloat16 [2, 1024, 1024], replicated, may hold values from -0.1875 to 0.1875
- conv_out: bfloat16 [2, 1024, 1024], replicated, may hold values from -0.1875 to 0.1875
- depth_taps: bfloat16 [2, 9, 1024], replicated, may hold values from -2 to 2
- norm_gain: float32 [2, 3, 1024], replicated, may hold values from 0.1 to 1.9
- norm_bias: float32 [2, 3, 1024], replicated, may hold values from -3 to 3
- read_in: bfloat16 [1024, 4096], P(None, 'wide'), may hold values from -0.1875 to 0.1875
- read_bias: float32 [2, 4096], P(None, 'wide'), may hold values from -3 to 3
- read_out: bfloat16 [4096, 4096], P('wide'), may hold values from -0.125 to 0.125
- cotangent: bfloat16 [64, 12, 12, 4096], P('dp', 'row', None, 'wide'), may hold values from -6 to 6
Outputs:
- tokens: bfloat16 [64, 12, 12, 4096], P('dp', 'row', None, 'wide')
- patch_grad: bfloat16 [64, 24, 24, 1024], P(('dp', 'wide'), 'row')
- grad_conv_in: float32 [2, 1024, 1024], P(None, None, ('dp', 'wide'))
- grad_conv_out: float32 [2, 1024, 1024], P(None, None, ('dp', 'wide'))
- grad_taps: float32 [2, 9, 1024], P(None, None, ('dp', 'wide'))
- grad_gain: float32 [2, 3, 1024], P(None, None, ('dp', 'wide'))
- grad_bias: float32 [2, 3, 1024], P(None, None, ('dp', 'wide'))
- grad_read_in: float32 [1024, 4096], P(None, 'wide')
- grad_read_bias: float32 [2, 4096], P(None, 'wide')
- grad_read_out: float32 [4096, 4096], P('wide')
The draws below stay inside these ranges and needn't reach their ends.
Inputs may be any that keep to these rules, and one draw needn't show every extreme that they name: `grid_sizes`: each entry is 16 or 24; exactly one of the 64 grids has side 16.
All inputs are finite; a program needn't handle non-finite values.
Results may differ from the reference program's by a relative error of at most 0.02.
Values may be sent and summed in bfloat16 or wider, within the bound.
A program may use at most 256 MiB of HBM per device.

```python
import jax
import jax.numpy as jnp
from jax import lax

C = 1024
LLM = 4096
GRID = 24
POOL = 12
G_DEV = 4
GRIDS = 64
N_WIDE = 4


def draw_grid_sizes(key, part):
    key = jax.random.fold_in(key, 11)
    chosen = jax.random.randint(key, (), 0, GRIDS)
    return jnp.where(jnp.arange(GRIDS) == chosen, 16, 24).astype(jnp.int32)


def strengthened(values, rng, source, target, shards_of, factor):
    owner, partner = [(jnp.arange(values.shape[dim]) // (values.shape[dim] // shards_of)).reshape([-1 if axis == dim else 1 for axis in range(values.ndim)]) for dim in (source, target)]
    chosen = jax.random.permutation(rng, shards_of)[partner]
    strong = (owner == chosen) | (owner == (partner + shards_of // 2) % shards_of)
    return jnp.where(strong, factor * values, values)


def steps_of(own_key, shape, shards, low, largest):
    factor_of = 1.0
    for axis_at, parts in shards:
        draws = jax.random.uniform(jax.random.fold_in(jax.random.fold_in(own_key, 6), axis_at), (parts,), jnp.float32, low / len(shards), largest / len(shards))
        factor_of = factor_of * jnp.repeat(jnp.exp(draws), shape[axis_at] // parts).reshape((-1,) + (1,) * (len(shape) - 1 - axis_at))
    return factor_of


def normal_values(rng, shape, width, reach, pieces=(), kind=jnp.bfloat16):
    gain = steps_of(rng, shape, pieces, -0.22, 0.18) if pieces else 1.0
    values = jax.random.normal(rng, shape, jnp.float32) * width * gain
    return jnp.minimum(jnp.maximum(values, -reach), reach).astype(kind)


def bell_draw_with(stream_key, extent, deviation, limit, split, heavy, kind=jnp.bfloat16):
    drawn = deviation * jax.random.normal(stream_key, extent, jnp.float32)
    if split:
        drawn = drawn * steps_of(stream_key, extent, split, -0.22, 0.18)
    return jnp.clip(strengthened(drawn, jax.random.fold_in(stream_key, 3), *heavy), -limit, limit).astype(kind)


def setup_inputs(seed: int = 0) -> dict:
    key_list = jax.random.split(jax.random.key(seed), 12)
    return {
        "patches": normal_values(key_list[0], (GRIDS, GRID, GRID, C), 1.0, 6.0, ((0, 16), (1, 2))),
        "grid_sizes": draw_grid_sizes(jax.random.fold_in(key_list[11], 71), 0),
        "conv_in": normal_values(key_list[2], (2, C, C), C ** -0.5, 0.1875),
        "conv_out": normal_values(key_list[3], (2, C, C), C ** -0.5, 0.1875),
        "depth_taps": normal_values(key_list[4], (2, 9, C), 9 ** -0.5, 2.0),
        "norm_gain": jnp.clip(1.0 + 0.18 * jax.random.normal(key_list[5], (2, 3, C), jnp.float32), 0.1, 1.9),
        "norm_bias": normal_values(key_list[6], (2, 3, C), 0.3, 3.0, (), jnp.float32),
        "read_in": normal_values(key_list[7], (C, LLM), C ** -0.5, 0.1875, ((1, 4),)),
        "read_bias": normal_values(key_list[8], (2, LLM), 0.3, 3.0, ((1, 4),), jnp.float32),
        "read_out": bell_draw_with(key_list[9], (LLM, LLM), LLM ** -0.5, 0.125, ((0, 4),), (0, 1, 4, 2.0)),
        "cotangent": normal_values(key_list[10], (GRIDS, POOL, POOL, LLM), 1.0, 6.0, ((0, 4), (1, 2), (3, 4))),
    }


@jax.custom_vjp
def low(v):
    return lax.optimization_barrier(v.astype(jnp.bfloat16)).astype(jnp.float32)

@jax.custom_vjp
def low_back(v):
    return v

def low_keep(v):
    return (low(v), None)

def low_pass(kept, grad):
    return (grad,)

def back_keep(v):
    return (v, None)

def back_low(kept, grad):
    return (low(grad),)
low.defvjp(low_keep, low_pass)
low_back.defvjp(back_keep, back_low)
eps_norm = 1e-06
exact_mode = lax.Precision.HIGHEST

def layer_norm(values, gain_row, bias_row):
    centre = lax.optimization_barrier(jnp.mean(values, axis=-1, keepdims=True))
    centred = values - centre
    variance = lax.optimization_barrier(jnp.mean(centred * centred, axis=-1, keepdims=True))
    return centred * lax.rsqrt(variance + eps_norm) * gain_row + bias_row

def depthwise(image, tap_table):
    row_count, col_count = (image.shape[0], image.shape[1])
    padded = jnp.pad(image, ((1, 1), (1, 1), (0, 0)))
    result = jnp.zeros(image.shape, jnp.float32)
    for offset in range(9):
        result = result + tap_table[offset] * padded[offset // 3:offset // 3 + row_count, offset % 3:offset % 3 + col_count]
    return result

def block(source, live_mask, w_first, w_last, tap_table, gain_rows, bias_rows):
    first_pre = low_back(jnp.einsum('rwc,cd->rwd', low(source), w_first, precision=exact_mode))
    hidden_one = low(jax.nn.silu(layer_norm(first_pre, gain_rows[0], bias_rows[0])) * live_mask)
    second_pre = low_back(depthwise(hidden_one, tap_table))
    hidden_two = low(jax.nn.silu(layer_norm(second_pre, gain_rows[1], bias_rows[1])) * live_mask)
    third_pre = low_back(jnp.einsum('rwc,cd->rwd', hidden_two, w_last, precision=exact_mode))
    return jax.nn.silu(source + layer_norm(third_pre, gain_rows[2], bias_rows[2])) * live_mask

def pool_weights(grid_side, row_shift, pooled_index, slot_index):
    place = slot_index - row_shift
    begin = pooled_index * grid_side // POOL
    finish = ((pooled_index + 1) * grid_side + POOL - 1) // POOL
    inside = (place >= begin) & (place < finish)
    return jnp.where(inside, 1.0, 0.0).astype(jnp.float32) / (finish - begin).astype(jnp.float32)

def encode_grid(patch_grid, grid_side, w_first, w_last, tap_all, gain_all, bias_all):
    slot_index = jnp.arange(GRID, dtype=jnp.int32)
    row_shift = (GRID - grid_side) // 2
    row_live = (slot_index >= row_shift) & (slot_index < row_shift + grid_side)
    col_live = slot_index < grid_side
    live_mask = (row_live[:, None] & col_live[None, :]).astype(jnp.float32)[:, :, None]
    source = patch_grid * live_mask
    encoded = block(source, live_mask, w_first[0], w_last[0], tap_all[0], gain_all[0], bias_all[0])
    pooled_index = jnp.arange(POOL, dtype=jnp.int32)
    row_pool = pool_weights(grid_side, row_shift, pooled_index[:, None], slot_index[None, :])
    col_pool = pool_weights(grid_side, 0, pooled_index[:, None], slot_index[None, :])
    pooled = jnp.einsum('ir,jw,rwc->ijc', row_pool, col_pool, encoded, precision=exact_mode)
    all_live = jnp.ones((POOL, POOL, 1), jnp.float32)
    return block(pooled, all_live, w_first[1], w_last[1], tap_all[1], gain_all[1], bias_all[1])

def readout(pooled_rows, entry_weight, entry_bias, exit_weight):
    mixed_pre = low_back(jnp.dot(low(pooled_rows), entry_weight, precision=exact_mode) + entry_bias[0])
    hidden = low(jax.nn.gelu(mixed_pre, approximate=False))
    block_width = LLM // N_WIDE
    hidden_blocks = hidden.reshape(hidden.shape[0], N_WIDE, block_width)
    weight_blocks = exit_weight.reshape(N_WIDE, block_width, LLM)
    partial_sums = low(jnp.einsum('nwk,wkj->wnj', hidden_blocks, weight_blocks, precision=exact_mode))
    return lax.optimization_barrier(jnp.sum(partial_sums, axis=0)) + entry_bias[1]

def reference(patches, grid_sizes, conv_in, conv_out, depth_taps, norm_gain, norm_bias, read_in, read_bias, read_out, cotangent):

    def forward(patch_all, w_first, w_last, tap_all, gain_all, bias_all, entry_weight, entry_bias, exit_weight):

        def one_grid(grid_pair):
            return encode_grid(grid_pair[0], grid_pair[1], w_first, w_last, tap_all, gain_all, bias_all)
        encoded = lax.map(jax.checkpoint(one_grid), (patch_all, grid_sizes))
        group_size = G_DEV * N_WIDE
        grouped = encoded.reshape(GRIDS // group_size, group_size * POOL * POOL, C)

        def one_group(group_rows):
            return readout(group_rows, entry_weight, entry_bias, exit_weight)
        mapped = lax.map(jax.checkpoint(one_group), grouped)
        return mapped.reshape(GRIDS, POOL, POOL, LLM)
    tokens, back_fn = jax.vjp(forward, patches.astype(jnp.float32), conv_in.astype(jnp.float32), conv_out.astype(jnp.float32), depth_taps.astype(jnp.float32), norm_gain.astype(jnp.float32), norm_bias.astype(jnp.float32), read_in.astype(jnp.float32), read_bias.astype(jnp.float32), read_out.astype(jnp.float32))
    grads = back_fn(cotangent.astype(jnp.float32))
    return (tokens.astype(jnp.bfloat16), grads[0].astype(jnp.bfloat16), grads[1], grads[2], grads[3], grads[4], grads[5], grads[6], grads[7], grads[8])
```

```python
import functools

import jax
import jax.numpy as jnp
from jax import lax
from jax.experimental import pallas as pl
from jax.experimental.pallas import tpu as pltpu
from jax.sharding import PartitionSpec as P

MESH = pl.DeviceIdType.MESH
BF = jnp.bfloat16
F32 = jnp.float32
VMEM = pltpu.VMEM


class Place:
    def __init__(self, nz, ndp, nrow):
        self.nz, self.ndp, self.nrow = nz, ndp, nrow
        self.nx = ndp // 2
        self.nq = self.nx * nrow
        self.k = lax.axis_index("wide")
        self.r = lax.axis_index("row")
        d = lax.axis_index("dp")
        self.c = lax.rem(d, 2)
        self.x = d // 2
        self.q = self.x * nrow + self.r

    def at(self, q=None, c=None, k=None):
        q = self.q if q is None else q
        c = self.c if c is None else c
        k = self.k if k is None else k
        return {"dp": (q // self.nrow) * 2 + c, "row": lax.rem(q, self.nrow), "wide": k}

    def chip(self, t):
        return lax.rem(self.q + t, self.nq)

    def deep(self, t):
        return lax.rem(self.k + t, self.nz)

    def peers(self):
        return (
            [self.at(q=self.chip(t)) for t in range(1, self.nq)]
            + [self.at(c=1 - self.c)]
            + [self.at(k=self.deep(t)) for t in range(1, self.nz)]
        )

    def greet(self):
        barrier = pltpu.get_barrier_semaphore()
        peers = self.peers()
        for peer in peers:
            pl.semaphore_signal(barrier, inc=1, device_id=peer, device_id_type=MESH)
        pl.semaphore_wait(barrier, len(peers))


class Links:
    def __init__(self, send, recv):
        self.send, self.recv, self.used = send, recv, 0

    def copy(self, src, dst, peer):
        at = self.used
        self.used += 1
        return pltpu.make_async_remote_copy(
            src_ref=src, dst_ref=dst, send_sem=self.send.at[at], recv_sem=self.recv.at[at],
            device_id=peer, device_id_type=MESH,
        )


def start_all(copies):
    for copy in copies:
        copy.start()
    return copies


def recv_all(copies):
    for copy in copies:
        copy.wait_recv()


def sent_all(copies):
    for copy in copies:
        copy.wait_send()


def rows_of(start, size, unit):
    return pl.ds(pl.multiple_of(start, unit), size)


def fold(out, parts, rows, step):
    def body(i, carry):
        at = rows_of(i * step, step, step)
        total = parts[0](at).astype(F32)
        for part in parts[1:]:
            total = total + part(at).astype(F32)
        out(at, total)
        return carry

    lax.fori_loop(0, rows // step, body, 0)


def nt(a, b):
    return lax.dot_general(a, b, (((1,), (1,)), ((), ())), preferred_element_type=F32)


def nn(a, b):
    return jnp.dot(a, b, preferred_element_type=F32)


def tn(a, b):
    return lax.dot_general(a, b, (((0,), (0,)), ((), ())), preferred_element_type=F32)


def gelu_pair(v):
    dense = jnp.exp(-0.5 * v * v)
    s = 1.0 / (1.0 + (0.3275911 * 0.7071067811865476) * jnp.abs(v))
    poly = s * (0.254829592 + s * (-0.284496736 + s * (1.421413741 + s * (-1.453152027 + s * 1.061405429))))
    tail = 0.5 * poly * dense
    phi = jnp.where(v >= 0, 1.0 - tail, tail)
    return v * phi, phi + v * dense * 0.3989422804014327


def readout_kernel(
    nz, ndp, nrow,
    mine, cot, rin_part, rout_part, bias_part, bias_out,
    tokens, agrad, s1, f2, hsum, rc2, rp2,
    rin, rout, bias, abst, abst_t, hid, mg, ag_send, ag_recv, s2, send, recv, local,
):
    me = Place(nz, ndp, nrow)
    links = Links(send, recv)
    T, C = mine.shape
    hw, ow = rout.shape[1], rout.shape[2]
    tall = nz * T
    np_ = 2 * me.nq
    strip = me.c * me.nq + me.q
    ra, rb = C // np_, hw // np_
    me.greet()

    own = [
        pltpu.make_async_copy(rin_part, rin.at[0], local.at[0]),
        pltpu.make_async_copy(rout_part.at[:, rows_of(me.k * ow, ow, 128)], rout.at[0], local.at[1]),
        pltpu.make_async_copy(mine, abst.at[rows_of(me.k * T, T, 16)], local.at[2]),
    ]
    for copy in own:
        copy.start()
    za, zb, zc = [], [], []
    row_a = rows_of(strip * ra, ra, ra)
    row_b = rows_of(strip * rb, rb, rb)
    for t in range(1, nz):
        there = lax.rem(me.k + nz - t, nz)
        za.append(links.copy(rin_part.at[row_a], rin.at[t, row_a], me.at(k=there)))
        zc.append(links.copy(bias_part, bias.at[t], me.at(k=there)))
    start_all(za)
    start_all(zc)
    here = rows_of(me.k * T, T, 16)
    zg = [links.copy(mine, abst.at[here], me.at(k=lax.rem(me.k + nz - t, nz))) for t in range(1, nz)]
    start_all(zg)
    for t in range(1, nz):
        there = lax.rem(me.k + nz - t, nz)
        zb.append(links.copy(
            rout_part.at[row_b, rows_of(there * ow, ow, 128)], rout.at[t, row_b], me.at(k=there)))
    start_all(zb)
    bias[0] = bias_part[...]

    def across(weights, row, height, arrived):
        recv_all(arrived)
        part = weights.at[pl.ds(1, nz - 1), row]
        return start_all([links.copy(part, part, me.at(q=me.chip(t))) for t in range(1, me.nq)])

    def between_cores(weights, height, arrived):
        recv_all(arrived)
        half = rows_of(me.c * (me.nq * height), me.nq * height, height)
        part = weights.at[pl.ds(1, nz - 1), half]
        return start_all([links.copy(part, part, me.at(c=1 - me.c))])

    pa = across(rin, row_a, ra, za)
    pb = across(rout, row_b, rb, zb)
    ca = between_cores(rin, ra, pa)
    cb = between_cores(rout, rb, pb)
    for copy in own:
        copy.wait()
    recv_all(zc)
    recv_all(ca)
    recv_all(cb)

    hsum[...] = jnp.zeros_like(hsum)
    ag = [None] + [
        links.copy(ag_send.at[t - 1], ag_recv.at[t - 1], me.at(k=me.deep(t))) for t in range(1, nz)
    ]
    NT = min(512, hw)

    def group(t):
        z = me.deep(t)
        rows = rows_of(z * T, T, 16)

        def unit(i, carry):
            u = i // (hw // NT)
            cols = rows_of(lax.rem(i, hw // NT) * NT, NT, 128)
            pre = nn(abst[rows], rin[u, :, cols]) + bias[u, 0:1, cols]
            up = nt(cot[rows], rout[u, cols, :])
            value, slope = gelu_pair(pre)
            hid[u, rows, cols] = value.astype(BF)
            grad = (up * slope).astype(BF)
            mg[u, rows, cols] = grad
            hsum[me.deep(u), 0:1, cols] += jnp.sum(grad.astype(F32), axis=0, keepdims=True)
            return carry

        lax.fori_loop(0, nz * (hw // NT), unit, 0)
        CT = 256

        def back(i, carry):
            at = rows_of(i * CT, CT, CT)
            total = nt(mg[0, rows, :], rin[0, at, :])
            for u in range(1, nz):
                total = total + nt(mg[u, rows, :], rin[u, at, :])
            if t == 0:
                agrad[:, at] = total
            else:
                ag_send[t - 1, :, at] = total.astype(BF)
            return carry

        lax.fori_loop(0, C // CT, back, 0)

    for t in range(nz):
        if t:
            zg[t - 1].wait_recv()
        group(t)
        if t:
            ag[t].start()

    HT = 256

    def g2(i, carry):
        u = i // (hw // HT)
        at = rows_of(lax.rem(i, hw // HT) * HT, HT, HT)
        s2[me.deep(u), at, :] = tn(hid[u, :, at], cot[...]).astype(BF)
        return carry

    lax.fori_loop(0, nz * (hw // HT), g2, 0)
    half = me.nq * rb
    theirs = rows_of((1 - me.c) * half, half, half)
    core2 = start_all([links.copy(s2.at[:, theirs], rc2, me.at(c=1 - me.c))])

    def f2_body(i, carry):
        at = rows_of(i * 256, 256, 256)
        total = nn(hid[0], rout[0, :, at]) + bias_out[0:1, at]
        for u in range(1, nz):
            total = total + nn(hid[u], rout[u, :, at])
        tokens[:, at] = total.astype(BF)
        return carry

    lax.fori_loop(0, ow // 256, f2_body, 0)
    recv_all(core2)
    sent_all(core2)
    loads = [
        pltpu.make_async_copy(rc2.at[j], hid.at[j, pl.ds(0, half)], local.at[j]) for j in range(nz)
    ]
    for copy in loads:
        copy.start()
    for j in range(nz):
        loads[j].wait()
        fold(
            lambda at, v, j=j: s2.__setitem__((j, rows_of(me.c * half + at.start, at.size, 16)), v.astype(BF)),
            [lambda at, j=j: s2[j, rows_of(me.c * half + at.start, at.size, 16)], lambda at, j=j: hid[j, at]],
            half, 32,
        )
    sends2 = []
    for t in range(1, me.nq):
        q = me.chip(t)
        src = s2.at[:, rows_of((me.c * me.nq + q) * rb, rb, rb)]
        sends2.append(links.copy(src, rp2.at[t - 1], me.at(q=q)))
    start_all(sends2)

    abst_t[...] = abst[...].T

    def g1(i, carry):
        u = i // (C // 256)
        at = rows_of(lax.rem(i, C // 256) * 256, 256, 256)
        hid[u, at, :] = nn(abst_t[at, :], mg[u]).astype(BF)
        return carry

    lax.fori_loop(0, nz * (C // 256), g1, 0)
    outs = [
        pltpu.make_async_copy(hid.at[u, pl.ds(0, C)], s1.at[me.deep(u)], local.at[2 + u]) for u in range(nz)
    ]
    for copy in outs:
        copy.start()
    recv_all(ag[1:])
    fold(
        lambda at, v: agrad.__setitem__(at, v),
        [lambda at: agrad[at]] + [lambda at, t=t: ag_recv[t - 1, at] for t in range(1, nz)],
        T, 32,
    )
    for copy in outs:
        copy.wait()
    recv_all(sends2)
    loads = [
        pltpu.make_async_copy(rp2.at[t - 1], mg.at[pl.ds(0, nz), pl.ds(t * rb, rb)], local.at[t - 1])
        for t in range(1, me.nq)
    ]
    for copy in loads:
        copy.start()
    for copy in loads:
        copy.wait()
    for j in range(nz):
        fold(
            lambda at, v, j=j: f2.__setitem__((j, at), v.astype(BF)),
            [lambda at, j=j: s2[j, rows_of(strip * rb + at.start, at.size, 16)]]
            + [lambda at, j=j, t=t: mg[j, rows_of(t * rb + at.start, at.size, 16)] for t in range(1, me.nq)],
            rb, min(rb, 32),
        )
    for group_of in (za, zb, zc, zg, pa, pb, ca, cb, ag[1:], sends2):
        sent_all(group_of)


def grads_kernel(
    nz, ndp, nrow,
    s1, f2, conv, small,
    out1, out2, out3, small_out,
    m1, rc1, rp1, f1, rz1, m3, rc3, rp3, f3, rz3, sc, sp, sz, send, recv, local,
):
    me = Place(nz, ndp, nrow)
    links = Links(send, recv)
    C, hw = out1.shape
    ow = f2.shape[2]
    np_ = 2 * me.nq
    strip = me.c * me.nq + me.q
    ra, rb = C // np_, hw // np_
    width = C // nrow
    R = out3.shape[2] // 2
    other = me.at(c=1 - me.c)
    half = me.nq * ra
    me.greet()

    sums = start_all([links.copy(small, sc, other)])
    theirs = rows_of((1 - me.c) * half, half, half)
    core3 = [links.copy(conv.at[b, :, :, 1 - me.c], rc3.at[b], other) for b in range(2)]
    core1 = links.copy(s1.at[:, theirs], rc1, other)
    core1.start()
    start_all(core3)
    row_b = rows_of(strip * rb, rb, rb)
    col_k = rows_of(me.k * ow, ow, 128)
    z2 = start_all([
        links.copy(f2.at[me.deep(t)], out2.at[row_b, col_k], me.at(k=me.deep(t))) for t in range(1, nz)
    ])
    own = [
        pltpu.make_async_copy(s1.at[:, rows_of(me.c * half, half, half)], m1, local.at[0]),
        pltpu.make_async_copy(conv.at[0, :, :, me.c], m3.at[0], local.at[1]),
        pltpu.make_async_copy(conv.at[1, :, :, me.c], m3.at[1], local.at[2]),
    ]
    for copy in own:
        copy.start()
    out2[row_b, col_k] = f2[me.k]
    recv_all(sums)
    sent_all(sums)
    small_out[...] = small[...] + sc[...]
    sums_p = start_all([links.copy(small_out, sp.at[t - 1], me.at(q=me.chip(t))) for t in range(1, me.nq)])

    for copy in own:
        copy.wait()
    core1.wait_recv()
    for j in range(nz):
        fold(
            lambda at, v, j=j: m1.__setitem__((j, at), v.astype(BF)),
            [lambda at, j=j: m1[j, at], lambda at, j=j: rc1[j, at]],
            half, 32,
        )
    p1 = start_all([
        links.copy(m1.at[:, rows_of(me.chip(t) * ra, ra, ra)], rp1.at[t - 1], me.at(q=me.chip(t)))
        for t in range(1, me.nq)
    ])
    p3 = []
    for b in range(2):
        core3[b].wait_recv()
        for m in range(2):
            for x in range(me.nx):
                fold(
                    lambda at, v, i=(b, m, x): m3.__setitem__((*i, at), v.astype(BF)),
                    [lambda at, i=(b, m, x): m3[(*i, at)], lambda at, i=(b, m, x): rc3[(*i, at)]],
                    nz * R, 32,
                )
        sends = []
        for t in range(1, me.nq):
            q = me.chip(t)
            cols = rows_of(lax.rem(q, nrow) * width, width, 128)
            sends.append(links.copy(m3.at[b, :, q // nrow, :, cols], rp3.at[b, t - 1], me.at(q=q)))
        p3.append(start_all(sends))

    recv_all(z2)
    g2 = start_all([
        links.copy(out2.at[row_b], out2.at[row_b], me.at(q=me.chip(t))) for t in range(1, me.nq)
    ])

    sent_all(sums_p)
    recv_all(sums_p)
    for t in range(1, me.nq):
        small_out[...] += sp[t - 1]
    sums_z = start_all([links.copy(small_out, sz.at[t - 1], me.at(k=me.deep(t))) for t in range(1, nz)])

    recv_all(p1)
    mine = rows_of(me.q * ra, ra, ra)
    for j in range(nz):
        fold(
            lambda at, v, j=j: f1.__setitem__((j, at), v.astype(BF)),
            [lambda at, j=j: m1[j, rows_of(me.q * ra + at.start, at.size, 16)]]
            + [lambda at, j=j, t=t: rp1[t - 1, j, at] for t in range(1, me.nq)],
            ra, 32,
        )
    z1 = start_all([links.copy(f1.at[me.deep(t)], rz1.at[t - 1], me.at(k=me.deep(t))) for t in range(1, nz)])
    z3 = []
    my_cols = rows_of(me.r * width, width, 128)
    for b in range(2):
        recv_all(p3[b])
        for m in range(2):
            for j in range(nz):
                rows = pl.ds(j * R, R)
                total = m3[b, m, me.x, rows, my_cols].astype(F32)
                for t in range(1, me.nq):
                    total = total + rp3[b, t - 1, m, rows, :].astype(F32)
                f3[b, j, pl.ds(m * R, R)] = total.astype(BF)
        z3.append(start_all([
            links.copy(f3.at[b, me.deep(t)], rz3.at[b, t - 1], me.at(k=me.deep(t))) for t in range(1, nz)
        ]))

    recv_all(z1)
    row_a = rows_of(strip * ra, ra, ra)
    fold(
        lambda at, v: out1.__setitem__(rows_of(strip * ra + at.start, at.size, 16), v.astype(BF)),
        [lambda at: f1[me.k, at]] + [lambda at, t=t: rz1[t - 1, at] for t in range(1, nz)],
        ra, 32,
    )
    g1 = start_all([
        links.copy(out1.at[row_a], out1.at[row_a], me.at(q=me.chip(t))) for t in range(1, me.nq)
    ])
    g3 = []
    for b in range(2):
        recv_all(z3[b])
        total = f3[b, me.k].astype(F32)
        for t in range(1, nz):
            total = total + rz3[b, t - 1].astype(F32)
        out3[b, me.r] = total.astype(BF)
        g3 += start_all([
            links.copy(out3.at[b, me.r], out3.at[b, me.r], me.at(q=me.x * nrow + lax.rem(me.r + t, nrow)))
            for t in range(1, nrow)
        ])
    recv_all(g2)
    half_b = rows_of(me.c * me.nq * rb, me.nq * rb, me.nq * rb)
    h2 = start_all([links.copy(out2.at[half_b], out2.at[half_b], other)])
    recv_all(g1)
    half_a = rows_of(me.c * half, half, half)
    h1 = start_all([links.copy(out1.at[half_a], out1.at[half_a], other)])
    sent_all(sums_z)
    recv_all(sums_z)
    for t in range(1, nz):
        small_out[...] += sz[t - 1]
    recv_all(g3)
    recv_all(h1)
    recv_all(h2)
    for group_of in ([core1], core3, z2, p1, p3[0], p3[1], g2, z1, z3[0], z3[1], g1, g3, h1, h2):
        sent_all(group_of)


def spec(*kinds):
    return [pl.BlockSpec(memory_space=kind) for kind in kinds]


def run_readout(mesh, token_rows, cot, read_in, read_out, read_bias):
    nz, ndp, nrow = mesh.shape["wide"], mesh.shape["dp"], mesh.shape["row"]
    nq = ndp // 2 * nrow
    T, C = token_rows.shape
    hw, ow = read_out.shape[0], cot.shape[1]
    tall = nz * T
    rb = hw // (2 * nq)
    copies = 4 * (nz - 1) + 2 * (nq - 1) + 2 + (nz - 1) + 1 + (nq - 1)
    bias_part = jnp.broadcast_to(read_bias[0:1], (8, hw))
    bias_out = jnp.broadcast_to(read_bias[1:2], (8, ow))
    ANY = pl.ANY
    return pl.pallas_call(
        functools.partial(readout_kernel, nz, ndp, nrow),
        out_shape=[
            jax.ShapeDtypeStruct((tall, ow), BF),
            jax.ShapeDtypeStruct((T, C), F32),
            jax.ShapeDtypeStruct((nz, C, hw), BF),
            jax.ShapeDtypeStruct((nz, rb, ow), BF),
            jax.ShapeDtypeStruct((nz, 1, hw), F32),
            jax.ShapeDtypeStruct((nz, nq * rb, ow), BF),
            jax.ShapeDtypeStruct((nq - 1, nz, rb, ow), BF),
        ],
        in_specs=spec(ANY, VMEM, ANY, ANY, VMEM, VMEM),
        out_specs=spec(VMEM, VMEM, ANY, VMEM, VMEM, ANY, ANY),
        scratch_shapes=[
            VMEM((nz, C, hw), BF),
            VMEM((nz, hw, ow), BF),
            VMEM((nz, 8, hw), F32),
            VMEM((tall, C), BF),
            VMEM((C, tall), BF),
            VMEM((nz, tall, hw), BF),
            VMEM((nz, tall, hw), BF),
            VMEM((nz - 1, T, C), BF),
            VMEM((nz - 1, T, C), BF),
            VMEM((nz, hw, ow), BF),
            pltpu.SemaphoreType.DMA((copies,)),
            pltpu.SemaphoreType.DMA((copies,)),
            pltpu.SemaphoreType.DMA((nz + 2,)),
        ],
        compiler_params=pltpu.CompilerParams(
            collective_id=0, has_side_effects=True, vmem_limit_bytes=LIMIT
        ),
        name="readout",
    )(token_rows, cot, read_in, read_out, bias_part, bias_out)


LIMIT = 60 * 1024 * 1024


def run_grads(mesh, s1, f2, conv, small):
    nz, ndp, nrow = mesh.shape["wide"], mesh.shape["dp"], mesh.shape["row"]
    nq = ndp // 2 * nrow
    nx = ndp // 2
    _, C, hw = s1.shape
    _, rb, ow = f2.shape
    ra = C // (2 * nq)
    R = C // (ndp * nz)
    S = small.shape[0]
    copies = 3 + 1 + (nz - 1) + (nq - 1) * 2 + 2 * (nq - 1) + (nq - 1) + (nz - 1) * 2 + 2 * (nz - 1) + (nq - 1) + 2 * (nrow - 1) + 2
    width = C // nrow
    ANY = pl.ANY
    return pl.pallas_call(
        functools.partial(grads_kernel, nz, ndp, nrow),
        out_shape=[
            jax.ShapeDtypeStruct((C, hw), BF),
            jax.ShapeDtypeStruct((hw, nz * ow), BF),
            jax.ShapeDtypeStruct((2, nrow, 2 * R, width), BF),
            jax.ShapeDtypeStruct((S, C), F32),
        ],
        in_specs=spec(ANY, VMEM, ANY, VMEM),
        out_specs=spec(VMEM, VMEM, VMEM, VMEM),
        scratch_shapes=[
            VMEM((nz, C // 2, hw), BF),
            VMEM((nz, C // 2, hw), BF),
            VMEM((nq - 1, nz, ra, hw), BF),
            VMEM((nz, ra, hw), BF),
            VMEM((nz - 1, ra, hw), BF),
            VMEM((2, 2, nx, nz * R, C), BF),
            VMEM((2, 2, nx, nz * R, C), BF),
            VMEM((2, nq - 1, 2, nz * R, width), BF),
            VMEM((2, nz, 2 * R, width), BF),
            VMEM((2, nz - 1, 2 * R, width), BF),
            VMEM((S, C), F32),
            VMEM((nq - 1, S, C), F32),
            VMEM((nz - 1, S, C), F32),
            pltpu.SemaphoreType.DMA((copies,)),
            pltpu.SemaphoreType.DMA((copies,)),
            pltpu.SemaphoreType.DMA((3,)),
        ],
        compiler_params=pltpu.CompilerParams(
            collective_id=1, has_side_effects=True, vmem_limit_bytes=LIMIT
        ),
        name="grads",
    )(s1, f2, conv, small)


POOL = 12


eps_norm = 1e-06
exact_mode = lax.Precision.HIGHEST


def extended(cells, sides, width):
    for axis, dim in sides:
        count = lax.axis_size(axis)
        ends = count - 1
        head = lax.slice_in_dim(cells, 0, width, axis=dim)
        tail = lax.slice_in_dim(cells, cells.shape[dim] - width, cells.shape[dim], axis=dim)
        cells = jnp.concatenate(
            [
                lax.ppermute(tail, axis, [(i, (i + 1) % count) for i in range(ends)]),
                cells,
                lax.ppermute(head, axis, [((i + 1) % count, i) for i in range(ends)]),
            ],
            axis=dim,
        )
    return cells


def layer_norm(values, gain_row, bias_row):
    centre = jnp.mean(values, axis=-1, keepdims=True)
    centred = values - centre
    variance = jnp.mean(centred * centred, axis=-1, keepdims=True)
    return centred * lax.rsqrt(variance + eps_norm) * gain_row + bias_row


def head_piece(pre_values, gain_row, bias_row, live_mask):
    return jax.nn.silu(layer_norm(pre_values, gain_row, bias_row)) * live_mask


def tail_piece(source, third_pre, gain_row, bias_row, live_mask):
    return jax.nn.silu(source + layer_norm(third_pre, gain_row, bias_row)) * live_mask


def outer_sum(left_rows, right_rows):
    return lax.dot_general(
        left_rows, right_rows, (((0,), (0,)), ((), ())), preferred_element_type=jnp.float32
    )


def times_transposed(left_rows, weight):
    return lax.dot_general(
        left_rows, weight, (((1,), (1,)), ((), ())), preferred_element_type=jnp.float32
    )


def pad_columns(values):
    return jnp.pad(values, ((0, 0), (0, 0), (1, 1), (0, 0)))


def rows_forward(hidden_one):
    return extended(hidden_one, (("row", 1),), 1)


def rows_backward(second_low):
    return extended(second_low, (("row", 1),), 1)


def depth_apply(padded, tap_table, row_count, col_count):
    result = jnp.zeros((padded.shape[0], row_count, col_count, padded.shape[3]), jnp.float32)
    for offset in range(9):
        window = padded[
            :, offset // 3 : offset // 3 + row_count, offset % 3 : offset % 3 + col_count, :
        ]
        result = result + window.astype(jnp.float32) * tap_table[offset].astype(jnp.float32)
    return result


def block_forward(source, live_mask, weights):
    w_first, w_last, tap_table, gain_rows, bias_rows = weights
    grid_count, row_count, col_count, channels = source.shape
    flat_rows = source.astype(jnp.bfloat16).reshape(-1, channels)
    first_pre = jnp.dot(flat_rows, w_first, preferred_element_type=jnp.float32).reshape(
        source.shape
    )
    hidden_one = head_piece(first_pre, gain_rows[0], bias_rows[0], live_mask).astype(jnp.bfloat16)
    padded_one = pad_columns(rows_forward(hidden_one))
    second_pre = depth_apply(padded_one, tap_table, row_count, col_count)
    hidden_two = head_piece(second_pre, gain_rows[1], bias_rows[1], live_mask).astype(jnp.bfloat16)
    two_rows = hidden_two.reshape(-1, channels)
    third_pre = jnp.dot(two_rows, w_last, preferred_element_type=jnp.float32).reshape(source.shape)
    output = tail_piece(source, third_pre, gain_rows[2], bias_rows[2], live_mask)
    return (output, (flat_rows, first_pre, padded_one, second_pre, two_rows, third_pre))


def block_backward(output_grad, source, live_mask, weights, kept, turned=False):
    w_first, w_last, tap_table, gain_rows, bias_rows = weights
    flat_rows, first_pre, padded_one, second_pre, two_rows, third_pre = kept
    grid_count, row_count, col_count, channels = source.shape
    _, tail_back = jax.vjp(
        functools.partial(tail_piece, live_mask=live_mask), source, third_pre, gain_rows[2], bias_rows[2]
    )
    residual_grad, third_grad, gain_three, bias_three = tail_back(output_grad)
    third_low = third_grad.astype(jnp.bfloat16).reshape(-1, channels)
    grad_last = outer_sum(third_low, two_rows) if turned else outer_sum(two_rows, third_low)
    two_grad = times_transposed(third_low, w_last).reshape(source.shape)
    _, middle_back = jax.vjp(
        functools.partial(head_piece, live_mask=live_mask), second_pre, gain_rows[1], bias_rows[1]
    )
    second_grad, gain_two, bias_two = middle_back(two_grad)
    second_low = second_grad.astype(jnp.bfloat16)
    padded_grad = pad_columns(rows_backward(second_low))
    one_grad = depth_apply(padded_grad, tap_table[::-1], row_count, col_count)
    second_wide = second_low.astype(jnp.float32)
    tap_grads = []
    for offset in range(9):
        window = padded_one[
            :, offset // 3 : offset // 3 + row_count, offset % 3 : offset % 3 + col_count, :
        ]
        tap_grads.append(jnp.sum(second_wide * window.astype(jnp.float32), axis=(0, 1, 2)))
    _, first_back = jax.vjp(
        functools.partial(head_piece, live_mask=live_mask), first_pre, gain_rows[0], bias_rows[0]
    )
    first_grad, gain_one, bias_one = first_back(one_grad)
    first_low = first_grad.astype(jnp.bfloat16).reshape(-1, channels)
    grad_first = outer_sum(first_low, flat_rows) if turned else outer_sum(flat_rows, first_low)
    source_grad = residual_grad + times_transposed(first_low, w_first).reshape(source.shape)
    grads = (
        grad_first,
        grad_last,
        jnp.stack(tap_grads),
        jnp.stack([gain_one, gain_two, gain_three]),
        jnp.stack([bias_one, bias_two, bias_three]),
    )
    return (source_grad, grads)


def pool_weights(grid_side, row_shift, pooled_index, slot_index):
    place = slot_index - row_shift
    begin = pooled_index * grid_side // POOL
    finish = ((pooled_index + 1) * grid_side + POOL - 1) // POOL
    inside = (place >= begin) & (place < finish)
    return jnp.where(inside, 1.0, 0.0).astype(jnp.float32) / (finish - begin).astype(jnp.float32)


def plain(
    patches,
    grid_sizes,
    conv_in,
    conv_out,
    depth_taps,
    norm_gain,
    norm_bias,
    read_in,
    read_bias,
    read_out,
    cotangent,
):
    grid_count, local_rows, grid_width, channels = patches.shape
    row_place = lax.axis_index("row")
    slot_rows = row_place * local_rows + jnp.arange(local_rows, dtype=jnp.int32)
    column_index = jnp.arange(grid_width, dtype=jnp.int32)
    row_shift = (grid_width - grid_sizes) // 2
    row_live = (slot_rows[None, :] >= row_shift[:, None]) & (
        slot_rows[None, :] < (row_shift + grid_sizes)[:, None]
    )
    col_live = column_index[None, :] < grid_sizes[:, None]
    live_mask = (row_live[:, :, None] & col_live[:, None, :]).astype(jnp.float32)[..., None]
    weights_one = (conv_in[0], conv_out[0], depth_taps[0], norm_gain[0], norm_bias[0])
    weights_two = (conv_in[1], conv_out[1], depth_taps[1], norm_gain[1], norm_bias[1])
    source = patches.astype(jnp.float32) * live_mask
    encoded, kept_one = block_forward(source, live_mask, weights_one)
    pool_local = POOL // lax.axis_size("row")
    pooled_index = row_place * pool_local + jnp.arange(pool_local, dtype=jnp.int32)
    side_shaped = grid_sizes[:, None, None]
    row_pool = pool_weights(
        side_shaped, row_shift[:, None, None], pooled_index[None, :, None], slot_rows[None, None, :]
    )
    col_pool = pool_weights(
        side_shaped,
        0,
        jnp.arange(POOL, dtype=jnp.int32)[None, :, None],
        column_index[None, None, :],
    )
    pooled = jnp.einsum("gir,gjw,grwc->gijc", row_pool, col_pool, encoded, precision=exact_mode)
    all_live = jnp.ones((grid_count, pool_local, POOL, 1), jnp.float32)
    abstract, kept_two = block_forward(pooled, all_live, weights_two)
    token_rows = abstract.astype(jnp.bfloat16).reshape(-1, channels)
    gathered = lax.all_gather(token_rows, "wide", axis=0, tiled=True)
    gelu_exact = functools.partial(jax.nn.gelu, approximate=False)
    mixed_pre = jnp.dot(gathered, read_in, preferred_element_type=jnp.float32) + read_bias[0]
    hidden_wide, gelu_back = jax.vjp(gelu_exact, mixed_pre)
    hidden = hidden_wide.astype(jnp.bfloat16)
    partial_out = jnp.dot(hidden, read_out, preferred_element_type=jnp.float32)
    summed = (
        lax.psum_scatter(
            partial_out.astype(jnp.bfloat16), "wide", scatter_dimension=1, tiled=True
        ).astype(jnp.float32)
        + read_bias[1]
    )
    tokens = summed.astype(jnp.bfloat16).reshape(cotangent.shape)
    cot_local = cotangent.reshape(-1, cotangent.shape[-1])
    cot_all = lax.all_gather(cot_local, "wide", axis=1, tiled=True)
    hidden_grad = times_transposed(cot_all, read_out)
    mixed_grad = gelu_back(hidden_grad)[0].astype(jnp.bfloat16)
    grad_exit = outer_sum(hidden, cot_all)
    grad_entry = outer_sum(gathered, mixed_grad)
    bias_pair = jnp.stack(
        [
            jnp.sum(mixed_grad.astype(jnp.float32), axis=0),
            jnp.sum(cot_local.astype(jnp.float32), axis=0),
        ]
    )
    abstract_grad = lax.psum_scatter(
        times_transposed(mixed_grad, read_in).astype(jnp.bfloat16),
        "wide",
        scatter_dimension=0,
        tiled=True,
    ).astype(jnp.float32)
    grad_entry, bias_pair, grad_exit = (
        lax.psum(grad_entry.astype(jnp.bfloat16), ("dp", "row")).astype(jnp.float32),
        lax.psum(bias_pair.astype(jnp.bfloat16), ("dp", "row")).astype(jnp.float32),
        lax.psum(grad_exit.astype(jnp.bfloat16), ("dp", "row")).astype(jnp.float32),
    )
    pooled_grad, grads_two = block_backward(
        abstract_grad.reshape(abstract.shape), pooled, all_live, weights_two, kept_two
    )
    encoded_grad = jnp.einsum(
        "gir,gjw,gijc->grwc", row_pool, col_pool, pooled_grad, precision=exact_mode
    )
    source_grad, grads_one = block_backward(encoded_grad, source, live_mask, weights_one, kept_one)
    patch_grad = (source_grad * live_mask).astype(jnp.bfloat16)
    stacked = tuple((jnp.stack([grads_one[index], grads_two[index]]) for index in range(5)))
    totals = (
        lax.psum_scatter(stacked[0], ("dp", "wide"), scatter_dimension=2, tiled=True),
        lax.psum_scatter(stacked[1], ("dp", "wide"), scatter_dimension=2, tiled=True),
        lax.psum_scatter(stacked[2], ("dp", "wide"), scatter_dimension=2, tiled=True),
        lax.psum_scatter(stacked[3], ("dp", "wide"), scatter_dimension=2, tiled=True),
        lax.psum_scatter(stacked[4], ("dp", "wide"), scatter_dimension=2, tiled=True),
    )
    totals = (
        lax.psum(totals[0].astype(jnp.bfloat16), "row").astype(jnp.float32),
        lax.psum(totals[1].astype(jnp.bfloat16), "row").astype(jnp.float32),
        lax.psum(totals[2].astype(jnp.bfloat16), "row").astype(jnp.float32),
        lax.psum(totals[3].astype(jnp.bfloat16), "row").astype(jnp.float32),
        lax.psum(totals[4].astype(jnp.bfloat16), "row").astype(jnp.float32),
    )
    return (
        tokens,
        patch_grad,
        totals[0],
        totals[1],
        totals[2],
        totals[3],
        totals[4],
        grad_entry,
        bias_pair,
        grad_exit,
    )


def on_device(
    mesh,
    patches,
    grid_sizes,
    conv_in,
    conv_out,
    depth_taps,
    norm_gain,
    norm_bias,
    read_in,
    read_bias,
    read_out,
    cotangent,
):
    nz, ndp = mesh.shape["wide"], mesh.shape["dp"]
    grid_count, local_rows, grid_width, channels = patches.shape
    row_place = lax.axis_index("row")
    slot_rows = row_place * local_rows + jnp.arange(local_rows, dtype=jnp.int32)
    column_index = jnp.arange(grid_width, dtype=jnp.int32)
    row_shift = (grid_width - grid_sizes) // 2
    row_live = (slot_rows[None, :] >= row_shift[:, None]) & (
        slot_rows[None, :] < (row_shift + grid_sizes)[:, None]
    )
    col_live = column_index[None, :] < grid_sizes[:, None]
    live_mask = (row_live[:, :, None] & col_live[:, None, :]).astype(jnp.float32)[..., None]
    weights_one = (conv_in[0], conv_out[0], depth_taps[0], norm_gain[0], norm_bias[0])
    weights_two = (conv_in[1], conv_out[1], depth_taps[1], norm_gain[1], norm_bias[1])
    source = patches.astype(jnp.float32) * live_mask
    encoded, kept_one = block_forward(source, live_mask, weights_one)
    pool_local = POOL // lax.axis_size("row")
    pooled_index = row_place * pool_local + jnp.arange(pool_local, dtype=jnp.int32)
    side_shaped = grid_sizes[:, None, None]
    row_pool = pool_weights(
        side_shaped, row_shift[:, None, None], pooled_index[None, :, None], slot_rows[None, None, :]
    )
    col_pool = pool_weights(
        side_shaped,
        0,
        jnp.arange(POOL, dtype=jnp.int32)[None, :, None],
        column_index[None, None, :],
    )
    pooled = jnp.einsum("gir,gjw,grwc->gijc", row_pool, col_pool, encoded, precision=exact_mode)
    all_live = jnp.ones((grid_count, pool_local, POOL, 1), jnp.float32)
    abstract, kept_two = block_forward(pooled, all_live, weights_two)
    token_rows = abstract.astype(jnp.bfloat16).reshape(-1, channels)
    cot_local = cotangent.reshape(-1, cotangent.shape[-1])
    tokens, abstract_grad, s1, f2, hsum, _, _ = run_readout(
        mesh, token_rows, cot_local, read_in, read_out, read_bias
    )
    tokens = tokens.reshape(cotangent.shape)
    pooled_grad, grads_two = block_backward(
        abstract_grad.reshape(abstract.shape), pooled, all_live, weights_two, kept_two, True
    )
    encoded_grad = jnp.einsum(
        "gir,gjw,gijc->grwc", row_pool, col_pool, pooled_grad, precision=exact_mode
    )
    source_grad, grads_one = block_backward(encoded_grad, source, live_mask, weights_one, kept_one, True)
    patch_grad = (source_grad * live_mask).astype(jnp.bfloat16)
    R = channels // (ndp * nz)
    conv = jnp.stack(
        [jnp.stack([g[0].astype(BF), g[1].astype(BF)]) for g in (grads_one, grads_two)]
    ).reshape(2, 2, ndp // 2, 2, nz * R, channels)
    cot_sum = jnp.sum(cot_local.astype(F32), axis=0)
    width = cot_sum.shape[0]
    cot_row = lax.dynamic_update_slice(
        jnp.zeros((nz * width,), F32), cot_sum, (lax.axis_index("wide") * width,)
    )
    small = jnp.concatenate(
        [piece for g in (grads_one, grads_two) for piece in g[2:]]
        + [hsum.reshape(-1, channels), cot_row.reshape(-1, channels)]
    )
    lines = small.shape[0]
    small = jnp.pad(small, ((0, -lines % 8), (0, 0)))
    out1, out2, out3, small = run_grads(mesh, s1, f2, conv, small)
    out3 = out3.reshape(2, -1, 2, R, out3.shape[-1]).transpose(0, 2, 1, 4, 3).reshape(2, 2, channels, R).astype(F32)
    place = lax.axis_index("dp") * nz + lax.axis_index("wide")
    own = lax.dynamic_slice_in_dim(small, place * R, R, axis=1)
    taps = jnp.stack([own[0:9], own[15:24]])
    gains = jnp.stack([own[9:12], own[24:27]])
    biases = jnp.stack([own[12:15], own[27:30]])
    per = (lines - 30) // 2
    flat = small[30:lines].reshape(2, per * channels)
    bias_pair = lax.dynamic_slice_in_dim(flat, lax.axis_index("wide") * width, width, axis=1)
    return (
        tokens,
        patch_grad,
        out3[:, 0],
        out3[:, 1],
        taps,
        gains,
        biases,
        out1.astype(F32),
        bias_pair,
        out2.astype(F32),
    )


def fits(mesh):
    return mesh.shape["wide"] <= 4 and mesh.shape["dp"] % 2 == 0


def solution(mesh):

    placed = (
        P(("dp", "wide"), "row", None, None),
        P(("dp", "wide")),
        P(),
        P(),
        P(),
        P(),
        P(),
        P(None, "wide"),
        P(None, "wide"),
        P("wide", None),
        P("dp", "row", None, "wide"),
    )
    return jax.shard_map(
        functools.partial(on_device, mesh) if fits(mesh) else plain,
        mesh=mesh,
        in_specs=placed,
        out_specs=(
            P("dp", "row", None, "wide"),
            P(("dp", "wide"), "row", None, None),
            P(None, None, ("dp", "wide")),
            P(None, None, ("dp", "wide")),
            P(None, None, ("dp", "wide")),
            P(None, None, ("dp", "wide")),
            P(None, None, ("dp", "wide")),
            P(None, "wide"),
            P(None, "wide"),
            P("wide", None),
        ),
        check_vma=False,
    )
```

```python
import functools

import jax
import jax.numpy as jnp
from jax import lax
from jax.experimental import pallas as pl
from jax.experimental.pallas import tpu as pltpu
from jax.sharding import PartitionSpec as P

MESH = pl.DeviceIdType.MESH
BF = jnp.bfloat16
F32 = jnp.float32
VMEM = pltpu.VMEM


class Place:
    def __init__(self, nz, ndp, nrow):
        self.nz, self.ndp, self.nrow = nz, ndp, nrow
        self.nx = ndp // 2
        self.nq = self.nx * nrow
        self.k = lax.axis_index("wide")
        self.r = lax.axis_index("row")
        d = lax.axis_index("dp")
        self.c = lax.rem(d, 2)
        self.x = d // 2
        self.q = self.x * nrow + self.r

    def at(self, q=None, c=None, k=None):
        q = self.q if q is None else q
        c = self.c if c is None else c
        k = self.k if k is None else k
        return {"dp": (q // self.nrow) * 2 + c, "row": lax.rem(q, self.nrow), "wide": k}

    def chip(self, t):
        return lax.rem(self.q + t, self.nq)

    def deep(self, t):
        return lax.rem(self.k + t, self.nz)

    def peers(self):
        return (
            [self.at(q=self.chip(t)) for t in range(1, self.nq)]
            + [self.at(c=1 - self.c)]
            + [self.at(k=self.deep(t)) for t in range(1, self.nz)]
        )

    def greet(self):
        barrier = pltpu.get_barrier_semaphore()
        peers = self.peers()
        for peer in peers:
            pl.semaphore_signal(barrier, inc=1, device_id=peer, device_id_type=MESH)
        pl.semaphore_wait(barrier, len(peers))


class Links:
    def __init__(self, send, recv):
        self.send, self.recv, self.used = send, recv, 0

    def copy(self, src, dst, peer):
        at = self.used
        self.used += 1
        return pltpu.make_async_remote_copy(
            src_ref=src, dst_ref=dst, send_sem=self.send.at[at], recv_sem=self.recv.at[at],
            device_id=peer, device_id_type=MESH,
        )


def start_all(copies):
    for copy in copies:
        copy.start()
    return copies


def recv_all(copies):
    for copy in copies:
        copy.wait_recv()


def sent_all(copies):
    for copy in copies:
        copy.wait_send()


def rows_of(start, size, unit):
    return pl.ds(pl.multiple_of(start, unit), size)


def fold(out, parts, rows, step):
    def body(i, carry):
        at = rows_of(i * step, step, step)
        total = parts[0](at).astype(F32)
        for part in parts[1:]:
            total = total + part(at).astype(F32)
        out(at, total)
        return carry

    lax.fori_loop(0, rows // step, body, 0)


def nt(a, b):
    return lax.dot_general(a, b, (((1,), (1,)), ((), ())), preferred_element_type=F32)


def nn(a, b):
    return jnp.dot(a, b, preferred_element_type=F32)


def tn(a, b):
    return lax.dot_general(a, b, (((0,), (0,)), ((), ())), preferred_element_type=F32)


def gelu_pair(v):
    dense = jnp.exp(-0.5 * v * v)
    s = 1.0 / (1.0 + (0.3275911 * 0.7071067811865476) * jnp.abs(v))
    poly = s * (0.254829592 + s * (-0.284496736 + s * (1.421413741 + s * (-1.453152027 + s * 1.061405429))))
    tail = 0.5 * poly * dense
    phi = jnp.where(v >= 0, 1.0 - tail, tail)
    return v * phi, phi + v * dense * 0.3989422804014327


def normal(v):
    centred = v - jnp.mean(v, axis=-1, keepdims=True)
    scale = lax.rsqrt(jnp.mean(centred * centred, axis=-1, keepdims=True) + 1e-06)
    return centred * scale, scale


def sigmoid(v):
    return 1.0 / (1.0 + jnp.exp(-v))


def silu_of(v):
    return v * sigmoid(v)


def column_masks(cmask, width):
    place = lax.rem(lax.broadcasted_iota(jnp.int32, cmask.shape[1:], 0), width)
    cmask[0] = jnp.where(place != 0, 1.0, 0.0)
    cmask[1] = jnp.where(place != width - 1, 1.0, 0.0)


def windows(cells, rim, first, masks):
    middle = jnp.concatenate([rim * (1.0 - first), cells, rim * first], axis=0)
    count = middle.shape[0]
    left, right = pltpu.roll(middle, 1, 0), pltpu.roll(middle, count - 1, 0)
    if masks is not None:
        left, right = left * masks[0], right * masks[1]
    return left, middle, right


class Geometry:
    def __init__(self, count, height, width):
        self.count, self.height, self.width = count, height, width
        self.cells = height * width

    def rows(self, g):
        return rows_of(g * self.cells, self.cells, 16)


def head_stage(shape, per, x_of, w, gains, biases, mask, pre, hidden, rim_send, first):
    cells = shape.cells * per

    def body(i, carry):
        rows = rows_of(i * cells, cells, 16)
        x = x_of(rows)
        value = nn(x, w[...])
        pre[rows] = value.astype(BF)
        n, _ = normal(value)
        h = silu_of(n * gains[0:1] + biases[0:1]) * mask[rows]
        hidden[rows] = h.astype(BF)
        for g in range(per):
            at = g * shape.cells
            top = h[at : at + shape.width]
            bottom = h[at + shape.cells - shape.width : at + shape.cells]
            rim_send[i * per + g, pl.ds(0, shape.width)] = (bottom * first + top * (1.0 - first)).astype(BF)
        return carry

    lax.fori_loop(0, shape.count // per, body, 0)


def depth_stage(shape, hidden, rim, taps, cmask, pre, first, channels):
    def body(i, carry):
        g, l = i // (channels // 128), lax.rem(i, channels // 128)
        rows, lanes = shape.rows(g), rows_of(l * 128, 128, 128)
        shifted = windows(
            hidden[rows, lanes].astype(F32),
            rim[g, pl.ds(0, shape.width), lanes].astype(F32),
            first,
            None if cmask is None else (cmask[0], cmask[1]),
        )
        total = jnp.zeros((shape.cells, 128), F32)
        for a in range(3):
            for b in range(3):
                piece = shifted[b][a * shape.width : a * shape.width + shape.cells]
                total = total + piece * taps[3 * a + b : 3 * a + b + 1, lanes]
        pre[rows, lanes] = total.astype(BF)
        return carry

    lax.fori_loop(0, shape.count * (channels // 128), body, 0)


def tail_stage(shape, per, x, w, gains, biases, mask, pre_two, pre_three, result):
    cells = shape.cells * per

    def body(i, carry):
        rows = rows_of(i * cells, cells, 16)
        n, _ = normal(pre_two[rows].astype(F32))
        h = (silu_of(n * gains[1:2] + biases[1:2]) * mask[rows]).astype(BF)
        value = nn(h, w[...])
        pre_three[rows] = value.astype(BF)
        n, _ = normal(value)
        out = silu_of(x[rows].astype(F32) + n * gains[2:3] + biases[2:3]) * mask[rows]
        result(i, rows, out)
        return carry

    lax.fori_loop(0, shape.count // per, body, 0)


def slope_of(v, s):
    return s * (1.0 + v * (1.0 - s))


def norm_back(n, scale, grad, gain, sums, at):
    sums[at : at + 1] += jnp.sum(grad * n, axis=0, keepdims=True)
    sums[at + 3 : at + 4] += jnp.sum(grad, axis=0, keepdims=True)
    dn = grad * gain
    return scale * (dn - jnp.mean(dn, axis=-1, keepdims=True) - n * jnp.mean(dn * n, axis=-1, keepdims=True))


def back_tail_stage(shape, per, grad_of, x, w, gains, biases, mask, pre_two, pre_three, resid, third, hidden_two, second, edge, first, sums, base):
    cells = shape.cells * per

    def body(i, carry):
        rows = rows_of(i * cells, cells, 16)
        live = mask[rows]
        n, scale = normal(pre_three[rows].astype(F32))
        v = x[rows].astype(F32) + n * gains[2:3] + biases[2:3]
        grad = grad_of(i) * slope_of(v, sigmoid(v)) * live
        resid[rows] = grad.astype(BF)
        low = norm_back(n, scale, grad, gains[2:3], sums, base + 11).astype(BF)
        third[rows] = low
        grad = nt(low, w[...])
        n, scale = normal(pre_two[rows].astype(F32))
        v = n * gains[1:2] + biases[1:2]
        s = sigmoid(v)
        hidden_two[rows] = (v * s * live).astype(BF)
        grad = norm_back(n, scale, grad * live * slope_of(v, s), gains[1:2], sums, base + 10)
        second[rows] = grad.astype(BF)
        for g in range(per):
            at = g * shape.cells
            top = grad[at : at + shape.width]
            bottom = grad[at + shape.cells - shape.width : at + shape.cells]
            edge[i * per + g, pl.ds(0, shape.width)] = (bottom * first + top * (1.0 - first)).astype(BF)
        return carry

    lax.fori_loop(0, shape.count // per, body, 0)


def back_depth_stage(shape, second, rim, hidden, hidden_rim, taps, cmask, result, first, channels, sums, base):
    masks = None if cmask is None else (cmask[0], cmask[1])

    def body(i, carry):
        g, l = i // (channels // 128), lax.rem(i, channels // 128)
        rows, lanes = shape.rows(g), rows_of(l * 128, 128, 128)
        edge = pl.ds(0, shape.width)
        grad = second[rows, lanes].astype(F32)
        shifted = windows(grad, rim[g, edge, lanes].astype(F32), first, masks)
        total = jnp.zeros((shape.cells, 128), F32)
        for a in range(3):
            for b in range(3):
                at = (2 - a) * shape.width
                total = total + shifted[2 - b][at : at + shape.cells] * taps[3 * a + b : 3 * a + b + 1, lanes]
        result[rows, lanes] = total.astype(BF)
        shifted = windows(hidden[rows, lanes].astype(F32), hidden_rim[g, edge, lanes].astype(F32), first, masks)
        for a in range(3):
            for b in range(3):
                at = a * shape.width
                line = base + 3 * a + b
                sums[line : line + 1, lanes] += jnp.sum(
                    grad * shifted[b][at : at + shape.cells], axis=0, keepdims=True
                )
        return carry

    lax.fori_loop(0, shape.count * (channels // 128), body, 0)


def back_head_stage(shape, per, one_grad, w, gains, biases, mask, pre_one, resid, first_low, result, sums, base):
    cells = shape.cells * per

    def body(i, carry):
        rows = rows_of(i * cells, cells, 16)
        n, scale = normal(pre_one[rows].astype(F32))
        v = n * gains[0:1] + biases[0:1]
        grad = one_grad[rows].astype(F32) * mask[rows] * slope_of(v, sigmoid(v))
        low = norm_back(n, scale, grad, gains[0:1], sums, base + 9).astype(BF)
        first_low[rows] = low
        result(i, rows, resid[rows].astype(F32) + nt(low, w[...]))
        return carry

    lax.fori_loop(0, shape.count // per, body, 0)


def outer_stage(left, right, out):
    high = out.shape[2]

    def body(i, carry):
        at = rows_of(i * high, high, 128)
        out[i // 2, lax.rem(i, 2)] = tn(left[:, at], right[...]).astype(BF)
        return carry

    lax.fori_loop(0, out.shape[0] * 2, body, 0)


def readout_kernel(
    nz, ndp, nrow, zero, one,
    patches, cot, rin_part, rout_part, bias_part, bias_out, conv_in, conv_out, taps, gains, biases, mask_zero, mask_one, pool, pick,
    tokens, agrad, s1, f2, hsum, rc1, rc2, rp2, keep_zero, keep_one, rim_zero, rim_one,
    rin, rout, bias, abst, abst_t, hid, mg, ag_send, ag_recv, s2, cmask, edge_zero, edge_one, send, recv, local,
):
    me = Place(nz, ndp, nrow)
    links = Links(send, recv)
    T, C = agrad.shape
    hw, ow = rout.shape[1], rout.shape[2]
    tall = nz * T
    np_ = 2 * me.nq
    strip = me.c * me.nq + me.q
    ra, rb = C // np_, hw // np_
    me.greet()

    own = [
        pltpu.make_async_copy(rin_part, rin.at[0], local.at[0]),
        pltpu.make_async_copy(rout_part.at[:, rows_of(me.k * ow, ow, 128)], rout.at[0], local.at[1]),
    ]
    convs = [
        pltpu.make_async_copy(part.at[b], s2.at[2 * b + i], local.at[2 + 2 * b + i])
        for b in range(2)
        for i, part in enumerate((conv_in, conv_out))
    ]
    given = pltpu.make_async_copy(patches, mg.at[0], local.at[6])
    convs[0].start()
    given.start()
    za, zb, zc = [], [], []
    row_a = rows_of(strip * ra, ra, ra)
    row_b = rows_of(strip * rb, rb, rb)
    for t in range(1, nz):
        there = lax.rem(me.k + nz - t, nz)
        za.append(links.copy(rin_part.at[row_a], rin.at[t, row_a], me.at(k=there)))
        zc.append(links.copy(bias_part, bias.at[t], me.at(k=there)))
    start_all(za)
    start_all(zc)
    for t in range(1, nz):
        there = lax.rem(me.k + nz - t, nz)
        zb.append(links.copy(
            rout_part.at[row_b, rows_of(there * ow, ow, 128)], rout.at[t, row_b], me.at(k=there)))
    start_all(zb)
    for copy in convs[1:] + own:
        copy.start()
    bias[0] = bias_part[...]
    column_masks(cmask, zero.width)

    def across(weights, row, arrived):
        recv_all(arrived)
        part = weights.at[pl.ds(1, nz - 1), row]
        return start_all([links.copy(part, part, me.at(q=me.chip(t))) for t in range(1, me.nq)])

    def between_cores(weights, height, arrived):
        recv_all(arrived)
        half = rows_of(me.c * (me.nq * height), me.nq * height, height)
        part = weights.at[pl.ds(1, nz - 1), half]
        return start_all([links.copy(part, part, me.at(c=1 - me.c))])

    first = (1 - me.r).astype(F32)
    neighbour = me.at(q=me.x * nrow + (nrow - 1 - me.r))

    def masked(rows):
        x = (mg[0, rows].astype(F32) * mask_zero[rows]).astype(BF)
        mg[0, rows] = x
        return x

    convs[0].wait()
    given.wait()
    head_stage(zero, 1, masked, s2.at[0], gains.at[0], biases.at[0], mask_zero, hid.at[0], hid.at[1], edge_zero, first)
    rim0 = links.copy(edge_zero, rim_zero, neighbour)
    rim0.start()
    pa = across(rin, row_a, za)
    rim0.wait_recv()
    depth_stage(zero, hid.at[1], rim_zero, taps.at[0], cmask, hid.at[2], first, C)
    for copy in convs[1:]:
        copy.wait()

    def to_pooled(i, rows, out):
        mg[1, one.rows(i)] = nn(pool[i], out.astype(BF)).astype(BF)

    tail_stage(zero, 1, mg.at[0], s2.at[1], gains.at[0], biases.at[0], mask_zero, hid.at[2], hid.at[3], to_pooled)
    kept_zero = pltpu.make_async_copy(hid, keep_zero, local.at[2])
    kept_zero.start()
    all_one = one.cells * one.count
    part = [mg.at[1 + i // 3, pl.ds((i % 3) * all_one, all_one)] for i in range(5)]
    pooled, pre_one, hidden, pre_two, pre_three = part
    head_stage(one, one.count, lambda rows: pooled[rows], s2.at[2], gains.at[1], biases.at[1], mask_one, pre_one, hidden, edge_one, first)
    rim1 = links.copy(edge_one, rim_one, neighbour)
    rim1.start()
    pb = across(rout, row_b, zb)
    rim1.wait_recv()
    depth_stage(one, hidden, rim_one, taps.at[1], None, pre_two, first, C)
    here = rows_of(me.k * T, T, 16)

    def to_tokens(i, rows, out):
        abst[here] = nn(pick[...], out.astype(BF)).astype(BF)

    tail_stage(one, one.count, pooled, s2.at[3], gains.at[1], biases.at[1], mask_one, pre_two, pre_three, to_tokens)
    kept_one = pltpu.make_async_copy(mg.at[pl.ds(1, 2)], keep_one, local.at[3])
    kept_one.start()
    zg = start_all([
        links.copy(abst.at[here], abst.at[here], me.at(k=lax.rem(me.k + nz - t, nz))) for t in range(1, nz)
    ])
    ca = between_cores(rin, ra, pa)
    cb = between_cores(rout, rb, pb)
    for copy in own + [kept_zero, kept_one]:
        copy.wait()
    recv_all(zc)
    recv_all(ca)
    recv_all(cb)

    hsum[...] = jnp.zeros_like(hsum)
    ag = [None] + [
        links.copy(ag_send.at[t - 1], ag_recv.at[t - 1], me.at(k=me.deep(t))) for t in range(1, nz)
    ]
    NT = min(512, hw)

    def group(t):
        z = me.deep(t)
        rows = rows_of(z * T, T, 16)

        def unit(i, carry):
            u = i // (hw // NT)
            cols = rows_of(lax.rem(i, hw // NT) * NT, NT, 128)
            pre = nn(abst[rows], rin[u, :, cols]) + bias[u, 0:1, cols]
            up = nt(cot[rows], rout[u, cols, :])
            value, slope = gelu_pair(pre)
            hid[u, rows, cols] = value.astype(BF)
            grad = (up * slope).astype(BF)
            mg[u, rows, cols] = grad
            hsum[me.deep(u), 0:1, cols] += jnp.sum(grad.astype(F32), axis=0, keepdims=True)
            return carry

        lax.fori_loop(0, nz * (hw // NT), unit, 0)
        CT = 256

        def back(i, carry):
            at = rows_of(i * CT, CT, CT)
            total = nt(mg[0, rows, :], rin[0, at, :])
            for u in range(1, nz):
                total = total + nt(mg[u, rows, :], rin[u, at, :])
            if t == 0:
                agrad[:, at] = total
            else:
                ag_send[t - 1, :, at] = total.astype(BF)
            return carry

        lax.fori_loop(0, C // CT, back, 0)

    for t in range(nz):
        if t:
            zg[t - 1].wait_recv()
        group(t)
        if t:
            ag[t].start()

    HT = 256

    def g2(i, carry):
        u = i // (hw // HT)
        at = rows_of(lax.rem(i, hw // HT) * HT, HT, HT)
        s2[me.deep(u), at, :] = tn(hid[u, :, at], cot[...]).astype(BF)
        return carry

    lax.fori_loop(0, nz * (hw // HT), g2, 0)
    half = me.nq * rb
    theirs = rows_of((1 - me.c) * half, half, half)
    core2 = start_all([links.copy(s2.at[:, theirs], rc2, me.at(c=1 - me.c))])

    abst_t[...] = abst[...].T
    sent_all(zg)

    def f2_body(i, carry):
        at = rows_of(i * 256, 256, 256)
        total = nn(hid[0], rout[0, :, at]) + bias_out[0:1, at]
        for u in range(1, nz):
            total = total + nn(hid[u], rout[u, :, at])
        abst[:, at] = total.astype(BF)
        return carry

    lax.fori_loop(0, ow // 256, f2_body, 0)
    out_tokens = pltpu.make_async_copy(abst, tokens, local.at[6])
    out_tokens.start()
    recv_all(core2)
    sent_all(core2)
    loads = [
        pltpu.make_async_copy(rc2.at[j], hid.at[j, pl.ds(0, half)], local.at[j]) for j in range(nz)
    ]
    for copy in loads:
        copy.start()
    for j in range(nz):
        loads[j].wait()
        fold(
            lambda at, v, j=j: s2.__setitem__((j, rows_of(me.c * half + at.start, at.size, 16)), v.astype(BF)),
            [lambda at, j=j: s2[j, rows_of(me.c * half + at.start, at.size, 16)], lambda at, j=j: hid[j, at]],
            half, 32,
        )
    sends2 = []
    for t in range(1, me.nq):
        q = me.chip(t)
        src = s2.at[:, rows_of((me.c * me.nq + q) * rb, rb, rb)]
        sends2.append(links.copy(src, rp2.at[t - 1], me.at(q=q)))
    start_all(sends2)


    def g1(i, carry):
        u = i // (C // 256)
        at = rows_of(lax.rem(i, C // 256) * 256, 256, 256)
        hid[u, at, :] = nn(abst_t[at, :], mg[u]).astype(BF)
        return carry

    lax.fori_loop(0, nz * (C // 256), g1, 0)
    low = me.nq * ra
    core1 = links.copy(hid.at[:, rows_of((1 - me.c) * low, low, low)], rc1, me.at(c=1 - me.c))
    core1.start()
    recv_all(ag[1:])
    fold(
        lambda at, v: agrad.__setitem__(at, v),
        [lambda at: agrad[at]] + [lambda at, t=t: ag_recv[t - 1, at] for t in range(1, nz)],
        T, 32,
    )
    core1.wait_recv()
    loads = [pltpu.make_async_copy(rc1.at[u], mg.at[u, pl.ds(0, low)], local.at[u]) for u in range(nz)]
    for copy in loads:
        copy.start()
    outs = []
    for u in range(nz):
        loads[u].wait()
        fold(
            lambda at, v, u=u: hid.__setitem__((u, rows_of(me.c * low + at.start, at.size, 16)), v.astype(BF)),
            [lambda at, u=u: hid[u, rows_of(me.c * low + at.start, at.size, 16)], lambda at, u=u: mg[u, at]],
            low, 32,
        )
        outs.append(pltpu.make_async_copy(hid.at[u, rows_of(me.c * low, low, low)], s1.at[u], local.at[u]))
        outs[-1].start()
    for copy in outs:
        copy.wait()
    recv_all(sends2)
    loads = [
        pltpu.make_async_copy(rp2.at[t - 1], mg.at[pl.ds(0, nz), pl.ds(t * rb, rb)], local.at[t - 1])
        for t in range(1, me.nq)
    ]
    for copy in loads:
        copy.start()
    for copy in loads:
        copy.wait()
    for j in range(nz):
        fold(
            lambda at, v, j=j: f2.__setitem__((j, at), v.astype(BF)),
            [lambda at, j=j: s2[j, rows_of(strip * rb + at.start, at.size, 16)]]
            + [lambda at, j=j, t=t: mg[j, rows_of(t * rb + at.start, at.size, 16)] for t in range(1, me.nq)],
            rb, min(rb, 32),
        )
    out_tokens.wait()
    for group_of in (za, zb, zc, pa, pb, ca, cb, ag[1:], sends2, [rim0, rim1, core1]):
        sent_all(group_of)


def grads_kernel(
    nz, ndp, nrow, zero, one,
    s1, f2, agrad, patches, keep_zero, keep_one, rim_zero, rim_one, conv_in, conv_out, taps, gains, biases,
    mask_zero, mask_one, pool, pick, small_in,
    out1, out2, out3, small, patch_grad, rp1,
    xs, kept, keep, third, resid, weights, cmask, edge_zero, edge_one, got_zero, got_one,
    f1, rz1, conv, rc3, rp3, f3, rz3, sc, sp, sz, send, recv, local,
):
    me = Place(nz, ndp, nrow)
    links = Links(send, recv)
    C, hw = out1.shape
    ow = f2.shape[2]
    np_ = 2 * me.nq
    strip = me.c * me.nq + me.q
    ra, rb = C // np_, hw // np_
    width = C // nrow
    R = out3.shape[2] // 2
    other = me.at(c=1 - me.c)
    first = (1 - me.r).astype(F32)
    neighbour = me.at(q=me.x * nrow + (nrow - 1 - me.r))
    me.greet()

    loads = [
        pltpu.make_async_copy(keep_one, keep, local.at[0]),
        pltpu.make_async_copy(conv_out.at[1], weights.at[1], local.at[1]),
        pltpu.make_async_copy(conv_in.at[1], weights.at[0], local.at[2]),
        pltpu.make_async_copy(keep_zero, kept, local.at[3]),
        pltpu.make_async_copy(patches, xs, local.at[4]),
    ]
    for copy in loads:
        copy.start()
    p1 = start_all([
        links.copy(s1.at[:, rows_of(me.chip(t) * ra, ra, ra)], rp1.at[t - 1], me.at(q=me.chip(t)))
        for t in range(1, me.nq)
    ])
    row_b = rows_of(strip * rb, rb, rb)
    col_k = rows_of(me.k * ow, ow, 128)
    z2 = start_all([
        links.copy(f2.at[me.deep(t)], out2.at[row_b, col_k], me.at(k=me.deep(t))) for t in range(1, nz)
    ])
    own2 = pltpu.make_async_copy(f2.at[me.k], out2.at[row_b, col_k], local.at[5])
    own2.start()
    small[...] = jnp.zeros_like(small)
    small[32:40] = small_in[...]
    column_masks(cmask, zero.width)

    def spread(b):
        core3[b].wait_recv()
        for m in range(2):
            for x in range(me.nx):
                fold(
                    lambda at, v, i=(b, m, x, me.c): conv.__setitem__((*i, at), v.astype(BF)),
                    [lambda at, i=(b, m, x, me.c): conv[(*i, at)], lambda at, i=(b, m, x): rc3[(*i, at)]],
                    nz * R, 32,
                )
        sends = []
        for t in range(1, me.nq):
            q = me.chip(t)
            cols = rows_of(lax.rem(q, nrow) * width, width, 128)
            sends.append(links.copy(conv.at[b, :, q // nrow, me.c, :, cols], rp3.at[b, t - 1], me.at(q=q)))
        return start_all(sends)

    core3, p3 = [None, None], [None, None]

    all_one = one.cells * one.count
    pooled, pre_one, hidden, pre_two, pre_three, pooled_grad = [
        keep.at[i // 3, pl.ds((i % 3) * all_one, all_one)] for i in range(6)
    ]
    third_one, resid_one = third.at[pl.ds(0, all_one)], resid.at[pl.ds(0, all_one)]
    loads[0].wait()
    loads[1].wait()
    back_tail_stage(
        one, one.count, lambda i: nn(pick[...], agrad[...].astype(BF)), pooled, weights.at[1], gains.at[1], biases.at[1], mask_one,
        pre_two, pre_three, resid_one, third_one, pre_three, pre_two, edge_one, first, small, 16,
    )
    rim1 = links.copy(edge_one, got_one, neighbour)
    rim1.start()
    outer_stage(third_one, pre_three, conv.at[1, 1])
    rim1.wait_recv()
    back_depth_stage(one, pre_two, got_one, hidden, rim_one, taps.at[1], None, third_one, first, C, small, 16)
    loads[2].wait()

    def to_pooled_grad(i, rows, grad):
        pooled_grad[rows] = grad.astype(BF)

    back_head_stage(
        one, one.count, third_one, weights.at[0], gains.at[1], biases.at[1], mask_one, pre_one, resid_one, pre_three, to_pooled_grad, small, 16
    )
    again = [
        pltpu.make_async_copy(conv_out.at[0], weights.at[1], local.at[1]),
        pltpu.make_async_copy(conv_in.at[0], weights.at[0], local.at[2]),
    ]
    for copy in again:
        copy.start()
    outer_stage(pre_three, pooled, conv.at[1, 0])
    core3[1] = links.copy(conv.at[1, :, :, 1 - me.c], rc3.at[1], other)
    core3[1].start()

    loads[3].wait()
    loads[4].wait()
    xs[...] = (xs[...].astype(F32) * mask_zero[...]).astype(BF)
    again[0].wait()
    back_tail_stage(
        zero, 1, lambda i: tn(pool[i], pooled_grad[one.rows(i)]), xs, weights.at[1], gains.at[0], biases.at[0], mask_zero,
        kept.at[2], kept.at[3], resid, third, kept.at[3], kept.at[2], edge_zero, first, small, 0,
    )
    rim0 = links.copy(edge_zero, got_zero, neighbour)
    rim0.start()
    p3[1] = spread(1)
    outer_stage(third, kept.at[3], conv.at[0, 1])
    rim0.wait_recv()
    back_depth_stage(zero, kept.at[2], got_zero, kept.at[1], rim_zero, taps.at[0], cmask, third, first, C, small, 0)
    again[1].wait()

    def to_patches(i, rows, grad):
        resid[rows] = (grad * mask_zero[rows]).astype(BF)

    back_head_stage(
        zero, 1, third, weights.at[0], gains.at[0], biases.at[0], mask_zero, kept.at[0], resid, kept.at[3], to_patches, small, 0
    )
    out_patches = pltpu.make_async_copy(resid, patch_grad, local.at[0])
    out_patches.start()
    outer_stage(kept.at[3], xs, conv.at[0, 0])
    core3[0] = links.copy(conv.at[0, :, :, 1 - me.c], rc3.at[0], other)
    core3[0].start()
    sums = start_all([links.copy(small, sc, other)])
    p3[0] = spread(0)

    own2.wait()
    recv_all(z2)
    g2 = start_all([
        links.copy(out2.at[row_b], out2.at[row_b], me.at(q=me.chip(t))) for t in range(1, me.nq)
    ])
    recv_all(sums)
    sent_all(sums)
    small[...] += sc[...]
    sums_p = start_all([links.copy(small, sp.at[t - 1], me.at(q=me.chip(t))) for t in range(1, me.nq)])

    recv_all(p1)
    pieces = [
        pltpu.make_async_copy(
            (s1.at[j, rows_of(me.q * ra, ra, ra)] if t == 0 else rp1.at[t - 1, j]), kept.at[t, pl.ds(j * ra, ra)], local.at[6 + t * nz + j]
        )
        for t in range(me.nq)
        for j in range(nz)
    ]
    for copy in pieces:
        copy.start()
    for copy in pieces:
        copy.wait()
    for j in range(nz):
        fold(
            lambda at, v, j=j: f1.__setitem__((j, at), v.astype(BF)),
            [lambda at, j=j, t=t: kept[t, rows_of(j * ra + at.start, at.size, 16)] for t in range(me.nq)],
            ra, 32,
        )
    z1 = start_all([links.copy(f1.at[t], rz1.at[t - 1], me.at(k=me.deep(t))) for t in range(1, nz)])
    z3 = [None, None]
    my_cols = rows_of(me.r * width, width, 128)
    for b in (1, 0):
        recv_all(p3[b])
        for m in range(2):
            for j in range(nz):
                rows = pl.ds(j * R, R)
                total = conv[b, m, me.x, me.c, rows, my_cols].astype(F32)
                for t in range(1, me.nq):
                    total = total + rp3[b, t - 1, m, rows, :].astype(F32)
                f3[b, j, pl.ds(m * R, R)] = total.astype(BF)
        z3[b] = start_all([
            links.copy(f3.at[b, me.deep(t)], rz3.at[b, t - 1], me.at(k=me.deep(t))) for t in range(1, nz)
        ])

    sent_all(sums_p)
    recv_all(sums_p)
    for t in range(1, me.nq):
        small[...] += sp[t - 1]
    sums_z = start_all([links.copy(small, sz.at[t - 1], me.at(k=me.deep(t))) for t in range(1, nz)])

    recv_all(z1)
    row_a = rows_of(strip * ra, ra, ra)
    fold(
        lambda at, v: out1.__setitem__(rows_of(strip * ra + at.start, at.size, 16), v.astype(BF)),
        [lambda at: f1[0, at]] + [lambda at, t=t: rz1[t - 1, at] for t in range(1, nz)],
        ra, 32,
    )
    g1 = start_all([
        links.copy(out1.at[row_a], out1.at[row_a], me.at(q=me.chip(t))) for t in range(1, me.nq)
    ])
    g3 = []
    for b in (1, 0):
        recv_all(z3[b])
        total = f3[b, me.k].astype(F32)
        for t in range(1, nz):
            total = total + rz3[b, t - 1].astype(F32)
        out3[b, me.r] = total.astype(BF)
        g3 += start_all([
            links.copy(out3.at[b, me.r], out3.at[b, me.r], me.at(q=me.x * nrow + lax.rem(me.r + t, nrow)))
            for t in range(1, nrow)
        ])
    recv_all(g2)
    half_b = rows_of(me.c * me.nq * rb, me.nq * rb, me.nq * rb)
    h2 = start_all([links.copy(out2.at[half_b], out2.at[half_b], other)])
    recv_all(g1)
    half_a = rows_of(me.c * me.nq * ra, me.nq * ra, me.nq * ra)
    h1 = start_all([links.copy(out1.at[half_a], out1.at[half_a], other)])
    sent_all(sums_z)
    recv_all(sums_z)
    for t in range(1, nz):
        small[...] += sz[t - 1]
    recv_all(g3)
    recv_all(h1)
    recv_all(h2)
    out_patches.wait()
    for group_of in (core3, z2, p1, p3[0], p3[1], g2, z1, z3[0], z3[1], g1, g3, h1, h2, [rim0, rim1]):
        sent_all(group_of)


def spec(*kinds):
    return [pl.BlockSpec(memory_space=kind) for kind in kinds]


def run_readout(mesh, zero, one, patches, cot, read_in, read_out, read_bias, conv_in, conv_out, taps, gains, biases, masks, pool, pick):
    nz, ndp, nrow = mesh.shape["wide"], mesh.shape["dp"], mesh.shape["row"]
    nq = ndp // 2 * nrow
    T, C = pick.shape[0], patches.shape[1]
    hw, ow = read_out.shape[0], cot.shape[1]
    tall = nz * T
    rb = hw // (2 * nq)
    copies = 4 * (nz - 1) + 2 * (nq - 1) + 2 + (nz - 1) + 1 + (nq - 1) + 3
    bias_part = jnp.broadcast_to(read_bias[0:1], (8, hw))
    bias_out = jnp.broadcast_to(read_bias[1:2], (8, ow))
    ANY = pl.ANY
    return pl.pallas_call(
        functools.partial(readout_kernel, nz, ndp, nrow, zero, one),
        out_shape=[
            jax.ShapeDtypeStruct((tall, ow), BF),
            jax.ShapeDtypeStruct((T, C), F32),
            jax.ShapeDtypeStruct((nz, C // 2, hw), BF),
            jax.ShapeDtypeStruct((nz, rb, ow), BF),
            jax.ShapeDtypeStruct((nz, 1, hw), F32),
            jax.ShapeDtypeStruct((nz, C // 2, hw), BF),
            jax.ShapeDtypeStruct((nz, nq * rb, ow), BF),
            jax.ShapeDtypeStruct((nq - 1, nz, rb, ow), BF),
            jax.ShapeDtypeStruct((4, tall, hw), BF),
            jax.ShapeDtypeStruct((2, tall, hw), BF),
            jax.ShapeDtypeStruct((zero.count, 32, C), BF),
            jax.ShapeDtypeStruct((one.count, 16, C), BF),
        ],
        in_specs=spec(ANY, VMEM, ANY, ANY, VMEM, VMEM, ANY, ANY, VMEM, VMEM, VMEM, VMEM, VMEM, VMEM, VMEM),
        out_specs=spec(ANY, VMEM, ANY, VMEM, VMEM, ANY, ANY, ANY, ANY, ANY, VMEM, VMEM),
        scratch_shapes=[
            VMEM((nz, C, hw), BF),
            VMEM((nz, hw, ow), BF),
            VMEM((nz, 8, hw), F32),
            VMEM((tall, C), BF),
            VMEM((C, tall), BF),
            VMEM((nz, tall, hw), BF),
            VMEM((nz, tall, hw), BF),
            VMEM((nz - 1, T, C), BF),
            VMEM((nz - 1, T, C), BF),
            VMEM((nz, hw, ow), BF),
            VMEM((2, zero.cells + 2 * zero.width, 128), F32),
            VMEM((zero.count, 32, C), BF),
            VMEM((one.count, 16, C), BF),
            pltpu.SemaphoreType.DMA((copies,)),
            pltpu.SemaphoreType.DMA((copies,)),
            pltpu.SemaphoreType.DMA((7,)),
        ],
        compiler_params=pltpu.CompilerParams(
            collective_id=0, has_side_effects=True, vmem_limit_bytes=LIMIT
        ),
        name="readout",
    )(patches, cot, read_in, read_out, bias_part, bias_out, conv_in, conv_out, taps, gains, biases, *masks, pool, pick)


LIMIT = 62 * 1024 * 1024


def run_grads(mesh, zero, one, s1, f2, agrad, patches, keep_zero, keep_one, rim_zero, rim_one, conv_in, conv_out, taps, gains, biases, masks, pool, pick, small_in):
    nz, ndp, nrow = mesh.shape["wide"], mesh.shape["dp"], mesh.shape["row"]
    nq = ndp // 2 * nrow
    nx = ndp // 2
    C, hw = s1.shape[1] * 2, s1.shape[2]
    _, rb, ow = f2.shape
    ra = C // (2 * nq)
    R = C // (ndp * nz)
    tall = patches.shape[0]
    S = 40
    copies = 1 + 2 + (nz - 1) + (nq - 1) * 2 + 2 * (nq - 1) + (nq - 1) + (nz - 1) * 2 + 2 * (nz - 1) + (nq - 1) + 2 * (nrow - 1) + 2 + 2
    width = C // nrow
    ANY = pl.ANY
    return pl.pallas_call(
        functools.partial(grads_kernel, nz, ndp, nrow, zero, one),
        out_shape=[
            jax.ShapeDtypeStruct((C, hw), BF),
            jax.ShapeDtypeStruct((hw, nz * ow), BF),
            jax.ShapeDtypeStruct((2, nrow, 2 * R, width), BF),
            jax.ShapeDtypeStruct((S, C), F32),
            jax.ShapeDtypeStruct((tall, C), BF),
            jax.ShapeDtypeStruct((nq - 1, nz, ra, hw), BF),
        ],
        in_specs=spec(ANY, VMEM, VMEM, ANY, ANY, ANY, VMEM, VMEM, ANY, ANY, VMEM, VMEM, VMEM, VMEM, VMEM, VMEM, VMEM, VMEM),
        out_specs=spec(VMEM, ANY, VMEM, VMEM, ANY, ANY),
        scratch_shapes=[
            VMEM((tall, C), BF),
            VMEM((4, tall, C), BF),
            VMEM((2, tall, C), BF),
            VMEM((tall, C), BF),
            VMEM((tall, C), BF),
            VMEM((2, C, C), BF),
            VMEM((2, zero.cells + 2 * zero.width, 128), F32),
            VMEM((zero.count, 32, C), BF),
            VMEM((one.count, 16, C), BF),
            VMEM((zero.count, 32, C), BF),
            VMEM((one.count, 16, C), BF),
            VMEM((nz, ra, hw), BF),
            VMEM((nz - 1, ra, hw), BF),
            VMEM((2, 2, nx, 2, nz * R, C), BF),
            VMEM((2, 2, nx, nz * R, C), BF),
            VMEM((2, nq - 1, 2, nz * R, width), BF),
            VMEM((2, nz, 2 * R, width), BF),
            VMEM((2, nz - 1, 2 * R, width), BF),
            VMEM((S, C), F32),
            VMEM((nq - 1, S, C), F32),
            VMEM((nz - 1, S, C), F32),
            pltpu.SemaphoreType.DMA((copies,)),
            pltpu.SemaphoreType.DMA((copies,)),
            pltpu.SemaphoreType.DMA((6 + nq * nz,)),
        ],
        compiler_params=pltpu.CompilerParams(
            collective_id=1, has_side_effects=True, vmem_limit_bytes=LIMIT
        ),
        name="grads",
    )(s1, f2, agrad, patches, keep_zero, keep_one, rim_zero, rim_one, conv_in, conv_out, taps, gains, biases, *masks, pool, pick, small_in)


POOL = 12


eps_norm = 1e-06
exact_mode = lax.Precision.HIGHEST


def extended(cells, sides, width):
    for axis, dim in sides:
        count = lax.axis_size(axis)
        ends = count - 1
        head = lax.slice_in_dim(cells, 0, width, axis=dim)
        tail = lax.slice_in_dim(cells, cells.shape[dim] - width, cells.shape[dim], axis=dim)
        cells = jnp.concatenate(
            [
                lax.ppermute(tail, axis, [(i, (i + 1) % count) for i in range(ends)]),
                cells,
                lax.ppermute(head, axis, [((i + 1) % count, i) for i in range(ends)]),
            ],
            axis=dim,
        )
    return cells


def layer_norm(values, gain_row, bias_row):
    centre = jnp.mean(values, axis=-1, keepdims=True)
    centred = values - centre
    variance = jnp.mean(centred * centred, axis=-1, keepdims=True)
    return centred * lax.rsqrt(variance + eps_norm) * gain_row + bias_row


def head_piece(pre_values, gain_row, bias_row, live_mask):
    return jax.nn.silu(layer_norm(pre_values, gain_row, bias_row)) * live_mask


def tail_piece(source, third_pre, gain_row, bias_row, live_mask):
    return jax.nn.silu(source + layer_norm(third_pre, gain_row, bias_row)) * live_mask


def outer_sum(left_rows, right_rows):
    return lax.dot_general(
        left_rows, right_rows, (((0,), (0,)), ((), ())), preferred_element_type=jnp.float32
    )


def times_transposed(left_rows, weight):
    return lax.dot_general(
        left_rows, weight, (((1,), (1,)), ((), ())), preferred_element_type=jnp.float32
    )


def pad_columns(values):
    return jnp.pad(values, ((0, 0), (0, 0), (1, 1), (0, 0)))


def rows_forward(hidden_one):
    return extended(hidden_one, (("row", 1),), 1)


def rows_backward(second_low):
    return extended(second_low, (("row", 1),), 1)


def depth_apply(padded, tap_table, row_count, col_count):
    result = jnp.zeros((padded.shape[0], row_count, col_count, padded.shape[3]), jnp.float32)
    for offset in range(9):
        window = padded[
            :, offset // 3 : offset // 3 + row_count, offset % 3 : offset % 3 + col_count, :
        ]
        result = result + window.astype(jnp.float32) * tap_table[offset].astype(jnp.float32)
    return result


def block_forward(source, live_mask, weights):
    w_first, w_last, tap_table, gain_rows, bias_rows = weights
    grid_count, row_count, col_count, channels = source.shape
    flat_rows = source.astype(jnp.bfloat16).reshape(-1, channels)
    first_pre = jnp.dot(flat_rows, w_first, preferred_element_type=jnp.float32).reshape(
        source.shape
    )
    hidden_one = head_piece(first_pre, gain_rows[0], bias_rows[0], live_mask).astype(jnp.bfloat16)
    padded_one = pad_columns(rows_forward(hidden_one))
    second_pre = depth_apply(padded_one, tap_table, row_count, col_count)
    hidden_two = head_piece(second_pre, gain_rows[1], bias_rows[1], live_mask).astype(jnp.bfloat16)
    two_rows = hidden_two.reshape(-1, channels)
    third_pre = jnp.dot(two_rows, w_last, preferred_element_type=jnp.float32).reshape(source.shape)
    output = tail_piece(source, third_pre, gain_rows[2], bias_rows[2], live_mask)
    return (output, (flat_rows, first_pre, padded_one, second_pre, two_rows, third_pre))


def block_backward(output_grad, source, live_mask, weights, kept):
    w_first, w_last, tap_table, gain_rows, bias_rows = weights
    flat_rows, first_pre, padded_one, second_pre, two_rows, third_pre = kept
    grid_count, row_count, col_count, channels = source.shape
    _, tail_back = jax.vjp(
        functools.partial(tail_piece, live_mask=live_mask), source, third_pre, gain_rows[2], bias_rows[2]
    )
    residual_grad, third_grad, gain_three, bias_three = tail_back(output_grad)
    third_low = third_grad.astype(jnp.bfloat16).reshape(-1, channels)
    grad_last = outer_sum(two_rows, third_low)
    two_grad = times_transposed(third_low, w_last).reshape(source.shape)
    _, middle_back = jax.vjp(
        functools.partial(head_piece, live_mask=live_mask), second_pre, gain_rows[1], bias_rows[1]
    )
    second_grad, gain_two, bias_two = middle_back(two_grad)
    second_low = second_grad.astype(jnp.bfloat16)
    padded_grad = pad_columns(rows_backward(second_low))
    one_grad = depth_apply(padded_grad, tap_table[::-1], row_count, col_count)
    second_wide = second_low.astype(jnp.float32)
    tap_grads = []
    for offset in range(9):
        window = padded_one[
            :, offset // 3 : offset // 3 + row_count, offset % 3 : offset % 3 + col_count, :
        ]
        tap_grads.append(jnp.sum(second_wide * window.astype(jnp.float32), axis=(0, 1, 2)))
    _, first_back = jax.vjp(
        functools.partial(head_piece, live_mask=live_mask), first_pre, gain_rows[0], bias_rows[0]
    )
    first_grad, gain_one, bias_one = first_back(one_grad)
    first_low = first_grad.astype(jnp.bfloat16).reshape(-1, channels)
    grad_first = outer_sum(flat_rows, first_low)
    source_grad = residual_grad + times_transposed(first_low, w_first).reshape(source.shape)
    grads = (
        grad_first,
        grad_last,
        jnp.stack(tap_grads),
        jnp.stack([gain_one, gain_two, gain_three]),
        jnp.stack([bias_one, bias_two, bias_three]),
    )
    return (source_grad, grads)


def pool_weights(grid_side, row_shift, pooled_index, slot_index):
    place = slot_index - row_shift
    begin = pooled_index * grid_side // POOL
    finish = ((pooled_index + 1) * grid_side + POOL - 1) // POOL
    inside = (place >= begin) & (place < finish)
    return jnp.where(inside, 1.0, 0.0).astype(jnp.float32) / (finish - begin).astype(jnp.float32)


def plain(
    patches,
    grid_sizes,
    conv_in,
    conv_out,
    depth_taps,
    norm_gain,
    norm_bias,
    read_in,
    read_bias,
    read_out,
    cotangent,
):
    grid_count, local_rows, grid_width, channels = patches.shape
    row_place = lax.axis_index("row")
    slot_rows = row_place * local_rows + jnp.arange(local_rows, dtype=jnp.int32)
    column_index = jnp.arange(grid_width, dtype=jnp.int32)
    row_shift = (grid_width - grid_sizes) // 2
    row_live = (slot_rows[None, :] >= row_shift[:, None]) & (
        slot_rows[None, :] < (row_shift + grid_sizes)[:, None]
    )
    col_live = column_index[None, :] < grid_sizes[:, None]
    live_mask = (row_live[:, :, None] & col_live[:, None, :]).astype(jnp.float32)[..., None]
    weights_one = (conv_in[0], conv_out[0], depth_taps[0], norm_gain[0], norm_bias[0])
    weights_two = (conv_in[1], conv_out[1], depth_taps[1], norm_gain[1], norm_bias[1])
    source = patches.astype(jnp.float32) * live_mask
    encoded, kept_one = block_forward(source, live_mask, weights_one)
    pool_local = POOL // lax.axis_size("row")
    pooled_index = row_place * pool_local + jnp.arange(pool_local, dtype=jnp.int32)
    side_shaped = grid_sizes[:, None, None]
    row_pool = pool_weights(
        side_shaped, row_shift[:, None, None], pooled_index[None, :, None], slot_rows[None, None, :]
    )
    col_pool = pool_weights(
        side_shaped,
        0,
        jnp.arange(POOL, dtype=jnp.int32)[None, :, None],
        column_index[None, None, :],
    )
    pooled = jnp.einsum("gir,gjw,grwc->gijc", row_pool, col_pool, encoded, precision=exact_mode)
    all_live = jnp.ones((grid_count, pool_local, POOL, 1), jnp.float32)
    abstract, kept_two = block_forward(pooled, all_live, weights_two)
    token_rows = abstract.astype(jnp.bfloat16).reshape(-1, channels)
    gathered = lax.all_gather(token_rows, "wide", axis=0, tiled=True)
    gelu_exact = functools.partial(jax.nn.gelu, approximate=False)
    mixed_pre = jnp.dot(gathered, read_in, preferred_element_type=jnp.float32) + read_bias[0]
    hidden_wide, gelu_back = jax.vjp(gelu_exact, mixed_pre)
    hidden = hidden_wide.astype(jnp.bfloat16)
    partial_out = jnp.dot(hidden, read_out, preferred_element_type=jnp.float32)
    summed = (
        lax.psum_scatter(
            partial_out.astype(jnp.bfloat16), "wide", scatter_dimension=1, tiled=True
        ).astype(jnp.float32)
        + read_bias[1]
    )
    tokens = summed.astype(jnp.bfloat16).reshape(cotangent.shape)
    cot_local = cotangent.reshape(-1, cotangent.shape[-1])
    cot_all = lax.all_gather(cot_local, "wide", axis=1, tiled=True)
    hidden_grad = times_transposed(cot_all, read_out)
    mixed_grad = gelu_back(hidden_grad)[0].astype(jnp.bfloat16)
    grad_exit = outer_sum(hidden, cot_all)
    grad_entry = outer_sum(gathered, mixed_grad)
    bias_pair = jnp.stack(
        [
            jnp.sum(mixed_grad.astype(jnp.float32), axis=0),
            jnp.sum(cot_local.astype(jnp.float32), axis=0),
        ]
    )
    abstract_grad = lax.psum_scatter(
        times_transposed(mixed_grad, read_in).astype(jnp.bfloat16),
        "wide",
        scatter_dimension=0,
        tiled=True,
    ).astype(jnp.float32)
    grad_entry, bias_pair, grad_exit = (
        lax.psum(grad_entry.astype(jnp.bfloat16), ("dp", "row")).astype(jnp.float32),
        lax.psum(bias_pair.astype(jnp.bfloat16), ("dp", "row")).astype(jnp.float32),
        lax.psum(grad_exit.astype(jnp.bfloat16), ("dp", "row")).astype(jnp.float32),
    )
    pooled_grad, grads_two = block_backward(
        abstract_grad.reshape(abstract.shape), pooled, all_live, weights_two, kept_two
    )
    encoded_grad = jnp.einsum(
        "gir,gjw,gijc->grwc", row_pool, col_pool, pooled_grad, precision=exact_mode
    )
    source_grad, grads_one = block_backward(encoded_grad, source, live_mask, weights_one, kept_one)
    patch_grad = (source_grad * live_mask).astype(jnp.bfloat16)
    stacked = tuple((jnp.stack([grads_one[index], grads_two[index]]) for index in range(5)))
    totals = (
        lax.psum_scatter(stacked[0], ("dp", "wide"), scatter_dimension=2, tiled=True),
        lax.psum_scatter(stacked[1], ("dp", "wide"), scatter_dimension=2, tiled=True),
        lax.psum_scatter(stacked[2], ("dp", "wide"), scatter_dimension=2, tiled=True),
        lax.psum_scatter(stacked[3], ("dp", "wide"), scatter_dimension=2, tiled=True),
        lax.psum_scatter(stacked[4], ("dp", "wide"), scatter_dimension=2, tiled=True),
    )
    totals = (
        lax.psum(totals[0].astype(jnp.bfloat16), "row").astype(jnp.float32),
        lax.psum(totals[1].astype(jnp.bfloat16), "row").astype(jnp.float32),
        lax.psum(totals[2].astype(jnp.bfloat16), "row").astype(jnp.float32),
        lax.psum(totals[3].astype(jnp.bfloat16), "row").astype(jnp.float32),
        lax.psum(totals[4].astype(jnp.bfloat16), "row").astype(jnp.float32),
    )
    return (
        tokens,
        patch_grad,
        totals[0],
        totals[1],
        totals[2],
        totals[3],
        totals[4],
        grad_entry,
        bias_pair,
        grad_exit,
    )


def on_device(
    mesh,
    patches,
    grid_sizes,
    conv_in,
    conv_out,
    depth_taps,
    norm_gain,
    norm_bias,
    read_in,
    read_bias,
    read_out,
    cotangent,
):
    nz, ndp = mesh.shape["wide"], mesh.shape["dp"]
    grid_count, local_rows, grid_width, channels = patches.shape
    row_place = lax.axis_index("row")
    slot_rows = row_place * local_rows + jnp.arange(local_rows, dtype=jnp.int32)
    column_index = jnp.arange(grid_width, dtype=jnp.int32)
    row_shift = (grid_width - grid_sizes) // 2
    row_live = (slot_rows[None, :] >= row_shift[:, None]) & (
        slot_rows[None, :] < (row_shift + grid_sizes)[:, None]
    )
    col_live = column_index[None, :] < grid_sizes[:, None]
    live_mask = (row_live[:, :, None] & col_live[:, None, :]).astype(jnp.float32)[..., None]
    pool_local = POOL // lax.axis_size("row")
    pooled_index = row_place * pool_local + jnp.arange(pool_local, dtype=jnp.int32)
    side_shaped = grid_sizes[:, None, None]
    row_pool = pool_weights(
        side_shaped, row_shift[:, None, None], pooled_index[None, :, None], slot_rows[None, None, :]
    )
    col_pool = pool_weights(
        side_shaped,
        0,
        jnp.arange(POOL, dtype=jnp.int32)[None, :, None],
        column_index[None, None, :],
    )
    zero = Geometry(grid_count, local_rows, grid_width)
    one = Geometry(grid_count, pool_local, 16)
    col_wide = jnp.pad(col_pool, ((0, 0), (0, one.width - POOL), (0, 0)))
    pool = (row_pool[:, :, None, :, None] * col_wide[:, None, :, None, :]).reshape(grid_count, one.cells, zero.cells)
    places = jnp.arange(grid_count * pool_local * POOL, dtype=jnp.int32)
    places = places // POOL * one.width + places % POOL
    pick = (places[:, None] == jnp.arange(grid_count * one.cells, dtype=jnp.int32)[None, :]).astype(BF)
    mask_zero = live_mask.reshape(-1, 1)
    mask_one = (jnp.arange(grid_count * one.cells, dtype=jnp.int32) % one.width < POOL).astype(F32)[:, None]
    cot_local = cotangent.reshape(-1, cotangent.shape[-1])
    shared = (conv_in, conv_out, depth_taps.astype(F32), norm_gain, norm_bias, (mask_zero, mask_one), pool.astype(BF))
    flat = patches.reshape(-1, channels)
    tokens, agrad, s1, f2, hsum, _, _, _, keep_zero, keep_one, rim_zero, rim_one = run_readout(
        mesh, zero, one, flat, cot_local, read_in, read_out, read_bias, *shared, pick
    )
    tokens = tokens.reshape(cotangent.shape)
    cot_sum = jnp.sum(cot_local.astype(F32), axis=0)
    width = cot_sum.shape[0]
    cot_row = lax.dynamic_update_slice(
        jnp.zeros((nz * width,), F32), cot_sum, (lax.axis_index("wide") * width,)
    )
    small = jnp.concatenate([hsum.reshape(-1, channels), cot_row.reshape(-1, channels)])
    out1, out2, out3, small, patch_grad, _ = run_grads(
        mesh, zero, one, s1, f2, agrad, flat, keep_zero, keep_one, rim_zero, rim_one, *shared, pick.T, small
    )
    patch_grad = patch_grad.reshape(patches.shape)
    R = channels // (ndp * nz)
    out3 = out3.reshape(2, -1, 2, R, out3.shape[-1]).transpose(0, 2, 1, 4, 3).reshape(2, 2, channels, R).astype(F32)
    place = lax.axis_index("dp") * nz + lax.axis_index("wide")
    own = lax.dynamic_slice_in_dim(small, place * R, R, axis=1)
    own = own[:32].reshape(2, 16, R)
    taps, gains, biases = own[:, 0:9], own[:, 9:12], own[:, 12:15]
    bias_pair = lax.dynamic_slice_in_dim(small[32:40].reshape(2, -1), lax.axis_index("wide") * width, width, axis=1)
    return (
        tokens,
        patch_grad,
        out3[:, 0],
        out3[:, 1],
        taps,
        gains,
        biases,
        out1.astype(F32),
        bias_pair,
        out2.astype(F32),
    )


def fits(mesh):
    return mesh.shape["wide"] == 4 and mesh.shape["dp"] % 2 == 0 and mesh.shape["row"] == 2


def solution(mesh):

    placed = (
        P(("dp", "wide"), "row", None, None),
        P(("dp", "wide")),
        P(),
        P(),
        P(),
        P(),
        P(),
        P(None, "wide"),
        P(None, "wide"),
        P("wide", None),
        P("dp", "row", None, "wide"),
    )
    return jax.shard_map(
        functools.partial(on_device, mesh) if fits(mesh) else plain,
        mesh=mesh,
        in_specs=placed,
        out_specs=(
            P("dp", "row", None, "wide"),
            P(("dp", "wide"), "row", None, None),
            P(None, None, ("dp", "wide")),
            P(None, None, ("dp", "wide")),
            P(None, None, ("dp", "wide")),
            P(None, None, ("dp", "wide")),
            P(None, None, ("dp", "wide")),
            P(None, "wide"),
            P(None, "wide"),
            P("wide", None),
        ),
        check_vma=False,
    )
```

```python
import functools

import jax
import jax.numpy as jnp
from jax import lax
from jax.experimental import pallas as pl
from jax.experimental.pallas import tpu as pltpu
from jax.sharding import PartitionSpec as P

MESH = pl.DeviceIdType.MESH
BF = jnp.bfloat16
F32 = jnp.float32
VMEM = pltpu.VMEM


class Place:
    def __init__(self, nz, ndp, nrow):
        self.nz, self.ndp, self.nrow = nz, ndp, nrow
        self.nx = ndp // 2
        self.nq = self.nx * nrow
        self.k = lax.axis_index("wide")
        self.r = lax.axis_index("row")
        d = lax.axis_index("dp")
        self.c = lax.rem(d, 2)
        self.x = d // 2
        self.q = self.x * nrow + self.r
        self.qx = (1 - self.x) * nrow + self.r
        self.qy = self.x * nrow + (1 - self.r)
        self.qd = (1 - self.x) * nrow + (1 - self.r)

    def at(self, q=None, c=None, k=None):
        q = self.q if q is None else q
        c = self.c if c is None else c
        k = self.k if k is None else k
        return {"dp": (q // self.nrow) * 2 + c, "row": lax.rem(q, self.nrow), "wide": k}

    def chip(self, t):
        return lax.rem(self.q + t, self.nq)

    def deep(self, t):
        return lax.rem(self.k + t, self.nz)

    def peers(self):
        return (
            [self.at(q=self.chip(t)) for t in range(1, self.nq)]
            + [self.at(c=1 - self.c)]
            + [self.at(k=self.deep(t)) for t in range(1, self.nz)]
        )

    def greet(self):
        barrier = pltpu.get_barrier_semaphore()
        peers = self.peers()
        for peer in peers:
            pl.semaphore_signal(barrier, inc=1, device_id=peer, device_id_type=MESH)
        pl.semaphore_wait(barrier, len(peers))


class Links:
    def __init__(self, send, recv):
        self.send, self.recv, self.used = send, recv, 0

    def copy(self, src, dst, peer):
        at = self.used
        self.used += 1
        assert self.used <= self.send.shape[0]
        return pltpu.make_async_remote_copy(
            src_ref=src, dst_ref=dst, send_sem=self.send.at[at], recv_sem=self.recv.at[at],
            device_id=peer, device_id_type=MESH,
        )


def start_all(copies):
    for copy in copies:
        copy.start()
    return copies


def recv_all(copies):
    for copy in copies:
        copy.wait_recv()


def sent_all(copies):
    for copy in copies:
        copy.wait_send()


class Spread:
    def __init__(self, me, links, strip):
        self.me, self.links, self.strip = me, links, strip
        self.first = self.second = ()

    def start(self):
        me = self.me
        own = self.strip(me.q, None)
        self.first = start_all([self.links.copy(own, own, me.at(q=q)) for q in (me.qx, me.qy)])

    def pass_on(self):
        me = self.me
        along_y = self.strip(me.qx, 0)
        along_x = self.strip(me.qy, 1)
        self.second = [
            self.links.copy(along_y, along_y, me.at(q=me.qy)),
            self.links.copy(along_x, along_x, me.at(q=me.qx)),
        ]
        for arrived, copy in zip(self.first, self.second):
            arrived.wait_recv()
            copy.start()

    def finish(self):
        recv_all(self.second)

    def sent(self):
        sent_all(self.first)
        sent_all(self.second)


class Gather:
    def __init__(self, me, links, chunk, slot):
        self.me, self.links, self.chunk, self.slot = me, links, chunk, slot
        self.early = [[], []]
        self.late = [None, None]

    def start(self, half):
        me = self.me
        to = me.qx if half == 0 else me.qy
        self.early[half] = start_all([
            self.links.copy(self.chunk(q, half), self.slot(i, half), me.at(q=to)) for i, q in ((1, me.qd), (0, to))
        ])

    def passing(self, half):
        self.early[half][0].wait_recv()
        return self.me.qy if half == 0 else self.me.qx

    def pass_on(self, half, total):
        to = self.me.qy if half == 0 else self.me.qx
        self.late[half] = self.links.copy(total, self.slot(2, half), self.me.at(q=to))
        self.late[half].start()

    def finish(self):
        for half in range(2):
            self.early[half][1].wait_recv()
            self.late[half].wait_recv()

    def sent(self):
        for half in range(2):
            sent_all(self.early[half])
            self.late[half].wait_send()


def rows_of(start, size, unit):
    return pl.ds(pl.multiple_of(start, unit), size)


def fold(out, parts, rows, step):
    def body(i, carry):
        at = rows_of(i * step, step, step)
        total = parts[0](at).astype(F32)
        for part in parts[1:]:
            total = total + part(at).astype(F32)
        out(at, total)
        return carry

    lax.fori_loop(0, rows // step, body, 0)


def nt(a, b):
    return lax.dot_general(a, b, (((1,), (1,)), ((), ())), preferred_element_type=F32)


def nn(a, b):
    return jnp.dot(a, b, preferred_element_type=F32)


def tn(a, b):
    return lax.dot_general(a, b, (((0,), (0,)), ((), ())), preferred_element_type=F32)


def gelu_pair(v):
    dense = jnp.exp(-0.5 * v * v)
    s = 1.0 / (1.0 + (0.3275911 * 0.7071067811865476) * jnp.abs(v))
    poly = s * (0.254829592 + s * (-0.284496736 + s * (1.421413741 + s * (-1.453152027 + s * 1.061405429))))
    tail = 0.5 * poly * dense
    phi = jnp.where(v >= 0, 1.0 - tail, tail)
    return v * phi, phi + v * dense * 0.3989422804014327


def normal(v):
    centred = v - jnp.mean(v, axis=-1, keepdims=True)
    scale = lax.rsqrt(jnp.mean(centred * centred, axis=-1, keepdims=True) + 1e-06)
    return centred * scale, scale


def sigmoid(v):
    return 1.0 / (1.0 + jnp.exp(-v))


def silu_of(v):
    return v * sigmoid(v)


def column_masks(cmask, width):
    place = lax.rem(lax.broadcasted_iota(jnp.int32, cmask.shape[1:], 0), width)
    cmask[0] = jnp.where(place != 0, 1.0, 0.0)
    cmask[1] = jnp.where(place != width - 1, 1.0, 0.0)


def windows(cells, rim, first, masks):
    middle = jnp.concatenate([rim * (1.0 - first), cells, rim * first], axis=0)
    count = middle.shape[0]
    left, right = pltpu.roll(middle, 1, 0), pltpu.roll(middle, count - 1, 0)
    if masks is not None:
        left, right = left * masks[0], right * masks[1]
    return left, middle, right


class Geometry:
    def __init__(self, count, height, width):
        self.count, self.height, self.width = count, height, width
        self.cells = height * width

    def rows(self, g):
        return rows_of(g * self.cells, self.cells, 16)


def head_stage(shape, per, x_of, w, gains, biases, mask, pre, hidden, rim_send, first):
    cells = shape.cells * per

    def body(i, carry):
        rows = rows_of(i * cells, cells, 16)
        x = x_of(rows)
        value = nn(x, w[...])
        pre[rows] = value.astype(BF)
        n, _ = normal(value)
        h = silu_of(n * gains[0:1] + biases[0:1]) * mask[rows]
        hidden[rows] = h.astype(BF)
        for g in range(per):
            at = g * shape.cells
            top = h[at : at + shape.width]
            bottom = h[at + shape.cells - shape.width : at + shape.cells]
            rim_send[i * per + g, pl.ds(0, shape.width)] = (bottom * first + top * (1.0 - first)).astype(BF)
        return carry

    lax.fori_loop(0, shape.count // per, body, 0)


def depth_stage(shape, hidden, rim, taps, cmask, pre, first, channels):
    def body(i, carry):
        g, l = i // (channels // 128), lax.rem(i, channels // 128)
        rows, lanes = shape.rows(g), rows_of(l * 128, 128, 128)
        shifted = windows(
            hidden[rows, lanes].astype(F32),
            rim[g, pl.ds(0, shape.width), lanes].astype(F32),
            first,
            None if cmask is None else (cmask[0], cmask[1]),
        )
        total = jnp.zeros((shape.cells, 128), F32)
        for a in range(3):
            for b in range(3):
                piece = shifted[b][a * shape.width : a * shape.width + shape.cells]
                total = total + piece * taps[3 * a + b : 3 * a + b + 1, lanes]
        pre[rows, lanes] = total.astype(BF)
        return carry

    lax.fori_loop(0, shape.count * (channels // 128), body, 0)


def tail_stage(shape, per, x, w, gains, biases, mask, pre_two, pre_three, result):
    cells = shape.cells * per

    def body(i, carry):
        rows = rows_of(i * cells, cells, 16)
        n, _ = normal(pre_two[rows].astype(F32))
        h = (silu_of(n * gains[1:2] + biases[1:2]) * mask[rows]).astype(BF)
        value = nn(h, w[...])
        pre_three[rows] = value.astype(BF)
        n, _ = normal(value)
        out = silu_of(x[rows].astype(F32) + n * gains[2:3] + biases[2:3]) * mask[rows]
        result(i, rows, out)
        return carry

    lax.fori_loop(0, shape.count // per, body, 0)


def slope_of(v, s):
    return s * (1.0 + v * (1.0 - s))


def norm_back(n, scale, grad, gain, sums, at):
    sums[at : at + 1] += jnp.sum(grad * n, axis=0, keepdims=True)
    sums[at + 3 : at + 4] += jnp.sum(grad, axis=0, keepdims=True)
    dn = grad * gain
    return scale * (dn - jnp.mean(dn, axis=-1, keepdims=True) - n * jnp.mean(dn * n, axis=-1, keepdims=True))


def back_tail_stage(shape, per, grad_of, x, w, gains, biases, mask, pre_two, pre_three, resid, third, hidden_two, second, edge, first, sums, base):
    cells = shape.cells * per

    def body(i, carry):
        rows = rows_of(i * cells, cells, 16)
        live = mask[rows]
        n, scale = normal(pre_three[rows].astype(F32))
        v = x[rows].astype(F32) + n * gains[2:3] + biases[2:3]
        grad = grad_of(i) * slope_of(v, sigmoid(v)) * live
        resid[rows] = grad.astype(BF)
        low = norm_back(n, scale, grad, gains[2:3], sums, base + 11).astype(BF)
        third[rows] = low
        grad = nt(low, w[...])
        n, scale = normal(pre_two[rows].astype(F32))
        v = n * gains[1:2] + biases[1:2]
        s = sigmoid(v)
        hidden_two[rows] = (v * s * live).astype(BF)
        grad = norm_back(n, scale, grad * live * slope_of(v, s), gains[1:2], sums, base + 10)
        second[rows] = grad.astype(BF)
        for g in range(per):
            at = g * shape.cells
            top = grad[at : at + shape.width]
            bottom = grad[at + shape.cells - shape.width : at + shape.cells]
            edge[i * per + g, pl.ds(0, shape.width)] = (bottom * first + top * (1.0 - first)).astype(BF)
        return carry

    lax.fori_loop(0, shape.count // per, body, 0)


def back_depth_stage(shape, second, rim, hidden, hidden_rim, taps, cmask, result, first, channels, sums, base):
    masks = None if cmask is None else (cmask[0], cmask[1])

    def body(i, carry):
        g, l = i // (channels // 128), lax.rem(i, channels // 128)
        rows, lanes = shape.rows(g), rows_of(l * 128, 128, 128)
        edge = pl.ds(0, shape.width)
        grad = second[rows, lanes].astype(F32)
        shifted = windows(grad, rim[g, edge, lanes].astype(F32), first, masks)
        total = jnp.zeros((shape.cells, 128), F32)
        for a in range(3):
            for b in range(3):
                at = (2 - a) * shape.width
                total = total + shifted[2 - b][at : at + shape.cells] * taps[3 * a + b : 3 * a + b + 1, lanes]
        result[rows, lanes] = total.astype(BF)
        shifted = windows(hidden[rows, lanes].astype(F32), hidden_rim[g, edge, lanes].astype(F32), first, masks)
        for a in range(3):
            for b in range(3):
                at = a * shape.width
                line = base + 3 * a + b
                sums[line : line + 1, lanes] += jnp.sum(
                    grad * shifted[b][at : at + shape.cells], axis=0, keepdims=True
                )
        return carry

    lax.fori_loop(0, shape.count * (channels // 128), body, 0)


def back_head_stage(shape, per, one_grad, w, gains, biases, mask, pre_one, resid, first_low, result, sums, base):
    cells = shape.cells * per

    def body(i, carry):
        rows = rows_of(i * cells, cells, 16)
        n, scale = normal(pre_one[rows].astype(F32))
        v = n * gains[0:1] + biases[0:1]
        grad = one_grad[rows].astype(F32) * mask[rows] * slope_of(v, sigmoid(v))
        low = norm_back(n, scale, grad, gains[0:1], sums, base + 9).astype(BF)
        first_low[rows] = low
        result(i, rows, resid[rows].astype(F32) + nt(low, w[...]))
        return carry

    lax.fori_loop(0, shape.count // per, body, 0)


def outer_stage(left, right, out):
    high = out.shape[2]

    def body(i, carry):
        at = rows_of(i * high, high, 128)
        out[i // 2, lax.rem(i, 2)] = tn(left[:, at], right[...]).astype(BF)
        return carry

    lax.fori_loop(0, out.shape[0] * 2, body, 0)


def readout_kernel(
    nz, ndp, nrow, zero, one,
    patches, cot, rin_part, rout_part, bias_part, bias_out, conv_in, conv_out, taps, gains, biases, mask_zero, mask_one, pool, pick,
    tokens, agrad, s1, f2, hsum, rc1, rc2, rp2, keep_zero, keep_one, rim_zero, rim_one,
    rin, rout, bias, abst, abst_t, hid, mg, ag_send, ag_recv, s2, cmask, edge_zero, edge_one, send, recv, local,
):
    me = Place(nz, ndp, nrow)
    links = Links(send, recv)
    T, C = agrad.shape
    hw, ow = rout.shape[1], rout.shape[2]
    tall = nz * T
    np_ = 2 * me.nq
    strip = me.c * me.nq + me.q
    ra, rb = C // np_, hw // np_
    me.greet()

    own = [
        pltpu.make_async_copy(rin_part, rin.at[0], local.at[0]),
        pltpu.make_async_copy(rout_part.at[:, rows_of(me.k * ow, ow, 128)], rout.at[0], local.at[1]),
    ]
    convs = [
        pltpu.make_async_copy(part.at[b], s2.at[2 * b + i], local.at[2 + 2 * b + i])
        for b in range(2)
        for i, part in enumerate((conv_in, conv_out))
    ]
    given = pltpu.make_async_copy(patches, mg.at[0], local.at[6])
    convs[0].start()
    given.start()
    za, zb, zc = [], [], []
    row_a = rows_of(strip * ra, ra, ra)
    row_b = rows_of(strip * rb, rb, rb)
    for t in range(1, nz):
        there = lax.rem(me.k + nz - t, nz)
        za.append(links.copy(rin_part.at[row_a], rin.at[t, row_a], me.at(k=there)))
        zc.append(links.copy(bias_part, bias.at[t], me.at(k=there)))
    start_all(za)
    start_all(zc)
    for t in range(1, nz):
        there = lax.rem(me.k + nz - t, nz)
        zb.append(links.copy(
            rout_part.at[row_b, rows_of(there * ow, ow, 128)], rout.at[t, row_b], me.at(k=there)))
    start_all(zb)
    for copy in convs[1:] + own:
        copy.start()
    bias[0] = bias_part[...]
    column_masks(cmask, zero.width)

    def strips(weights, height):
        wide = weights.shape[2]

        def strip(q, half):
            rows = rows_of((me.c * me.nq + q) * height, height, height)
            cols = pl.ds(0, wide) if half is None else pl.ds(half * (wide // 2), wide // 2)
            return weights.at[pl.ds(1, nz - 1), rows, cols]

        return Spread(me, links, strip)

    def between_cores(weights, height):
        half = rows_of(me.c * (me.nq * height), me.nq * height, height)
        part = weights.at[pl.ds(1, nz - 1), half]
        return start_all([links.copy(part, part, me.at(c=1 - me.c))])

    pa, pb = strips(rin, ra), strips(rout, rb)

    first = (1 - me.r).astype(F32)
    neighbour = me.at(q=me.x * nrow + (nrow - 1 - me.r))

    def masked(rows):
        x = (mg[0, rows].astype(F32) * mask_zero[rows]).astype(BF)
        mg[0, rows] = x
        return x

    convs[0].wait()
    given.wait()
    head_stage(zero, 1, masked, s2.at[0], gains.at[0], biases.at[0], mask_zero, hid.at[0], hid.at[1], edge_zero, first)
    rim0 = links.copy(edge_zero, rim_zero, neighbour)
    rim0.start()
    recv_all(za)
    pa.start()
    rim0.wait_recv()
    depth_stage(zero, hid.at[1], rim_zero, taps.at[0], cmask, hid.at[2], first, C)
    for copy in convs[1:]:
        copy.wait()

    def to_pooled(i, rows, out):
        mg[1, one.rows(i)] = nn(pool[i], out.astype(BF)).astype(BF)

    pa.pass_on()
    tail_stage(zero, 1, mg.at[0], s2.at[1], gains.at[0], biases.at[0], mask_zero, hid.at[2], hid.at[3], to_pooled)
    kept_zero = pltpu.make_async_copy(hid, keep_zero, local.at[2])
    kept_zero.start()
    recv_all(zb)
    pb.start()
    pa.finish()
    ca = between_cores(rin, ra)
    all_one = one.cells * one.count
    part = [mg.at[1 + i // 3, pl.ds((i % 3) * all_one, all_one)] for i in range(5)]
    pooled, pre_one, hidden, pre_two, pre_three = part
    head_stage(one, one.count, lambda rows: pooled[rows], s2.at[2], gains.at[1], biases.at[1], mask_one, pre_one, hidden, edge_one, first)
    rim1 = links.copy(edge_one, rim_one, neighbour)
    rim1.start()
    rim1.wait_recv()
    depth_stage(one, hidden, rim_one, taps.at[1], None, pre_two, first, C)
    here = rows_of(me.k * T, T, 16)

    def to_tokens(i, rows, out):
        abst[here] = nn(pick[...], out.astype(BF)).astype(BF)

    tail_stage(one, one.count, pooled, s2.at[3], gains.at[1], biases.at[1], mask_one, pre_two, pre_three, to_tokens)
    kept_one = pltpu.make_async_copy(mg.at[pl.ds(1, 2)], keep_one, local.at[3])
    kept_one.start()
    zg = start_all([
        links.copy(abst.at[here], abst.at[here], me.at(k=lax.rem(me.k + nz - t, nz))) for t in range(1, nz)
    ])
    pb.pass_on()
    for copy in own + [kept_zero, kept_one]:
        copy.wait()
    recv_all(zc)
    recv_all(ca)

    hsum[...] = jnp.zeros_like(hsum)
    ag = [None] + [
        links.copy(ag_send.at[t - 1], ag_recv.at[t - 1], me.at(k=me.deep(t))) for t in range(1, nz)
    ]
    NT = min(512, hw)

    def hidden_group(t):
        rows = rows_of(me.deep(t) * T, T, 16)

        def front(i, carry):
            u = i // (hw // NT)
            cols = rows_of(lax.rem(i, hw // NT) * NT, NT, 128)
            value, slope = gelu_pair(nn(abst[rows], rin[u, :, cols]) + bias[u, 0:1, cols])
            hid[u, rows, cols] = value.astype(BF)
            mg[u, rows, cols] = slope.astype(BF)
            return carry

        lax.fori_loop(0, nz * (hw // NT), front, 0)

    for t in range(nz):
        if t:
            zg[t - 1].wait_recv()
        hidden_group(t)
        if t == 1:
            pb.finish()
            cb = between_cores(rout, rb)

    HT = 256

    def g2(i, carry):
        u = i // (hw // HT)
        at = rows_of(lax.rem(i, hw // HT) * HT, HT, HT)
        s2[me.deep(u), at, :] = tn(hid[u, :, at], cot[...]).astype(BF)
        return carry

    lax.fori_loop(0, nz * (hw // HT), g2, 0)
    half = me.nq * rb
    theirs = rows_of((1 - me.c) * half, half, half)
    core2 = start_all([links.copy(s2.at[:, theirs], rc2, me.at(c=1 - me.c))])
    abst_t[...] = abst[...].T
    recv_all(cb)

    def unit(i, carry):
        u = i // (hw // 256)
        cols = rows_of(lax.rem(i, hw // 256) * 256, 256, 256)
        grad = (nt(cot[...], rout[u, cols, :]) * mg[u, :, cols].astype(F32)).astype(BF)
        mg[u, :, cols] = grad
        hsum[me.deep(u), 0:1, cols] += jnp.sum(grad.astype(F32), axis=0, keepdims=True)
        return carry

    lax.fori_loop(0, nz * (hw // 256), unit, 0)

    recv_all(core2)
    mine2 = me.c * half
    gather2 = Gather(
        me, links,
        lambda q, h: s2.at[pl.ds(h * (nz // 2), nz // 2), rows_of(mine2 + q * rb, rb, rb)],
        lambda i, h: rp2.at[i, pl.ds(h * (nz // 2), nz // 2)],
    )
    piece = 256
    parts = half // piece
    loads = [
        pltpu.make_async_copy(
            rc2.at[i // parts, pl.ds(i % parts * piece, piece)], ag_send.at[i % 2, pl.ds(0, piece)], local.at[i % 2]
        )
        for i in range(nz * parts)
    ]
    loads[0].start()
    for i in range(nz * parts):
        loads[i].wait()
        if i + 1 < nz * parts:
            loads[i + 1].start()
        j, where = i // parts, mine2 + i % parts * piece
        fold(
            lambda at, v, j=j, w=where: s2.__setitem__((j, rows_of(w + at.start, at.size, 16)), v.astype(BF)),
            [
                lambda at, j=j, w=where: s2[j, rows_of(w + at.start, at.size, 16)],
                lambda at, i=i: ag_send[i % 2, at],
            ],
            piece, 32,
        )
        if (i + 1) % (nz // 2 * parts) == 0:
            gather2.start(i // (nz // 2 * parts))

    def group_back(t):
        rows = rows_of(me.deep(t) * T, T, 16)

        def back(i, carry):
            at = rows_of(i * 256, 256, 256)
            total = nt(mg[0, rows, :], rin[0, at, :])
            for u in range(1, nz):
                total = total + nt(mg[u, rows, :], rin[u, at, :])
            if t == 0:
                agrad[:, at] = total
            else:
                ag_send[t - 1, :, at] = total.astype(BF)
            return carry

        lax.fori_loop(0, C // 256, back, 0)
        if t:
            ag[t].start()

    for t in (*range(1, nz), 0):
        group_back(t)


    sent_all(ca)
    pa.sent()

    def g1(i, carry):
        u = i // (C // 256)
        at = rows_of(lax.rem(i, C // 256) * 256, 256, 256)
        rin[u, at, :] = nn(abst_t[at, :], mg[u]).astype(BF)
        return carry

    lax.fori_loop(0, nz * (C // 256), g1, 0)
    low = me.nq * ra
    core1 = links.copy(rin.at[:, rows_of((1 - me.c) * low, low, low)], rc1, me.at(c=1 - me.c))
    core1.start()

    for h in range(2):
        to = gather2.passing(h)
        block = range(h * (nz // 2), (h + 1) * (nz // 2))
        loads = [pltpu.make_async_copy(rp2.at[1, j], mg.at[j, pl.ds(0, rb)], local.at[j]) for j in block]
        for copy in loads:
            copy.start()
        for j, copy in zip(block, loads):
            copy.wait()
            where = mine2 + to * rb
            fold(
                lambda at, v, j=j, w=where: s2.__setitem__((j, rows_of(w + at.start, at.size, 16)), v.astype(BF)),
                [lambda at, j=j, w=where: s2[j, rows_of(w + at.start, at.size, 16)], lambda at, j=j: mg[j, at]],
                rb, min(rb, 32),
            )
        gather2.pass_on(h, gather2.chunk(to, h))

    sent_all(zg)

    def f2_body(i, carry):
        at = rows_of(i * 256, 256, 256)
        total = nn(hid[0], rout[0, :, at]) + bias_out[0:1, at]
        for u in range(1, nz):
            total = total + nn(hid[u], rout[u, :, at])
        abst[:, at] = total.astype(BF)
        return carry

    lax.fori_loop(0, ow // 256, f2_body, 0)
    out_tokens = pltpu.make_async_copy(abst, tokens, local.at[6])
    out_tokens.start()
    recv_all(ag[1:])
    fold(
        lambda at, v: agrad.__setitem__(at, v),
        [lambda at: agrad[at]] + [lambda at, t=t: ag_recv[t - 1, at] for t in range(1, nz)],
        T, 32,
    )
    core1.wait_recv()
    loads = [pltpu.make_async_copy(rc1.at[u], mg.at[u, pl.ds(0, low)], local.at[u]) for u in range(nz)]
    for copy in loads:
        copy.start()
    outs = []
    for u in range(nz):
        loads[u].wait()
        fold(
            lambda at, v, u=u: rin.__setitem__((u, rows_of(me.c * low + at.start, at.size, 16)), v.astype(BF)),
            [lambda at, u=u: rin[u, rows_of(me.c * low + at.start, at.size, 16)], lambda at, u=u: mg[u, at]],
            low, 32,
        )
        outs.append(pltpu.make_async_copy(rin.at[u, rows_of(me.c * low, low, low)], s1.at[u], local.at[u]))
        outs[-1].start()
    gather2.finish()
    for copy in outs:
        copy.wait()
    loads = [
        pltpu.make_async_copy(rp2.at[i], mg.at[pl.ds(0, nz), pl.ds(i * rb, rb)], local.at[i]) for i in (0, 2)
    ]
    for copy in loads:
        copy.start()
    for copy in loads:
        copy.wait()
    for j in range(nz):
        fold(
            lambda at, v, j=j: f2.__setitem__((j, at), v.astype(BF)),
            [lambda at, j=j: s2[j, rows_of(strip * rb + at.start, at.size, 16)]]
            + [lambda at, j=j, i=i: mg[j, rows_of(i * rb + at.start, at.size, 16)] for i in (0, 2)],
            rb, min(rb, 32),
        )
    out_tokens.wait()
    for group in (pb, gather2):
        group.sent()
    for group_of in (za, zb, zc, cb, core2, ag[1:], [rim0, rim1, core1]):
        sent_all(group_of)


def grads_kernel(
    nz, ndp, nrow, zero, one,
    s1, f2, agrad, patches, keep_zero, keep_one, rim_zero, rim_one, conv_in, conv_out, taps, gains, biases,
    mask_zero, mask_one, pool, pick, small_in,
    out1, out2, out3, small, patch_grad, rp1,
    xs, kept, keep, third, resid, weights, cmask, edge_zero, edge_one, got_zero, got_one,
    sent_on, f1, rz1, conv, rc3, rp3, f3, rz3, sc, sp, sz, send, recv, local,
):
    me = Place(nz, ndp, nrow)
    links = Links(send, recv)
    C, hw = out1.shape
    ow = f2.shape[2]
    np_ = 2 * me.nq
    strip = me.c * me.nq + me.q
    ra, rb = C // np_, hw // np_
    width = C // nrow
    R = out3.shape[2] // 2
    other = me.at(c=1 - me.c)
    first = (1 - me.r).astype(F32)
    neighbour = me.at(q=me.x * nrow + (nrow - 1 - me.r))
    me.greet()

    loads = [
        pltpu.make_async_copy(keep_one, keep, local.at[0]),
        pltpu.make_async_copy(conv_out.at[1], weights.at[1], local.at[1]),
        pltpu.make_async_copy(conv_in.at[1], weights.at[0], local.at[2]),
        pltpu.make_async_copy(keep_zero, kept, local.at[3]),
        pltpu.make_async_copy(patches, xs, local.at[4]),
    ]
    for copy in loads:
        copy.start()
    lead = nz // 2
    gather1 = Gather(
        me, links,
        lambda q, h: s1.at[pl.ds(h * lead, lead), rows_of(q * ra, ra, ra)],
        lambda i, h: rp1.at[i, pl.ds(h * lead, lead)],
    )
    gather1.start(0)
    gather1.start(1)
    row_b = rows_of(strip * rb, rb, rb)
    col_k = rows_of(me.k * ow, ow, 128)
    z2 = start_all([
        links.copy(f2.at[me.deep(t)], out2.at[row_b, col_k], me.at(k=me.deep(t))) for t in range(1, nz)
    ])
    own2 = pltpu.make_async_copy(f2.at[me.k], out2.at[row_b, col_k], local.at[5])
    own2.start()
    small[...] = jnp.zeros_like(small)
    small[32:40] = small_in[...]
    column_masks(cmask, zero.width)

    def spread(b):
        core3[b].wait_recv()
        for m in range(2):
            for x in range(me.nx):
                fold(
                    lambda at, v, i=(b, m, x, me.c): conv.__setitem__((*i, at), v.astype(BF)),
                    [lambda at, i=(b, m, x, me.c): conv[(*i, at)], lambda at, i=(b, m, x): rc3[(*i, at)]],
                    nz * R, 32,
                )
        gather = Gather(
            me, links,
            lambda q, h: conv.at[b, h, q // nrow, me.c, :, rows_of(lax.rem(q, nrow) * width, width, 128)],
            lambda i, h: rp3.at[b, i, h],
        )
        gather.start(1)
        gather.start(0)
        return gather

    def spread_on(b):
        for h in (1, 0):
            to = p3[b].passing(h)
            cols = rows_of(lax.rem(to, nrow) * width, width, 128)
            x = to // nrow
            fold(
                lambda at, v: conv.__setitem__((b, h, x, me.c, at, cols), v.astype(BF)),
                [lambda at: conv[b, h, x, me.c, at, cols], lambda at: rp3[b, 1, h, at, :]],
                nz * R, 32,
            )
            p3[b].pass_on(h, p3[b].chunk(to, h))

    core3, p3 = [None, None], [None, None]

    all_one = one.cells * one.count
    pooled, pre_one, hidden, pre_two, pre_three, pooled_grad = [
        keep.at[i // 3, pl.ds((i % 3) * all_one, all_one)] for i in range(6)
    ]
    third_one, resid_one = third.at[pl.ds(0, all_one)], resid.at[pl.ds(0, all_one)]
    loads[0].wait()
    loads[1].wait()
    back_tail_stage(
        one, one.count, lambda i: nn(pick[...], agrad[...].astype(BF)), pooled, weights.at[1], gains.at[1], biases.at[1], mask_one,
        pre_two, pre_three, resid_one, third_one, pre_three, pre_two, edge_one, first, small, 16,
    )
    rim1 = links.copy(edge_one, got_one, neighbour)
    rim1.start()
    outer_stage(third_one, pre_three, conv.at[1, 1])
    rim1.wait_recv()
    back_depth_stage(one, pre_two, got_one, hidden, rim_one, taps.at[1], None, third_one, first, C, small, 16)
    loads[2].wait()

    def to_pooled_grad(i, rows, grad):
        pooled_grad[rows] = grad.astype(BF)

    back_head_stage(
        one, one.count, third_one, weights.at[0], gains.at[1], biases.at[1], mask_one, pre_one, resid_one, pre_three, to_pooled_grad, small, 16
    )
    again = [
        pltpu.make_async_copy(conv_out.at[0], weights.at[1], local.at[1]),
        pltpu.make_async_copy(conv_in.at[0], weights.at[0], local.at[2]),
    ]
    for copy in again:
        copy.start()
    outer_stage(pre_three, pooled, conv.at[1, 0])
    core3[1] = links.copy(conv.at[1, :, :, 1 - me.c], rc3.at[1], other)
    core3[1].start()

    loads[3].wait()
    loads[4].wait()
    xs[...] = (xs[...].astype(F32) * mask_zero[...]).astype(BF)
    again[0].wait()
    back_tail_stage(
        zero, 1, lambda i: tn(pool[i], pooled_grad[one.rows(i)]), xs, weights.at[1], gains.at[0], biases.at[0], mask_zero,
        kept.at[2], kept.at[3], resid, third, kept.at[3], kept.at[2], edge_zero, first, small, 0,
    )
    rim0 = links.copy(edge_zero, got_zero, neighbour)
    rim0.start()
    p3[1] = spread(1)
    temp = [keep.at[0, pl.ds(i * lead * ra, lead * ra)] for i in range(4)]

    def bring(sources):
        copies = [
            pltpu.make_async_copy(source.at[j], to.at[pl.ds(j * ra, ra)], local.at[6 + n * lead + j])
            for n, (source, to) in enumerate(sources)
            for j in range(lead)
        ]
        for copy in copies:
            copy.start()
        for copy in copies:
            copy.wait()

    for h in range(2):
        to = gather1.passing(h)
        bring([(gather1.chunk(to, h), temp[2 * h]), (gather1.slot(1, h), temp[2 * h + 1])])
        for j in range(lead):
            fold(
                lambda at, v: sent_on.__setitem__((h, j, at), v.astype(BF)),
                [lambda at, ref=ref: ref[rows_of(j * ra + at.start, at.size, 16)] for ref in temp[2 * h : 2 * h + 2]],
                ra, 32,
            )
        gather1.pass_on(h, sent_on.at[h])
    outer_stage(third, kept.at[3], conv.at[0, 1])
    rim0.wait_recv()
    own2.wait()
    recv_all(z2)
    spread2 = Spread(me, links, lambda q, h: out2.at[
        rows_of((me.c * me.nq + q) * rb, rb, rb),
        pl.ds(0, nz * ow) if h is None else pl.ds(h * (nz * ow // 2), nz * ow // 2),
    ])
    spread2.start()
    back_depth_stage(zero, kept.at[2], got_zero, kept.at[1], rim_zero, taps.at[0], cmask, third, first, C, small, 0)
    spread_on(1)
    gather1.finish()
    for h in range(2):
        mine = [keep.at[0, pl.ds(i * lead * ra, lead * ra)] for i in range(3)]
        bring([(gather1.chunk(me.q, h), mine[0]), (gather1.slot(0, h), mine[1]), (gather1.slot(2, h), mine[2])])
        for j in range(lead):
            fold(
                lambda at, v: f1.__setitem__((h * lead + j, at), v.astype(BF)),
                [lambda at, ref=ref: ref[rows_of(j * ra + at.start, at.size, 16)] for ref in mine],
                ra, 32,
            )
    z1 = start_all([links.copy(f1.at[t], rz1.at[t - 1], me.at(k=me.deep(t))) for t in range(1, nz)])
    again[1].wait()

    def to_patches(i, rows, grad):
        resid[rows] = (grad * mask_zero[rows]).astype(BF)

    back_head_stage(
        zero, 1, third, weights.at[0], gains.at[0], biases.at[0], mask_zero, kept.at[0], resid, kept.at[3], to_patches, small, 0
    )
    out_patches = pltpu.make_async_copy(resid, patch_grad, local.at[0])
    out_patches.start()
    outer_stage(kept.at[3], xs, conv.at[0, 0])
    core3[0] = links.copy(conv.at[0, :, :, 1 - me.c], rc3.at[0], other)
    core3[0].start()
    sums = start_all([links.copy(small, sc, other)])
    p3[0] = spread(0)

    spread2.pass_on()
    recv_all(z1)
    row_a = rows_of(strip * ra, ra, ra)
    fold(
        lambda at, v: out1.__setitem__(rows_of(strip * ra + at.start, at.size, 16), v.astype(BF)),
        [lambda at: f1[0, at]] + [lambda at, t=t: rz1[t - 1, at] for t in range(1, nz)],
        ra, 32,
    )
    spread1 = Spread(me, links, lambda q, h: out1.at[
        rows_of((me.c * me.nq + q) * ra, ra, ra), pl.ds(0, hw) if h is None else pl.ds(h * (hw // 2), hw // 2)
    ])
    spread1.start()
    recv_all(sums)
    sent_all(sums)
    small[...] += sc[...]
    sums_p = start_all([links.copy(small, sp.at[t - 1], me.at(q=me.chip(t))) for t in range(1, me.nq)])

    spread_on(0)
    z3 = [None, None]
    my_cols = rows_of(me.r * width, width, 128)

    def deepen(b):
        p3[b].finish()
        for m in range(2):
            for j in range(nz):
                rows = pl.ds(j * R, R)
                total = conv[b, m, me.x, me.c, rows, my_cols].astype(F32)
                for i in (0, 2):
                    total = total + rp3[b, i, m, rows, :].astype(F32)
                f3[b, j, pl.ds(m * R, R)] = total.astype(BF)
        z3[b] = start_all([
            links.copy(f3.at[b, me.deep(t)], rz3.at[b, t - 1], me.at(k=me.deep(t))) for t in range(1, nz)
        ])

    deepen(1)
    spread1.pass_on()
    sent_all(sums_p)
    recv_all(sums_p)
    for t in range(1, me.nq):
        small[...] += sp[t - 1]
    sums_z = start_all([links.copy(small, sz.at[t - 1], me.at(k=me.deep(t))) for t in range(1, nz)])
    deepen(0)

    g3 = []
    for b in (1, 0):
        recv_all(z3[b])
        total = f3[b, me.k].astype(F32)
        for t in range(1, nz):
            total = total + rz3[b, t - 1].astype(F32)
        out3[b, me.r] = total.astype(BF)
        g3 += start_all([
            links.copy(out3.at[b, me.r], out3.at[b, me.r], me.at(q=me.x * nrow + lax.rem(me.r + t, nrow)))
            for t in range(1, nrow)
        ])
    spread2.finish()
    half_b = rows_of(me.c * me.nq * rb, me.nq * rb, me.nq * rb)
    h2 = start_all([links.copy(out2.at[half_b], out2.at[half_b], other)])
    spread1.finish()
    half_a = rows_of(me.c * me.nq * ra, me.nq * ra, me.nq * ra)
    h1 = start_all([links.copy(out1.at[half_a], out1.at[half_a], other)])
    sent_all(sums_z)
    recv_all(sums_z)
    for t in range(1, nz):
        small[...] += sz[t - 1]
    recv_all(g3)
    recv_all(h1)
    recv_all(h2)
    out_patches.wait()
    for group_of in (core3, z2, z1, z3[0], z3[1], g3, h1, h2, [rim0, rim1]):
        sent_all(group_of)
    for group in (gather1, p3[0], p3[1], spread1, spread2):
        group.sent()


def spec(*kinds):
    return [pl.BlockSpec(memory_space=kind) for kind in kinds]


def run_readout(mesh, zero, one, patches, cot, read_in, read_out, read_bias, conv_in, conv_out, taps, gains, biases, masks, pool, pick):
    nz, ndp, nrow = mesh.shape["wide"], mesh.shape["dp"], mesh.shape["row"]
    nq = ndp // 2 * nrow
    T, C = pick.shape[0], patches.shape[1]
    hw, ow = read_out.shape[0], cot.shape[1]
    tall = nz * T
    rb = hw // (2 * nq)
    copies = 5 * (nz - 1) + 24
    bias_part = jnp.broadcast_to(read_bias[0:1], (8, hw))
    bias_out = jnp.broadcast_to(read_bias[1:2], (8, ow))
    ANY = pl.ANY
    return pl.pallas_call(
        functools.partial(readout_kernel, nz, ndp, nrow, zero, one),
        out_shape=[
            jax.ShapeDtypeStruct((tall, ow), BF),
            jax.ShapeDtypeStruct((T, C), F32),
            jax.ShapeDtypeStruct((nz, C // 2, hw), BF),
            jax.ShapeDtypeStruct((nz, rb, ow), BF),
            jax.ShapeDtypeStruct((nz, 1, hw), F32),
            jax.ShapeDtypeStruct((nz, C // 2, hw), BF),
            jax.ShapeDtypeStruct((nz, nq * rb, ow), BF),
            jax.ShapeDtypeStruct((nq - 1, nz, rb, ow), BF),
            jax.ShapeDtypeStruct((4, tall, hw), BF),
            jax.ShapeDtypeStruct((2, tall, hw), BF),
            jax.ShapeDtypeStruct((zero.count, 32, C), BF),
            jax.ShapeDtypeStruct((one.count, 16, C), BF),
        ],
        in_specs=spec(ANY, VMEM, ANY, ANY, VMEM, VMEM, ANY, ANY, VMEM, VMEM, VMEM, VMEM, VMEM, VMEM, VMEM),
        out_specs=spec(ANY, VMEM, ANY, VMEM, VMEM, ANY, ANY, ANY, ANY, ANY, VMEM, VMEM),
        scratch_shapes=[
            VMEM((nz, C, hw), BF),
            VMEM((nz, hw, ow), BF),
            VMEM((nz, 8, hw), F32),
            VMEM((tall, C), BF),
            VMEM((C, tall), BF),
            VMEM((nz, tall, hw), BF),
            VMEM((nz, tall, hw), BF),
            VMEM((nz - 1, T, C), BF),
            VMEM((nz - 1, T, C), BF),
            VMEM((nz, hw, ow), BF),
            VMEM((2, zero.cells + 2 * zero.width, 128), F32),
            VMEM((zero.count, 32, C), BF),
            VMEM((one.count, 16, C), BF),
            pltpu.SemaphoreType.DMA((copies,)),
            pltpu.SemaphoreType.DMA((copies,)),
            pltpu.SemaphoreType.DMA((7,)),
        ],
        compiler_params=pltpu.CompilerParams(
            collective_id=0, has_side_effects=True, vmem_limit_bytes=LIMIT
        ),
        name="readout",
    )(patches, cot, read_in, read_out, bias_part, bias_out, conv_in, conv_out, taps, gains, biases, *masks, pool, pick)


LIMIT = 62 * 1024 * 1024


def run_grads(mesh, zero, one, s1, f2, agrad, patches, keep_zero, keep_one, rim_zero, rim_one, conv_in, conv_out, taps, gains, biases, masks, pool, pick, small_in):
    nz, ndp, nrow = mesh.shape["wide"], mesh.shape["dp"], mesh.shape["row"]
    nq = ndp // 2 * nrow
    nx = ndp // 2
    C, hw = s1.shape[1] * 2, s1.shape[2]
    _, rb, ow = f2.shape
    ra = C // (2 * nq)
    R = C // (ndp * nz)
    tall = patches.shape[0]
    S = 40
    copies = 5 * (nz - 1) + 40
    width = C // nrow
    ANY = pl.ANY
    return pl.pallas_call(
        functools.partial(grads_kernel, nz, ndp, nrow, zero, one),
        out_shape=[
            jax.ShapeDtypeStruct((C, hw), BF),
            jax.ShapeDtypeStruct((hw, nz * ow), BF),
            jax.ShapeDtypeStruct((2, nrow, 2 * R, width), BF),
            jax.ShapeDtypeStruct((S, C), F32),
            jax.ShapeDtypeStruct((tall, C), BF),
            jax.ShapeDtypeStruct((nq - 1, nz, ra, hw), BF),
        ],
        in_specs=spec(ANY, VMEM, VMEM, ANY, ANY, ANY, VMEM, VMEM, ANY, ANY, VMEM, VMEM, VMEM, VMEM, VMEM, VMEM, VMEM, VMEM),
        out_specs=spec(VMEM, ANY, VMEM, VMEM, ANY, ANY),
        scratch_shapes=[
            VMEM((tall, C), BF),
            VMEM((4, tall, C), BF),
            VMEM((2, tall, C), BF),
            VMEM((tall, C), BF),
            VMEM((tall, C), BF),
            VMEM((2, C, C), BF),
            VMEM((2, zero.cells + 2 * zero.width, 128), F32),
            VMEM((zero.count, 32, C), BF),
            VMEM((one.count, 16, C), BF),
            VMEM((zero.count, 32, C), BF),
            VMEM((one.count, 16, C), BF),
            VMEM((2, nz // 2, ra, hw), BF),
            VMEM((nz, ra, hw), BF),
            VMEM((nz - 1, ra, hw), BF),
            VMEM((2, 2, nx, 2, nz * R, C), BF),
            VMEM((2, 2, nx, nz * R, C), BF),
            VMEM((2, nq - 1, 2, nz * R, width), BF),
            VMEM((2, nz, 2 * R, width), BF),
            VMEM((2, nz - 1, 2 * R, width), BF),
            VMEM((S, C), F32),
            VMEM((nq - 1, S, C), F32),
            VMEM((nz - 1, S, C), F32),
            pltpu.SemaphoreType.DMA((copies,)),
            pltpu.SemaphoreType.DMA((copies,)),
            pltpu.SemaphoreType.DMA((6 + nq * nz,)),
        ],
        compiler_params=pltpu.CompilerParams(
            collective_id=1, has_side_effects=True, vmem_limit_bytes=LIMIT
        ),
        name="grads",
    )(s1, f2, agrad, patches, keep_zero, keep_one, rim_zero, rim_one, conv_in, conv_out, taps, gains, biases, *masks, pool, pick, small_in)


POOL = 12


eps_norm = 1e-06
exact_mode = lax.Precision.HIGHEST


def extended(cells, sides, width):
    for axis, dim in sides:
        count = lax.axis_size(axis)
        ends = count - 1
        head = lax.slice_in_dim(cells, 0, width, axis=dim)
        tail = lax.slice_in_dim(cells, cells.shape[dim] - width, cells.shape[dim], axis=dim)
        cells = jnp.concatenate(
            [
                lax.ppermute(tail, axis, [(i, (i + 1) % count) for i in range(ends)]),
                cells,
                lax.ppermute(head, axis, [((i + 1) % count, i) for i in range(ends)]),
            ],
            axis=dim,
        )
    return cells


def layer_norm(values, gain_row, bias_row):
    centre = jnp.mean(values, axis=-1, keepdims=True)
    centred = values - centre
    variance = jnp.mean(centred * centred, axis=-1, keepdims=True)
    return centred * lax.rsqrt(variance + eps_norm) * gain_row + bias_row


def head_piece(pre_values, gain_row, bias_row, live_mask):
    return jax.nn.silu(layer_norm(pre_values, gain_row, bias_row)) * live_mask


def tail_piece(source, third_pre, gain_row, bias_row, live_mask):
    return jax.nn.silu(source + layer_norm(third_pre, gain_row, bias_row)) * live_mask


def outer_sum(left_rows, right_rows):
    return lax.dot_general(
        left_rows, right_rows, (((0,), (0,)), ((), ())), preferred_element_type=jnp.float32
    )


def times_transposed(left_rows, weight):
    return lax.dot_general(
        left_rows, weight, (((1,), (1,)), ((), ())), preferred_element_type=jnp.float32
    )


def pad_columns(values):
    return jnp.pad(values, ((0, 0), (0, 0), (1, 1), (0, 0)))


def rows_forward(hidden_one):
    return extended(hidden_one, (("row", 1),), 1)


def rows_backward(second_low):
    return extended(second_low, (("row", 1),), 1)


def depth_apply(padded, tap_table, row_count, col_count):
    result = jnp.zeros((padded.shape[0], row_count, col_count, padded.shape[3]), jnp.float32)
    for offset in range(9):
        window = padded[
            :, offset // 3 : offset // 3 + row_count, offset % 3 : offset % 3 + col_count, :
        ]
        result = result + window.astype(jnp.float32) * tap_table[offset].astype(jnp.float32)
    return result


def block_forward(source, live_mask, weights):
    w_first, w_last, tap_table, gain_rows, bias_rows = weights
    grid_count, row_count, col_count, channels = source.shape
    flat_rows = source.astype(jnp.bfloat16).reshape(-1, channels)
    first_pre = jnp.dot(flat_rows, w_first, preferred_element_type=jnp.float32).reshape(
        source.shape
    )
    hidden_one = head_piece(first_pre, gain_rows[0], bias_rows[0], live_mask).astype(jnp.bfloat16)
    padded_one = pad_columns(rows_forward(hidden_one))
    second_pre = depth_apply(padded_one, tap_table, row_count, col_count)
    hidden_two = head_piece(second_pre, gain_rows[1], bias_rows[1], live_mask).astype(jnp.bfloat16)
    two_rows = hidden_two.reshape(-1, channels)
    third_pre = jnp.dot(two_rows, w_last, preferred_element_type=jnp.float32).reshape(source.shape)
    output = tail_piece(source, third_pre, gain_rows[2], bias_rows[2], live_mask)
    return (output, (flat_rows, first_pre, padded_one, second_pre, two_rows, third_pre))


def block_backward(output_grad, source, live_mask, weights, kept):
    w_first, w_last, tap_table, gain_rows, bias_rows = weights
    flat_rows, first_pre, padded_one, second_pre, two_rows, third_pre = kept
    grid_count, row_count, col_count, channels = source.shape
    _, tail_back = jax.vjp(
        functools.partial(tail_piece, live_mask=live_mask), source, third_pre, gain_rows[2], bias_rows[2]
    )
    residual_grad, third_grad, gain_three, bias_three = tail_back(output_grad)
    third_low = third_grad.astype(jnp.bfloat16).reshape(-1, channels)
    grad_last = outer_sum(two_rows, third_low)
    two_grad = times_transposed(third_low, w_last).reshape(source.shape)
    _, middle_back = jax.vjp(
        functools.partial(head_piece, live_mask=live_mask), second_pre, gain_rows[1], bias_rows[1]
    )
    second_grad, gain_two, bias_two = middle_back(two_grad)
    second_low = second_grad.astype(jnp.bfloat16)
    padded_grad = pad_columns(rows_backward(second_low))
    one_grad = depth_apply(padded_grad, tap_table[::-1], row_count, col_count)
    second_wide = second_low.astype(jnp.float32)
    tap_grads = []
    for offset in range(9):
        window = padded_one[
            :, offset // 3 : offset // 3 + row_count, offset % 3 : offset % 3 + col_count, :
        ]
        tap_grads.append(jnp.sum(second_wide * window.astype(jnp.float32), axis=(0, 1, 2)))
    _, first_back = jax.vjp(
        functools.partial(head_piece, live_mask=live_mask), first_pre, gain_rows[0], bias_rows[0]
    )
    first_grad, gain_one, bias_one = first_back(one_grad)
    first_low = first_grad.astype(jnp.bfloat16).reshape(-1, channels)
    grad_first = outer_sum(flat_rows, first_low)
    source_grad = residual_grad + times_transposed(first_low, w_first).reshape(source.shape)
    grads = (
        grad_first,
        grad_last,
        jnp.stack(tap_grads),
        jnp.stack([gain_one, gain_two, gain_three]),
        jnp.stack([bias_one, bias_two, bias_three]),
    )
    return (source_grad, grads)


def pool_weights(grid_side, row_shift, pooled_index, slot_index):
    place = slot_index - row_shift
    begin = pooled_index * grid_side // POOL
    finish = ((pooled_index + 1) * grid_side + POOL - 1) // POOL
    inside = (place >= begin) & (place < finish)
    return jnp.where(inside, 1.0, 0.0).astype(jnp.float32) / (finish - begin).astype(jnp.float32)


def plain(
    patches,
    grid_sizes,
    conv_in,
    conv_out,
    depth_taps,
    norm_gain,
    norm_bias,
    read_in,
    read_bias,
    read_out,
    cotangent,
):
    grid_count, local_rows, grid_width, channels = patches.shape
    row_place = lax.axis_index("row")
    slot_rows = row_place * local_rows + jnp.arange(local_rows, dtype=jnp.int32)
    column_index = jnp.arange(grid_width, dtype=jnp.int32)
    row_shift = (grid_width - grid_sizes) // 2
    row_live = (slot_rows[None, :] >= row_shift[:, None]) & (
        slot_rows[None, :] < (row_shift + grid_sizes)[:, None]
    )
    col_live = column_index[None, :] < grid_sizes[:, None]
    live_mask = (row_live[:, :, None] & col_live[:, None, :]).astype(jnp.float32)[..., None]
    weights_one = (conv_in[0], conv_out[0], depth_taps[0], norm_gain[0], norm_bias[0])
    weights_two = (conv_in[1], conv_out[1], depth_taps[1], norm_gain[1], norm_bias[1])
    source = patches.astype(jnp.float32) * live_mask
    encoded, kept_one = block_forward(source, live_mask, weights_one)
    pool_local = POOL // lax.axis_size("row")
    pooled_index = row_place * pool_local + jnp.arange(pool_local, dtype=jnp.int32)
    side_shaped = grid_sizes[:, None, None]
    row_pool = pool_weights(
        side_shaped, row_shift[:, None, None], pooled_index[None, :, None], slot_rows[None, None, :]
    )
    col_pool = pool_weights(
        side_shaped,
        0,
        jnp.arange(POOL, dtype=jnp.int32)[None, :, None],
        column_index[None, None, :],
    )
    pooled = jnp.einsum("gir,gjw,grwc->gijc", row_pool, col_pool, encoded, precision=exact_mode)
    all_live = jnp.ones((grid_count, pool_local, POOL, 1), jnp.float32)
    abstract, kept_two = block_forward(pooled, all_live, weights_two)
    token_rows = abstract.astype(jnp.bfloat16).reshape(-1, channels)
    gathered = lax.all_gather(token_rows, "wide", axis=0, tiled=True)
    gelu_exact = functools.partial(jax.nn.gelu, approximate=False)
    mixed_pre = jnp.dot(gathered, read_in, preferred_element_type=jnp.float32) + read_bias[0]
    hidden_wide, gelu_back = jax.vjp(gelu_exact, mixed_pre)
    hidden = hidden_wide.astype(jnp.bfloat16)
    partial_out = jnp.dot(hidden, read_out, preferred_element_type=jnp.float32)
    summed = (
        lax.psum_scatter(
            partial_out.astype(jnp.bfloat16), "wide", scatter_dimension=1, tiled=True
        ).astype(jnp.float32)
        + read_bias[1]
    )
    tokens = summed.astype(jnp.bfloat16).reshape(cotangent.shape)
    cot_local = cotangent.reshape(-1, cotangent.shape[-1])
    cot_all = lax.all_gather(cot_local, "wide", axis=1, tiled=True)
    hidden_grad = times_transposed(cot_all, read_out)
    mixed_grad = gelu_back(hidden_grad)[0].astype(jnp.bfloat16)
    grad_exit = outer_sum(hidden, cot_all)
    grad_entry = outer_sum(gathered, mixed_grad)
    bias_pair = jnp.stack(
        [
            jnp.sum(mixed_grad.astype(jnp.float32), axis=0),
            jnp.sum(cot_local.astype(jnp.float32), axis=0),
        ]
    )
    abstract_grad = lax.psum_scatter(
        times_transposed(mixed_grad, read_in).astype(jnp.bfloat16),
        "wide",
        scatter_dimension=0,
        tiled=True,
    ).astype(jnp.float32)
    grad_entry, bias_pair, grad_exit = (
        lax.psum(grad_entry.astype(jnp.bfloat16), ("dp", "row")).astype(jnp.float32),
        lax.psum(bias_pair.astype(jnp.bfloat16), ("dp", "row")).astype(jnp.float32),
        lax.psum(grad_exit.astype(jnp.bfloat16), ("dp", "row")).astype(jnp.float32),
    )
    pooled_grad, grads_two = block_backward(
        abstract_grad.reshape(abstract.shape), pooled, all_live, weights_two, kept_two
    )
    encoded_grad = jnp.einsum(
        "gir,gjw,gijc->grwc", row_pool, col_pool, pooled_grad, precision=exact_mode
    )
    source_grad, grads_one = block_backward(encoded_grad, source, live_mask, weights_one, kept_one)
    patch_grad = (source_grad * live_mask).astype(jnp.bfloat16)
    stacked = tuple((jnp.stack([grads_one[index], grads_two[index]]) for index in range(5)))
    totals = (
        lax.psum_scatter(stacked[0], ("dp", "wide"), scatter_dimension=2, tiled=True),
        lax.psum_scatter(stacked[1], ("dp", "wide"), scatter_dimension=2, tiled=True),
        lax.psum_scatter(stacked[2], ("dp", "wide"), scatter_dimension=2, tiled=True),
        lax.psum_scatter(stacked[3], ("dp", "wide"), scatter_dimension=2, tiled=True),
        lax.psum_scatter(stacked[4], ("dp", "wide"), scatter_dimension=2, tiled=True),
    )
    totals = (
        lax.psum(totals[0].astype(jnp.bfloat16), "row").astype(jnp.float32),
        lax.psum(totals[1].astype(jnp.bfloat16), "row").astype(jnp.float32),
        lax.psum(totals[2].astype(jnp.bfloat16), "row").astype(jnp.float32),
        lax.psum(totals[3].astype(jnp.bfloat16), "row").astype(jnp.float32),
        lax.psum(totals[4].astype(jnp.bfloat16), "row").astype(jnp.float32),
    )
    return (
        tokens,
        patch_grad,
        totals[0],
        totals[1],
        totals[2],
        totals[3],
        totals[4],
        grad_entry,
        bias_pair,
        grad_exit,
    )


def on_device(
    mesh,
    patches,
    grid_sizes,
    conv_in,
    conv_out,
    depth_taps,
    norm_gain,
    norm_bias,
    read_in,
    read_bias,
    read_out,
    cotangent,
):
    nz, ndp = mesh.shape["wide"], mesh.shape["dp"]
    grid_count, local_rows, grid_width, channels = patches.shape
    row_place = lax.axis_index("row")
    slot_rows = row_place * local_rows + jnp.arange(local_rows, dtype=jnp.int32)
    column_index = jnp.arange(grid_width, dtype=jnp.int32)
    row_shift = (grid_width - grid_sizes) // 2
    row_live = (slot_rows[None, :] >= row_shift[:, None]) & (
        slot_rows[None, :] < (row_shift + grid_sizes)[:, None]
    )
    col_live = column_index[None, :] < grid_sizes[:, None]
    live_mask = (row_live[:, :, None] & col_live[:, None, :]).astype(jnp.float32)[..., None]
    pool_local = POOL // lax.axis_size("row")
    pooled_index = row_place * pool_local + jnp.arange(pool_local, dtype=jnp.int32)
    side_shaped = grid_sizes[:, None, None]
    row_pool = pool_weights(
        side_shaped, row_shift[:, None, None], pooled_index[None, :, None], slot_rows[None, None, :]
    )
    col_pool = pool_weights(
        side_shaped,
        0,
        jnp.arange(POOL, dtype=jnp.int32)[None, :, None],
        column_index[None, None, :],
    )
    zero = Geometry(grid_count, local_rows, grid_width)
    one = Geometry(grid_count, pool_local, 16)
    col_wide = jnp.pad(col_pool, ((0, 0), (0, one.width - POOL), (0, 0)))
    pool = (row_pool[:, :, None, :, None] * col_wide[:, None, :, None, :]).reshape(grid_count, one.cells, zero.cells)
    places = jnp.arange(grid_count * pool_local * POOL, dtype=jnp.int32)
    places = places // POOL * one.width + places % POOL
    pick = (places[:, None] == jnp.arange(grid_count * one.cells, dtype=jnp.int32)[None, :]).astype(BF)
    mask_zero = live_mask.reshape(-1, 1)
    mask_one = (jnp.arange(grid_count * one.cells, dtype=jnp.int32) % one.width < POOL).astype(F32)[:, None]
    cot_local = cotangent.reshape(-1, cotangent.shape[-1])
    shared = (conv_in, conv_out, depth_taps.astype(F32), norm_gain, norm_bias, (mask_zero, mask_one), pool.astype(BF))
    flat = patches.reshape(-1, channels)
    tokens, agrad, s1, f2, hsum, _, _, _, keep_zero, keep_one, rim_zero, rim_one = run_readout(
        mesh, zero, one, flat, cot_local, read_in, read_out, read_bias, *shared, pick
    )
    tokens = tokens.reshape(cotangent.shape)
    cot_sum = jnp.sum(cot_local.astype(F32), axis=0)
    width = cot_sum.shape[0]
    cot_row = lax.dynamic_update_slice(
        jnp.zeros((nz * width,), F32), cot_sum, (lax.axis_index("wide") * width,)
    )
    small = jnp.concatenate([hsum.reshape(-1, channels), cot_row.reshape(-1, channels)])
    out1, out2, out3, small, patch_grad, _ = run_grads(
        mesh, zero, one, s1, f2, agrad, flat, keep_zero, keep_one, rim_zero, rim_one, *shared, pick.T, small
    )
    patch_grad = patch_grad.reshape(patches.shape)
    R = channels // (ndp * nz)
    out3 = out3.reshape(2, -1, 2, R, out3.shape[-1]).transpose(0, 2, 1, 4, 3).reshape(2, 2, channels, R).astype(F32)
    place = lax.axis_index("dp") * nz + lax.axis_index("wide")
    own = lax.dynamic_slice_in_dim(small, place * R, R, axis=1)
    own = own[:32].reshape(2, 16, R)
    taps, gains, biases = own[:, 0:9], own[:, 9:12], own[:, 12:15]
    bias_pair = lax.dynamic_slice_in_dim(small[32:40].reshape(2, -1), lax.axis_index("wide") * width, width, axis=1)
    return (
        tokens,
        patch_grad,
        out3[:, 0],
        out3[:, 1],
        taps,
        gains,
        biases,
        out1.astype(F32),
        bias_pair,
        out2.astype(F32),
    )


def fits(mesh):
    return mesh.shape["wide"] == 4 and mesh.shape["dp"] % 2 == 0 and mesh.shape["row"] == 2


def solution(mesh):

    placed = (
        P(("dp", "wide"), "row", None, None),
        P(("dp", "wide")),
        P(),
        P(),
        P(),
        P(),
        P(),
        P(None, "wide"),
        P(None, "wide"),
        P("wide", None),
        P("dp", "row", None, "wide"),
    )
    return jax.shard_map(
        functools.partial(on_device, mesh) if fits(mesh) else plain,
        mesh=mesh,
        in_specs=placed,
        out_specs=(
            P("dp", "row", None, "wide"),
            P(("dp", "wide"), "row", None, None),
            P(None, None, ("dp", "wide")),
            P(None, None, ("dp", "wide")),
            P(None, None, ("dp", "wide")),
            P(None, None, ("dp", "wide")),
            P(None, None, ("dp", "wide")),
            P(None, "wide"),
            P(None, "wide"),
            P("wide", None),
        ),
        check_vma=False,
    )
```

```python
import functools

import jax
import jax.numpy as jnp
from jax import lax
from jax.experimental import pallas as pl
from jax.experimental.pallas import tpu as pltpu
from jax.sharding import PartitionSpec as P

MESH = pl.DeviceIdType.MESH
BF = jnp.bfloat16
F32 = jnp.float32
VMEM = pltpu.VMEM


class Place:
    def __init__(self, nz, ndp, nrow):
        self.nz, self.ndp, self.nrow = nz, ndp, nrow
        self.nx = ndp // 2
        self.nq = self.nx * nrow
        self.k = lax.axis_index("wide")
        self.r = lax.axis_index("row")
        d = lax.axis_index("dp")
        self.c = lax.rem(d, 2)
        self.x = d // 2
        self.q = self.x * nrow + self.r
        self.qx = (1 - self.x) * nrow + self.r
        self.qy = self.x * nrow + (1 - self.r)
        self.qd = (1 - self.x) * nrow + (1 - self.r)

    def at(self, q=None, c=None, k=None):
        q = self.q if q is None else q
        c = self.c if c is None else c
        k = self.k if k is None else k
        return {"dp": (q // self.nrow) * 2 + c, "row": lax.rem(q, self.nrow), "wide": k}

    def chip(self, t):
        return lax.rem(self.q + t, self.nq)

    def deep(self, t):
        return lax.rem(self.k + t, self.nz)

    def peers(self):
        return (
            [self.at(q=self.chip(t)) for t in range(1, self.nq)]
            + [self.at(c=1 - self.c)]
            + [self.at(k=self.deep(t)) for t in range(1, self.nz)]
        )

    def greet(self):
        barrier = pltpu.get_barrier_semaphore()
        peers = self.peers()
        for peer in peers:
            pl.semaphore_signal(barrier, inc=1, device_id=peer, device_id_type=MESH)
        pl.semaphore_wait(barrier, len(peers))


class Links:
    def __init__(self, send, recv):
        self.send, self.recv, self.used = send, recv, 0

    def copy(self, src, dst, peer):
        at = self.used
        self.used += 1
        assert self.used <= self.send.shape[0]
        return pltpu.make_async_remote_copy(
            src_ref=src, dst_ref=dst, send_sem=self.send.at[at], recv_sem=self.recv.at[at],
            device_id=peer, device_id_type=MESH,
        )


def start_all(copies):
    for copy in copies:
        copy.start()
    return copies


def recv_all(copies):
    for copy in copies:
        copy.wait_recv()


def sent_all(copies):
    for copy in copies:
        copy.wait_send()


class Spread:
    def __init__(self, me, links, strip):
        self.me, self.links, self.strip = me, links, strip
        self.first = self.second = ()

    def start(self):
        me = self.me
        own = self.strip(me.q, None)
        self.first = start_all([self.links.copy(own, own, me.at(q=q)) for q in (me.qx, me.qy)])

    def pass_on(self):
        me = self.me
        along_y = self.strip(me.qx, 0)
        along_x = self.strip(me.qy, 1)
        self.second = [
            self.links.copy(along_y, along_y, me.at(q=me.qy)),
            self.links.copy(along_x, along_x, me.at(q=me.qx)),
        ]
        for arrived, copy in zip(self.first, self.second):
            arrived.wait_recv()
            copy.start()

    def finish(self):
        recv_all(self.second)

    def sent(self):
        sent_all(self.first)
        sent_all(self.second)


class Gather:
    def __init__(self, me, links, chunk, slot):
        self.me, self.links, self.chunk, self.slot = me, links, chunk, slot
        self.early = [[], []]
        self.late = [None, None]

    def start(self, half):
        me = self.me
        to = me.qx if half == 0 else me.qy
        self.early[half] = start_all([
            self.links.copy(self.chunk(q, half), self.slot(i, half), me.at(q=to)) for i, q in ((1, me.qd), (0, to))
        ])

    def passing(self, half):
        self.early[half][0].wait_recv()
        return self.me.qy if half == 0 else self.me.qx

    def pass_on(self, half, total):
        to = self.me.qy if half == 0 else self.me.qx
        self.late[half] = self.links.copy(total, self.slot(2, half), self.me.at(q=to))
        self.late[half].start()

    def finish(self):
        for half in range(2):
            self.early[half][1].wait_recv()
            self.late[half].wait_recv()

    def sent(self):
        for half in range(2):
            sent_all(self.early[half])
            self.late[half].wait_send()


def rows_of(start, size, unit):
    return pl.ds(pl.multiple_of(start, unit), size)


def fold(out, parts, rows, step):
    def body(i, carry):
        at = rows_of(i * step, step, step)
        total = parts[0](at).astype(F32)
        for part in parts[1:]:
            total = total + part(at).astype(F32)
        out(at, total)
        return carry

    lax.fori_loop(0, rows // step, body, 0)


def nt(a, b):
    return lax.dot_general(a, b, (((1,), (1,)), ((), ())), preferred_element_type=F32)


def nn(a, b):
    return jnp.dot(a, b, preferred_element_type=F32)


def tn(a, b):
    return lax.dot_general(a, b, (((0,), (0,)), ((), ())), preferred_element_type=F32)


def gelu_pair(v):
    dense = jnp.exp(-0.5 * v * v)
    s = 1.0 / (1.0 + (0.3275911 * 0.7071067811865476) * jnp.abs(v))
    poly = s * (0.254829592 + s * (-0.284496736 + s * (1.421413741 + s * (-1.453152027 + s * 1.061405429))))
    tail = 0.5 * poly * dense
    phi = jnp.where(v >= 0, 1.0 - tail, tail)
    return v * phi, phi + v * dense * 0.3989422804014327


def normal(v):
    centred = v - jnp.mean(v, axis=-1, keepdims=True)
    scale = lax.rsqrt(jnp.mean(centred * centred, axis=-1, keepdims=True) + 1e-06)
    return centred * scale, scale


def sigmoid(v):
    return 1.0 / (1.0 + jnp.exp(-v))


def silu_of(v):
    return v * sigmoid(v)


def column_masks(cmask, width):
    place = lax.rem(lax.broadcasted_iota(jnp.int32, cmask.shape[1:], 0), width)
    cmask[0] = jnp.where(place != 0, 1.0, 0.0)
    cmask[1] = jnp.where(place != width - 1, 1.0, 0.0)


def windows(cells, rim, first, masks):
    middle = jnp.concatenate([rim * (1.0 - first), cells, rim * first], axis=0)
    count = middle.shape[0]
    left, right = pltpu.roll(middle, 1, 0), pltpu.roll(middle, count - 1, 0)
    if masks is not None:
        left, right = left * masks[0], right * masks[1]
    return left, middle, right


class Geometry:
    def __init__(self, count, height, width):
        self.count, self.height, self.width = count, height, width
        self.cells = height * width

    def rows(self, g):
        return rows_of(g * self.cells, self.cells, 16)


def head_stage(shape, per, x_of, w, gains, biases, mask, pre, hidden, rim_send, first):
    cells = shape.cells * per

    def body(i, carry):
        rows = rows_of(i * cells, cells, 16)
        x = x_of(rows)
        value = nn(x, w[...])
        pre[rows] = value.astype(BF)
        n, _ = normal(value)
        h = silu_of(n * gains[0:1] + biases[0:1]) * mask[rows]
        hidden[rows] = h.astype(BF)
        for g in range(per):
            at = g * shape.cells
            top = h[at : at + shape.width]
            bottom = h[at + shape.cells - shape.width : at + shape.cells]
            rim_send[i * per + g, pl.ds(0, shape.width)] = (bottom * first + top * (1.0 - first)).astype(BF)
        return carry

    lax.fori_loop(0, shape.count // per, body, 0)


def depth_stage(shape, hidden, rim, taps, cmask, pre, first, channels):
    def body(i, carry):
        g, l = i // (channels // 128), lax.rem(i, channels // 128)
        rows, lanes = shape.rows(g), rows_of(l * 128, 128, 128)
        shifted = windows(
            hidden[rows, lanes].astype(F32),
            rim[g, pl.ds(0, shape.width), lanes].astype(F32),
            first,
            None if cmask is None else (cmask[0], cmask[1]),
        )
        total = jnp.zeros((shape.cells, 128), F32)
        for a in range(3):
            for b in range(3):
                piece = shifted[b][a * shape.width : a * shape.width + shape.cells]
                total = total + piece * taps[3 * a + b : 3 * a + b + 1, lanes]
        pre[rows, lanes] = total.astype(BF)
        return carry

    lax.fori_loop(0, shape.count * (channels // 128), body, 0)


def tail_stage(shape, per, x, w, gains, biases, mask, pre_two, pre_three, result):
    cells = shape.cells * per

    def body(i, carry):
        rows = rows_of(i * cells, cells, 16)
        n, _ = normal(pre_two[rows].astype(F32))
        h = (silu_of(n * gains[1:2] + biases[1:2]) * mask[rows]).astype(BF)
        value = nn(h, w[...])
        pre_three[rows] = value.astype(BF)
        n, _ = normal(value)
        out = silu_of(x[rows].astype(F32) + n * gains[2:3] + biases[2:3]) * mask[rows]
        result(i, rows, out)
        return carry

    lax.fori_loop(0, shape.count // per, body, 0)


def slope_of(v, s):
    return s * (1.0 + v * (1.0 - s))


def norm_back(n, scale, grad, gain, sums, at):
    sums[at : at + 1] += jnp.sum(grad * n, axis=0, keepdims=True)
    sums[at + 3 : at + 4] += jnp.sum(grad, axis=0, keepdims=True)
    dn = grad * gain
    return scale * (dn - jnp.mean(dn, axis=-1, keepdims=True) - n * jnp.mean(dn * n, axis=-1, keepdims=True))


def back_tail_stage(shape, per, grad_of, x, w, gains, biases, mask, pre_two, pre_three, resid, third, hidden_two, second, edge, first, sums, base):
    cells = shape.cells * per

    def body(i, carry):
        rows = rows_of(i * cells, cells, 16)
        live = mask[rows]
        n, scale = normal(pre_three[rows].astype(F32))
        v = x[rows].astype(F32) + n * gains[2:3] + biases[2:3]
        grad = grad_of(i) * slope_of(v, sigmoid(v)) * live
        resid[rows] = grad.astype(BF)
        low = norm_back(n, scale, grad, gains[2:3], sums, base + 11).astype(BF)
        third[rows] = low
        grad = nt(low, w[...])
        n, scale = normal(pre_two[rows].astype(F32))
        v = n * gains[1:2] + biases[1:2]
        s = sigmoid(v)
        hidden_two[rows] = (v * s * live).astype(BF)
        grad = norm_back(n, scale, grad * live * slope_of(v, s), gains[1:2], sums, base + 10)
        second[rows] = grad.astype(BF)
        for g in range(per):
            at = g * shape.cells
            top = grad[at : at + shape.width]
            bottom = grad[at + shape.cells - shape.width : at + shape.cells]
            edge[i * per + g, pl.ds(0, shape.width)] = (bottom * first + top * (1.0 - first)).astype(BF)
        return carry

    lax.fori_loop(0, shape.count // per, body, 0)


def back_depth_stage(shape, second, rim, hidden, hidden_rim, taps, cmask, result, first, channels, sums, base):
    masks = None if cmask is None else (cmask[0], cmask[1])

    def body(i, carry):
        g, l = i // (channels // 128), lax.rem(i, channels // 128)
        rows, lanes = shape.rows(g), rows_of(l * 128, 128, 128)
        edge = pl.ds(0, shape.width)
        grad = second[rows, lanes].astype(F32)
        shifted = windows(grad, rim[g, edge, lanes].astype(F32), first, masks)
        total = jnp.zeros((shape.cells, 128), F32)
        for a in range(3):
            for b in range(3):
                at = (2 - a) * shape.width
                total = total + shifted[2 - b][at : at + shape.cells] * taps[3 * a + b : 3 * a + b + 1, lanes]
        result[rows, lanes] = total.astype(BF)
        shifted = windows(hidden[rows, lanes].astype(F32), hidden_rim[g, edge, lanes].astype(F32), first, masks)
        for a in range(3):
            for b in range(3):
                at = a * shape.width
                line = base + 3 * a + b
                sums[line : line + 1, lanes] += jnp.sum(
                    grad * shifted[b][at : at + shape.cells], axis=0, keepdims=True
                )
        return carry

    lax.fori_loop(0, shape.count * (channels // 128), body, 0)


def back_head_stage(shape, per, one_grad, w, gains, biases, mask, pre_one, resid, first_low, result, sums, base):
    cells = shape.cells * per

    def body(i, carry):
        rows = rows_of(i * cells, cells, 16)
        n, scale = normal(pre_one[rows].astype(F32))
        v = n * gains[0:1] + biases[0:1]
        grad = one_grad[rows].astype(F32) * mask[rows] * slope_of(v, sigmoid(v))
        low = norm_back(n, scale, grad, gains[0:1], sums, base + 9).astype(BF)
        first_low[rows] = low
        result(i, rows, resid[rows].astype(F32) + nt(low, w[...]))
        return carry

    lax.fori_loop(0, shape.count // per, body, 0)


def outer_stage(left, right, out):
    high = out.shape[2]

    def body(i, carry):
        at = rows_of(i * high, high, 128)
        out[i // 2, lax.rem(i, 2)] = tn(left[:, at], right[...]).astype(BF)
        return carry

    lax.fori_loop(0, out.shape[0] * 2, body, 0)


def readout_kernel(
    nz, ndp, nrow, zero, one,
    patches, cot, rin_part, rout_part, bias_part, bias_out, conv_in, conv_out, taps, gains, biases, mask_zero, mask_one, pool, pick,
    tokens, agrad, s1, f2, hsum, rc1, rc2, rp2, keep_zero, keep_one, rim_zero, rim_one,
    rin, rout, bias, abst, abst_t, hid, mg, ag_send, ag_recv, s2, cmask, edge_zero, edge_one, send, recv, local,
):
    me = Place(nz, ndp, nrow)
    links = Links(send, recv)
    T, C = agrad.shape
    hw, ow = rout.shape[1], rout.shape[2]
    tall = nz * T
    np_ = 2 * me.nq
    strip = me.c * me.nq + me.q
    ra, rb = C // np_, hw // np_
    me.greet()

    own = [
        pltpu.make_async_copy(rin_part, rin.at[0], local.at[0]),
        pltpu.make_async_copy(rout_part.at[:, rows_of(me.k * ow, ow, 128)], rout.at[0], local.at[1]),
    ]
    convs = [
        pltpu.make_async_copy(part.at[b], s2.at[2 * b + i], local.at[2 + 2 * b + i])
        for b in range(2)
        for i, part in enumerate((conv_in, conv_out))
    ]
    given = pltpu.make_async_copy(patches, mg.at[0], local.at[6])
    convs[0].start()
    given.start()
    za, zb, zc = [], [], []
    row_a = rows_of(strip * ra, ra, ra)
    row_b = rows_of(strip * rb, rb, rb)
    for t in range(1, nz):
        there = lax.rem(me.k + nz - t, nz)
        za.append(links.copy(rin_part.at[row_a], rin.at[t, row_a], me.at(k=there)))
        zc.append(links.copy(bias_part, bias.at[t], me.at(k=there)))
    start_all(za)
    start_all(zc)
    for t in range(1, nz):
        there = lax.rem(me.k + nz - t, nz)
        zb.append(links.copy(
            rout_part.at[row_b, rows_of(there * ow, ow, 128)], rout.at[t, row_b], me.at(k=there)))
    for copy in convs[1:] + own:
        copy.start()
    bias[0] = bias_part[...]
    column_masks(cmask, zero.width)

    def strips(weights, height):
        wide = weights.shape[2]

        def strip(q, half):
            rows = rows_of((me.c * me.nq + q) * height, height, height)
            cols = pl.ds(0, wide) if half is None else pl.ds(half * (wide // 2), wide // 2)
            return weights.at[pl.ds(1, nz - 1), rows, cols]

        return Spread(me, links, strip)

    def between_cores(weights, height):
        half = rows_of(me.c * (me.nq * height), me.nq * height, height)
        part = weights.at[pl.ds(1, nz - 1), half]
        return start_all([links.copy(part, part, me.at(c=1 - me.c))])

    pa, pb = strips(rin, ra), strips(rout, rb)

    first = (1 - me.r).astype(F32)
    neighbour = me.at(q=me.x * nrow + (nrow - 1 - me.r))

    def masked(rows):
        x = (mg[0, rows].astype(F32) * mask_zero[rows]).astype(BF)
        mg[0, rows] = x
        return x

    convs[0].wait()
    given.wait()
    head_stage(zero, 1, masked, s2.at[0], gains.at[0], biases.at[0], mask_zero, hid.at[0], hid.at[1], edge_zero, first)
    rim0 = links.copy(edge_zero, rim_zero, neighbour)
    rim0.start()
    rim0.wait_recv()
    depth_stage(zero, hid.at[1], rim_zero, taps.at[0], cmask, hid.at[2], first, C)
    for copy in convs[1:]:
        copy.wait()

    def to_pooled(i, rows, out):
        mg[1, one.rows(i)] = nn(pool[i], out.astype(BF)).astype(BF)

    sent_all(za)
    start_all(zb)
    recv_all(za)
    pa.start()
    tail_stage(zero, 1, mg.at[0], s2.at[1], gains.at[0], biases.at[0], mask_zero, hid.at[2], hid.at[3], to_pooled)
    kept_zero = pltpu.make_async_copy(hid, keep_zero, local.at[2])
    kept_zero.start()
    all_one = one.cells * one.count
    part = [mg.at[1 + i // 3, pl.ds((i % 3) * all_one, all_one)] for i in range(5)]
    pooled, pre_one, hidden, pre_two, pre_three = part
    head_stage(one, one.count, lambda rows: pooled[rows], s2.at[2], gains.at[1], biases.at[1], mask_one, pre_one, hidden, edge_one, first)
    rim1 = links.copy(edge_one, rim_one, neighbour)
    rim1.start()
    rim1.wait_recv()
    depth_stage(one, hidden, rim_one, taps.at[1], None, pre_two, first, C)
    here = rows_of(me.k * T, T, 16)

    def to_tokens(i, rows, out):
        abst[here] = nn(pick[...], out.astype(BF)).astype(BF)

    tail_stage(one, one.count, pooled, s2.at[3], gains.at[1], biases.at[1], mask_one, pre_two, pre_three, to_tokens)
    kept_one = pltpu.make_async_copy(mg.at[pl.ds(1, 2)], keep_one, local.at[3])
    kept_one.start()
    def along(step, group, to):
        rows = rows_of(lax.rem(group + nz, nz) * T, T, 16)
        return links.copy(abst.at[rows], abst.at[rows], me.at(k=lax.rem(to + nz, nz)))

    up = [along(step, me.k - step, me.k + 1) for step in range(nz - 1)]
    down = [along(step, me.k + step, me.k - 1) for step in range(nz - 1)]
    more, less = me.k + 1 < nz, me.k > 0

    def hop(step):
        if step < nz - 1:
            pl.when(jnp.logical_and(more, me.k - step >= 0))(up[step].start)
            pl.when(jnp.logical_and(less, me.k + step < nz))(down[step].start)

    hop(0)
    pa.pass_on()
    recv_all(zb)
    pa.finish()
    pb.start()
    ca = between_cores(rin, ra)
    for copy in own + [kept_zero, kept_one]:
        copy.wait()
    recv_all(zc)
    recv_all(ca)

    hsum[...] = jnp.zeros_like(hsum)
    ag = [None] + [
        links.copy(ag_send.at[t - 1], ag_recv.at[t - 1], me.at(k=me.deep(t))) for t in range(1, nz)
    ]
    NT = min(512, hw)

    def hidden_group(z):
        rows = rows_of(z * T, T, 16)

        def front(i, carry):
            u = i // (hw // NT)
            cols = rows_of(lax.rem(i, hw // NT) * NT, NT, 128)
            value, slope = gelu_pair(nn(abst[rows], rin[u, :, cols]) + bias[u, 0:1, cols])
            hid[u, rows, cols] = value.astype(BF)
            mg[u, rows, cols] = slope.astype(BF)
            return carry

        lax.fori_loop(0, nz * (hw // NT), front, 0)

    hidden_group(me.k)
    pb.pass_on()
    for step in range(nz - 1):
        from_less, from_more = me.k - 1 - step >= 0, me.k + 1 + step < nz
        pl.when(from_less)(up[step].wait_recv)
        pl.when(from_more)(down[step].wait_recv)
        hop(step + 1)
        lower = from_less.astype(jnp.int32)

        def arrived(i, carry):
            hidden_group(jnp.where(i < lower, me.k - 1 - step, me.k + 1 + step))
            return carry

        lax.fori_loop(0, lower + from_more.astype(jnp.int32), arrived, 0)
        if step == 0:
            pb.finish()
            cb = between_cores(rout, rb)

    HT = 256

    def g2(i, carry):
        u = i // (hw // HT)
        at = rows_of(lax.rem(i, hw // HT) * HT, HT, HT)
        s2[me.deep(u), at, :] = tn(hid[u, :, at], cot[...]).astype(BF)
        return carry

    lax.fori_loop(0, nz * (hw // HT), g2, 0)
    half = me.nq * rb
    theirs = rows_of((1 - me.c) * half, half, half)
    core2 = start_all([links.copy(s2.at[:, theirs], rc2, me.at(c=1 - me.c))])
    abst_t[...] = abst[...].T
    recv_all(cb)

    def unit(i, carry):
        u = i // (hw // 256)
        cols = rows_of(lax.rem(i, hw // 256) * 256, 256, 256)
        grad = (nt(cot[...], rout[u, cols, :]) * mg[u, :, cols].astype(F32)).astype(BF)
        mg[u, :, cols] = grad
        hsum[me.deep(u), 0:1, cols] += jnp.sum(grad.astype(F32), axis=0, keepdims=True)
        return carry

    lax.fori_loop(0, nz * (hw // 256), unit, 0)

    recv_all(core2)
    mine2 = me.c * half
    gather2 = Gather(
        me, links,
        lambda q, h: s2.at[pl.ds(h * (nz // 2), nz // 2), rows_of(mine2 + q * rb, rb, rb)],
        lambda i, h: rp2.at[i, pl.ds(h * (nz // 2), nz // 2)],
    )
    piece = 256
    parts = half // piece
    loads = [
        pltpu.make_async_copy(
            rc2.at[i // parts, pl.ds(i % parts * piece, piece)], ag_send.at[i % 2, pl.ds(0, piece)], local.at[i % 2]
        )
        for i in range(nz * parts)
    ]
    loads[0].start()
    for i in range(nz * parts):
        loads[i].wait()
        if i + 1 < nz * parts:
            loads[i + 1].start()
        j, where = i // parts, mine2 + i % parts * piece
        fold(
            lambda at, v, j=j, w=where: s2.__setitem__((j, rows_of(w + at.start, at.size, 16)), v.astype(BF)),
            [
                lambda at, j=j, w=where: s2[j, rows_of(w + at.start, at.size, 16)],
                lambda at, i=i: ag_send[i % 2, at],
            ],
            piece, 32,
        )
        if (i + 1) % (nz // 2 * parts) == 0:
            gather2.start(i // (nz // 2 * parts))

    def group_back(t):
        rows = rows_of(me.deep(t) * T, T, 16)

        def back(i, carry):
            at = rows_of(i * 256, 256, 256)
            total = nt(mg[0, rows, :], rin[0, at, :])
            for u in range(1, nz):
                total = total + nt(mg[u, rows, :], rin[u, at, :])
            if t == 0:
                agrad[:, at] = total
            else:
                ag_send[t - 1, :, at] = total.astype(BF)
            return carry

        lax.fori_loop(0, C // 256, back, 0)
        if t:
            ag[t].start()

    for t in (*range(1, nz), 0):
        group_back(t)


    sent_all(ca)
    pa.sent()

    def g1(i, carry):
        u = i // (C // 256)
        at = rows_of(lax.rem(i, C // 256) * 256, 256, 256)
        rin[u, at, :] = nn(abst_t[at, :], mg[u]).astype(BF)
        return carry

    lax.fori_loop(0, nz * (C // 256), g1, 0)
    low = me.nq * ra
    core1 = links.copy(rin.at[:, rows_of((1 - me.c) * low, low, low)], rc1, me.at(c=1 - me.c))
    core1.start()

    for h in range(2):
        to = gather2.passing(h)
        block = range(h * (nz // 2), (h + 1) * (nz // 2))
        loads = [pltpu.make_async_copy(rp2.at[1, j], mg.at[j, pl.ds(0, rb)], local.at[j]) for j in block]
        for copy in loads:
            copy.start()
        for j, copy in zip(block, loads):
            copy.wait()
            where = mine2 + to * rb
            fold(
                lambda at, v, j=j, w=where: s2.__setitem__((j, rows_of(w + at.start, at.size, 16)), v.astype(BF)),
                [lambda at, j=j, w=where: s2[j, rows_of(w + at.start, at.size, 16)], lambda at, j=j: mg[j, at]],
                rb, min(rb, 32),
            )
        gather2.pass_on(h, gather2.chunk(to, h))

    for step in range(nz - 1):
        pl.when(jnp.logical_and(more, me.k - step >= 0))(up[step].wait_send)
        pl.when(jnp.logical_and(less, me.k + step < nz))(down[step].wait_send)

    def f2_body(i, carry):
        at = rows_of(i * 256, 256, 256)
        total = nn(hid[0], rout[0, :, at]) + bias_out[0:1, at]
        for u in range(1, nz):
            total = total + nn(hid[u], rout[u, :, at])
        abst[:, at] = total.astype(BF)
        return carry

    lax.fori_loop(0, ow // 256, f2_body, 0)
    out_tokens = pltpu.make_async_copy(abst, tokens, local.at[6])
    out_tokens.start()
    recv_all(ag[1:])
    fold(
        lambda at, v: agrad.__setitem__(at, v),
        [lambda at: agrad[at]] + [lambda at, t=t: ag_recv[t - 1, at] for t in range(1, nz)],
        T, 32,
    )
    core1.wait_recv()
    loads = [pltpu.make_async_copy(rc1.at[u], mg.at[u, pl.ds(0, low)], local.at[u]) for u in range(nz)]
    for copy in loads:
        copy.start()
    outs = []
    for u in range(nz):
        loads[u].wait()
        fold(
            lambda at, v, u=u: rin.__setitem__((u, rows_of(me.c * low + at.start, at.size, 16)), v.astype(BF)),
            [lambda at, u=u: rin[u, rows_of(me.c * low + at.start, at.size, 16)], lambda at, u=u: mg[u, at]],
            low, 32,
        )
        outs.append(pltpu.make_async_copy(rin.at[u, rows_of(me.c * low, low, low)], s1.at[u], local.at[u]))
        outs[-1].start()
    gather2.finish()
    for copy in outs:
        copy.wait()
    loads = [
        pltpu.make_async_copy(rp2.at[i], mg.at[pl.ds(0, nz), pl.ds(i * rb, rb)], local.at[i]) for i in (0, 2)
    ]
    for copy in loads:
        copy.start()
    for copy in loads:
        copy.wait()
    for j in range(nz):
        fold(
            lambda at, v, j=j: f2.__setitem__((j, at), v.astype(BF)),
            [lambda at, j=j: s2[j, rows_of(strip * rb + at.start, at.size, 16)]]
            + [lambda at, j=j, i=i: mg[j, rows_of(i * rb + at.start, at.size, 16)] for i in (0, 2)],
            rb, min(rb, 32),
        )
    out_tokens.wait()
    for group in (pb, gather2):
        group.sent()
    for group_of in (zb, zc, cb, core2, ag[1:], [rim0, rim1, core1]):
        sent_all(group_of)


def grads_kernel(
    nz, ndp, nrow, zero, one,
    s1, f2, agrad, patches, keep_zero, keep_one, rim_zero, rim_one, conv_in, conv_out, taps, gains, biases,
    mask_zero, mask_one, pool, pick, small_in,
    out1, out2, out3, small, patch_grad, rp1,
    xs, kept, keep, third, resid, weights, cmask, edge_zero, edge_one, got_zero, got_one,
    sent_on, f1, rz1, conv, rc3, rp3, f3, rz3, sc, sp, sz, send, recv, local,
):
    me = Place(nz, ndp, nrow)
    links = Links(send, recv)
    C, hw = out1.shape
    ow = f2.shape[2]
    np_ = 2 * me.nq
    strip = me.c * me.nq + me.q
    ra, rb = C // np_, hw // np_
    width = C // nrow
    R = out3.shape[2] // 2
    other = me.at(c=1 - me.c)
    first = (1 - me.r).astype(F32)
    neighbour = me.at(q=me.x * nrow + (nrow - 1 - me.r))
    me.greet()

    loads = [
        pltpu.make_async_copy(keep_one, keep, local.at[0]),
        pltpu.make_async_copy(conv_out.at[1], weights.at[1], local.at[1]),
        pltpu.make_async_copy(conv_in.at[1], weights.at[0], local.at[2]),
        pltpu.make_async_copy(keep_zero, kept, local.at[3]),
        pltpu.make_async_copy(patches, xs, local.at[4]),
    ]
    for copy in loads:
        copy.start()
    lead = nz // 2
    gather1 = Gather(
        me, links,
        lambda q, h: s1.at[pl.ds(h * lead, lead), rows_of(q * ra, ra, ra)],
        lambda i, h: rp1.at[i, pl.ds(h * lead, lead)],
    )
    gather1.start(0)
    gather1.start(1)
    row_b = rows_of(strip * rb, rb, rb)
    col_k = rows_of(me.k * ow, ow, 128)
    z2 = start_all([
        links.copy(f2.at[me.deep(t)], out2.at[row_b, col_k], me.at(k=me.deep(t))) for t in range(1, nz)
    ])
    own2 = pltpu.make_async_copy(f2.at[me.k], out2.at[row_b, col_k], local.at[5])
    own2.start()
    small[...] = jnp.zeros_like(small)
    small[32:40] = small_in[...]
    column_masks(cmask, zero.width)

    def spread(b):
        core3[b].wait_recv()
        for m in range(2):
            for x in range(me.nx):
                fold(
                    lambda at, v, i=(b, m, x, me.c): conv.__setitem__((*i, at), v.astype(BF)),
                    [lambda at, i=(b, m, x, me.c): conv[(*i, at)], lambda at, i=(b, m, x): rc3[(*i, at)]],
                    nz * R, 32,
                )
        gather = Gather(
            me, links,
            lambda q, h: conv.at[b, h, q // nrow, me.c, :, rows_of(lax.rem(q, nrow) * width, width, 128)],
            lambda i, h: rp3.at[b, i, h],
        )
        gather.start(1)
        gather.start(0)
        return gather

    def spread_on(b):
        for h in (1, 0):
            to = p3[b].passing(h)
            cols = rows_of(lax.rem(to, nrow) * width, width, 128)
            x = to // nrow
            fold(
                lambda at, v: conv.__setitem__((b, h, x, me.c, at, cols), v.astype(BF)),
                [lambda at: conv[b, h, x, me.c, at, cols], lambda at: rp3[b, 1, h, at, :]],
                nz * R, 32,
            )
            p3[b].pass_on(h, p3[b].chunk(to, h))

    core3, p3 = [None, None], [None, None]

    all_one = one.cells * one.count
    pooled, pre_one, hidden, pre_two, pre_three, pooled_grad = [
        keep.at[i // 3, pl.ds((i % 3) * all_one, all_one)] for i in range(6)
    ]
    third_one, resid_one = third.at[pl.ds(0, all_one)], resid.at[pl.ds(0, all_one)]
    loads[0].wait()
    loads[1].wait()
    back_tail_stage(
        one, one.count, lambda i: nn(pick[...], agrad[...].astype(BF)), pooled, weights.at[1], gains.at[1], biases.at[1], mask_one,
        pre_two, pre_three, resid_one, third_one, pre_three, pre_two, edge_one, first, small, 16,
    )
    rim1 = links.copy(edge_one, got_one, neighbour)
    rim1.start()
    outer_stage(third_one, pre_three, conv.at[1, 1])
    rim1.wait_recv()
    back_depth_stage(one, pre_two, got_one, hidden, rim_one, taps.at[1], None, third_one, first, C, small, 16)
    loads[2].wait()

    def to_pooled_grad(i, rows, grad):
        pooled_grad[rows] = grad.astype(BF)

    back_head_stage(
        one, one.count, third_one, weights.at[0], gains.at[1], biases.at[1], mask_one, pre_one, resid_one, pre_three, to_pooled_grad, small, 16
    )
    again = [
        pltpu.make_async_copy(conv_out.at[0], weights.at[1], local.at[1]),
        pltpu.make_async_copy(conv_in.at[0], weights.at[0], local.at[2]),
    ]
    for copy in again:
        copy.start()
    outer_stage(pre_three, pooled, conv.at[1, 0])
    core3[1] = links.copy(conv.at[1, :, :, 1 - me.c], rc3.at[1], other)
    core3[1].start()

    loads[3].wait()
    loads[4].wait()
    xs[...] = (xs[...].astype(F32) * mask_zero[...]).astype(BF)
    again[0].wait()
    back_tail_stage(
        zero, 1, lambda i: tn(pool[i], pooled_grad[one.rows(i)]), xs, weights.at[1], gains.at[0], biases.at[0], mask_zero,
        kept.at[2], kept.at[3], resid, third, kept.at[3], kept.at[2], edge_zero, first, small, 0,
    )
    rim0 = links.copy(edge_zero, got_zero, neighbour)
    rim0.start()
    p3[1] = spread(1)
    temp = [keep.at[0, pl.ds(i * lead * ra, lead * ra)] for i in range(4)]

    def bring(sources):
        copies = [
            pltpu.make_async_copy(source.at[j], to.at[pl.ds(j * ra, ra)], local.at[6 + n * lead + j])
            for n, (source, to) in enumerate(sources)
            for j in range(lead)
        ]
        for copy in copies:
            copy.start()
        for copy in copies:
            copy.wait()

    for h in range(2):
        to = gather1.passing(h)
        bring([(gather1.chunk(to, h), temp[2 * h]), (gather1.slot(1, h), temp[2 * h + 1])])
        for j in range(lead):
            fold(
                lambda at, v: sent_on.__setitem__((h, j, at), v.astype(BF)),
                [lambda at, ref=ref: ref[rows_of(j * ra + at.start, at.size, 16)] for ref in temp[2 * h : 2 * h + 2]],
                ra, 32,
            )
        gather1.pass_on(h, sent_on.at[h])
    outer_stage(third, kept.at[3], conv.at[0, 1])
    rim0.wait_recv()
    own2.wait()
    recv_all(z2)
    spread2 = Spread(me, links, lambda q, h: out2.at[
        rows_of((me.c * me.nq + q) * rb, rb, rb),
        pl.ds(0, nz * ow) if h is None else pl.ds(h * (nz * ow // 2), nz * ow // 2),
    ])
    spread2.start()
    back_depth_stage(zero, kept.at[2], got_zero, kept.at[1], rim_zero, taps.at[0], cmask, third, first, C, small, 0)
    spread_on(1)
    gather1.finish()
    for h in range(2):
        mine = [keep.at[0, pl.ds(i * lead * ra, lead * ra)] for i in range(3)]
        bring([(gather1.chunk(me.q, h), mine[0]), (gather1.slot(0, h), mine[1]), (gather1.slot(2, h), mine[2])])
        for j in range(lead):
            fold(
                lambda at, v: f1.__setitem__((h * lead + j, at), v.astype(BF)),
                [lambda at, ref=ref: ref[rows_of(j * ra + at.start, at.size, 16)] for ref in mine],
                ra, 32,
            )
    z1 = start_all([links.copy(f1.at[t], rz1.at[t - 1], me.at(k=me.deep(t))) for t in range(1, nz)])
    again[1].wait()

    def to_patches(i, rows, grad):
        resid[rows] = (grad * mask_zero[rows]).astype(BF)

    back_head_stage(
        zero, 1, third, weights.at[0], gains.at[0], biases.at[0], mask_zero, kept.at[0], resid, kept.at[3], to_patches, small, 0
    )
    out_patches = pltpu.make_async_copy(resid, patch_grad, local.at[0])
    out_patches.start()
    outer_stage(kept.at[3], xs, conv.at[0, 0])
    core3[0] = links.copy(conv.at[0, :, :, 1 - me.c], rc3.at[0], other)
    core3[0].start()
    sums = start_all([links.copy(small, sc, other)])
    p3[0] = spread(0)

    spread2.pass_on()
    recv_all(z1)
    row_a = rows_of(strip * ra, ra, ra)
    fold(
        lambda at, v: out1.__setitem__(rows_of(strip * ra + at.start, at.size, 16), v.astype(BF)),
        [lambda at: f1[0, at]] + [lambda at, t=t: rz1[t - 1, at] for t in range(1, nz)],
        ra, 32,
    )
    spread1 = Spread(me, links, lambda q, h: out1.at[
        rows_of((me.c * me.nq + q) * ra, ra, ra), pl.ds(0, hw) if h is None else pl.ds(h * (hw // 2), hw // 2)
    ])
    spread1.start()
    recv_all(sums)
    sent_all(sums)
    small[...] += sc[...]
    sums_p = start_all([links.copy(small, sp.at[t - 1], me.at(q=me.chip(t))) for t in range(1, me.nq)])

    spread_on(0)
    z3 = [None, None]
    my_cols = rows_of(me.r * width, width, 128)

    def deepen(b):
        p3[b].finish()
        for m in range(2):
            for j in range(nz):
                rows = pl.ds(j * R, R)
                total = conv[b, m, me.x, me.c, rows, my_cols].astype(F32)
                for i in (0, 2):
                    total = total + rp3[b, i, m, rows, :].astype(F32)
                f3[b, j, pl.ds(m * R, R)] = total.astype(BF)
        z3[b] = start_all([
            links.copy(f3.at[b, me.deep(t)], rz3.at[b, t - 1], me.at(k=me.deep(t))) for t in range(1, nz)
        ])

    deepen(1)
    spread1.pass_on()
    sent_all(sums_p)
    recv_all(sums_p)
    for t in range(1, me.nq):
        small[...] += sp[t - 1]
    sums_z = start_all([links.copy(small, sz.at[t - 1], me.at(k=me.deep(t))) for t in range(1, nz)])
    deepen(0)

    g3 = []
    for b in (1, 0):
        recv_all(z3[b])
        total = f3[b, me.k].astype(F32)
        for t in range(1, nz):
            total = total + rz3[b, t - 1].astype(F32)
        out3[b, me.r] = total.astype(BF)
        g3 += start_all([
            links.copy(out3.at[b, me.r], out3.at[b, me.r], me.at(q=me.x * nrow + lax.rem(me.r + t, nrow)))
            for t in range(1, nrow)
        ])
    spread2.finish()
    half_b = rows_of(me.c * me.nq * rb, me.nq * rb, me.nq * rb)
    h2 = start_all([links.copy(out2.at[half_b], out2.at[half_b], other)])
    spread1.finish()
    half_a = rows_of(me.c * me.nq * ra, me.nq * ra, me.nq * ra)
    h1 = start_all([links.copy(out1.at[half_a], out1.at[half_a], other)])
    sent_all(sums_z)
    recv_all(sums_z)
    for t in range(1, nz):
        small[...] += sz[t - 1]
    recv_all(g3)
    recv_all(h1)
    recv_all(h2)
    out_patches.wait()
    for group_of in (core3, z2, z1, z3[0], z3[1], g3, h1, h2, [rim0, rim1]):
        sent_all(group_of)
    for group in (gather1, p3[0], p3[1], spread1, spread2):
        group.sent()


def spec(*kinds):
    return [pl.BlockSpec(memory_space=kind) for kind in kinds]


def run_readout(mesh, zero, one, patches, cot, read_in, read_out, read_bias, conv_in, conv_out, taps, gains, biases, masks, pool, pick):
    nz, ndp, nrow = mesh.shape["wide"], mesh.shape["dp"], mesh.shape["row"]
    nq = ndp // 2 * nrow
    T, C = pick.shape[0], patches.shape[1]
    hw, ow = read_out.shape[0], cot.shape[1]
    tall = nz * T
    rb = hw // (2 * nq)
    copies = 6 * (nz - 1) + 24
    bias_part = jnp.broadcast_to(read_bias[0:1], (8, hw))
    bias_out = jnp.broadcast_to(read_bias[1:2], (8, ow))
    ANY = pl.ANY
    return pl.pallas_call(
        functools.partial(readout_kernel, nz, ndp, nrow, zero, one),
        out_shape=[
            jax.ShapeDtypeStruct((tall, ow), BF),
            jax.ShapeDtypeStruct((T, C), F32),
            jax.ShapeDtypeStruct((nz, C // 2, hw), BF),
            jax.ShapeDtypeStruct((nz, rb, ow), BF),
            jax.ShapeDtypeStruct((nz, 1, hw), F32),
            jax.ShapeDtypeStruct((nz, C // 2, hw), BF),
            jax.ShapeDtypeStruct((nz, nq * rb, ow), BF),
            jax.ShapeDtypeStruct((nq - 1, nz, rb, ow), BF),
            jax.ShapeDtypeStruct((4, tall, hw), BF),
            jax.ShapeDtypeStruct((2, tall, hw), BF),
            jax.ShapeDtypeStruct((zero.count, 32, C), BF),
            jax.ShapeDtypeStruct((one.count, 16, C), BF),
        ],
        in_specs=spec(ANY, VMEM, ANY, ANY, VMEM, VMEM, ANY, ANY, VMEM, VMEM, VMEM, VMEM, VMEM, VMEM, VMEM),
        out_specs=spec(ANY, VMEM, ANY, VMEM, VMEM, ANY, ANY, ANY, ANY, ANY, VMEM, VMEM),
        scratch_shapes=[
            VMEM((nz, C, hw), BF),
            VMEM((nz, hw, ow), BF),
            VMEM((nz, 8, hw), F32),
            VMEM((tall, C), BF),
            VMEM((C, tall), BF),
            VMEM((nz, tall, hw), BF),
            VMEM((nz, tall, hw), BF),
            VMEM((nz - 1, T, C), BF),
            VMEM((nz - 1, T, C), BF),
            VMEM((nz, hw, ow), BF),
            VMEM((2, zero.cells + 2 * zero.width, 128), F32),
            VMEM((zero.count, 32, C), BF),
            VMEM((one.count, 16, C), BF),
            pltpu.SemaphoreType.DMA((copies,)),
            pltpu.SemaphoreType.DMA((copies,)),
            pltpu.SemaphoreType.DMA((7,)),
        ],
        compiler_params=pltpu.CompilerParams(
            collective_id=0, has_side_effects=True, vmem_limit_bytes=LIMIT
        ),
        name="readout",
    )(patches, cot, read_in, read_out, bias_part, bias_out, conv_in, conv_out, taps, gains, biases, *masks, pool, pick)


LIMIT = 62 * 1024 * 1024


def run_grads(mesh, zero, one, s1, f2, agrad, patches, keep_zero, keep_one, rim_zero, rim_one, conv_in, conv_out, taps, gains, biases, masks, pool, pick, small_in):
    nz, ndp, nrow = mesh.shape["wide"], mesh.shape["dp"], mesh.shape["row"]
    nq = ndp // 2 * nrow
    nx = ndp // 2
    C, hw = s1.shape[1] * 2, s1.shape[2]
    _, rb, ow = f2.shape
    ra = C // (2 * nq)
    R = C // (ndp * nz)
    tall = patches.shape[0]
    S = 40
    copies = 5 * (nz - 1) + 40
    width = C // nrow
    ANY = pl.ANY
    return pl.pallas_call(
        functools.partial(grads_kernel, nz, ndp, nrow, zero, one),
        out_shape=[
            jax.ShapeDtypeStruct((C, hw), BF),
            jax.ShapeDtypeStruct((hw, nz * ow), BF),
            jax.ShapeDtypeStruct((2, nrow, 2 * R, width), BF),
            jax.ShapeDtypeStruct((S, C), F32),
            jax.ShapeDtypeStruct((tall, C), BF),
            jax.ShapeDtypeStruct((nq - 1, nz, ra, hw), BF),
        ],
        in_specs=spec(ANY, VMEM, VMEM, ANY, ANY, ANY, VMEM, VMEM, ANY, ANY, VMEM, VMEM, VMEM, VMEM, VMEM, VMEM, VMEM, VMEM),
        out_specs=spec(VMEM, ANY, VMEM, VMEM, ANY, ANY),
        scratch_shapes=[
            VMEM((tall, C), BF),
            VMEM((4, tall, C), BF),
            VMEM((2, tall, C), BF),
            VMEM((tall, C), BF),
            VMEM((tall, C), BF),
            VMEM((2, C, C), BF),
            VMEM((2, zero.cells + 2 * zero.width, 128), F32),
            VMEM((zero.count, 32, C), BF),
            VMEM((one.count, 16, C), BF),
            VMEM((zero.count, 32, C), BF),
            VMEM((one.count, 16, C), BF),
            VMEM((2, nz // 2, ra, hw), BF),
            VMEM((nz, ra, hw), BF),
            VMEM((nz - 1, ra, hw), BF),
            VMEM((2, 2, nx, 2, nz * R, C), BF),
            VMEM((2, 2, nx, nz * R, C), BF),
            VMEM((2, nq - 1, 2, nz * R, width), BF),
            VMEM((2, nz, 2 * R, width), BF),
            VMEM((2, nz - 1, 2 * R, width), BF),
            VMEM((S, C), F32),
            VMEM((nq - 1, S, C), F32),
            VMEM((nz - 1, S, C), F32),
            pltpu.SemaphoreType.DMA((copies,)),
            pltpu.SemaphoreType.DMA((copies,)),
            pltpu.SemaphoreType.DMA((6 + nq * nz,)),
        ],
        compiler_params=pltpu.CompilerParams(
            collective_id=1, has_side_effects=True, vmem_limit_bytes=LIMIT
        ),
        name="grads",
    )(s1, f2, agrad, patches, keep_zero, keep_one, rim_zero, rim_one, conv_in, conv_out, taps, gains, biases, *masks, pool, pick, small_in)


POOL = 12


eps_norm = 1e-06
exact_mode = lax.Precision.HIGHEST


def extended(cells, sides, width):
    for axis, dim in sides:
        count = lax.axis_size(axis)
        ends = count - 1
        head = lax.slice_in_dim(cells, 0, width, axis=dim)
        tail = lax.slice_in_dim(cells, cells.shape[dim] - width, cells.shape[dim], axis=dim)
        cells = jnp.concatenate(
            [
                lax.ppermute(tail, axis, [(i, (i + 1) % count) for i in range(ends)]),
                cells,
                lax.ppermute(head, axis, [((i + 1) % count, i) for i in range(ends)]),
            ],
            axis=dim,
        )
    return cells


def layer_norm(values, gain_row, bias_row):
    centre = jnp.mean(values, axis=-1, keepdims=True)
    centred = values - centre
    variance = jnp.mean(centred * centred, axis=-1, keepdims=True)
    return centred * lax.rsqrt(variance + eps_norm) * gain_row + bias_row


def head_piece(pre_values, gain_row, bias_row, live_mask):
    return jax.nn.silu(layer_norm(pre_values, gain_row, bias_row)) * live_mask


def tail_piece(source, third_pre, gain_row, bias_row, live_mask):
    return jax.nn.silu(source + layer_norm(third_pre, gain_row, bias_row)) * live_mask


def outer_sum(left_rows, right_rows):
    return lax.dot_general(
        left_rows, right_rows, (((0,), (0,)), ((), ())), preferred_element_type=jnp.float32
    )


def times_transposed(left_rows, weight):
    return lax.dot_general(
        left_rows, weight, (((1,), (1,)), ((), ())), preferred_element_type=jnp.float32
    )


def pad_columns(values):
    return jnp.pad(values, ((0, 0), (0, 0), (1, 1), (0, 0)))


def rows_forward(hidden_one):
    return extended(hidden_one, (("row", 1),), 1)


def rows_backward(second_low):
    return extended(second_low, (("row", 1),), 1)


def depth_apply(padded, tap_table, row_count, col_count):
    result = jnp.zeros((padded.shape[0], row_count, col_count, padded.shape[3]), jnp.float32)
    for offset in range(9):
        window = padded[
            :, offset // 3 : offset // 3 + row_count, offset % 3 : offset % 3 + col_count, :
        ]
        result = result + window.astype(jnp.float32) * tap_table[offset].astype(jnp.float32)
    return result


def block_forward(source, live_mask, weights):
    w_first, w_last, tap_table, gain_rows, bias_rows = weights
    grid_count, row_count, col_count, channels = source.shape
    flat_rows = source.astype(jnp.bfloat16).reshape(-1, channels)
    first_pre = jnp.dot(flat_rows, w_first, preferred_element_type=jnp.float32).reshape(
        source.shape
    )
    hidden_one = head_piece(first_pre, gain_rows[0], bias_rows[0], live_mask).astype(jnp.bfloat16)
    padded_one = pad_columns(rows_forward(hidden_one))
    second_pre = depth_apply(padded_one, tap_table, row_count, col_count)
    hidden_two = head_piece(second_pre, gain_rows[1], bias_rows[1], live_mask).astype(jnp.bfloat16)
    two_rows = hidden_two.reshape(-1, channels)
    third_pre = jnp.dot(two_rows, w_last, preferred_element_type=jnp.float32).reshape(source.shape)
    output = tail_piece(source, third_pre, gain_rows[2], bias_rows[2], live_mask)
    return (output, (flat_rows, first_pre, padded_one, second_pre, two_rows, third_pre))


def block_backward(output_grad, source, live_mask, weights, kept):
    w_first, w_last, tap_table, gain_rows, bias_rows = weights
    flat_rows, first_pre, padded_one, second_pre, two_rows, third_pre = kept
    grid_count, row_count, col_count, channels = source.shape
    _, tail_back = jax.vjp(
        functools.partial(tail_piece, live_mask=live_mask), source, third_pre, gain_rows[2], bias_rows[2]
    )
    residual_grad, third_grad, gain_three, bias_three = tail_back(output_grad)
    third_low = third_grad.astype(jnp.bfloat16).reshape(-1, channels)
    grad_last = outer_sum(two_rows, third_low)
    two_grad = times_transposed(third_low, w_last).reshape(source.shape)
    _, middle_back = jax.vjp(
        functools.partial(head_piece, live_mask=live_mask), second_pre, gain_rows[1], bias_rows[1]
    )
    second_grad, gain_two, bias_two = middle_back(two_grad)
    second_low = second_grad.astype(jnp.bfloat16)
    padded_grad = pad_columns(rows_backward(second_low))
    one_grad = depth_apply(padded_grad, tap_table[::-1], row_count, col_count)
    second_wide = second_low.astype(jnp.float32)
    tap_grads = []
    for offset in range(9):
        window = padded_one[
            :, offset // 3 : offset // 3 + row_count, offset % 3 : offset % 3 + col_count, :
        ]
        tap_grads.append(jnp.sum(second_wide * window.astype(jnp.float32), axis=(0, 1, 2)))
    _, first_back = jax.vjp(
        functools.partial(head_piece, live_mask=live_mask), first_pre, gain_rows[0], bias_rows[0]
    )
    first_grad, gain_one, bias_one = first_back(one_grad)
    first_low = first_grad.astype(jnp.bfloat16).reshape(-1, channels)
    grad_first = outer_sum(flat_rows, first_low)
    source_grad = residual_grad + times_transposed(first_low, w_first).reshape(source.shape)
    grads = (
        grad_first,
        grad_last,
        jnp.stack(tap_grads),
        jnp.stack([gain_one, gain_two, gain_three]),
        jnp.stack([bias_one, bias_two, bias_three]),
    )
    return (source_grad, grads)


def pool_weights(grid_side, row_shift, pooled_index, slot_index):
    place = slot_index - row_shift
    begin = pooled_index * grid_side // POOL
    finish = ((pooled_index + 1) * grid_side + POOL - 1) // POOL
    inside = (place >= begin) & (place < finish)
    return jnp.where(inside, 1.0, 0.0).astype(jnp.float32) / (finish - begin).astype(jnp.float32)


def plain(
    patches,
    grid_sizes,
    conv_in,
    conv_out,
    depth_taps,
    norm_gain,
    norm_bias,
    read_in,
    read_bias,
    read_out,
    cotangent,
):
    grid_count, local_rows, grid_width, channels = patches.shape
    row_place = lax.axis_index("row")
    slot_rows = row_place * local_rows + jnp.arange(local_rows, dtype=jnp.int32)
    column_index = jnp.arange(grid_width, dtype=jnp.int32)
    row_shift = (grid_width - grid_sizes) // 2
    row_live = (slot_rows[None, :] >= row_shift[:, None]) & (
        slot_rows[None, :] < (row_shift + grid_sizes)[:, None]
    )
    col_live = column_index[None, :] < grid_sizes[:, None]
    live_mask = (row_live[:, :, None] & col_live[:, None, :]).astype(jnp.float32)[..., None]
    weights_one = (conv_in[0], conv_out[0], depth_taps[0], norm_gain[0], norm_bias[0])
    weights_two = (conv_in[1], conv_out[1], depth_taps[1], norm_gain[1], norm_bias[1])
    source = patches.astype(jnp.float32) * live_mask
    encoded, kept_one = block_forward(source, live_mask, weights_one)
    pool_local = POOL // lax.axis_size("row")
    pooled_index = row_place * pool_local + jnp.arange(pool_local, dtype=jnp.int32)
    side_shaped = grid_sizes[:, None, None]
    row_pool = pool_weights(
        side_shaped, row_shift[:, None, None], pooled_index[None, :, None], slot_rows[None, None, :]
    )
    col_pool = pool_weights(
        side_shaped,
        0,
        jnp.arange(POOL, dtype=jnp.int32)[None, :, None],
        column_index[None, None, :],
    )
    pooled = jnp.einsum("gir,gjw,grwc->gijc", row_pool, col_pool, encoded, precision=exact_mode)
    all_live = jnp.ones((grid_count, pool_local, POOL, 1), jnp.float32)
    abstract, kept_two = block_forward(pooled, all_live, weights_two)
    token_rows = abstract.astype(jnp.bfloat16).reshape(-1, channels)
    gathered = lax.all_gather(token_rows, "wide", axis=0, tiled=True)
    gelu_exact = functools.partial(jax.nn.gelu, approximate=False)
    mixed_pre = jnp.dot(gathered, read_in, preferred_element_type=jnp.float32) + read_bias[0]
    hidden_wide, gelu_back = jax.vjp(gelu_exact, mixed_pre)
    hidden = hidden_wide.astype(jnp.bfloat16)
    partial_out = jnp.dot(hidden, read_out, preferred_element_type=jnp.float32)
    summed = (
        lax.psum_scatter(
            partial_out.astype(jnp.bfloat16), "wide", scatter_dimension=1, tiled=True
        ).astype(jnp.float32)
        + read_bias[1]
    )
    tokens = summed.astype(jnp.bfloat16).reshape(cotangent.shape)
    cot_local = cotangent.reshape(-1, cotangent.shape[-1])
    cot_all = lax.all_gather(cot_local, "wide", axis=1, tiled=True)
    hidden_grad = times_transposed(cot_all, read_out)
    mixed_grad = gelu_back(hidden_grad)[0].astype(jnp.bfloat16)
    grad_exit = outer_sum(hidden, cot_all)
    grad_entry = outer_sum(gathered, mixed_grad)
    bias_pair = jnp.stack(
        [
            jnp.sum(mixed_grad.astype(jnp.float32), axis=0),
            jnp.sum(cot_local.astype(jnp.float32), axis=0),
        ]
    )
    abstract_grad = lax.psum_scatter(
        times_transposed(mixed_grad, read_in).astype(jnp.bfloat16),
        "wide",
        scatter_dimension=0,
        tiled=True,
    ).astype(jnp.float32)
    grad_entry, bias_pair, grad_exit = (
        lax.psum(grad_entry.astype(jnp.bfloat16), ("dp", "row")).astype(jnp.float32),
        lax.psum(bias_pair.astype(jnp.bfloat16), ("dp", "row")).astype(jnp.float32),
        lax.psum(grad_exit.astype(jnp.bfloat16), ("dp", "row")).astype(jnp.float32),
    )
    pooled_grad, grads_two = block_backward(
        abstract_grad.reshape(abstract.shape), pooled, all_live, weights_two, kept_two
    )
    encoded_grad = jnp.einsum(
        "gir,gjw,gijc->grwc", row_pool, col_pool, pooled_grad, precision=exact_mode
    )
    source_grad, grads_one = block_backward(encoded_grad, source, live_mask, weights_one, kept_one)
    patch_grad = (source_grad * live_mask).astype(jnp.bfloat16)
    stacked = tuple((jnp.stack([grads_one[index], grads_two[index]]) for index in range(5)))
    totals = (
        lax.psum_scatter(stacked[0], ("dp", "wide"), scatter_dimension=2, tiled=True),
        lax.psum_scatter(stacked[1], ("dp", "wide"), scatter_dimension=2, tiled=True),
        lax.psum_scatter(stacked[2], ("dp", "wide"), scatter_dimension=2, tiled=True),
        lax.psum_scatter(stacked[3], ("dp", "wide"), scatter_dimension=2, tiled=True),
        lax.psum_scatter(stacked[4], ("dp", "wide"), scatter_dimension=2, tiled=True),
    )
    totals = (
        lax.psum(totals[0].astype(jnp.bfloat16), "row").astype(jnp.float32),
        lax.psum(totals[1].astype(jnp.bfloat16), "row").astype(jnp.float32),
        lax.psum(totals[2].astype(jnp.bfloat16), "row").astype(jnp.float32),
        lax.psum(totals[3].astype(jnp.bfloat16), "row").astype(jnp.float32),
        lax.psum(totals[4].astype(jnp.bfloat16), "row").astype(jnp.float32),
    )
    return (
        tokens,
        patch_grad,
        totals[0],
        totals[1],
        totals[2],
        totals[3],
        totals[4],
        grad_entry,
        bias_pair,
        grad_exit,
    )


def on_device(
    mesh,
    patches,
    grid_sizes,
    conv_in,
    conv_out,
    depth_taps,
    norm_gain,
    norm_bias,
    read_in,
    read_bias,
    read_out,
    cotangent,
):
    nz, ndp = mesh.shape["wide"], mesh.shape["dp"]
    grid_count, local_rows, grid_width, channels = patches.shape
    row_place = lax.axis_index("row")
    slot_rows = row_place * local_rows + jnp.arange(local_rows, dtype=jnp.int32)
    column_index = jnp.arange(grid_width, dtype=jnp.int32)
    row_shift = (grid_width - grid_sizes) // 2
    row_live = (slot_rows[None, :] >= row_shift[:, None]) & (
        slot_rows[None, :] < (row_shift + grid_sizes)[:, None]
    )
    col_live = column_index[None, :] < grid_sizes[:, None]
    live_mask = (row_live[:, :, None] & col_live[:, None, :]).astype(jnp.float32)[..., None]
    pool_local = POOL // lax.axis_size("row")
    pooled_index = row_place * pool_local + jnp.arange(pool_local, dtype=jnp.int32)
    side_shaped = grid_sizes[:, None, None]
    row_pool = pool_weights(
        side_shaped, row_shift[:, None, None], pooled_index[None, :, None], slot_rows[None, None, :]
    )
    col_pool = pool_weights(
        side_shaped,
        0,
        jnp.arange(POOL, dtype=jnp.int32)[None, :, None],
        column_index[None, None, :],
    )
    zero = Geometry(grid_count, local_rows, grid_width)
    one = Geometry(grid_count, pool_local, 16)
    col_wide = jnp.pad(col_pool, ((0, 0), (0, one.width - POOL), (0, 0)))
    pool = (row_pool[:, :, None, :, None] * col_wide[:, None, :, None, :]).reshape(grid_count, one.cells, zero.cells)
    places = jnp.arange(grid_count * pool_local * POOL, dtype=jnp.int32)
    places = places // POOL * one.width + places % POOL
    pick = (places[:, None] == jnp.arange(grid_count * one.cells, dtype=jnp.int32)[None, :]).astype(BF)
    mask_zero = live_mask.reshape(-1, 1)
    mask_one = (jnp.arange(grid_count * one.cells, dtype=jnp.int32) % one.width < POOL).astype(F32)[:, None]
    cot_local = cotangent.reshape(-1, cotangent.shape[-1])
    shared = (conv_in, conv_out, depth_taps.astype(F32), norm_gain, norm_bias, (mask_zero, mask_one), pool.astype(BF))
    flat = patches.reshape(-1, channels)
    tokens, agrad, s1, f2, hsum, _, _, _, keep_zero, keep_one, rim_zero, rim_one = run_readout(
        mesh, zero, one, flat, cot_local, read_in, read_out, read_bias, *shared, pick
    )
    tokens = tokens.reshape(cotangent.shape)
    cot_sum = jnp.sum(cot_local.astype(F32), axis=0)
    width = cot_sum.shape[0]
    cot_row = lax.dynamic_update_slice(
        jnp.zeros((nz * width,), F32), cot_sum, (lax.axis_index("wide") * width,)
    )
    small = jnp.concatenate([hsum.reshape(-1, channels), cot_row.reshape(-1, channels)])
    out1, out2, out3, small, patch_grad, _ = run_grads(
        mesh, zero, one, s1, f2, agrad, flat, keep_zero, keep_one, rim_zero, rim_one, *shared, pick.T, small
    )
    patch_grad = patch_grad.reshape(patches.shape)
    R = channels // (ndp * nz)
    out3 = out3.reshape(2, -1, 2, R, out3.shape[-1]).transpose(0, 2, 1, 4, 3).reshape(2, 2, channels, R).astype(F32)
    place = lax.axis_index("dp") * nz + lax.axis_index("wide")
    own = lax.dynamic_slice_in_dim(small, place * R, R, axis=1)
    own = own[:32].reshape(2, 16, R)
    taps, gains, biases = own[:, 0:9], own[:, 9:12], own[:, 12:15]
    bias_pair = lax.dynamic_slice_in_dim(small[32:40].reshape(2, -1), lax.axis_index("wide") * width, width, axis=1)
    return (
        tokens,
        patch_grad,
        out3[:, 0],
        out3[:, 1],
        taps,
        gains,
        biases,
        out1.astype(F32),
        bias_pair,
        out2.astype(F32),
    )


def fits(mesh):
    return mesh.shape["wide"] == 4 and mesh.shape["dp"] % 2 == 0 and mesh.shape["row"] == 2


def solution(mesh):

    placed = (
        P(("dp", "wide"), "row", None, None),
        P(("dp", "wide")),
        P(),
        P(),
        P(),
        P(),
        P(),
        P(None, "wide"),
        P(None, "wide"),
        P("wide", None),
        P("dp", "row", None, "wide"),
    )
    return jax.shard_map(
        functools.partial(on_device, mesh) if fits(mesh) else plain,
        mesh=mesh,
        in_specs=placed,
        out_specs=(
            P("dp", "row", None, "wide"),
            P(("dp", "wide"), "row", None, None),
            P(None, None, ("dp", "wide")),
            P(None, None, ("dp", "wide")),
            P(None, None, ("dp", "wide")),
            P(None, None, ("dp", "wide")),
            P(None, None, ("dp", "wide")),
            P(None, "wide"),
            P(None, "wide"),
            P("wide", None),
        ),
        check_vma=False,
    )
```

```python
import functools

import jax
import jax.numpy as jnp
from jax import lax
from jax.experimental import pallas as pl
from jax.experimental.pallas import tpu as pltpu
from jax.sharding import PartitionSpec as P

MESH = pl.DeviceIdType.MESH
BF = jnp.bfloat16
F32 = jnp.float32
VMEM = pltpu.VMEM


class Place:
    def __init__(self, nz, ndp, nrow):
        self.nz, self.ndp, self.nrow = nz, ndp, nrow
        self.nx = ndp // 2
        self.nq = self.nx * nrow
        self.k = lax.axis_index("wide")
        self.r = lax.axis_index("row")
        d = lax.axis_index("dp")
        self.c = lax.rem(d, 2)
        self.x = d // 2
        self.q = self.x * nrow + self.r
        self.qx = (1 - self.x) * nrow + self.r
        self.qy = self.x * nrow + (1 - self.r)
        self.qd = (1 - self.x) * nrow + (1 - self.r)

    def at(self, q=None, c=None, k=None):
        q = self.q if q is None else q
        c = self.c if c is None else c
        k = self.k if k is None else k
        return {"dp": (q // self.nrow) * 2 + c, "row": lax.rem(q, self.nrow), "wide": k}

    def chip(self, t):
        return lax.rem(self.q + t, self.nq)

    def deep(self, t):
        return lax.rem(self.k + t, self.nz)

    def peers(self):
        return (
            [self.at(q=self.chip(t)) for t in range(1, self.nq)]
            + [self.at(c=1 - self.c)]
            + [self.at(k=self.deep(t)) for t in range(1, self.nz)]
        )

    def greet(self):
        barrier = pltpu.get_barrier_semaphore()
        peers = self.peers()
        for peer in peers:
            pl.semaphore_signal(barrier, inc=1, device_id=peer, device_id_type=MESH)
        pl.semaphore_wait(barrier, len(peers))


class Links:
    def __init__(self, send, recv):
        self.send, self.recv, self.used = send, recv, 0

    def copy(self, src, dst, peer):
        at = self.used
        self.used += 1
        assert self.used <= self.send.shape[0]
        return pltpu.make_async_remote_copy(
            src_ref=src, dst_ref=dst, send_sem=self.send.at[at], recv_sem=self.recv.at[at],
            device_id=peer, device_id_type=MESH,
        )


def start_all(copies):
    for copy in copies:
        copy.start()
    return copies


def recv_all(copies):
    for copy in copies:
        copy.wait_recv()


def sent_all(copies):
    for copy in copies:
        copy.wait_send()


class Spread:
    def __init__(self, me, links, strip):
        self.me, self.links, self.strip = me, links, strip
        self.first = self.second = ()

    def start(self):
        me = self.me
        own = self.strip(me.q, None)
        self.first = start_all([self.links.copy(own, own, me.at(q=q)) for q in (me.qx, me.qy)])

    def pass_on(self):
        me = self.me
        along_y = self.strip(me.qx, 0)
        along_x = self.strip(me.qy, 1)
        self.second = [
            self.links.copy(along_y, along_y, me.at(q=me.qy)),
            self.links.copy(along_x, along_x, me.at(q=me.qx)),
        ]
        for arrived, copy in zip(self.first, self.second):
            arrived.wait_recv()
            copy.start()

    def finish(self):
        recv_all(self.second)

    def sent(self):
        sent_all(self.first)
        sent_all(self.second)


class Gather:
    def __init__(self, me, links, chunk, slot):
        self.me, self.links, self.chunk, self.slot = me, links, chunk, slot
        self.early = [[], []]
        self.late = [None, None]

    def start(self, half):
        me = self.me
        to = me.qx if half == 0 else me.qy
        self.early[half] = start_all([
            self.links.copy(self.chunk(q, half), self.slot(i, half), me.at(q=to)) for i, q in ((1, me.qd), (0, to))
        ])

    def passing(self, half):
        self.early[half][0].wait_recv()
        return self.me.qy if half == 0 else self.me.qx

    def pass_on(self, half, total):
        to = self.me.qy if half == 0 else self.me.qx
        self.late[half] = self.links.copy(total, self.slot(2, half), self.me.at(q=to))
        self.late[half].start()

    def finish(self):
        for half in range(2):
            self.early[half][1].wait_recv()
            self.late[half].wait_recv()

    def sent(self):
        for half in range(2):
            sent_all(self.early[half])
            self.late[half].wait_send()


def rows_of(start, size, unit):
    return pl.ds(pl.multiple_of(start, unit), size)


def fold(out, parts, rows, step):
    def body(i, carry):
        at = rows_of(i * step, step, step)
        total = parts[0](at).astype(F32)
        for part in parts[1:]:
            total = total + part(at).astype(F32)
        out(at, total)
        return carry

    lax.fori_loop(0, rows // step, body, 0)


def nt(a, b):
    return lax.dot_general(a, b, (((1,), (1,)), ((), ())), preferred_element_type=F32)


def nn(a, b):
    return jnp.dot(a, b, preferred_element_type=F32)


def tn(a, b):
    return lax.dot_general(a, b, (((0,), (0,)), ((), ())), preferred_element_type=F32)


def gelu_pair(v):
    dense = jnp.exp(-0.5 * v * v)
    s = 1.0 / (1.0 + (0.3275911 * 0.7071067811865476) * jnp.abs(v))
    poly = s * (0.254829592 + s * (-0.284496736 + s * (1.421413741 + s * (-1.453152027 + s * 1.061405429))))
    tail = 0.5 * poly * dense
    phi = jnp.where(v >= 0, 1.0 - tail, tail)
    return v * phi, phi + v * dense * 0.3989422804014327


def normal(v):
    centred = v - jnp.mean(v, axis=-1, keepdims=True)
    scale = lax.rsqrt(jnp.mean(centred * centred, axis=-1, keepdims=True) + 1e-06)
    return centred * scale, scale


def sigmoid(v):
    return 1.0 / (1.0 + jnp.exp(-v))


def live_stage(sizes, row, zero, one, mask_zero, mask_one, pool):
    side, across, pooled = zero.width, one.width, POOL

    def counted(shape, axis, width):
        place = lax.broadcasted_iota(jnp.int32, shape, axis)
        return lax.div(place, jnp.int32(width)), lax.rem(place, jnp.int32(width))

    def share(cell, out, size):
        begin = lax.div(out * size, jnp.int32(pooled))
        end = lax.div((out + 1) * size + (pooled - 1), jnp.int32(pooled))
        return jnp.where((cell >= begin) & (cell < end), 1.0 / (end - begin).astype(F32), 0.0)

    for g in range(zero.count):
        size = sizes[g]
        shift = lax.div(side - size, jnp.int32(2))
        r, c = counted((zero.cells, 1), 0, side)
        r = r + row * zero.height - shift
        mask_zero[zero.rows(g)] = jnp.where((r >= 0) & (r < size) & (c < size), 1.0, 0.0)
        i, j = counted((one.cells, zero.cells), 0, across)
        r, c = counted((one.cells, zero.cells), 1, side)
        weight = share(r + row * zero.height - shift, i + row * one.height, size) * share(c, j, size)
        pool[g] = jnp.where(j < pooled, weight, 0.0).astype(BF)
    _, c = counted(mask_one.shape, 0, across)
    mask_one[...] = jnp.where(c < pooled, 1.0, 0.0)


def picked(shape, axis, width):
    cell, place = lax.broadcasted_iota(jnp.int32, shape, axis), lax.broadcasted_iota(jnp.int32, shape, 1 - axis)
    cell = lax.div(cell, jnp.int32(POOL)) * width + lax.rem(cell, jnp.int32(POOL))
    return jnp.where(cell == place, 1.0, 0.0).astype(BF)


def silu_of(v):
    return v * sigmoid(v)


def column_masks(cmask, width):
    place = lax.rem(lax.broadcasted_iota(jnp.int32, cmask.shape[1:], 0), width)
    cmask[0] = jnp.where(place != 0, 1.0, 0.0)
    cmask[1] = jnp.where(place != width - 1, 1.0, 0.0)


def windows(cells, rim, first, masks):
    middle = jnp.concatenate([rim * (1.0 - first), cells, rim * first], axis=0)
    count = middle.shape[0]
    left, right = pltpu.roll(middle, 1, 0), pltpu.roll(middle, count - 1, 0)
    if masks is not None:
        left, right = left * masks[0], right * masks[1]
    return left, middle, right


class Geometry:
    def __init__(self, count, height, width):
        self.count, self.height, self.width = count, height, width
        self.cells = height * width

    def rows(self, g):
        return rows_of(g * self.cells, self.cells, 16)


def head_stage(shape, per, x_of, w, gains, biases, mask, pre, hidden, rim_send, first):
    cells = shape.cells * per

    def body(i, carry):
        rows = rows_of(i * cells, cells, 16)
        x = x_of(rows)
        value = nn(x, w[...])
        pre[rows] = value.astype(BF)
        n, _ = normal(value)
        h = silu_of(n * gains[0:1] + biases[0:1]) * mask[rows]
        hidden[rows] = h.astype(BF)
        for g in range(per):
            at = g * shape.cells
            top = h[at : at + shape.width]
            bottom = h[at + shape.cells - shape.width : at + shape.cells]
            rim_send[i * per + g, pl.ds(0, shape.width)] = (bottom * first + top * (1.0 - first)).astype(BF)
        return carry

    lax.fori_loop(0, shape.count // per, body, 0)


def depth_stage(shape, hidden, rim, taps, cmask, pre, first, channels):
    def body(i, carry):
        g, l = i // (channels // 128), lax.rem(i, channels // 128)
        rows, lanes = shape.rows(g), rows_of(l * 128, 128, 128)
        shifted = windows(
            hidden[rows, lanes].astype(F32),
            rim[g, pl.ds(0, shape.width), lanes].astype(F32),
            first,
            None if cmask is None else (cmask[0], cmask[1]),
        )
        total = jnp.zeros((shape.cells, 128), F32)
        for a in range(3):
            for b in range(3):
                piece = shifted[b][a * shape.width : a * shape.width + shape.cells]
                total = total + piece * taps[3 * a + b : 3 * a + b + 1, lanes]
        pre[rows, lanes] = total.astype(BF)
        return carry

    lax.fori_loop(0, shape.count * (channels // 128), body, 0)


def tail_stage(shape, per, x, w, gains, biases, mask, pre_two, pre_three, result):
    cells = shape.cells * per

    def body(i, carry):
        rows = rows_of(i * cells, cells, 16)
        n, _ = normal(pre_two[rows].astype(F32))
        h = (silu_of(n * gains[1:2] + biases[1:2]) * mask[rows]).astype(BF)
        value = nn(h, w[...])
        pre_three[rows] = value.astype(BF)
        n, _ = normal(value)
        out = silu_of(x[rows].astype(F32) + n * gains[2:3] + biases[2:3]) * mask[rows]
        result(i, rows, out)
        return carry

    lax.fori_loop(0, shape.count // per, body, 0)


def slope_of(v, s):
    return s * (1.0 + v * (1.0 - s))


def norm_back(n, scale, grad, gain, sums, at):
    sums[at : at + 1] += jnp.sum(grad * n, axis=0, keepdims=True)
    sums[at + 3 : at + 4] += jnp.sum(grad, axis=0, keepdims=True)
    dn = grad * gain
    return scale * (dn - jnp.mean(dn, axis=-1, keepdims=True) - n * jnp.mean(dn * n, axis=-1, keepdims=True))


def back_tail_stage(shape, per, grad_of, x, w, gains, biases, mask, pre_two, pre_three, resid, third, hidden_two, second, edge, first, sums, base):
    cells = shape.cells * per

    def body(i, carry):
        rows = rows_of(i * cells, cells, 16)
        live = mask[rows]
        n, scale = normal(pre_three[rows].astype(F32))
        v = x[rows].astype(F32) + n * gains[2:3] + biases[2:3]
        grad = grad_of(i) * slope_of(v, sigmoid(v)) * live
        resid[rows] = grad.astype(BF)
        low = norm_back(n, scale, grad, gains[2:3], sums, base + 11).astype(BF)
        third[rows] = low
        grad = nt(low, w[...])
        n, scale = normal(pre_two[rows].astype(F32))
        v = n * gains[1:2] + biases[1:2]
        s = sigmoid(v)
        hidden_two[rows] = (v * s * live).astype(BF)
        grad = norm_back(n, scale, grad * live * slope_of(v, s), gains[1:2], sums, base + 10)
        second[rows] = grad.astype(BF)
        for g in range(per):
            at = g * shape.cells
            top = grad[at : at + shape.width]
            bottom = grad[at + shape.cells - shape.width : at + shape.cells]
            edge[i * per + g, pl.ds(0, shape.width)] = (bottom * first + top * (1.0 - first)).astype(BF)
        return carry

    lax.fori_loop(0, shape.count // per, body, 0)


def back_depth_stage(shape, second, rim, hidden, hidden_rim, taps, cmask, result, first, channels, sums, base):
    masks = None if cmask is None else (cmask[0], cmask[1])

    def body(i, carry):
        g, l = i // (channels // 128), lax.rem(i, channels // 128)
        rows, lanes = shape.rows(g), rows_of(l * 128, 128, 128)
        edge = pl.ds(0, shape.width)
        grad = second[rows, lanes].astype(F32)
        shifted = windows(grad, rim[g, edge, lanes].astype(F32), first, masks)
        total = jnp.zeros((shape.cells, 128), F32)
        for a in range(3):
            for b in range(3):
                at = (2 - a) * shape.width
                total = total + shifted[2 - b][at : at + shape.cells] * taps[3 * a + b : 3 * a + b + 1, lanes]
        result[rows, lanes] = total.astype(BF)
        shifted = windows(hidden[rows, lanes].astype(F32), hidden_rim[g, edge, lanes].astype(F32), first, masks)
        for a in range(3):
            for b in range(3):
                at = a * shape.width
                line = base + 3 * a + b
                sums[line : line + 1, lanes] += jnp.sum(
                    grad * shifted[b][at : at + shape.cells], axis=0, keepdims=True
                )
        return carry

    lax.fori_loop(0, shape.count * (channels // 128), body, 0)


def back_head_stage(shape, per, one_grad, w, gains, biases, mask, pre_one, resid, first_low, result, sums, base):
    cells = shape.cells * per

    def body(i, carry):
        rows = rows_of(i * cells, cells, 16)
        n, scale = normal(pre_one[rows].astype(F32))
        v = n * gains[0:1] + biases[0:1]
        grad = one_grad[rows].astype(F32) * mask[rows] * slope_of(v, sigmoid(v))
        low = norm_back(n, scale, grad, gains[0:1], sums, base + 9).astype(BF)
        first_low[rows] = low
        result(i, rows, resid[rows].astype(F32) + nt(low, w[...]))
        return carry

    lax.fori_loop(0, shape.count // per, body, 0)


def outer_stage(left, right, out):
    high = out.shape[2]

    def body(i, carry):
        at = rows_of(i * high, high, 128)
        out[i // 2, lax.rem(i, 2)] = tn(left[:, at], right[...]).astype(BF)
        return carry

    lax.fori_loop(0, out.shape[0] * 2, body, 0)


def readout_kernel(
    nz, ndp, nrow, zero, one,
    sizes, patches, cot, rin_part, rout_part, bias_part, conv_in, conv_out, pack,
    tokens, agrad, s1, f2, early, rc1, rc2, rp2, keep_zero, keep_one, rim_zero, rim_one,
    mask_zero, mask_one, pool, hsum, rin, rout, bias, abst, abst_t, hid, mg, ag_send, ag_recv, s2, cmask, edge_zero, edge_one, send, recv, local,
):
    me = Place(nz, ndp, nrow)
    links = Links(send, recv)
    taps, gains, biases = [[pack.at[b, pl.ds(at, n)] for b in range(2)] for at, n in ((0, 16), (16, 8), (24, 8))]
    T, C = agrad.shape
    hw, ow = rout.shape[1], rout.shape[2]
    tall = nz * T
    np_ = 2 * me.nq
    strip = me.c * me.nq + me.q
    ra, rb = C // np_, hw // np_
    me.greet()

    own = [
        pltpu.make_async_copy(rin_part, rin.at[0], local.at[0]),
        pltpu.make_async_copy(rout_part.at[:, rows_of(me.k * ow, ow, 128)], rout.at[0], local.at[1]),
    ]
    convs = [
        pltpu.make_async_copy(part.at[b], s2.at[2 * b + i], local.at[2 + 2 * b + i])
        for b in range(2)
        for i, part in enumerate((conv_in, conv_out))
    ]
    given = pltpu.make_async_copy(patches, mg.at[0], local.at[6])
    convs[0].start()
    given.start()
    za, zb, zc = [[], []], [], []
    rh = ra // 2
    row_b = rows_of(strip * rb, rb, rb)
    for t in range(1, nz):
        there = lax.rem(me.k + nz - t, nz)
        for h in range(2):
            row_a = rows_of(strip * ra + h * rh, rh, rh)
            za[h].append(links.copy(rin_part.at[row_a], rin.at[t, row_a], me.at(k=there)))
        zc.append(links.copy(bias_part, bias.at[t], me.at(k=there)))
    start_all(za[0])
    start_all(zc)
    start_all(za[1])
    for t in range(1, nz):
        there = lax.rem(me.k + nz - t, nz)
        zb.append(links.copy(
            rout_part.at[row_b, rows_of(there * ow, ow, 128)], rout.at[t, row_b], me.at(k=there)))
    for copy in convs[1:] + own:
        copy.start()
    bias[0] = bias_part[...]
    column_masks(cmask, zero.width)
    live_stage(sizes, me.r, zero, one, mask_zero, mask_one, pool)

    def strips(weights, height, part, parts):
        wide = weights.shape[2]

        def strip(q, half):
            few = height // parts
            rows = rows_of((me.c * me.nq + q) * height + part * few, few, few)
            cols = pl.ds(0, wide) if half is None else pl.ds(half * (wide // 2), wide // 2)
            return weights.at[pl.ds(1, nz - 1), rows, cols]

        return Spread(me, links, strip)

    def between_cores(weights, height):
        half = rows_of(me.c * (me.nq * height), me.nq * height, height)
        part = weights.at[pl.ds(1, nz - 1), half]
        return start_all([links.copy(part, part, me.at(c=1 - me.c))])

    pa, pb = [strips(rin, ra, h, 2) for h in range(2)], strips(rout, rb, 0, 1)

    first = (1 - me.r).astype(F32)
    neighbour = me.at(q=me.x * nrow + (nrow - 1 - me.r))

    def masked(rows):
        x = (mg[0, rows].astype(F32) * mask_zero[rows]).astype(BF)
        mg[0, rows] = x
        return x

    convs[0].wait()
    given.wait()
    head_stage(zero, 1, masked, s2.at[0], gains[0], biases[0], mask_zero, hid.at[0], hid.at[1], edge_zero, first)
    rim0 = links.copy(edge_zero, rim_zero, neighbour)
    rim0.start()
    recv_all(za[0])
    pa[0].start()
    rim0.wait_recv()
    depth_stage(zero, hid.at[1], rim_zero, taps[0], cmask, hid.at[2], first, C)
    for copy in convs[1:]:
        copy.wait()

    def to_pooled(i, rows, out):
        mg[1, one.rows(i)] = nn(pool[i], out.astype(BF)).astype(BF)

    sent_all(za[0])
    sent_all(za[1])
    start_all(zb)
    recv_all(za[1])
    pa[1].start()
    pa[0].pass_on()
    tail_stage(zero, 1, mg.at[0], s2.at[1], gains[0], biases[0], mask_zero, hid.at[2], hid.at[3], to_pooled)
    kept_zero = pltpu.make_async_copy(hid, keep_zero, local.at[2])
    kept_zero.start()
    all_one = one.cells * one.count
    part = [mg.at[1 + i // 3, pl.ds((i % 3) * all_one, all_one)] for i in range(5)]
    pooled, pre_one, hidden, pre_two, pre_three = part
    head_stage(one, one.count, lambda rows: pooled[rows], s2.at[2], gains[1], biases[1], mask_one, pre_one, hidden, edge_one, first)
    rim1 = links.copy(edge_one, rim_one, neighbour)
    rim1.start()
    rim1.wait_recv()
    depth_stage(one, hidden, rim_one, taps[1], None, pre_two, first, C)
    here = rows_of(me.k * T, T, 16)

    def to_tokens(i, rows, out):
        abst[here] = nn(picked((T, all_one), 0, one.width), out.astype(BF)).astype(BF)

    tail_stage(one, one.count, pooled, s2.at[3], gains[1], biases[1], mask_one, pre_two, pre_three, to_tokens)
    kept_one = pltpu.make_async_copy(mg.at[pl.ds(1, 2)], keep_one, local.at[3])
    kept_one.start()
    def along(step, group, to):
        rows = rows_of(lax.rem(group + nz, nz) * T, T, 16)
        return links.copy(abst.at[rows], abst.at[rows], me.at(k=lax.rem(to + nz, nz)))

    up = [along(step, me.k - step, me.k + 1) for step in range(nz - 1)]
    down = [along(step, me.k + step, me.k - 1) for step in range(nz - 1)]
    more, less = me.k + 1 < nz, me.k > 0

    def hop(step):
        if step < nz - 1:
            pl.when(jnp.logical_and(more, me.k - step >= 0))(up[step].start)
            pl.when(jnp.logical_and(less, me.k + step < nz))(down[step].start)

    hop(0)
    pa[1].pass_on()
    recv_all(zb)
    pa[0].finish()
    pa[1].finish()
    pb.start()
    ca = between_cores(rin, ra)
    for copy in own + [kept_zero, kept_one]:
        copy.wait()
    recv_all(zc)
    recv_all(ca)

    hsum[...] = jnp.zeros_like(hsum)
    total = jnp.sum(cot[...].astype(F32), axis=0, keepdims=True)
    for j in range(nz):
        early[nz + j : nz + j + 1] = jnp.where(me.k == j, total, 0.0)
    ag = [None] + [
        links.copy(ag_send.at[t - 1], ag_recv.at[t - 1], me.at(k=me.deep(t))) for t in range(1, nz)
    ]
    NT = min(512, hw)

    def hidden_group(z):
        rows = rows_of(z * T, T, 16)

        def front(i, carry):
            u = i // (hw // NT)
            cols = rows_of(lax.rem(i, hw // NT) * NT, NT, 128)
            value, slope = gelu_pair(nn(abst[rows], rin[u, :, cols]) + bias[u, 0:1, cols])
            hid[u, rows, cols] = value.astype(BF)
            mg[u, rows, cols] = slope.astype(BF)
            return carry

        lax.fori_loop(0, nz * (hw // NT), front, 0)

    hidden_group(me.k)
    pb.pass_on()
    for step in range(nz - 1):
        from_less, from_more = me.k - 1 - step >= 0, me.k + 1 + step < nz
        pl.when(from_less)(up[step].wait_recv)
        pl.when(from_more)(down[step].wait_recv)
        hop(step + 1)
        lower = from_less.astype(jnp.int32)

        def arrived(i, carry):
            hidden_group(jnp.where(i < lower, me.k - 1 - step, me.k + 1 + step))
            return carry

        lax.fori_loop(0, lower + from_more.astype(jnp.int32), arrived, 0)
        if step == 0:
            pb.finish()
            cb = between_cores(rout, rb)

    HT = 256

    def g2(i, carry):
        u = i // (hw // HT)
        at = rows_of(lax.rem(i, hw // HT) * HT, HT, HT)
        s2[me.deep(u), at, :] = tn(hid[u, :, at], cot[...]).astype(BF)
        return carry

    lax.fori_loop(0, nz * (hw // HT), g2, 0)
    half = me.nq * rb
    theirs = rows_of((1 - me.c) * half, half, half)
    core2 = start_all([links.copy(s2.at[:, theirs], rc2, me.at(c=1 - me.c))])
    abst_t[...] = abst[...].T
    recv_all(cb)

    def unit(i, carry):
        u = i // (hw // 256)
        cols = rows_of(lax.rem(i, hw // 256) * 256, 256, 256)
        grad = (nt(cot[...], rout[u, cols, :]) * mg[u, :, cols].astype(F32)).astype(BF)
        mg[u, :, cols] = grad
        hsum[me.deep(u), 0:1, cols] += jnp.sum(grad.astype(F32), axis=0, keepdims=True)
        return carry

    lax.fori_loop(0, nz * (hw // 256), unit, 0)

    recv_all(core2)
    mine2 = me.c * half
    gather2 = Gather(
        me, links,
        lambda q, h: s2.at[pl.ds(h * (nz // 2), nz // 2), rows_of(mine2 + q * rb, rb, rb)],
        lambda i, h: rp2.at[i, pl.ds(h * (nz // 2), nz // 2)],
    )
    piece = 256
    parts = half // piece
    loads = [
        pltpu.make_async_copy(
            rc2.at[i // parts, pl.ds(i % parts * piece, piece)], ag_send.at[i % 2, pl.ds(0, piece)], local.at[i % 2]
        )
        for i in range(nz * parts)
    ]
    loads[0].start()
    for i in range(nz * parts):
        loads[i].wait()
        if i + 1 < nz * parts:
            loads[i + 1].start()
        j, where = i // parts, mine2 + i % parts * piece
        fold(
            lambda at, v, j=j, w=where: s2.__setitem__((j, rows_of(w + at.start, at.size, 16)), v.astype(BF)),
            [
                lambda at, j=j, w=where: s2[j, rows_of(w + at.start, at.size, 16)],
                lambda at, i=i: ag_send[i % 2, at],
            ],
            piece, 32,
        )
        if (i + 1) % (nz // 2 * parts) == 0:
            gather2.start(i // (nz // 2 * parts))

    def group_back(t):
        rows = rows_of(me.deep(t) * T, T, 16)

        def back(i, carry):
            at = rows_of(i * 256, 256, 256)
            total = nt(mg[0, rows, :], rin[0, at, :])
            for u in range(1, nz):
                total = total + nt(mg[u, rows, :], rin[u, at, :])
            if t == 0:
                agrad[:, at] = total
            else:
                ag_send[t - 1, :, at] = total.astype(BF)
            return carry

        lax.fori_loop(0, C // 256, back, 0)
        if t:
            ag[t].start()

    for t in (*range(1, nz), 0):
        group_back(t)


    sent_all(ca)
    for group in pa:
        group.sent()

    def g1(i, carry):
        u = i // (C // 256)
        at = rows_of(lax.rem(i, C // 256) * 256, 256, 256)
        rin[u, at, :] = nn(abst_t[at, :], mg[u]).astype(BF)
        return carry

    lax.fori_loop(0, nz * (C // 256), g1, 0)
    low = me.nq * ra
    core1 = links.copy(rin.at[:, rows_of((1 - me.c) * low, low, low)], rc1, me.at(c=1 - me.c))
    core1.start()

    for h in range(2):
        to = gather2.passing(h)
        block = range(h * (nz // 2), (h + 1) * (nz // 2))
        loads = [pltpu.make_async_copy(rp2.at[1, j], mg.at[j, pl.ds(0, rb)], local.at[j]) for j in block]
        for copy in loads:
            copy.start()
        for j, copy in zip(block, loads):
            copy.wait()
            where = mine2 + to * rb
            fold(
                lambda at, v, j=j, w=where: s2.__setitem__((j, rows_of(w + at.start, at.size, 16)), v.astype(BF)),
                [lambda at, j=j, w=where: s2[j, rows_of(w + at.start, at.size, 16)], lambda at, j=j: mg[j, at]],
                rb, min(rb, 32),
            )
        gather2.pass_on(h, gather2.chunk(to, h))

    for step in range(nz - 1):
        pl.when(jnp.logical_and(more, me.k - step >= 0))(up[step].wait_send)
        pl.when(jnp.logical_and(less, me.k + step < nz))(down[step].wait_send)

    def f2_body(i, carry):
        at = rows_of(i * 256, 256, 256)
        total = nn(hid[0], rout[0, :, at]) + bias_part[1:2, at]
        for u in range(1, nz):
            total = total + nn(hid[u], rout[u, :, at])
        abst[:, at] = total.astype(BF)
        return carry

    lax.fori_loop(0, ow // 256, f2_body, 0)
    out_tokens = pltpu.make_async_copy(abst, tokens, local.at[6])
    out_tokens.start()
    recv_all(ag[1:])
    fold(
        lambda at, v: agrad.__setitem__(at, v),
        [lambda at: agrad[at]] + [lambda at, t=t: ag_recv[t - 1, at] for t in range(1, nz)],
        T, 32,
    )
    core1.wait_recv()
    loads = [pltpu.make_async_copy(rc1.at[u], mg.at[u, pl.ds(0, low)], local.at[u]) for u in range(nz)]
    for copy in loads:
        copy.start()
    outs = []
    for u in range(nz):
        loads[u].wait()
        fold(
            lambda at, v, u=u: rin.__setitem__((u, rows_of(me.c * low + at.start, at.size, 16)), v.astype(BF)),
            [lambda at, u=u: rin[u, rows_of(me.c * low + at.start, at.size, 16)], lambda at, u=u: mg[u, at]],
            low, 32,
        )
        outs.append(pltpu.make_async_copy(rin.at[u, rows_of(me.c * low, low, low)], s1.at[u], local.at[u]))
        outs[-1].start()
    gather2.finish()
    for copy in outs:
        copy.wait()
    loads = [
        pltpu.make_async_copy(rp2.at[i], mg.at[pl.ds(0, nz), pl.ds(i * rb, rb)], local.at[i]) for i in (0, 2)
    ]
    for copy in loads:
        copy.start()
    for copy in loads:
        copy.wait()
    for j in range(nz):
        fold(
            lambda at, v, j=j: f2.__setitem__((j, at), v.astype(BF)),
            [lambda at, j=j: s2[j, rows_of(strip * rb + at.start, at.size, 16)]]
            + [lambda at, j=j, i=i: mg[j, rows_of(i * rb + at.start, at.size, 16)] for i in (0, 2)],
            rb, min(rb, 32),
        )
    for j in range(nz):
        early[j : j + 1] = hsum[j]
    out_tokens.wait()
    for group in (pb, gather2):
        group.sent()
    for group_of in (zb, zc, cb, core2, ag[1:], [rim0, rim1, core1]):
        sent_all(group_of)


def grads_kernel(
    nz, ndp, nrow, zero, one,
    sizes, s1, f2, agrad, patches, keep_zero, keep_one, rim_zero, rim_one, conv_in, conv_out, pack, early_in,
    out1, out2, out3, small_out, early, patch_grad, rp1,
    mask_zero, mask_one, pool, small, ec, ep, ez, xs, kept, keep, third, resid, weights, cmask, edge_zero, edge_one, got_zero, got_one,
    sent_on, f1, rz1, conv, rc3, rp3, f3, rz3, sc, sp, sz, send, recv, local,
):
    me = Place(nz, ndp, nrow)
    links = Links(send, recv)
    C, hw = out1.shape
    ow = f2.shape[2]
    np_ = 2 * me.nq
    strip = me.c * me.nq + me.q
    ra, rb = C // np_, hw // np_
    width = C // nrow
    R = out3.shape[2] // 2
    other = me.at(c=1 - me.c)
    first = (1 - me.r).astype(F32)
    neighbour = me.at(q=me.x * nrow + (nrow - 1 - me.r))
    me.greet()

    loads = [
        pltpu.make_async_copy(keep_one, keep, local.at[0]),
        pltpu.make_async_copy(conv_out.at[1], weights.at[1], local.at[1]),
        pltpu.make_async_copy(conv_in.at[1], weights.at[0], local.at[2]),
        pltpu.make_async_copy(keep_zero, kept, local.at[3]),
        pltpu.make_async_copy(patches, xs, local.at[4]),
    ]
    for copy in loads:
        copy.start()
    lead = nz // 2
    gather1 = Gather(
        me, links,
        lambda q, h: s1.at[pl.ds(h * lead, lead), rows_of(q * ra, ra, ra)],
        lambda i, h: rp1.at[i, pl.ds(h * lead, lead)],
    )
    gather1.start(0)
    gather1.start(1)
    row_b = rows_of(strip * rb, rb, rb)
    col_k = rows_of(me.k * ow, ow, 128)
    z2 = start_all([
        links.copy(f2.at[me.deep(t)], out2.at[row_b, col_k], me.at(k=me.deep(t))) for t in range(1, nz)
    ])
    own2 = pltpu.make_async_copy(f2.at[me.k], out2.at[row_b, col_k], local.at[5])
    own2.start()
    early_c = links.copy(early_in, ec, other)
    early_c.start()
    small[...] = jnp.zeros_like(small)
    column_masks(cmask, zero.width)
    live_stage(sizes, me.r, zero, one, mask_zero, mask_one, pool)
    taps, gains, biases = [[pack.at[b, pl.ds(at, n)] for b in range(2)] for at, n in ((0, 16), (16, 8), (24, 8))]

    def spread(b):
        core3[b].wait_recv()
        for m in range(2):
            for x in range(me.nx):
                fold(
                    lambda at, v, i=(b, m, x, me.c): conv.__setitem__((*i, at), v.astype(BF)),
                    [lambda at, i=(b, m, x, me.c): conv[(*i, at)], lambda at, i=(b, m, x): rc3[(*i, at)]],
                    nz * R, 32,
                )
        gather = Gather(
            me, links,
            lambda q, h: conv.at[b, h, q // nrow, me.c, :, rows_of(lax.rem(q, nrow) * width, width, 128)],
            lambda i, h: rp3.at[b, i, h],
        )
        gather.start(1)
        gather.start(0)
        return gather

    def spread_on(b):
        for h in (1, 0):
            to = p3[b].passing(h)
            cols = rows_of(lax.rem(to, nrow) * width, width, 128)
            x = to // nrow
            fold(
                lambda at, v: conv.__setitem__((b, h, x, me.c, at, cols), v.astype(BF)),
                [lambda at: conv[b, h, x, me.c, at, cols], lambda at: rp3[b, 1, h, at, :]],
                nz * R, 32,
            )
            p3[b].pass_on(h, p3[b].chunk(to, h))

    core3, p3 = [None, None], [None, None]

    all_one = one.cells * one.count
    pooled, pre_one, hidden, pre_two, pre_three, pooled_grad = [
        keep.at[i // 3, pl.ds((i % 3) * all_one, all_one)] for i in range(6)
    ]
    third_one, resid_one = third.at[pl.ds(0, all_one)], resid.at[pl.ds(0, all_one)]
    loads[0].wait()
    loads[1].wait()
    back_tail_stage(
        one, one.count, lambda i: nn(picked((all_one, agrad.shape[0]), 1, one.width), agrad[...].astype(BF)), pooled, weights.at[1], gains[1], biases[1], mask_one,
        pre_two, pre_three, resid_one, third_one, pre_three, pre_two, edge_one, first, small, 16,
    )
    rim1 = links.copy(edge_one, got_one, neighbour)
    rim1.start()
    early_c.wait_recv()
    early[...] = early_in[...] + ec[...]
    early_p = start_all([links.copy(early, ep.at[t - 1], me.at(q=me.chip(t))) for t in range(1, me.nq)])
    outer_stage(third_one, pre_three, conv.at[1, 1])
    rim1.wait_recv()
    back_depth_stage(one, pre_two, got_one, hidden, rim_one, taps[1], None, third_one, first, C, small, 16)
    loads[2].wait()

    def to_pooled_grad(i, rows, grad):
        pooled_grad[rows] = grad.astype(BF)

    back_head_stage(
        one, one.count, third_one, weights.at[0], gains[1], biases[1], mask_one, pre_one, resid_one, pre_three, to_pooled_grad, small, 16
    )
    again = [
        pltpu.make_async_copy(conv_out.at[0], weights.at[1], local.at[1]),
        pltpu.make_async_copy(conv_in.at[0], weights.at[0], local.at[2]),
    ]
    for copy in again:
        copy.start()
    outer_stage(pre_three, pooled, conv.at[1, 0])
    core3[1] = links.copy(conv.at[1, :, :, 1 - me.c], rc3.at[1], other)
    core3[1].start()

    sent_all(early_p)
    recv_all(early_p)
    for t in range(1, me.nq):
        early[...] += ep[t - 1]
    early_z = start_all([links.copy(early, ez.at[t - 1], me.at(k=me.deep(t))) for t in range(1, nz)])
    loads[3].wait()
    loads[4].wait()
    xs[...] = (xs[...].astype(F32) * mask_zero[...]).astype(BF)
    again[0].wait()
    back_tail_stage(
        zero, 1, lambda i: tn(pool[i], pooled_grad[one.rows(i)]), xs, weights.at[1], gains[0], biases[0], mask_zero,
        kept.at[2], kept.at[3], resid, third, kept.at[3], kept.at[2], edge_zero, first, small, 0,
    )
    rim0 = links.copy(edge_zero, got_zero, neighbour)
    rim0.start()
    p3[1] = spread(1)
    temp = [keep.at[0, pl.ds(i * lead * ra, lead * ra)] for i in range(4)]

    def bring(sources):
        copies = [
            pltpu.make_async_copy(source.at[j], to.at[pl.ds(j * ra, ra)], local.at[6 + n * lead + j])
            for n, (source, to) in enumerate(sources)
            for j in range(lead)
        ]
        for copy in copies:
            copy.start()
        for copy in copies:
            copy.wait()

    for h in range(2):
        to = gather1.passing(h)
        bring([(gather1.chunk(to, h), temp[2 * h]), (gather1.slot(1, h), temp[2 * h + 1])])
        for j in range(lead):
            fold(
                lambda at, v: sent_on.__setitem__((h, j, at), v.astype(BF)),
                [lambda at, ref=ref: ref[rows_of(j * ra + at.start, at.size, 16)] for ref in temp[2 * h : 2 * h + 2]],
                ra, 32,
            )
        gather1.pass_on(h, sent_on.at[h])
    outer_stage(third, kept.at[3], conv.at[0, 1])
    rim0.wait_recv()
    own2.wait()
    recv_all(z2)
    spread2 = Spread(me, links, lambda q, h: out2.at[
        rows_of((me.c * me.nq + q) * rb, rb, rb),
        pl.ds(0, nz * ow) if h is None else pl.ds(h * (nz * ow // 2), nz * ow // 2),
    ])
    spread2.start()
    back_depth_stage(zero, kept.at[2], got_zero, kept.at[1], rim_zero, taps[0], cmask, third, first, C, small, 0)
    spread_on(1)
    gather1.finish()
    for h in range(2):
        mine = [keep.at[0, pl.ds(i * lead * ra, lead * ra)] for i in range(3)]
        bring([(gather1.chunk(me.q, h), mine[0]), (gather1.slot(0, h), mine[1]), (gather1.slot(2, h), mine[2])])
        for j in range(lead):
            fold(
                lambda at, v: f1.__setitem__((h * lead + j, at), v.astype(BF)),
                [lambda at, ref=ref: ref[rows_of(j * ra + at.start, at.size, 16)] for ref in mine],
                ra, 32,
            )
    z1 = start_all([links.copy(f1.at[t], rz1.at[t - 1], me.at(k=me.deep(t))) for t in range(1, nz)])
    again[1].wait()

    def to_patches(i, rows, grad):
        resid[rows] = (grad * mask_zero[rows]).astype(BF)

    back_head_stage(
        zero, 1, third, weights.at[0], gains[0], biases[0], mask_zero, kept.at[0], resid, kept.at[3], to_patches, small, 0
    )
    out_patches = pltpu.make_async_copy(resid, patch_grad, local.at[0])
    out_patches.start()
    outer_stage(kept.at[3], xs, conv.at[0, 0])
    core3[0] = links.copy(conv.at[0, :, :, 1 - me.c], rc3.at[0], other)
    core3[0].start()
    sums = start_all([links.copy(small, sc, other)])
    p3[0] = spread(0)

    spread2.pass_on()
    recv_all(z1)
    row_a = rows_of(strip * ra, ra, ra)
    fold(
        lambda at, v: out1.__setitem__(rows_of(strip * ra + at.start, at.size, 16), v.astype(BF)),
        [lambda at: f1[0, at]] + [lambda at, t=t: rz1[t - 1, at] for t in range(1, nz)],
        ra, 32,
    )
    spread1 = Spread(me, links, lambda q, h: out1.at[
        rows_of((me.c * me.nq + q) * ra, ra, ra), pl.ds(0, hw) if h is None else pl.ds(h * (hw // 2), hw // 2)
    ])
    spread1.start()
    recv_all(sums)
    sent_all(sums)
    small[...] += sc[...]
    few = C // ndp

    def columns(q):
        return rows_of((q // nrow * 2 + me.c) * few, few, 128)

    sums_p = start_all([
        links.copy(small.at[:, columns(me.chip(t))], sp.at[t - 1], me.at(q=me.chip(t))) for t in range(1, me.nq)
    ])

    spread_on(0)
    z3 = [None, None]
    my_cols = rows_of(me.r * width, width, 128)

    def deepen(b):
        p3[b].finish()
        for m in range(2):
            for j in range(nz):
                rows = pl.ds(j * R, R)
                total = conv[b, m, me.x, me.c, rows, my_cols].astype(F32)
                for i in (0, 2):
                    total = total + rp3[b, i, m, rows, :].astype(F32)
                f3[b, j, pl.ds(m * R, R)] = total.astype(BF)
        z3[b] = start_all([
            links.copy(f3.at[b, me.deep(t)], rz3.at[b, t - 1], me.at(k=me.deep(t))) for t in range(1, nz)
        ])

    deepen(1)
    spread1.pass_on()
    recv_all(sums_p)
    total = small[:, columns(me.q)]
    for t in range(1, me.nq):
        total = total + sp[t - 1]
    small_out[...] = total
    sums_z = start_all([links.copy(small_out, sz.at[t - 1], me.at(k=me.deep(t))) for t in range(1, nz)])
    deepen(0)

    g3 = []
    for b in (1, 0):
        recv_all(z3[b])
        total = f3[b, me.k].astype(F32)
        for t in range(1, nz):
            total = total + rz3[b, t - 1].astype(F32)
        out3[b, me.r] = total.astype(BF)
        g3 += start_all([
            links.copy(out3.at[b, me.r], out3.at[b, me.r], me.at(q=me.x * nrow + lax.rem(me.r + t, nrow)))
            for t in range(1, nrow)
        ])
    spread2.finish()
    half_b = rows_of(me.c * me.nq * rb, me.nq * rb, me.nq * rb)
    h2 = start_all([links.copy(out2.at[half_b], out2.at[half_b], other)])
    spread1.finish()
    half_a = rows_of(me.c * me.nq * ra, me.nq * ra, me.nq * ra)
    h1 = start_all([links.copy(out1.at[half_a], out1.at[half_a], other)])
    sent_all(sums_z)
    recv_all(sums_z)
    sent_all(early_z)
    recv_all(early_z)
    for t in range(1, nz):
        small_out[...] += sz[t - 1]
        early[...] += ez[t - 1]
    recv_all(g3)
    recv_all(h1)
    recv_all(h2)
    out_patches.wait()
    for group_of in ([early_c], sums_p, core3, z2, z1, z3[0], z3[1], g3, h1, h2, [rim0, rim1]):
        sent_all(group_of)
    for group in (gather1, p3[0], p3[1], spread1, spread2):
        group.sent()


def spec(*kinds):
    return [pl.BlockSpec(memory_space=kind) for kind in kinds]


def run_readout(mesh, zero, one, sizes, patches, cot, read_in, read_out, read_bias, conv_in, conv_out, pack):
    nz, ndp, nrow = mesh.shape["wide"], mesh.shape["dp"], mesh.shape["row"]
    nq = ndp // 2 * nrow
    T, C = one.count * one.height * POOL, patches.shape[1]
    hw, ow = read_out.shape[0], cot.shape[1]
    tall = nz * T
    rb = hw // (2 * nq)
    copies = 7 * (nz - 1) + 28
    bias_part = jnp.pad(read_bias, ((0, 6), (0, 0)))
    ANY = pl.ANY
    return pl.pallas_call(
        functools.partial(readout_kernel, nz, ndp, nrow, zero, one),
        out_shape=[
            jax.ShapeDtypeStruct((tall, ow), BF),
            jax.ShapeDtypeStruct((T, C), F32),
            jax.ShapeDtypeStruct((nz, C // 2, hw), BF),
            jax.ShapeDtypeStruct((nz, rb, ow), BF),
            jax.ShapeDtypeStruct((2 * nz, C), F32),
            jax.ShapeDtypeStruct((nz, C // 2, hw), BF),
            jax.ShapeDtypeStruct((nz, nq * rb, ow), BF),
            jax.ShapeDtypeStruct((nq - 1, nz, rb, ow), BF),
            jax.ShapeDtypeStruct((4, tall, hw), BF),
            jax.ShapeDtypeStruct((2, tall, hw), BF),
            jax.ShapeDtypeStruct((zero.count, 32, C), BF),
            jax.ShapeDtypeStruct((one.count, 16, C), BF),
        ],
        in_specs=spec(pltpu.SMEM, ANY, VMEM, ANY, ANY, VMEM, ANY, ANY, VMEM),
        out_specs=spec(ANY, VMEM, ANY, VMEM, VMEM, ANY, ANY, ANY, ANY, ANY, VMEM, VMEM),
        scratch_shapes=[
            VMEM((tall, 1), F32),
            VMEM((one.count * one.cells, 1), F32),
            VMEM((zero.count, one.cells, zero.cells), BF),
            VMEM((nz, 1, hw), F32),
            VMEM((nz, C, hw), BF),
            VMEM((nz, hw, ow), BF),
            VMEM((nz, 8, hw), F32),
            VMEM((tall, C), BF),
            VMEM((C, tall), BF),
            VMEM((nz, tall, hw), BF),
            VMEM((nz, tall, hw), BF),
            VMEM((nz - 1, T, C), BF),
            VMEM((nz - 1, T, C), BF),
            VMEM((nz, hw, ow), BF),
            VMEM((2, zero.cells + 2 * zero.width, 128), F32),
            VMEM((zero.count, 32, C), BF),
            VMEM((one.count, 16, C), BF),
            pltpu.SemaphoreType.DMA((copies,)),
            pltpu.SemaphoreType.DMA((copies,)),
            pltpu.SemaphoreType.DMA((7,)),
        ],
        compiler_params=pltpu.CompilerParams(
            collective_id=0, has_side_effects=True, vmem_limit_bytes=LIMIT
        ),
        name="readout",
    )(sizes, patches, cot, read_in, read_out, bias_part, conv_in, conv_out, pack)


LIMIT = 62 * 1024 * 1024


def run_grads(mesh, zero, one, sizes, s1, f2, agrad, patches, keep_zero, keep_one, rim_zero, rim_one, conv_in, conv_out, pack, early):
    nz, ndp, nrow = mesh.shape["wide"], mesh.shape["dp"], mesh.shape["row"]
    nq = ndp // 2 * nrow
    nx = ndp // 2
    C, hw = s1.shape[1] * 2, s1.shape[2]
    _, rb, ow = f2.shape
    ra = C // (2 * nq)
    R = C // (ndp * nz)
    tall = patches.shape[0]
    S = 32
    copies = 7 * (nz - 1) + 40
    width = C // nrow
    ANY = pl.ANY
    return pl.pallas_call(
        functools.partial(grads_kernel, nz, ndp, nrow, zero, one),
        out_shape=[
            jax.ShapeDtypeStruct((C, hw), BF),
            jax.ShapeDtypeStruct((hw, nz * ow), BF),
            jax.ShapeDtypeStruct((2, nrow, 2 * R, width), BF),
            jax.ShapeDtypeStruct((S, C // ndp), F32),
            jax.ShapeDtypeStruct(early.shape, F32),
            jax.ShapeDtypeStruct((tall, C), BF),
            jax.ShapeDtypeStruct((nq - 1, nz, ra, hw), BF),
        ],
        in_specs=spec(pltpu.SMEM, ANY, VMEM, VMEM, ANY, ANY, ANY, VMEM, VMEM, ANY, ANY, VMEM, VMEM),
        out_specs=spec(VMEM, ANY, VMEM, VMEM, VMEM, ANY, ANY),
        scratch_shapes=[
            VMEM((tall, 1), F32),
            VMEM((one.count * one.cells, 1), F32),
            VMEM((zero.count, one.cells, zero.cells), BF),
            VMEM((S, C), F32),
            VMEM(early.shape, F32),
            VMEM((nq - 1, *early.shape), F32),
            VMEM((nz - 1, *early.shape), F32),
            VMEM((tall, C), BF),
            VMEM((4, tall, C), BF),
            VMEM((2, tall, C), BF),
            VMEM((tall, C), BF),
            VMEM((tall, C), BF),
            VMEM((2, C, C), BF),
            VMEM((2, zero.cells + 2 * zero.width, 128), F32),
            VMEM((zero.count, 32, C), BF),
            VMEM((one.count, 16, C), BF),
            VMEM((zero.count, 32, C), BF),
            VMEM((one.count, 16, C), BF),
            VMEM((2, nz // 2, ra, hw), BF),
            VMEM((nz, ra, hw), BF),
            VMEM((nz - 1, ra, hw), BF),
            VMEM((2, 2, nx, 2, nz * R, C), BF),
            VMEM((2, 2, nx, nz * R, C), BF),
            VMEM((2, nq - 1, 2, nz * R, width), BF),
            VMEM((2, nz, 2 * R, width), BF),
            VMEM((2, nz - 1, 2 * R, width), BF),
            VMEM((S, C), F32),
            VMEM((nq - 1, S, C // ndp), F32),
            VMEM((nz - 1, S, C // ndp), F32),
            pltpu.SemaphoreType.DMA((copies,)),
            pltpu.SemaphoreType.DMA((copies,)),
            pltpu.SemaphoreType.DMA((6 + nq * nz,)),
        ],
        compiler_params=pltpu.CompilerParams(
            collective_id=1, has_side_effects=True, vmem_limit_bytes=LIMIT
        ),
        name="grads",
    )(sizes, s1, f2, agrad, patches, keep_zero, keep_one, rim_zero, rim_one, conv_in, conv_out, pack, early)


POOL = 12


eps_norm = 1e-06
exact_mode = lax.Precision.HIGHEST


def extended(cells, sides, width):
    for axis, dim in sides:
        count = lax.axis_size(axis)
        ends = count - 1
        head = lax.slice_in_dim(cells, 0, width, axis=dim)
        tail = lax.slice_in_dim(cells, cells.shape[dim] - width, cells.shape[dim], axis=dim)
        cells = jnp.concatenate(
            [
                lax.ppermute(tail, axis, [(i, (i + 1) % count) for i in range(ends)]),
                cells,
                lax.ppermute(head, axis, [((i + 1) % count, i) for i in range(ends)]),
            ],
            axis=dim,
        )
    return cells


def layer_norm(values, gain_row, bias_row):
    centre = jnp.mean(values, axis=-1, keepdims=True)
    centred = values - centre
    variance = jnp.mean(centred * centred, axis=-1, keepdims=True)
    return centred * lax.rsqrt(variance + eps_norm) * gain_row + bias_row


def head_piece(pre_values, gain_row, bias_row, live_mask):
    return jax.nn.silu(layer_norm(pre_values, gain_row, bias_row)) * live_mask


def tail_piece(source, third_pre, gain_row, bias_row, live_mask):
    return jax.nn.silu(source + layer_norm(third_pre, gain_row, bias_row)) * live_mask


def outer_sum(left_rows, right_rows):
    return lax.dot_general(
        left_rows, right_rows, (((0,), (0,)), ((), ())), preferred_element_type=jnp.float32
    )


def times_transposed(left_rows, weight):
    return lax.dot_general(
        left_rows, weight, (((1,), (1,)), ((), ())), preferred_element_type=jnp.float32
    )


def pad_columns(values):
    return jnp.pad(values, ((0, 0), (0, 0), (1, 1), (0, 0)))


def rows_forward(hidden_one):
    return extended(hidden_one, (("row", 1),), 1)


def rows_backward(second_low):
    return extended(second_low, (("row", 1),), 1)


def depth_apply(padded, tap_table, row_count, col_count):
    result = jnp.zeros((padded.shape[0], row_count, col_count, padded.shape[3]), jnp.float32)
    for offset in range(9):
        window = padded[
            :, offset // 3 : offset // 3 + row_count, offset % 3 : offset % 3 + col_count, :
        ]
        result = result + window.astype(jnp.float32) * tap_table[offset].astype(jnp.float32)
    return result


def block_forward(source, live_mask, weights):
    w_first, w_last, tap_table, gain_rows, bias_rows = weights
    grid_count, row_count, col_count, channels = source.shape
    flat_rows = source.astype(jnp.bfloat16).reshape(-1, channels)
    first_pre = jnp.dot(flat_rows, w_first, preferred_element_type=jnp.float32).reshape(
        source.shape
    )
    hidden_one = head_piece(first_pre, gain_rows[0], bias_rows[0], live_mask).astype(jnp.bfloat16)
    padded_one = pad_columns(rows_forward(hidden_one))
    second_pre = depth_apply(padded_one, tap_table, row_count, col_count)
    hidden_two = head_piece(second_pre, gain_rows[1], bias_rows[1], live_mask).astype(jnp.bfloat16)
    two_rows = hidden_two.reshape(-1, channels)
    third_pre = jnp.dot(two_rows, w_last, preferred_element_type=jnp.float32).reshape(source.shape)
    output = tail_piece(source, third_pre, gain_rows[2], bias_rows[2], live_mask)
    return (output, (flat_rows, first_pre, padded_one, second_pre, two_rows, third_pre))


def block_backward(output_grad, source, live_mask, weights, kept):
    w_first, w_last, tap_table, gain_rows, bias_rows = weights
    flat_rows, first_pre, padded_one, second_pre, two_rows, third_pre = kept
    grid_count, row_count, col_count, channels = source.shape
    _, tail_back = jax.vjp(
        functools.partial(tail_piece, live_mask=live_mask), source, third_pre, gain_rows[2], bias_rows[2]
    )
    residual_grad, third_grad, gain_three, bias_three = tail_back(output_grad)
    third_low = third_grad.astype(jnp.bfloat16).reshape(-1, channels)
    grad_last = outer_sum(two_rows, third_low)
    two_grad = times_transposed(third_low, w_last).reshape(source.shape)
    _, middle_back = jax.vjp(
        functools.partial(head_piece, live_mask=live_mask), second_pre, gain_rows[1], bias_rows[1]
    )
    second_grad, gain_two, bias_two = middle_back(two_grad)
    second_low = second_grad.astype(jnp.bfloat16)
    padded_grad = pad_columns(rows_backward(second_low))
    one_grad = depth_apply(padded_grad, tap_table[::-1], row_count, col_count)
    second_wide = second_low.astype(jnp.float32)
    tap_grads = []
    for offset in range(9):
        window = padded_one[
            :, offset // 3 : offset // 3 + row_count, offset % 3 : offset % 3 + col_count, :
        ]
        tap_grads.append(jnp.sum(second_wide * window.astype(jnp.float32), axis=(0, 1, 2)))
    _, first_back = jax.vjp(
        functools.partial(head_piece, live_mask=live_mask), first_pre, gain_rows[0], bias_rows[0]
    )
    first_grad, gain_one, bias_one = first_back(one_grad)
    first_low = first_grad.astype(jnp.bfloat16).reshape(-1, channels)
    grad_first = outer_sum(flat_rows, first_low)
    source_grad = residual_grad + times_transposed(first_low, w_first).reshape(source.shape)
    grads = (
        grad_first,
        grad_last,
        jnp.stack(tap_grads),
        jnp.stack([gain_one, gain_two, gain_three]),
        jnp.stack([bias_one, bias_two, bias_three]),
    )
    return (source_grad, grads)


def pool_weights(grid_side, row_shift, pooled_index, slot_index):
    place = slot_index - row_shift
    begin = pooled_index * grid_side // POOL
    finish = ((pooled_index + 1) * grid_side + POOL - 1) // POOL
    inside = (place >= begin) & (place < finish)
    return jnp.where(inside, 1.0, 0.0).astype(jnp.float32) / (finish - begin).astype(jnp.float32)


def plain(
    patches,
    grid_sizes,
    conv_in,
    conv_out,
    depth_taps,
    norm_gain,
    norm_bias,
    read_in,
    read_bias,
    read_out,
    cotangent,
):
    grid_count, local_rows, grid_width, channels = patches.shape
    row_place = lax.axis_index("row")
    slot_rows = row_place * local_rows + jnp.arange(local_rows, dtype=jnp.int32)
    column_index = jnp.arange(grid_width, dtype=jnp.int32)
    row_shift = (grid_width - grid_sizes) // 2
    row_live = (slot_rows[None, :] >= row_shift[:, None]) & (
        slot_rows[None, :] < (row_shift + grid_sizes)[:, None]
    )
    col_live = column_index[None, :] < grid_sizes[:, None]
    live_mask = (row_live[:, :, None] & col_live[:, None, :]).astype(jnp.float32)[..., None]
    weights_one = (conv_in[0], conv_out[0], depth_taps[0], norm_gain[0], norm_bias[0])
    weights_two = (conv_in[1], conv_out[1], depth_taps[1], norm_gain[1], norm_bias[1])
    source = patches.astype(jnp.float32) * live_mask
    encoded, kept_one = block_forward(source, live_mask, weights_one)
    pool_local = POOL // lax.axis_size("row")
    pooled_index = row_place * pool_local + jnp.arange(pool_local, dtype=jnp.int32)
    side_shaped = grid_sizes[:, None, None]
    row_pool = pool_weights(
        side_shaped, row_shift[:, None, None], pooled_index[None, :, None], slot_rows[None, None, :]
    )
    col_pool = pool_weights(
        side_shaped,
        0,
        jnp.arange(POOL, dtype=jnp.int32)[None, :, None],
        column_index[None, None, :],
    )
    pooled = jnp.einsum("gir,gjw,grwc->gijc", row_pool, col_pool, encoded, precision=exact_mode)
    all_live = jnp.ones((grid_count, pool_local, POOL, 1), jnp.float32)
    abstract, kept_two = block_forward(pooled, all_live, weights_two)
    token_rows = abstract.astype(jnp.bfloat16).reshape(-1, channels)
    gathered = lax.all_gather(token_rows, "wide", axis=0, tiled=True)
    gelu_exact = functools.partial(jax.nn.gelu, approximate=False)
    mixed_pre = jnp.dot(gathered, read_in, preferred_element_type=jnp.float32) + read_bias[0]
    hidden_wide, gelu_back = jax.vjp(gelu_exact, mixed_pre)
    hidden = hidden_wide.astype(jnp.bfloat16)
    partial_out = jnp.dot(hidden, read_out, preferred_element_type=jnp.float32)
    summed = (
        lax.psum_scatter(
            partial_out.astype(jnp.bfloat16), "wide", scatter_dimension=1, tiled=True
        ).astype(jnp.float32)
        + read_bias[1]
    )
    tokens = summed.astype(jnp.bfloat16).reshape(cotangent.shape)
    cot_local = cotangent.reshape(-1, cotangent.shape[-1])
    cot_all = lax.all_gather(cot_local, "wide", axis=1, tiled=True)
    hidden_grad = times_transposed(cot_all, read_out)
    mixed_grad = gelu_back(hidden_grad)[0].astype(jnp.bfloat16)
    grad_exit = outer_sum(hidden, cot_all)
    grad_entry = outer_sum(gathered, mixed_grad)
    bias_pair = jnp.stack(
        [
            jnp.sum(mixed_grad.astype(jnp.float32), axis=0),
            jnp.sum(cot_local.astype(jnp.float32), axis=0),
        ]
    )
    abstract_grad = lax.psum_scatter(
        times_transposed(mixed_grad, read_in).astype(jnp.bfloat16),
        "wide",
        scatter_dimension=0,
        tiled=True,
    ).astype(jnp.float32)
    grad_entry, bias_pair, grad_exit = (
        lax.psum(grad_entry.astype(jnp.bfloat16), ("dp", "row")).astype(jnp.float32),
        lax.psum(bias_pair.astype(jnp.bfloat16), ("dp", "row")).astype(jnp.float32),
        lax.psum(grad_exit.astype(jnp.bfloat16), ("dp", "row")).astype(jnp.float32),
    )
    pooled_grad, grads_two = block_backward(
        abstract_grad.reshape(abstract.shape), pooled, all_live, weights_two, kept_two
    )
    encoded_grad = jnp.einsum(
        "gir,gjw,gijc->grwc", row_pool, col_pool, pooled_grad, precision=exact_mode
    )
    source_grad, grads_one = block_backward(encoded_grad, source, live_mask, weights_one, kept_one)
    patch_grad = (source_grad * live_mask).astype(jnp.bfloat16)
    stacked = tuple((jnp.stack([grads_one[index], grads_two[index]]) for index in range(5)))
    totals = (
        lax.psum_scatter(stacked[0], ("dp", "wide"), scatter_dimension=2, tiled=True),
        lax.psum_scatter(stacked[1], ("dp", "wide"), scatter_dimension=2, tiled=True),
        lax.psum_scatter(stacked[2], ("dp", "wide"), scatter_dimension=2, tiled=True),
        lax.psum_scatter(stacked[3], ("dp", "wide"), scatter_dimension=2, tiled=True),
        lax.psum_scatter(stacked[4], ("dp", "wide"), scatter_dimension=2, tiled=True),
    )
    totals = (
        lax.psum(totals[0].astype(jnp.bfloat16), "row").astype(jnp.float32),
        lax.psum(totals[1].astype(jnp.bfloat16), "row").astype(jnp.float32),
        lax.psum(totals[2].astype(jnp.bfloat16), "row").astype(jnp.float32),
        lax.psum(totals[3].astype(jnp.bfloat16), "row").astype(jnp.float32),
        lax.psum(totals[4].astype(jnp.bfloat16), "row").astype(jnp.float32),
    )
    return (
        tokens,
        patch_grad,
        totals[0],
        totals[1],
        totals[2],
        totals[3],
        totals[4],
        grad_entry,
        bias_pair,
        grad_exit,
    )


def on_device(
    mesh,
    patches,
    grid_sizes,
    conv_in,
    conv_out,
    depth_taps,
    norm_gain,
    norm_bias,
    read_in,
    read_bias,
    read_out,
    cotangent,
):
    nz, ndp = mesh.shape["wide"], mesh.shape["dp"]
    grid_count, local_rows, grid_width, channels = patches.shape
    zero = Geometry(grid_count, local_rows, grid_width)
    one = Geometry(grid_count, POOL // mesh.shape["row"], 16)
    flat = patches.reshape(-1, channels)
    cot_local = cotangent.reshape(-1, cotangent.shape[-1])
    pack = jnp.concatenate(
        [
            jnp.pad(piece.astype(F32), ((0, 0), (0, height - piece.shape[1]), (0, 0)))
            for piece, height in ((depth_taps, 16), (norm_gain, 8), (norm_bias, 8))
        ],
        axis=1,
    )
    tokens, agrad, s1, f2, early, _, _, _, keep_zero, keep_one, rim_zero, rim_one = run_readout(
        mesh, zero, one, grid_sizes, flat, cot_local, read_in, read_out, read_bias, conv_in, conv_out, pack
    )
    tokens = tokens.reshape(cotangent.shape)
    out1, out2, out3, small, early, patch_grad, _ = run_grads(
        mesh, zero, one, grid_sizes, s1, f2, agrad, flat, keep_zero, keep_one, rim_zero, rim_one, conv_in, conv_out, pack, early
    )
    patch_grad = patch_grad.reshape(patches.shape)
    R = channels // (ndp * nz)
    out3 = out3.reshape(2, -1, 2, R, out3.shape[-1]).transpose(0, 2, 1, 4, 3).reshape(2, 2, channels, R).astype(F32)
    place = lax.axis_index("wide")
    own = lax.dynamic_slice_in_dim(small, place * R, R, axis=1).reshape(2, 16, R)
    taps, gains, biases = own[:, 0:9], own[:, 9:12], own[:, 12:15]
    bias_pair = lax.dynamic_slice_in_dim(early.reshape(2, nz, -1), place, 1, axis=1)[:, 0]
    return (
        tokens,
        patch_grad,
        out3[:, 0],
        out3[:, 1],
        taps,
        gains,
        biases,
        out1.astype(F32),
        bias_pair,
        out2.astype(F32),
    )


def fits(mesh):
    return mesh.shape["wide"] == 4 and mesh.shape["dp"] % 2 == 0 and mesh.shape["row"] == 2


def solution(mesh):

    placed = (
        P(("dp", "wide"), "row", None, None),
        P(("dp", "wide")),
        P(),
        P(),
        P(),
        P(),
        P(),
        P(None, "wide"),
        P(None, "wide"),
        P("wide", None),
        P("dp", "row", None, "wide"),
    )
    return jax.shard_map(
        functools.partial(on_device, mesh) if fits(mesh) else plain,
        mesh=mesh,
        in_specs=placed,
        out_specs=(
            P("dp", "row", None, "wide"),
            P(("dp", "wide"), "row", None, None),
            P(None, None, ("dp", "wide")),
            P(None, None, ("dp", "wide")),
            P(None, None, ("dp", "wide")),
            P(None, None, ("dp", "wide")),
            P(None, None, ("dp", "wide")),
            P(None, "wide"),
            P(None, "wide"),
            P("wide", None),
        ),
        check_vma=False,
    )
```

```python
import functools

import jax
import jax.numpy as jnp
from jax import lax
from jax.experimental import pallas as pl
from jax.experimental.pallas import tpu as pltpu
from jax.sharding import PartitionSpec as P

MESH = pl.DeviceIdType.MESH
BF = jnp.bfloat16
F32 = jnp.float32
VMEM = pltpu.VMEM


class Place:
    def __init__(self, nz, ndp, nrow):
        self.nz, self.ndp, self.nrow = nz, ndp, nrow
        self.nx = ndp // 2
        self.nq = self.nx * nrow
        self.k = lax.axis_index("wide")
        self.r = lax.axis_index("row")
        d = lax.axis_index("dp")
        self.c = lax.rem(d, 2)
        self.x = d // 2
        self.q = self.x * nrow + self.r
        self.qx = (1 - self.x) * nrow + self.r
        self.qy = self.x * nrow + (1 - self.r)
        self.qd = (1 - self.x) * nrow + (1 - self.r)

    def at(self, q=None, c=None, k=None):
        q = self.q if q is None else q
        c = self.c if c is None else c
        k = self.k if k is None else k
        return {"dp": (q // self.nrow) * 2 + c, "row": lax.rem(q, self.nrow), "wide": k}

    def chip(self, t):
        return lax.rem(self.q + t, self.nq)

    def deep(self, t):
        return lax.rem(self.k + t, self.nz)

    def peers(self):
        return (
            [self.at(q=self.chip(t)) for t in range(1, self.nq)]
            + [self.at(c=1 - self.c)]
            + [self.at(k=self.deep(t)) for t in range(1, self.nz)]
        )

    def greet(self):
        barrier = pltpu.get_barrier_semaphore()
        peers = self.peers()
        for peer in peers:
            pl.semaphore_signal(barrier, inc=1, device_id=peer, device_id_type=MESH)
        pl.semaphore_wait(barrier, len(peers))


class Links:
    def __init__(self, send, recv):
        self.send, self.recv, self.used = send, recv, 0

    def copy(self, src, dst, peer):
        at = self.used
        self.used += 1
        assert self.used <= self.send.shape[0]
        return pltpu.make_async_remote_copy(
            src_ref=src, dst_ref=dst, send_sem=self.send.at[at], recv_sem=self.recv.at[at],
            device_id=peer, device_id_type=MESH,
        )


def start_all(copies):
    for copy in copies:
        copy.start()
    return copies


def recv_all(copies):
    for copy in copies:
        copy.wait_recv()


def sent_all(copies):
    for copy in copies:
        copy.wait_send()


class Spread:
    def __init__(self, me, links, strip):
        self.me, self.links, self.strip = me, links, strip
        self.first = self.second = ()

    def start(self):
        me = self.me
        own = self.strip(me.q, None)
        self.first = start_all([self.links.copy(own, own, me.at(q=q)) for q in (me.qx, me.qy)])

    def pass_on(self):
        me = self.me
        along_y = self.strip(me.qx, 0)
        along_x = self.strip(me.qy, 1)
        self.second = [
            self.links.copy(along_y, along_y, me.at(q=me.qy)),
            self.links.copy(along_x, along_x, me.at(q=me.qx)),
        ]
        for arrived, copy in zip(self.first, self.second):
            arrived.wait_recv()
            copy.start()

    def finish(self):
        recv_all(self.second)

    def sent(self):
        sent_all(self.first)
        sent_all(self.second)


class Gather:
    def __init__(self, me, links, chunk, slot):
        self.me, self.links, self.chunk, self.slot = me, links, chunk, slot
        self.early = [[], []]
        self.late = [None, None]

    def start(self, half):
        me = self.me
        to = me.qx if half == 0 else me.qy
        self.early[half] = start_all([
            self.links.copy(self.chunk(q, half), self.slot(i, half), me.at(q=to)) for i, q in ((1, me.qd), (0, to))
        ])

    def passing(self, half):
        self.early[half][0].wait_recv()
        return self.me.qy if half == 0 else self.me.qx

    def pass_on(self, half, total):
        to = self.me.qy if half == 0 else self.me.qx
        self.late[half] = self.links.copy(total, self.slot(2, half), self.me.at(q=to))
        self.late[half].start()

    def finish(self):
        for half in range(2):
            self.early[half][1].wait_recv()
            self.late[half].wait_recv()

    def sent(self):
        for half in range(2):
            sent_all(self.early[half])
            self.late[half].wait_send()


def rows_of(start, size, unit):
    return pl.ds(pl.multiple_of(start, unit), size)


def fold(out, parts, rows, step):
    def body(i, carry):
        at = rows_of(i * step, step, step)
        total = parts[0](at).astype(F32)
        for part in parts[1:]:
            total = total + part(at).astype(F32)
        out(at, total)
        return carry

    lax.fori_loop(0, rows // step, body, 0)


def nt(a, b):
    return lax.dot_general(a, b, (((1,), (1,)), ((), ())), preferred_element_type=F32)


def nn(a, b):
    return jnp.dot(a, b, preferred_element_type=F32)


def tn(a, b):
    return lax.dot_general(a, b, (((0,), (0,)), ((), ())), preferred_element_type=F32)


def gelu_pair(v):
    dense = jnp.exp(-0.5 * v * v)
    s = 1.0 / (1.0 + (0.3275911 * 0.7071067811865476) * jnp.abs(v))
    poly = s * (0.254829592 + s * (-0.284496736 + s * (1.421413741 + s * (-1.453152027 + s * 1.061405429))))
    tail = 0.5 * poly * dense
    phi = jnp.where(v >= 0, 1.0 - tail, tail)
    return v * phi, phi + v * dense * 0.3989422804014327


def normal(v):
    centred = v - jnp.mean(v, axis=-1, keepdims=True)
    scale = lax.rsqrt(jnp.mean(centred * centred, axis=-1, keepdims=True) + 1e-06)
    return centred * scale, scale


def sigmoid(v):
    return 1.0 / (1.0 + jnp.exp(-v))


def live_stage(sizes, row, zero, one, mask_zero, mask_one, pool):
    side, across, pooled = zero.width, one.width, POOL

    def counted(shape, axis, width):
        place = lax.broadcasted_iota(jnp.int32, shape, axis)
        return lax.div(place, jnp.int32(width)), lax.rem(place, jnp.int32(width))

    def share(cell, out, size):
        begin = lax.div(out * size, jnp.int32(pooled))
        end = lax.div((out + 1) * size + (pooled - 1), jnp.int32(pooled))
        return jnp.where((cell >= begin) & (cell < end), 1.0 / (end - begin).astype(F32), 0.0)

    for g in range(zero.count):
        size = sizes[g]
        shift = lax.div(side - size, jnp.int32(2))
        r, c = counted((zero.cells, 1), 0, side)
        r = r + row * zero.height - shift
        mask_zero[zero.rows(g)] = jnp.where((r >= 0) & (r < size) & (c < size), 1.0, 0.0)
        i, j = counted((one.cells, zero.cells), 0, across)
        r, c = counted((one.cells, zero.cells), 1, side)
        weight = share(r + row * zero.height - shift, i + row * one.height, size) * share(c, j, size)
        pool[g] = jnp.where(j < pooled, weight, 0.0).astype(BF)
    _, c = counted(mask_one.shape, 0, across)
    mask_one[...] = jnp.where(c < pooled, 1.0, 0.0)


def picked(shape, axis, width):
    cell, place = lax.broadcasted_iota(jnp.int32, shape, axis), lax.broadcasted_iota(jnp.int32, shape, 1 - axis)
    cell = lax.div(cell, jnp.int32(POOL)) * width + lax.rem(cell, jnp.int32(POOL))
    return jnp.where(cell == place, 1.0, 0.0).astype(BF)


def silu_of(v):
    return v * sigmoid(v)


def column_masks(cmask, width):
    place = lax.rem(lax.broadcasted_iota(jnp.int32, cmask.shape[1:], 0), width)
    cmask[0] = jnp.where(place != 0, 1.0, 0.0)
    cmask[1] = jnp.where(place != width - 1, 1.0, 0.0)


def windows(cells, rim, first, masks):
    middle = jnp.concatenate([rim * (1.0 - first), cells, rim * first], axis=0)
    count = middle.shape[0]
    left, right = pltpu.roll(middle, 1, 0), pltpu.roll(middle, count - 1, 0)
    if masks is not None:
        left, right = left * masks[0], right * masks[1]
    return left, middle, right


class Geometry:
    def __init__(self, count, height, width):
        self.count, self.height, self.width = count, height, width
        self.cells = height * width

    def rows(self, g):
        return rows_of(g * self.cells, self.cells, 16)


def head_stage(shape, per, x_of, w, gains, biases, mask, pre, hidden, rim_send, first):
    cells = shape.cells * per

    def body(i, carry):
        rows = rows_of(i * cells, cells, 16)
        x = x_of(rows)
        value = nn(x, w[...])
        pre[rows] = value.astype(BF)
        n, _ = normal(value)
        h = silu_of(n * gains[0:1] + biases[0:1]) * mask[rows]
        hidden[rows] = h.astype(BF)
        for g in range(per):
            at = g * shape.cells
            top = h[at : at + shape.width]
            bottom = h[at + shape.cells - shape.width : at + shape.cells]
            rim_send[i * per + g, pl.ds(0, shape.width)] = (bottom * first + top * (1.0 - first)).astype(BF)
        return carry

    lax.fori_loop(0, shape.count // per, body, 0)


def depth_stage(shape, hidden, rim, taps, cmask, pre, first, channels):
    def body(i, carry):
        g, l = i // (channels // 128), lax.rem(i, channels // 128)
        rows, lanes = shape.rows(g), rows_of(l * 128, 128, 128)
        shifted = windows(
            hidden[rows, lanes].astype(F32),
            rim[g, pl.ds(0, shape.width), lanes].astype(F32),
            first,
            None if cmask is None else (cmask[0], cmask[1]),
        )
        total = jnp.zeros((shape.cells, 128), F32)
        for a in range(3):
            for b in range(3):
                piece = shifted[b][a * shape.width : a * shape.width + shape.cells]
                total = total + piece * taps[3 * a + b : 3 * a + b + 1, lanes]
        pre[rows, lanes] = total.astype(BF)
        return carry

    lax.fori_loop(0, shape.count * (channels // 128), body, 0)


def tail_stage(shape, per, x, w, gains, biases, mask, pre_two, pre_three, result):
    cells = shape.cells * per

    def body(i, carry):
        rows = rows_of(i * cells, cells, 16)
        n, _ = normal(pre_two[rows].astype(F32))
        h = (silu_of(n * gains[1:2] + biases[1:2]) * mask[rows]).astype(BF)
        value = nn(h, w[...])
        pre_three[rows] = value.astype(BF)
        n, _ = normal(value)
        out = silu_of(x[rows].astype(F32) + n * gains[2:3] + biases[2:3]) * mask[rows]
        result(i, rows, out)
        return carry

    lax.fori_loop(0, shape.count // per, body, 0)


def slope_of(v, s):
    return s * (1.0 + v * (1.0 - s))


def norm_back(n, scale, grad, gain, sums, at):
    sums[at : at + 1] += jnp.sum(grad * n, axis=0, keepdims=True)
    sums[at + 3 : at + 4] += jnp.sum(grad, axis=0, keepdims=True)
    dn = grad * gain
    return scale * (dn - jnp.mean(dn, axis=-1, keepdims=True) - n * jnp.mean(dn * n, axis=-1, keepdims=True))


def back_tail_stage(shape, per, grad_of, x, w, gains, biases, mask, pre_two, pre_three, resid, third, hidden_two, second, edge, first, sums, base):
    cells = shape.cells * per

    def body(i, carry):
        rows = rows_of(i * cells, cells, 16)
        live = mask[rows]
        n, scale = normal(pre_three[rows].astype(F32))
        v = x[rows].astype(F32) + n * gains[2:3] + biases[2:3]
        grad = grad_of(i) * slope_of(v, sigmoid(v)) * live
        resid[rows] = grad.astype(BF)
        low = norm_back(n, scale, grad, gains[2:3], sums, base + 11).astype(BF)
        third[rows] = low
        grad = nt(low, w[...])
        n, scale = normal(pre_two[rows].astype(F32))
        v = n * gains[1:2] + biases[1:2]
        s = sigmoid(v)
        hidden_two[rows] = (v * s * live).astype(BF)
        grad = norm_back(n, scale, grad * live * slope_of(v, s), gains[1:2], sums, base + 10)
        second[rows] = grad.astype(BF)
        for g in range(per):
            at = g * shape.cells
            top = grad[at : at + shape.width]
            bottom = grad[at + shape.cells - shape.width : at + shape.cells]
            edge[i * per + g, pl.ds(0, shape.width)] = (bottom * first + top * (1.0 - first)).astype(BF)
        return carry

    lax.fori_loop(0, shape.count // per, body, 0)


def back_depth_stage(shape, second, rim, hidden, hidden_rim, taps, cmask, result, first, channels, sums, base):
    masks = None if cmask is None else (cmask[0], cmask[1])

    def body(i, carry):
        g, l = i // (channels // 128), lax.rem(i, channels // 128)
        rows, lanes = shape.rows(g), rows_of(l * 128, 128, 128)
        edge = pl.ds(0, shape.width)
        grad = second[rows, lanes].astype(F32)
        shifted = windows(grad, rim[g, edge, lanes].astype(F32), first, masks)
        total = jnp.zeros((shape.cells, 128), F32)
        for a in range(3):
            for b in range(3):
                at = (2 - a) * shape.width
                total = total + shifted[2 - b][at : at + shape.cells] * taps[3 * a + b : 3 * a + b + 1, lanes]
        result[rows, lanes] = total.astype(BF)
        shifted = windows(hidden[rows, lanes].astype(F32), hidden_rim[g, edge, lanes].astype(F32), first, masks)
        for a in range(3):
            for b in range(3):
                at = a * shape.width
                line = base + 3 * a + b
                sums[line : line + 1, lanes] += jnp.sum(
                    grad * shifted[b][at : at + shape.cells], axis=0, keepdims=True
                )
        return carry

    lax.fori_loop(0, shape.count * (channels // 128), body, 0)


def back_head_stage(shape, per, one_grad, w, gains, biases, mask, pre_one, resid, first_low, result, sums, base):
    cells = shape.cells * per

    def body(i, carry):
        rows = rows_of(i * cells, cells, 16)
        n, scale = normal(pre_one[rows].astype(F32))
        v = n * gains[0:1] + biases[0:1]
        grad = one_grad[rows].astype(F32) * mask[rows] * slope_of(v, sigmoid(v))
        low = norm_back(n, scale, grad, gains[0:1], sums, base + 9).astype(BF)
        first_low[rows] = low
        result(i, rows, resid[rows].astype(F32) + nt(low, w[...]))
        return carry

    lax.fori_loop(0, shape.count // per, body, 0)


def outer_stage(left, right, out):
    high = out.shape[2]

    def body(i, carry):
        at = rows_of(i * high, high, 128)
        out[i // 2, lax.rem(i, 2)] = tn(left[:, at], right[...]).astype(BF)
        return carry

    lax.fori_loop(0, out.shape[0] * 2, body, 0)


def readout_kernel(
    nz, ndp, nrow, zero, one,
    sizes, patches, cot, rin_part, rout_part, bias_part, conv_in, conv_out, pack,
    tokens, agrad, s1, f2, early, rc1, rc2, rp2, keep_zero, keep_one, rim_zero, rim_one,
    mask_zero, mask_one, pool, hsum, rin, rout, bias, abst, abst_t, hid, mg, ag_send, ag_recv, s2, cmask, edge_zero, edge_one, send, recv, local,
):
    me = Place(nz, ndp, nrow)
    links = Links(send, recv)
    taps, gains, biases = [[pack.at[b, pl.ds(at, n)] for b in range(2)] for at, n in ((0, 16), (16, 8), (24, 8))]
    T, C = agrad.shape
    hw, ow = rout.shape[1], rout.shape[2]
    tall = nz * T
    np_ = 2 * me.nq
    strip = me.c * me.nq + me.q
    ra, rb = C // np_, hw // np_
    me.greet()

    own = [
        pltpu.make_async_copy(rin_part, rin.at[0], local.at[0]),
        pltpu.make_async_copy(rout_part.at[:, rows_of(me.k * ow, ow, 128)], rout.at[0], local.at[1]),
    ]
    convs = [
        pltpu.make_async_copy(part.at[b], s2.at[2 * b + i], local.at[2 + 2 * b + i])
        for b in range(2)
        for i, part in enumerate((conv_in, conv_out))
    ]
    given = pltpu.make_async_copy(patches, mg.at[0], local.at[6])
    convs[0].start()
    given.start()
    za, zb, zc = [[], []], [], []
    rh = ra // 2
    row_b = rows_of(strip * rb, rb, rb)
    for t in range(1, nz):
        there = lax.rem(me.k + nz - t, nz)
        for h in range(2):
            row_a = rows_of(strip * ra + h * rh, rh, rh)
            za[h].append(links.copy(rin_part.at[row_a], rin.at[t, row_a], me.at(k=there)))
        zc.append(links.copy(bias_part, bias.at[t], me.at(k=there)))
    start_all(za[0])
    start_all(zc)
    start_all(za[1])
    for t in range(1, nz):
        there = lax.rem(me.k + nz - t, nz)
        zb.append(links.copy(
            rout_part.at[row_b, rows_of(there * ow, ow, 128)], rout.at[t, row_b], me.at(k=there)))
    for copy in convs[1:] + own:
        copy.start()
    bias[0] = bias_part[...]
    column_masks(cmask, zero.width)
    live_stage(sizes, me.r, zero, one, mask_zero, mask_one, pool)

    def strips(weights, height, part, parts):
        wide = weights.shape[2]

        def strip(q, half):
            few = height // parts
            rows = rows_of((me.c * me.nq + q) * height + part * few, few, few)
            cols = pl.ds(0, wide) if half is None else pl.ds(half * (wide // 2), wide // 2)
            return weights.at[pl.ds(1, nz - 1), rows, cols]

        return Spread(me, links, strip)

    def between_cores(weights, height):
        half = rows_of(me.c * (me.nq * height), me.nq * height, height)
        part = weights.at[pl.ds(1, nz - 1), half]
        return start_all([links.copy(part, part, me.at(c=1 - me.c))])

    pa, pb = [strips(rin, ra, h, 2) for h in range(2)], strips(rout, rb, 0, 1)

    first = (1 - me.r).astype(F32)
    neighbour = me.at(q=me.x * nrow + (nrow - 1 - me.r))

    def masked(rows):
        x = (mg[0, rows].astype(F32) * mask_zero[rows]).astype(BF)
        mg[0, rows] = x
        return x

    convs[0].wait()
    given.wait()
    head_stage(zero, 1, masked, s2.at[0], gains[0], biases[0], mask_zero, hid.at[0], hid.at[1], edge_zero, first)
    rim0 = links.copy(edge_zero, rim_zero, neighbour)
    rim0.start()
    recv_all(za[0])
    pa[0].start()
    rim0.wait_recv()
    depth_stage(zero, hid.at[1], rim_zero, taps[0], cmask, hid.at[2], first, C)
    for copy in convs[1:]:
        copy.wait()

    def to_pooled(i, rows, out):
        mg[1, one.rows(i)] = nn(pool[i], out.astype(BF)).astype(BF)

    sent_all(za[0])
    sent_all(za[1])
    start_all(zb)
    recv_all(za[1])
    pa[1].start()
    pa[0].pass_on()
    tail_stage(zero, 1, mg.at[0], s2.at[1], gains[0], biases[0], mask_zero, hid.at[2], hid.at[3], to_pooled)
    kept_zero = pltpu.make_async_copy(hid, keep_zero, local.at[2])
    kept_zero.start()
    all_one = one.cells * one.count
    part = [mg.at[1 + i // 3, pl.ds((i % 3) * all_one, all_one)] for i in range(5)]
    pooled, pre_one, hidden, pre_two, pre_three = part
    head_stage(one, one.count, lambda rows: pooled[rows], s2.at[2], gains[1], biases[1], mask_one, pre_one, hidden, edge_one, first)
    rim1 = links.copy(edge_one, rim_one, neighbour)
    rim1.start()
    rim1.wait_recv()
    depth_stage(one, hidden, rim_one, taps[1], None, pre_two, first, C)
    here = rows_of(me.k * T, T, 16)

    def to_tokens(i, rows, out):
        abst[here] = nn(picked((T, all_one), 0, one.width), out.astype(BF)).astype(BF)

    tail_stage(one, one.count, pooled, s2.at[3], gains[1], biases[1], mask_one, pre_two, pre_three, to_tokens)
    kept_one = pltpu.make_async_copy(mg.at[pl.ds(1, 2)], keep_one, local.at[3])
    kept_one.start()
    def along(step, group, to):
        rows = rows_of(lax.rem(group + nz, nz) * T, T, 16)
        return links.copy(abst.at[rows], abst.at[rows], me.at(k=lax.rem(to + nz, nz)))

    up = [along(step, me.k - step, me.k + 1) for step in range(nz - 1)]
    down = [along(step, me.k + step, me.k - 1) for step in range(nz - 1)]
    more, less = me.k + 1 < nz, me.k > 0

    def hop(step):
        if step < nz - 1:
            pl.when(jnp.logical_and(more, me.k - step >= 0))(up[step].start)
            pl.when(jnp.logical_and(less, me.k + step < nz))(down[step].start)

    hop(0)
    pa[1].pass_on()
    recv_all(zb)
    pa[0].finish()
    pa[1].finish()
    pb.start()
    ca = between_cores(rin, ra)
    for copy in own + [kept_zero, kept_one]:
        copy.wait()
    recv_all(zc)
    recv_all(ca)

    hsum[...] = jnp.zeros_like(hsum)
    total = jnp.sum(cot[...].astype(F32), axis=0, keepdims=True)
    for j in range(nz):
        early[nz + j : nz + j + 1] = jnp.where(me.k == j, total, 0.0)
    ag = [None] + [
        links.copy(ag_send.at[t - 1], ag_recv.at[t - 1], me.at(k=me.deep(t))) for t in range(1, nz)
    ]
    NT = min(512, hw)

    def hidden_group(z):
        rows = rows_of(z * T, T, 16)

        def front(i, carry):
            u = i // (hw // NT)
            cols = rows_of(lax.rem(i, hw // NT) * NT, NT, 128)
            value, slope = gelu_pair(nn(abst[rows], rin[u, :, cols]) + bias[u, 0:1, cols])
            hid[u, rows, cols] = value.astype(BF)
            mg[u, rows, cols] = slope.astype(BF)
            return carry

        lax.fori_loop(0, nz * (hw // NT), front, 0)

    hidden_group(me.k)
    pb.pass_on()
    for step in range(nz - 1):
        from_less, from_more = me.k - 1 - step >= 0, me.k + 1 + step < nz
        pl.when(from_less)(up[step].wait_recv)
        pl.when(from_more)(down[step].wait_recv)
        hop(step + 1)
        lower = from_less.astype(jnp.int32)

        def arrived(i, carry):
            hidden_group(jnp.where(i < lower, me.k - 1 - step, me.k + 1 + step))
            return carry

        lax.fori_loop(0, lower + from_more.astype(jnp.int32), arrived, 0)
        if step == 0:
            pb.finish()
            cb = between_cores(rout, rb)

    HT = 256

    def g2(i, carry):
        u = i // (hw // HT)
        at = rows_of(lax.rem(i, hw // HT) * HT, HT, HT)
        s2[me.deep(u), at, :] = tn(hid[u, :, at], cot[...]).astype(BF)
        return carry

    lax.fori_loop(0, nz * (hw // HT), g2, 0)
    half = me.nq * rb
    theirs = rows_of((1 - me.c) * half, half, half)
    core2 = start_all([links.copy(s2.at[:, theirs], rc2, me.at(c=1 - me.c))])
    abst_t[...] = abst[...].T
    recv_all(cb)

    def unit(i, carry):
        u = i // (hw // 256)
        cols = rows_of(lax.rem(i, hw // 256) * 256, 256, 256)
        grad = (nt(cot[...], rout[u, cols, :]) * mg[u, :, cols].astype(F32)).astype(BF)
        mg[u, :, cols] = grad
        hsum[me.deep(u), 0:1, cols] += jnp.sum(grad.astype(F32), axis=0, keepdims=True)
        return carry

    lax.fori_loop(0, nz * (hw // 256), unit, 0)

    recv_all(core2)
    mine2 = me.c * half
    gather2 = Gather(
        me, links,
        lambda q, h: s2.at[pl.ds(h * (nz // 2), nz // 2), rows_of(mine2 + q * rb, rb, rb)],
        lambda i, h: rp2.at[i, pl.ds(h * (nz // 2), nz // 2)],
    )
    piece = 256
    parts = half // piece
    loads = [
        pltpu.make_async_copy(
            rc2.at[i // parts, pl.ds(i % parts * piece, piece)], ag_send.at[i % 2, pl.ds(0, piece)], local.at[i % 2]
        )
        for i in range(nz * parts)
    ]
    loads[0].start()
    for i in range(nz * parts):
        loads[i].wait()
        if i + 1 < nz * parts:
            loads[i + 1].start()
        j, where = i // parts, mine2 + i % parts * piece
        fold(
            lambda at, v, j=j, w=where: s2.__setitem__((j, rows_of(w + at.start, at.size, 16)), v.astype(BF)),
            [
                lambda at, j=j, w=where: s2[j, rows_of(w + at.start, at.size, 16)],
                lambda at, i=i: ag_send[i % 2, at],
            ],
            piece, 32,
        )
        if (i + 1) % (nz // 2 * parts) == 0:
            gather2.start(i // (nz // 2 * parts))

    def group_back(t):
        rows = rows_of(me.deep(t) * T, T, 16)

        def back(i, carry):
            at = rows_of(i * 256, 256, 256)
            total = nt(mg[0, rows, :], rin[0, at, :])
            for u in range(1, nz):
                total = total + nt(mg[u, rows, :], rin[u, at, :])
            if t == 0:
                agrad[:, at] = total
            else:
                ag_send[t - 1, :, at] = total.astype(BF)
            return carry

        lax.fori_loop(0, C // 256, back, 0)
        if t:
            ag[t].start()

    for t in (*range(1, nz), 0):
        group_back(t)


    sent_all(ca)
    for group in pa:
        group.sent()

    def g1(i, carry):
        u = i // (C // 256)
        at = rows_of(lax.rem(i, C // 256) * 256, 256, 256)
        rin[u, at, :] = nn(abst_t[at, :], mg[u]).astype(BF)
        return carry

    lax.fori_loop(0, nz * (C // 256), g1, 0)
    low = me.nq * ra
    core1 = links.copy(rin.at[:, rows_of((1 - me.c) * low, low, low)], rc1, me.at(c=1 - me.c))
    core1.start()

    for h in range(2):
        to = gather2.passing(h)
        block = range(h * (nz // 2), (h + 1) * (nz // 2))
        loads = [pltpu.make_async_copy(rp2.at[1, j], mg.at[j, pl.ds(0, rb)], local.at[j]) for j in block]
        for copy in loads:
            copy.start()
        for j, copy in zip(block, loads):
            copy.wait()
            where = mine2 + to * rb
            fold(
                lambda at, v, j=j, w=where: s2.__setitem__((j, rows_of(w + at.start, at.size, 16)), v.astype(BF)),
                [lambda at, j=j, w=where: s2[j, rows_of(w + at.start, at.size, 16)], lambda at, j=j: mg[j, at]],
                rb, min(rb, 32),
            )
        gather2.pass_on(h, gather2.chunk(to, h))

    for step in range(nz - 1):
        pl.when(jnp.logical_and(more, me.k - step >= 0))(up[step].wait_send)
        pl.when(jnp.logical_and(less, me.k + step < nz))(down[step].wait_send)

    def f2_body(i, carry):
        at = rows_of(i * 256, 256, 256)
        total = nn(hid[0], rout[0, :, at]) + bias_part[1:2, at]
        for u in range(1, nz):
            total = total + nn(hid[u], rout[u, :, at])
        abst[:, at] = total.astype(BF)
        return carry

    lax.fori_loop(0, ow // 256, f2_body, 0)
    out_tokens = pltpu.make_async_copy(abst, tokens, local.at[6])
    out_tokens.start()
    recv_all(ag[1:])
    fold(
        lambda at, v: agrad.__setitem__(at, v),
        [lambda at: agrad[at]] + [lambda at, t=t: ag_recv[t - 1, at] for t in range(1, nz)],
        T, 32,
    )
    core1.wait_recv()
    loads = [pltpu.make_async_copy(rc1.at[u], mg.at[u, pl.ds(0, low)], local.at[u]) for u in range(nz)]
    for copy in loads:
        copy.start()
    outs = []
    for u in range(nz):
        loads[u].wait()
        fold(
            lambda at, v, u=u: rin.__setitem__((u, rows_of(me.c * low + at.start, at.size, 16)), v.astype(BF)),
            [lambda at, u=u: rin[u, rows_of(me.c * low + at.start, at.size, 16)], lambda at, u=u: mg[u, at]],
            low, 32,
        )
        outs.append(pltpu.make_async_copy(rin.at[u, rows_of(me.c * low, low, low)], s1.at[u], local.at[u]))
        outs[-1].start()
    gather2.finish()
    for copy in outs:
        copy.wait()
    loads = [
        pltpu.make_async_copy(rp2.at[i], mg.at[pl.ds(0, nz), pl.ds(i * rb, rb)], local.at[i]) for i in (0, 2)
    ]
    for copy in loads:
        copy.start()
    for copy in loads:
        copy.wait()
    for j in range(nz):
        fold(
            lambda at, v, j=j: f2.__setitem__((j, at), v.astype(BF)),
            [lambda at, j=j: s2[j, rows_of(strip * rb + at.start, at.size, 16)]]
            + [lambda at, j=j, i=i: mg[j, rows_of(i * rb + at.start, at.size, 16)] for i in (0, 2)],
            rb, min(rb, 32),
        )
    for j in range(nz):
        early[j : j + 1] = hsum[j]
    out_tokens.wait()
    for group in (pb, gather2):
        group.sent()
    for group_of in (zb, zc, cb, core2, ag[1:], [rim0, rim1, core1]):
        sent_all(group_of)


def grads_kernel(
    nz, ndp, nrow, zero, one,
    sizes, s1, f2, agrad, patches, keep_zero, keep_one, rim_zero, rim_one, conv_in, conv_out, pack, early_in,
    out1, out2, out3, small_out, early, patch_grad, rp1,
    mask_zero, mask_one, pool, small, ec, ep, ez, xs, kept, keep, third, resid, weights, cmask, edge_zero, edge_one, got_zero, got_one,
    sent_on, f1, rz1, conv, rc3, rp3, f3, rz3, sc, sp, sz, send, recv, local,
):
    me = Place(nz, ndp, nrow)
    links = Links(send, recv)
    C, hw = out1.shape
    ow = f2.shape[2]
    np_ = 2 * me.nq
    strip = me.c * me.nq + me.q
    ra, rb = C // np_, hw // np_
    width = C // nrow
    R = out3.shape[2] // 2
    other = me.at(c=1 - me.c)
    first = (1 - me.r).astype(F32)
    neighbour = me.at(q=me.x * nrow + (nrow - 1 - me.r))
    me.greet()

    loads = [
        pltpu.make_async_copy(keep_one, keep, local.at[0]),
        pltpu.make_async_copy(conv_out.at[1], weights.at[1], local.at[1]),
        pltpu.make_async_copy(conv_in.at[1], weights.at[0], local.at[2]),
        pltpu.make_async_copy(keep_zero, kept, local.at[3]),
        pltpu.make_async_copy(patches, xs, local.at[4]),
    ]
    for copy in loads:
        copy.start()
    lead = nz // 2
    gather1 = Gather(
        me, links,
        lambda q, h: s1.at[pl.ds(h * lead, lead), rows_of(q * ra, ra, ra)],
        lambda i, h: rp1.at[i, pl.ds(h * lead, lead)],
    )
    gather1.start(0)
    gather1.start(1)
    row_b = rows_of(strip * rb, rb, rb)
    col_k = rows_of(me.k * ow, ow, 128)
    z2 = start_all([
        links.copy(f2.at[me.deep(t)], out2.at[row_b, col_k], me.at(k=me.deep(t))) for t in range(1, nz)
    ])
    own2 = pltpu.make_async_copy(f2.at[me.k], out2.at[row_b, col_k], local.at[5])
    own2.start()
    early_c = links.copy(early_in, ec, other)
    early_c.start()
    small[...] = jnp.zeros_like(small)
    column_masks(cmask, zero.width)
    live_stage(sizes, me.r, zero, one, mask_zero, mask_one, pool)
    taps, gains, biases = [[pack.at[b, pl.ds(at, n)] for b in range(2)] for at, n in ((0, 16), (16, 8), (24, 8))]

    def spread(b):
        core3[b].wait_recv()
        for m in range(2):
            for x in range(me.nx):
                fold(
                    lambda at, v, i=(b, m, x, me.c): conv.__setitem__((*i, at), v.astype(BF)),
                    [lambda at, i=(b, m, x, me.c): conv[(*i, at)], lambda at, i=(b, m, x): rc3[(*i, at)]],
                    nz * R, 32,
                )
        gather = Gather(
            me, links,
            lambda q, h: conv.at[b, h, q // nrow, me.c, :, rows_of(lax.rem(q, nrow) * width, width, 128)],
            lambda i, h: rp3.at[b, i, h],
        )
        gather.start(1)
        gather.start(0)
        return gather

    def spread_on(b):
        for h in (1, 0):
            to = p3[b].passing(h)
            cols = rows_of(lax.rem(to, nrow) * width, width, 128)
            x = to // nrow
            fold(
                lambda at, v: conv.__setitem__((b, h, x, me.c, at, cols), v.astype(BF)),
                [lambda at: conv[b, h, x, me.c, at, cols], lambda at: rp3[b, 1, h, at, :]],
                nz * R, 32,
            )
            p3[b].pass_on(h, p3[b].chunk(to, h))

    core3, p3 = [None, None], [None, None]

    all_one = one.cells * one.count
    pooled, pre_one, hidden, pre_two, pre_three, pooled_grad = [
        keep.at[i // 3, pl.ds((i % 3) * all_one, all_one)] for i in range(6)
    ]
    third_one, resid_one = third.at[pl.ds(0, all_one)], resid.at[pl.ds(0, all_one)]
    loads[0].wait()
    loads[1].wait()
    back_tail_stage(
        one, one.count, lambda i: nn(picked((all_one, agrad.shape[0]), 1, one.width), agrad[...].astype(BF)), pooled, weights.at[1], gains[1], biases[1], mask_one,
        pre_two, pre_three, resid_one, third_one, pre_three, pre_two, edge_one, first, small, 16,
    )
    rim1 = links.copy(edge_one, got_one, neighbour)
    rim1.start()
    early_c.wait_recv()
    early[...] = early_in[...] + ec[...]
    early_p = start_all([links.copy(early, ep.at[t - 1], me.at(q=me.chip(t))) for t in range(1, me.nq)])
    outer_stage(third_one, pre_three, conv.at[1, 1])
    rim1.wait_recv()
    back_depth_stage(one, pre_two, got_one, hidden, rim_one, taps[1], None, third_one, first, C, small, 16)
    loads[2].wait()

    def to_pooled_grad(i, rows, grad):
        pooled_grad[rows] = grad.astype(BF)

    back_head_stage(
        one, one.count, third_one, weights.at[0], gains[1], biases[1], mask_one, pre_one, resid_one, pre_three, to_pooled_grad, small, 16
    )
    again = [
        pltpu.make_async_copy(conv_out.at[0], weights.at[1], local.at[1]),
        pltpu.make_async_copy(conv_in.at[0], weights.at[0], local.at[2]),
    ]
    for copy in again:
        copy.start()
    outer_stage(pre_three, pooled, conv.at[1, 0])
    core3[1] = links.copy(conv.at[1, :, :, 1 - me.c], rc3.at[1], other)
    core3[1].start()

    temp = [keep.at[0, pl.ds(i * lead * ra, lead * ra)] for i in range(4)]

    def bring(sources):
        copies = [
            pltpu.make_async_copy(source.at[j], to.at[pl.ds(j * ra, ra)], local.at[6 + n * lead + j])
            for n, (source, to) in enumerate(sources)
            for j in range(lead)
        ]
        for copy in copies:
            copy.start()
        for copy in copies:
            copy.wait()

    for h in range(2):
        to = gather1.passing(h)
        bring([(gather1.chunk(to, h), temp[2 * h]), (gather1.slot(1, h), temp[2 * h + 1])])
        for j in range(lead):
            fold(
                lambda at, v: sent_on.__setitem__((h, j, at), v.astype(BF)),
                [lambda at, ref=ref: ref[rows_of(j * ra + at.start, at.size, 16)] for ref in temp[2 * h : 2 * h + 2]],
                ra, 32,
            )
        gather1.pass_on(h, sent_on.at[h])
    p3[1] = spread(1)
    sent_all(early_p)
    recv_all(early_p)
    for t in range(1, me.nq):
        early[...] += ep[t - 1]
    early_z = start_all([links.copy(early, ez.at[t - 1], me.at(k=me.deep(t))) for t in range(1, nz)])
    loads[3].wait()
    loads[4].wait()
    xs[...] = (xs[...].astype(F32) * mask_zero[...]).astype(BF)
    again[0].wait()
    back_tail_stage(
        zero, 1, lambda i: tn(pool[i], pooled_grad[one.rows(i)]), xs, weights.at[1], gains[0], biases[0], mask_zero,
        kept.at[2], kept.at[3], resid, third, kept.at[3], kept.at[2], edge_zero, first, small, 0,
    )
    rim0 = links.copy(edge_zero, got_zero, neighbour)
    rim0.start()
    outer_stage(third, kept.at[3], conv.at[0, 1])
    rim0.wait_recv()
    back_depth_stage(zero, kept.at[2], got_zero, kept.at[1], rim_zero, taps[0], cmask, third, first, C, small, 0)
    spread_on(1)
    own2.wait()
    recv_all(z2)
    spread2 = Spread(me, links, lambda q, h: out2.at[
        rows_of((me.c * me.nq + q) * rb, rb, rb),
        pl.ds(0, nz * ow) if h is None else pl.ds(h * (nz * ow // 2), nz * ow // 2),
    ])
    spread2.start()
    gather1.finish()
    for h in range(2):
        mine = [keep.at[0, pl.ds(i * lead * ra, lead * ra)] for i in range(3)]
        bring([(gather1.chunk(me.q, h), mine[0]), (gather1.slot(0, h), mine[1]), (gather1.slot(2, h), mine[2])])
        for j in range(lead):
            fold(
                lambda at, v: f1.__setitem__((h * lead + j, at), v.astype(BF)),
                [lambda at, ref=ref: ref[rows_of(j * ra + at.start, at.size, 16)] for ref in mine],
                ra, 32,
            )
    z1 = start_all([links.copy(f1.at[t], rz1.at[t - 1], me.at(k=me.deep(t))) for t in range(1, nz)])
    again[1].wait()

    def to_patches(i, rows, grad):
        resid[rows] = (grad * mask_zero[rows]).astype(BF)

    back_head_stage(
        zero, 1, third, weights.at[0], gains[0], biases[0], mask_zero, kept.at[0], resid, kept.at[3], to_patches, small, 0
    )
    out_patches = pltpu.make_async_copy(resid, patch_grad, local.at[0])
    out_patches.start()
    outer_stage(kept.at[3], xs, conv.at[0, 0])
    core3[0] = links.copy(conv.at[0, :, :, 1 - me.c], rc3.at[0], other)
    core3[0].start()
    sums = start_all([links.copy(small, sc, other)])
    z3 = [None, None]
    my_cols = rows_of(me.r * width, width, 128)

    def deepen(b):
        p3[b].finish()
        for m in range(2):
            for j in range(nz):
                rows = pl.ds(j * R, R)
                total = conv[b, m, me.x, me.c, rows, my_cols].astype(F32)
                for i in (0, 2):
                    total = total + rp3[b, i, m, rows, :].astype(F32)
                f3[b, j, pl.ds(m * R, R)] = total.astype(BF)
        z3[b] = start_all([
            links.copy(f3.at[b, me.deep(t)], rz3.at[b, t - 1], me.at(k=me.deep(t))) for t in range(1, nz)
        ])

    g3 = []

    def settle(b):
        recv_all(z3[b])
        total = f3[b, me.k].astype(F32)
        for t in range(1, nz):
            total = total + rz3[b, t - 1].astype(F32)
        out3[b, me.r] = total.astype(BF)
        g3.extend(start_all([
            links.copy(out3.at[b, me.r], out3.at[b, me.r], me.at(q=me.x * nrow + lax.rem(me.r + t, nrow)))
            for t in range(1, nrow)
        ]))

    p3[0] = spread(0)
    deepen(1)
    recv_all(z1)
    row_a = rows_of(strip * ra, ra, ra)
    fold(
        lambda at, v: out1.__setitem__(rows_of(strip * ra + at.start, at.size, 16), v.astype(BF)),
        [lambda at: f1[0, at]] + [lambda at, t=t: rz1[t - 1, at] for t in range(1, nz)],
        ra, 32,
    )
    spread1 = Spread(me, links, lambda q, h: out1.at[
        rows_of((me.c * me.nq + q) * ra, ra, ra), pl.ds(0, hw) if h is None else pl.ds(h * (hw // 2), hw // 2)
    ])
    spread1.start()
    recv_all(sums)
    sent_all(sums)
    small[...] += sc[...]
    few = C // ndp

    def columns(q):
        return rows_of((q // nrow * 2 + me.c) * few, few, 128)

    sums_p = start_all([
        links.copy(small.at[:, columns(me.chip(t))], sp.at[t - 1], me.at(q=me.chip(t))) for t in range(1, me.nq)
    ])
    spread_on(0)
    spread2.pass_on()
    spread1.pass_on()
    settle(1)
    recv_all(sums_p)
    total = small[:, columns(me.q)]
    for t in range(1, me.nq):
        total = total + sp[t - 1]
    small_out[...] = total
    sums_z = start_all([links.copy(small_out, sz.at[t - 1], me.at(k=me.deep(t))) for t in range(1, nz)])
    deepen(0)
    spread1.finish()
    half_a = rows_of(me.c * me.nq * ra, me.nq * ra, me.nq * ra)
    h1 = start_all([links.copy(out1.at[half_a], out1.at[half_a], other)])
    spread2.finish()
    half_b = rows_of(me.c * me.nq * rb, me.nq * rb, me.nq * rb)
    h2 = start_all([links.copy(out2.at[half_b], out2.at[half_b], other)])
    settle(0)
    sent_all(sums_z)
    recv_all(sums_z)
    sent_all(early_z)
    recv_all(early_z)
    for t in range(1, nz):
        small_out[...] += sz[t - 1]
        early[...] += ez[t - 1]
    recv_all(g3)
    recv_all(h1)
    recv_all(h2)
    out_patches.wait()
    for group_of in ([early_c], sums_p, core3, z2, z1, z3[0], z3[1], g3, h1, h2, [rim0, rim1]):
        sent_all(group_of)
    for group in (gather1, p3[0], p3[1], spread1, spread2):
        group.sent()


def spec(*kinds):
    return [pl.BlockSpec(memory_space=kind) for kind in kinds]


def run_readout(mesh, zero, one, sizes, patches, cot, read_in, read_out, read_bias, conv_in, conv_out, pack):
    nz, ndp, nrow = mesh.shape["wide"], mesh.shape["dp"], mesh.shape["row"]
    nq = ndp // 2 * nrow
    T, C = one.count * one.height * POOL, patches.shape[1]
    hw, ow = read_out.shape[0], cot.shape[1]
    tall = nz * T
    rb = hw // (2 * nq)
    copies = 7 * (nz - 1) + 28
    bias_part = jnp.pad(read_bias, ((0, 6), (0, 0)))
    ANY = pl.ANY
    return pl.pallas_call(
        functools.partial(readout_kernel, nz, ndp, nrow, zero, one),
        out_shape=[
            jax.ShapeDtypeStruct((tall, ow), BF),
            jax.ShapeDtypeStruct((T, C), F32),
            jax.ShapeDtypeStruct((nz, C // 2, hw), BF),
            jax.ShapeDtypeStruct((nz, rb, ow), BF),
            jax.ShapeDtypeStruct((2 * nz, C), F32),
            jax.ShapeDtypeStruct((nz, C // 2, hw), BF),
            jax.ShapeDtypeStruct((nz, nq * rb, ow), BF),
            jax.ShapeDtypeStruct((nq - 1, nz, rb, ow), BF),
            jax.ShapeDtypeStruct((4, tall, hw), BF),
            jax.ShapeDtypeStruct((2, tall, hw), BF),
            jax.ShapeDtypeStruct((zero.count, 32, C), BF),
            jax.ShapeDtypeStruct((one.count, 16, C), BF),
        ],
        in_specs=spec(pltpu.SMEM, ANY, VMEM, ANY, ANY, VMEM, ANY, ANY, VMEM),
        out_specs=spec(ANY, VMEM, ANY, VMEM, VMEM, ANY, ANY, ANY, ANY, ANY, VMEM, VMEM),
        scratch_shapes=[
            VMEM((tall, 1), F32),
            VMEM((one.count * one.cells, 1), F32),
            VMEM((zero.count, one.cells, zero.cells), BF),
            VMEM((nz, 1, hw), F32),
            VMEM((nz, C, hw), BF),
            VMEM((nz, hw, ow), BF),
            VMEM((nz, 8, hw), F32),
            VMEM((tall, C), BF),
            VMEM((C, tall), BF),
            VMEM((nz, tall, hw), BF),
            VMEM((nz, tall, hw), BF),
            VMEM((nz - 1, T, C), BF),
            VMEM((nz - 1, T, C), BF),
            VMEM((nz, hw, ow), BF),
            VMEM((2, zero.cells + 2 * zero.width, 128), F32),
            VMEM((zero.count, 32, C), BF),
            VMEM((one.count, 16, C), BF),
            pltpu.SemaphoreType.DMA((copies,)),
            pltpu.SemaphoreType.DMA((copies,)),
            pltpu.SemaphoreType.DMA((7,)),
        ],
        compiler_params=pltpu.CompilerParams(
            collective_id=0, has_side_effects=True, vmem_limit_bytes=LIMIT
        ),
        name="readout",
    )(sizes, patches, cot, read_in, read_out, bias_part, conv_in, conv_out, pack)


LIMIT = 62 * 1024 * 1024


def run_grads(mesh, zero, one, sizes, s1, f2, agrad, patches, keep_zero, keep_one, rim_zero, rim_one, conv_in, conv_out, pack, early):
    nz, ndp, nrow = mesh.shape["wide"], mesh.shape["dp"], mesh.shape["row"]
    nq = ndp // 2 * nrow
    nx = ndp // 2
    C, hw = s1.shape[1] * 2, s1.shape[2]
    _, rb, ow = f2.shape
    ra = C // (2 * nq)
    R = C // (ndp * nz)
    tall = patches.shape[0]
    S = 32
    copies = 7 * (nz - 1) + 40
    width = C // nrow
    ANY = pl.ANY
    return pl.pallas_call(
        functools.partial(grads_kernel, nz, ndp, nrow, zero, one),
        out_shape=[
            jax.ShapeDtypeStruct((C, hw), BF),
            jax.ShapeDtypeStruct((hw, nz * ow), BF),
            jax.ShapeDtypeStruct((2, nrow, 2 * R, width), BF),
            jax.ShapeDtypeStruct((S, C // ndp), F32),
            jax.ShapeDtypeStruct(early.shape, F32),
            jax.ShapeDtypeStruct((tall, C), BF),
            jax.ShapeDtypeStruct((nq - 1, nz, ra, hw), BF),
        ],
        in_specs=spec(pltpu.SMEM, ANY, VMEM, VMEM, ANY, ANY, ANY, VMEM, VMEM, ANY, ANY, VMEM, VMEM),
        out_specs=spec(VMEM, ANY, VMEM, VMEM, VMEM, ANY, ANY),
        scratch_shapes=[
            VMEM((tall, 1), F32),
            VMEM((one.count * one.cells, 1), F32),
            VMEM((zero.count, one.cells, zero.cells), BF),
            VMEM((S, C), F32),
            VMEM(early.shape, F32),
            VMEM((nq - 1, *early.shape), F32),
            VMEM((nz - 1, *early.shape), F32),
            VMEM((tall, C), BF),
            VMEM((4, tall, C), BF),
            VMEM((2, tall, C), BF),
            VMEM((tall, C), BF),
            VMEM((tall, C), BF),
            VMEM((2, C, C), BF),
            VMEM((2, zero.cells + 2 * zero.width, 128), F32),
            VMEM((zero.count, 32, C), BF),
            VMEM((one.count, 16, C), BF),
            VMEM((zero.count, 32, C), BF),
            VMEM((one.count, 16, C), BF),
            VMEM((2, nz // 2, ra, hw), BF),
            VMEM((nz, ra, hw), BF),
            VMEM((nz - 1, ra, hw), BF),
            VMEM((2, 2, nx, 2, nz * R, C), BF),
            VMEM((2, 2, nx, nz * R, C), BF),
            VMEM((2, nq - 1, 2, nz * R, width), BF),
            VMEM((2, nz, 2 * R, width), BF),
            VMEM((2, nz - 1, 2 * R, width), BF),
            VMEM((S, C), F32),
            VMEM((nq - 1, S, C // ndp), F32),
            VMEM((nz - 1, S, C // ndp), F32),
            pltpu.SemaphoreType.DMA((copies,)),
            pltpu.SemaphoreType.DMA((copies,)),
            pltpu.SemaphoreType.DMA((6 + nq * nz,)),
        ],
        compiler_params=pltpu.CompilerParams(
            collective_id=1, has_side_effects=True, vmem_limit_bytes=LIMIT
        ),
        name="grads",
    )(sizes, s1, f2, agrad, patches, keep_zero, keep_one, rim_zero, rim_one, conv_in, conv_out, pack, early)


POOL = 12


eps_norm = 1e-06
exact_mode = lax.Precision.HIGHEST


def extended(cells, sides, width):
    for axis, dim in sides:
        count = lax.axis_size(axis)
        ends = count - 1
        head = lax.slice_in_dim(cells, 0, width, axis=dim)
        tail = lax.slice_in_dim(cells, cells.shape[dim] - width, cells.shape[dim], axis=dim)
        cells = jnp.concatenate(
            [
                lax.ppermute(tail, axis, [(i, (i + 1) % count) for i in range(ends)]),
                cells,
                lax.ppermute(head, axis, [((i + 1) % count, i) for i in range(ends)]),
            ],
            axis=dim,
        )
    return cells


def layer_norm(values, gain_row, bias_row):
    centre = jnp.mean(values, axis=-1, keepdims=True)
    centred = values - centre
    variance = jnp.mean(centred * centred, axis=-1, keepdims=True)
    return centred * lax.rsqrt(variance + eps_norm) * gain_row + bias_row


def head_piece(pre_values, gain_row, bias_row, live_mask):
    return jax.nn.silu(layer_norm(pre_values, gain_row, bias_row)) * live_mask


def tail_piece(source, third_pre, gain_row, bias_row, live_mask):
    return jax.nn.silu(source + layer_norm(third_pre, gain_row, bias_row)) * live_mask


def outer_sum(left_rows, right_rows):
    return lax.dot_general(
        left_rows, right_rows, (((0,), (0,)), ((), ())), preferred_element_type=jnp.float32
    )


def times_transposed(left_rows, weight):
    return lax.dot_general(
        left_rows, weight, (((1,), (1,)), ((), ())), preferred_element_type=jnp.float32
    )


def pad_columns(values):
    return jnp.pad(values, ((0, 0), (0, 0), (1, 1), (0, 0)))


def rows_forward(hidden_one):
    return extended(hidden_one, (("row", 1),), 1)


def rows_backward(second_low):
    return extended(second_low, (("row", 1),), 1)


def depth_apply(padded, tap_table, row_count, col_count):
    result = jnp.zeros((padded.shape[0], row_count, col_count, padded.shape[3]), jnp.float32)
    for offset in range(9):
        window = padded[
            :, offset // 3 : offset // 3 + row_count, offset % 3 : offset % 3 + col_count, :
        ]
        result = result + window.astype(jnp.float32) * tap_table[offset].astype(jnp.float32)
    return result


def block_forward(source, live_mask, weights):
    w_first, w_last, tap_table, gain_rows, bias_rows = weights
    grid_count, row_count, col_count, channels = source.shape
    flat_rows = source.astype(jnp.bfloat16).reshape(-1, channels)
    first_pre = jnp.dot(flat_rows, w_first, preferred_element_type=jnp.float32).reshape(
        source.shape
    )
    hidden_one = head_piece(first_pre, gain_rows[0], bias_rows[0], live_mask).astype(jnp.bfloat16)
    padded_one = pad_columns(rows_forward(hidden_one))
    second_pre = depth_apply(padded_one, tap_table, row_count, col_count)
    hidden_two = head_piece(second_pre, gain_rows[1], bias_rows[1], live_mask).astype(jnp.bfloat16)
    two_rows = hidden_two.reshape(-1, channels)
    third_pre = jnp.dot(two_rows, w_last, preferred_element_type=jnp.float32).reshape(source.shape)
    output = tail_piece(source, third_pre, gain_rows[2], bias_rows[2], live_mask)
    return (output, (flat_rows, first_pre, padded_one, second_pre, two_rows, third_pre))


def block_backward(output_grad, source, live_mask, weights, kept):
    w_first, w_last, tap_table, gain_rows, bias_rows = weights
    flat_rows, first_pre, padded_one, second_pre, two_rows, third_pre = kept
    grid_count, row_count, col_count, channels = source.shape
    _, tail_back = jax.vjp(
        functools.partial(tail_piece, live_mask=live_mask), source, third_pre, gain_rows[2], bias_rows[2]
    )
    residual_grad, third_grad, gain_three, bias_three = tail_back(output_grad)
    third_low = third_grad.astype(jnp.bfloat16).reshape(-1, channels)
    grad_last = outer_sum(two_rows, third_low)
    two_grad = times_transposed(third_low, w_last).reshape(source.shape)
    _, middle_back = jax.vjp(
        functools.partial(head_piece, live_mask=live_mask), second_pre, gain_rows[1], bias_rows[1]
    )
    second_grad, gain_two, bias_two = middle_back(two_grad)
    second_low = second_grad.astype(jnp.bfloat16)
    padded_grad = pad_columns(rows_backward(second_low))
    one_grad = depth_apply(padded_grad, tap_table[::-1], row_count, col_count)
    second_wide = second_low.astype(jnp.float32)
    tap_grads = []
    for offset in range(9):
        window = padded_one[
            :, offset // 3 : offset // 3 + row_count, offset % 3 : offset % 3 + col_count, :
        ]
        tap_grads.append(jnp.sum(second_wide * window.astype(jnp.float32), axis=(0, 1, 2)))
    _, first_back = jax.vjp(
        functools.partial(head_piece, live_mask=live_mask), first_pre, gain_rows[0], bias_rows[0]
    )
    first_grad, gain_one, bias_one = first_back(one_grad)
    first_low = first_grad.astype(jnp.bfloat16).reshape(-1, channels)
    grad_first = outer_sum(flat_rows, first_low)
    source_grad = residual_grad + times_transposed(first_low, w_first).reshape(source.shape)
    grads = (
        grad_first,
        grad_last,
        jnp.stack(tap_grads),
        jnp.stack([gain_one, gain_two, gain_three]),
        jnp.stack([bias_one, bias_two, bias_three]),
    )
    return (source_grad, grads)


def pool_weights(grid_side, row_shift, pooled_index, slot_index):
    place = slot_index - row_shift
    begin = pooled_index * grid_side // POOL
    finish = ((pooled_index + 1) * grid_side + POOL - 1) // POOL
    inside = (place >= begin) & (place < finish)
    return jnp.where(inside, 1.0, 0.0).astype(jnp.float32) / (finish - begin).astype(jnp.float32)


def plain(
    patches,
    grid_sizes,
    conv_in,
    conv_out,
    depth_taps,
    norm_gain,
    norm_bias,
    read_in,
    read_bias,
    read_out,
    cotangent,
):
    grid_count, local_rows, grid_width, channels = patches.shape
    row_place = lax.axis_index("row")
    slot_rows = row_place * local_rows + jnp.arange(local_rows, dtype=jnp.int32)
    column_index = jnp.arange(grid_width, dtype=jnp.int32)
    row_shift = (grid_width - grid_sizes) // 2
    row_live = (slot_rows[None, :] >= row_shift[:, None]) & (
        slot_rows[None, :] < (row_shift + grid_sizes)[:, None]
    )
    col_live = column_index[None, :] < grid_sizes[:, None]
    live_mask = (row_live[:, :, None] & col_live[:, None, :]).astype(jnp.float32)[..., None]
    weights_one = (conv_in[0], conv_out[0], depth_taps[0], norm_gain[0], norm_bias[0])
    weights_two = (conv_in[1], conv_out[1], depth_taps[1], norm_gain[1], norm_bias[1])
    source = patches.astype(jnp.float32) * live_mask
    encoded, kept_one = block_forward(source, live_mask, weights_one)
    pool_local = POOL // lax.axis_size("row")
    pooled_index = row_place * pool_local + jnp.arange(pool_local, dtype=jnp.int32)
    side_shaped = grid_sizes[:, None, None]
    row_pool = pool_weights(
        side_shaped, row_shift[:, None, None], pooled_index[None, :, None], slot_rows[None, None, :]
    )
    col_pool = pool_weights(
        side_shaped,
        0,
        jnp.arange(POOL, dtype=jnp.int32)[None, :, None],
        column_index[None, None, :],
    )
    pooled = jnp.einsum("gir,gjw,grwc->gijc", row_pool, col_pool, encoded, precision=exact_mode)
    all_live = jnp.ones((grid_count, pool_local, POOL, 1), jnp.float32)
    abstract, kept_two = block_forward(pooled, all_live, weights_two)
    token_rows = abstract.astype(jnp.bfloat16).reshape(-1, channels)
    gathered = lax.all_gather(token_rows, "wide", axis=0, tiled=True)
    gelu_exact = functools.partial(jax.nn.gelu, approximate=False)
    mixed_pre = jnp.dot(gathered, read_in, preferred_element_type=jnp.float32) + read_bias[0]
    hidden_wide, gelu_back = jax.vjp(gelu_exact, mixed_pre)
    hidden = hidden_wide.astype(jnp.bfloat16)
    partial_out = jnp.dot(hidden, read_out, preferred_element_type=jnp.float32)
    summed = (
        lax.psum_scatter(
            partial_out.astype(jnp.bfloat16), "wide", scatter_dimension=1, tiled=True
        ).astype(jnp.float32)
        + read_bias[1]
    )
    tokens = summed.astype(jnp.bfloat16).reshape(cotangent.shape)
    cot_local = cotangent.reshape(-1, cotangent.shape[-1])
    cot_all = lax.all_gather(cot_local, "wide", axis=1, tiled=True)
    hidden_grad = times_transposed(cot_all, read_out)
    mixed_grad = gelu_back(hidden_grad)[0].astype(jnp.bfloat16)
    grad_exit = outer_sum(hidden, cot_all)
    grad_entry = outer_sum(gathered, mixed_grad)
    bias_pair = jnp.stack(
        [
            jnp.sum(mixed_grad.astype(jnp.float32), axis=0),
            jnp.sum(cot_local.astype(jnp.float32), axis=0),
        ]
    )
    abstract_grad = lax.psum_scatter(
        times_transposed(mixed_grad, read_in).astype(jnp.bfloat16),
        "wide",
        scatter_dimension=0,
        tiled=True,
    ).astype(jnp.float32)
    grad_entry, bias_pair, grad_exit = (
        lax.psum(grad_entry.astype(jnp.bfloat16), ("dp", "row")).astype(jnp.float32),
        lax.psum(bias_pair.astype(jnp.bfloat16), ("dp", "row")).astype(jnp.float32),
        lax.psum(grad_exit.astype(jnp.bfloat16), ("dp", "row")).astype(jnp.float32),
    )
    pooled_grad, grads_two = block_backward(
        abstract_grad.reshape(abstract.shape), pooled, all_live, weights_two, kept_two
    )
    encoded_grad = jnp.einsum(
        "gir,gjw,gijc->grwc", row_pool, col_pool, pooled_grad, precision=exact_mode
    )
    source_grad, grads_one = block_backward(encoded_grad, source, live_mask, weights_one, kept_one)
    patch_grad = (source_grad * live_mask).astype(jnp.bfloat16)
    stacked = tuple((jnp.stack([grads_one[index], grads_two[index]]) for index in range(5)))
    totals = (
        lax.psum_scatter(stacked[0], ("dp", "wide"), scatter_dimension=2, tiled=True),
        lax.psum_scatter(stacked[1], ("dp", "wide"), scatter_dimension=2, tiled=True),
        lax.psum_scatter(stacked[2], ("dp", "wide"), scatter_dimension=2, tiled=True),
        lax.psum_scatter(stacked[3], ("dp", "wide"), scatter_dimension=2, tiled=True),
        lax.psum_scatter(stacked[4], ("dp", "wide"), scatter_dimension=2, tiled=True),
    )
    totals = (
        lax.psum(totals[0].astype(jnp.bfloat16), "row").astype(jnp.float32),
        lax.psum(totals[1].astype(jnp.bfloat16), "row").astype(jnp.float32),
        lax.psum(totals[2].astype(jnp.bfloat16), "row").astype(jnp.float32),
        lax.psum(totals[3].astype(jnp.bfloat16), "row").astype(jnp.float32),
        lax.psum(totals[4].astype(jnp.bfloat16), "row").astype(jnp.float32),
    )
    return (
        tokens,
        patch_grad,
        totals[0],
        totals[1],
        totals[2],
        totals[3],
        totals[4],
        grad_entry,
        bias_pair,
        grad_exit,
    )


def on_device(
    mesh,
    patches,
    grid_sizes,
    conv_in,
    conv_out,
    depth_taps,
    norm_gain,
    norm_bias,
    read_in,
    read_bias,
    read_out,
    cotangent,
):
    nz, ndp = mesh.shape["wide"], mesh.shape["dp"]
    grid_count, local_rows, grid_width, channels = patches.shape
    zero = Geometry(grid_count, local_rows, grid_width)
    one = Geometry(grid_count, POOL // mesh.shape["row"], 16)
    flat = patches.reshape(-1, channels)
    cot_local = cotangent.reshape(-1, cotangent.shape[-1])
    pack = jnp.concatenate(
        [
            jnp.pad(piece.astype(F32), ((0, 0), (0, height - piece.shape[1]), (0, 0)))
            for piece, height in ((depth_taps, 16), (norm_gain, 8), (norm_bias, 8))
        ],
        axis=1,
    )
    tokens, agrad, s1, f2, early, _, _, _, keep_zero, keep_one, rim_zero, rim_one = run_readout(
        mesh, zero, one, grid_sizes, flat, cot_local, read_in, read_out, read_bias, conv_in, conv_out, pack
    )
    tokens = tokens.reshape(cotangent.shape)
    out1, out2, out3, small, early, patch_grad, _ = run_grads(
        mesh, zero, one, grid_sizes, s1, f2, agrad, flat, keep_zero, keep_one, rim_zero, rim_one, conv_in, conv_out, pack, early
    )
    patch_grad = patch_grad.reshape(patches.shape)
    R = channels // (ndp * nz)
    out3 = out3.reshape(2, -1, 2, R, out3.shape[-1]).transpose(0, 2, 1, 4, 3).reshape(2, 2, channels, R).astype(F32)
    place = lax.axis_index("wide")
    own = lax.dynamic_slice_in_dim(small, place * R, R, axis=1).reshape(2, 16, R)
    taps, gains, biases = own[:, 0:9], own[:, 9:12], own[:, 12:15]
    bias_pair = lax.dynamic_slice_in_dim(early.reshape(2, nz, -1), place, 1, axis=1)[:, 0]
    return (
        tokens,
        patch_grad,
        out3[:, 0],
        out3[:, 1],
        taps,
        gains,
        biases,
        out1.astype(F32),
        bias_pair,
        out2.astype(F32),
    )


def fits(mesh):
    return mesh.shape["wide"] == 4 and mesh.shape["dp"] % 2 == 0 and mesh.shape["row"] == 2


def solution(mesh):

    placed = (
        P(("dp", "wide"), "row", None, None),
        P(("dp", "wide")),
        P(),
        P(),
        P(),
        P(),
        P(),
        P(None, "wide"),
        P(None, "wide"),
        P("wide", None),
        P("dp", "row", None, "wide"),
    )
    return jax.shard_map(
        functools.partial(on_device, mesh) if fits(mesh) else plain,
        mesh=mesh,
        in_specs=placed,
        out_specs=(
            P("dp", "row", None, "wide"),
            P(("dp", "wide"), "row", None, None),
            P(None, None, ("dp", "wide")),
            P(None, None, ("dp", "wide")),
            P(None, None, ("dp", "wide")),
            P(None, None, ("dp", "wide")),
            P(None, None, ("dp", "wide")),
            P(None, "wide"),
            P(None, "wide"),
            P("wide", None),
        ),
        check_vma=False,
    )
```

```python
import functools

import jax
import jax.numpy as jnp
from jax import lax
from jax.experimental import pallas as pl
from jax.experimental.pallas import tpu as pltpu
from jax.sharding import PartitionSpec as P

MESH = pl.DeviceIdType.MESH
BF = jnp.bfloat16
F32 = jnp.float32
VMEM = pltpu.VMEM


class Place:
    def __init__(self, nz, ndp, nrow):
        self.nz, self.ndp, self.nrow = nz, ndp, nrow
        self.nx = ndp // 2
        self.nq = self.nx * nrow
        self.k = lax.axis_index("wide")
        self.r = lax.axis_index("row")
        d = lax.axis_index("dp")
        self.c = lax.rem(d, 2)
        self.x = d // 2
        self.q = self.x * nrow + self.r
        self.qx = (1 - self.x) * nrow + self.r
        self.qy = self.x * nrow + (1 - self.r)
        self.qd = (1 - self.x) * nrow + (1 - self.r)

    def at(self, q=None, c=None, k=None):
        q = self.q if q is None else q
        c = self.c if c is None else c
        k = self.k if k is None else k
        return {"dp": (q // self.nrow) * 2 + c, "row": lax.rem(q, self.nrow), "wide": k}

    def chip(self, t):
        return lax.rem(self.q + t, self.nq)

    def deep(self, t):
        return lax.rem(self.k + t, self.nz)

    def peers(self):
        return (
            [self.at(q=self.chip(t)) for t in range(1, self.nq)]
            + [self.at(c=1 - self.c)]
            + [self.at(k=self.deep(t)) for t in range(1, self.nz)]
        )

    def greet(self):
        barrier = pltpu.get_barrier_semaphore()
        peers = self.peers()
        for peer in peers:
            pl.semaphore_signal(barrier, inc=1, device_id=peer, device_id_type=MESH)
        pl.semaphore_wait(barrier, len(peers))


class Links:
    def __init__(self, send, recv):
        self.send, self.recv, self.used = send, recv, 0

    def copy(self, src, dst, peer):
        at = self.used
        self.used += 1
        assert self.used <= self.send.shape[0]
        return pltpu.make_async_remote_copy(
            src_ref=src, dst_ref=dst, send_sem=self.send.at[at], recv_sem=self.recv.at[at],
            device_id=peer, device_id_type=MESH,
        )


def start_all(copies):
    for copy in copies:
        copy.start()
    return copies


def recv_all(copies):
    for copy in copies:
        copy.wait_recv()


def sent_all(copies):
    for copy in copies:
        copy.wait_send()


class Spread:
    def __init__(self, me, links, strip):
        self.me, self.links, self.strip = me, links, strip
        self.first = self.second = ()

    def start(self):
        me = self.me
        own = self.strip(me.q, None)
        self.first = start_all([self.links.copy(own, own, me.at(q=q)) for q in (me.qx, me.qy)])

    def pass_on(self):
        me = self.me
        along_y = self.strip(me.qx, 0)
        along_x = self.strip(me.qy, 1)
        self.second = [
            self.links.copy(along_y, along_y, me.at(q=me.qy)),
            self.links.copy(along_x, along_x, me.at(q=me.qx)),
        ]
        for arrived, copy in zip(self.first, self.second):
            arrived.wait_recv()
            copy.start()

    def finish(self):
        recv_all(self.second)

    def sent(self):
        sent_all(self.first)
        sent_all(self.second)


class Gather:
    def __init__(self, me, links, chunk, slot):
        self.me, self.links, self.chunk, self.slot = me, links, chunk, slot
        self.early = [[], []]
        self.late = [None, None]

    def start(self, half):
        me = self.me
        to = me.qx if half == 0 else me.qy
        self.early[half] = start_all([
            self.links.copy(self.chunk(q, half), self.slot(i, half), me.at(q=to)) for i, q in ((1, me.qd), (0, to))
        ])

    def passing(self, half):
        self.early[half][0].wait_recv()
        return self.me.qy if half == 0 else self.me.qx

    def pass_on(self, half, total):
        to = self.me.qy if half == 0 else self.me.qx
        self.late[half] = self.links.copy(total, self.slot(2, half), self.me.at(q=to))
        self.late[half].start()

    def finish(self):
        for half in range(2):
            self.early[half][1].wait_recv()
            self.late[half].wait_recv()

    def sent(self):
        for half in range(2):
            sent_all(self.early[half])
            self.late[half].wait_send()


def rows_of(start, size, unit):
    return pl.ds(pl.multiple_of(start, unit), size)


def fold(out, parts, rows, step):
    def body(i, carry):
        at = rows_of(i * step, step, step)
        total = parts[0](at).astype(F32)
        for part in parts[1:]:
            total = total + part(at).astype(F32)
        out(at, total)
        return carry

    lax.fori_loop(0, rows // step, body, 0)


def nt(a, b):
    return lax.dot_general(a, b, (((1,), (1,)), ((), ())), preferred_element_type=F32)


def nn(a, b):
    return jnp.dot(a, b, preferred_element_type=F32)


def tn(a, b):
    return lax.dot_general(a, b, (((0,), (0,)), ((), ())), preferred_element_type=F32)


def gelu_pair(v):
    dense = jnp.exp(-0.5 * v * v)
    s = 1.0 / (1.0 + (0.3275911 * 0.7071067811865476) * jnp.abs(v))
    poly = s * (0.254829592 + s * (-0.284496736 + s * (1.421413741 + s * (-1.453152027 + s * 1.061405429))))
    tail = 0.5 * poly * dense
    phi = jnp.where(v >= 0, 1.0 - tail, tail)
    return v * phi, phi + v * dense * 0.3989422804014327


def normal(v):
    centred = v - jnp.mean(v, axis=-1, keepdims=True)
    scale = lax.rsqrt(jnp.mean(centred * centred, axis=-1, keepdims=True) + 1e-06)
    return centred * scale, scale


def sigmoid(v):
    return 1.0 / (1.0 + jnp.exp(-v))


def live_stage(sizes, row, zero, one, mask_zero, mask_one, pool):
    side, across, pooled = zero.width, one.width, POOL

    def counted(shape, axis, width):
        place = lax.broadcasted_iota(jnp.int32, shape, axis)
        return lax.div(place, jnp.int32(width)), lax.rem(place, jnp.int32(width))

    def share(cell, out, size):
        begin = lax.div(out * size, jnp.int32(pooled))
        end = lax.div((out + 1) * size + (pooled - 1), jnp.int32(pooled))
        return jnp.where((cell >= begin) & (cell < end), 1.0 / (end - begin).astype(F32), 0.0)

    for g in range(zero.count):
        size = sizes[g]
        shift = lax.div(side - size, jnp.int32(2))
        r, c = counted((zero.cells, 1), 0, side)
        r = r + row * zero.height - shift
        mask_zero[zero.rows(g)] = jnp.where((r >= 0) & (r < size) & (c < size), 1.0, 0.0)
        i, j = counted((one.cells, zero.cells), 0, across)
        r, c = counted((one.cells, zero.cells), 1, side)
        weight = share(r + row * zero.height - shift, i + row * one.height, size) * share(c, j, size)
        pool[g] = jnp.where(j < pooled, weight, 0.0).astype(BF)
    _, c = counted(mask_one.shape, 0, across)
    mask_one[...] = jnp.where(c < pooled, 1.0, 0.0)


def picked(shape, axis, width):
    cell, place = lax.broadcasted_iota(jnp.int32, shape, axis), lax.broadcasted_iota(jnp.int32, shape, 1 - axis)
    cell = lax.div(cell, jnp.int32(POOL)) * width + lax.rem(cell, jnp.int32(POOL))
    return jnp.where(cell == place, 1.0, 0.0).astype(BF)


def silu_of(v):
    return v * sigmoid(v)


def column_masks(cmask, width):
    place = lax.rem(lax.broadcasted_iota(jnp.int32, cmask.shape[1:], 0), width)
    cmask[0] = jnp.where(place != 0, 1.0, 0.0)
    cmask[1] = jnp.where(place != width - 1, 1.0, 0.0)


def windows(cells, rim, first, masks):
    middle = jnp.concatenate([rim * (1.0 - first), cells, rim * first], axis=0)
    count = middle.shape[0]
    left, right = pltpu.roll(middle, 1, 0), pltpu.roll(middle, count - 1, 0)
    if masks is not None:
        left, right = left * masks[0], right * masks[1]
    return left, middle, right


class Geometry:
    def __init__(self, count, height, width):
        self.count, self.height, self.width = count, height, width
        self.cells = height * width

    def rows(self, g):
        return rows_of(g * self.cells, self.cells, 16)


def head_stage(shape, per, x_of, w, gains, biases, mask, pre, hidden, rim_send, first):
    cells = shape.cells * per

    def body(i, carry):
        rows = rows_of(i * cells, cells, 16)
        x = x_of(rows)
        value = nn(x, w[...])
        pre[rows] = value.astype(BF)
        n, _ = normal(value)
        h = silu_of(n * gains[0:1] + biases[0:1]) * mask[rows]
        hidden[rows] = h.astype(BF)
        for g in range(per):
            at = g * shape.cells
            top = h[at : at + shape.width]
            bottom = h[at + shape.cells - shape.width : at + shape.cells]
            rim_send[i * per + g, pl.ds(0, shape.width)] = (bottom * first + top * (1.0 - first)).astype(BF)
        return carry

    lax.fori_loop(0, shape.count // per, body, 0)


def depth_stage(shape, hidden, rim, taps, cmask, pre, first, channels):
    def body(i, carry):
        g, l = i // (channels // 128), lax.rem(i, channels // 128)
        rows, lanes = shape.rows(g), rows_of(l * 128, 128, 128)
        shifted = windows(
            hidden[rows, lanes].astype(F32),
            rim[g, pl.ds(0, shape.width), lanes].astype(F32),
            first,
            None if cmask is None else (cmask[0], cmask[1]),
        )
        total = jnp.zeros((shape.cells, 128), F32)
        for a in range(3):
            for b in range(3):
                piece = shifted[b][a * shape.width : a * shape.width + shape.cells]
                total = total + piece * taps[3 * a + b : 3 * a + b + 1, lanes]
        pre[rows, lanes] = total.astype(BF)
        return carry

    lax.fori_loop(0, shape.count * (channels // 128), body, 0)


def tail_stage(shape, per, x, w, gains, biases, mask, pre_two, pre_three, result):
    cells = shape.cells * per

    def body(i, carry):
        rows = rows_of(i * cells, cells, 16)
        n, _ = normal(pre_two[rows].astype(F32))
        h = (silu_of(n * gains[1:2] + biases[1:2]) * mask[rows]).astype(BF)
        value = nn(h, w[...])
        pre_three[rows] = value.astype(BF)
        n, _ = normal(value)
        out = silu_of(x[rows].astype(F32) + n * gains[2:3] + biases[2:3]) * mask[rows]
        result(i, rows, out)
        return carry

    lax.fori_loop(0, shape.count // per, body, 0)


def slope_of(v, s):
    return s * (1.0 + v * (1.0 - s))


def norm_back(n, scale, grad, gain, sums, at):
    sums[at : at + 1] += jnp.sum(grad * n, axis=0, keepdims=True)
    sums[at + 3 : at + 4] += jnp.sum(grad, axis=0, keepdims=True)
    dn = grad * gain
    return scale * (dn - jnp.mean(dn, axis=-1, keepdims=True) - n * jnp.mean(dn * n, axis=-1, keepdims=True))


def back_tail_stage(shape, per, grad_of, x, w, gains, biases, mask, pre_two, pre_three, resid, third, hidden_two, second, edge, first, sums, base):
    cells = shape.cells * per

    def body(i, carry):
        rows = rows_of(i * cells, cells, 16)
        live = mask[rows]
        n, scale = normal(pre_three[rows].astype(F32))
        v = x[rows].astype(F32) + n * gains[2:3] + biases[2:3]
        grad = grad_of(i) * slope_of(v, sigmoid(v)) * live
        resid[rows] = grad.astype(BF)
        low = norm_back(n, scale, grad, gains[2:3], sums, base + 11).astype(BF)
        third[rows] = low
        grad = nt(low, w[...])
        n, scale = normal(pre_two[rows].astype(F32))
        v = n * gains[1:2] + biases[1:2]
        s = sigmoid(v)
        hidden_two[rows] = (v * s * live).astype(BF)
        grad = norm_back(n, scale, grad * live * slope_of(v, s), gains[1:2], sums, base + 10)
        second[rows] = grad.astype(BF)
        for g in range(per):
            at = g * shape.cells
            top = grad[at : at + shape.width]
            bottom = grad[at + shape.cells - shape.width : at + shape.cells]
            edge[i * per + g, pl.ds(0, shape.width)] = (bottom * first + top * (1.0 - first)).astype(BF)
        return carry

    lax.fori_loop(0, shape.count // per, body, 0)


def back_depth_stage(shape, second, rim, hidden, hidden_rim, taps, cmask, result, first, channels, sums, base):
    masks = None if cmask is None else (cmask[0], cmask[1])

    def body(i, carry):
        g, l = i // (channels // 128), lax.rem(i, channels // 128)
        rows, lanes = shape.rows(g), rows_of(l * 128, 128, 128)
        edge = pl.ds(0, shape.width)
        grad = second[rows, lanes].astype(F32)
        shifted = windows(grad, rim[g, edge, lanes].astype(F32), first, masks)
        total = jnp.zeros((shape.cells, 128), F32)
        for a in range(3):
            for b in range(3):
                at = (2 - a) * shape.width
                total = total + shifted[2 - b][at : at + shape.cells] * taps[3 * a + b : 3 * a + b + 1, lanes]
        result[rows, lanes] = total.astype(BF)
        shifted = windows(hidden[rows, lanes].astype(F32), hidden_rim[g, edge, lanes].astype(F32), first, masks)
        for a in range(3):
            for b in range(3):
                at = a * shape.width
                line = base + 3 * a + b
                sums[line : line + 1, lanes] += jnp.sum(
                    grad * shifted[b][at : at + shape.cells], axis=0, keepdims=True
                )
        return carry

    lax.fori_loop(0, shape.count * (channels // 128), body, 0)


def back_head_stage(shape, per, one_grad, w, gains, biases, mask, pre_one, resid, first_low, result, sums, base):
    cells = shape.cells * per

    def body(i, carry):
        rows = rows_of(i * cells, cells, 16)
        n, scale = normal(pre_one[rows].astype(F32))
        v = n * gains[0:1] + biases[0:1]
        grad = one_grad[rows].astype(F32) * mask[rows] * slope_of(v, sigmoid(v))
        low = norm_back(n, scale, grad, gains[0:1], sums, base + 9).astype(BF)
        first_low[rows] = low
        result(i, rows, resid[rows].astype(F32) + nt(low, w[...]))
        return carry

    lax.fori_loop(0, shape.count // per, body, 0)


def outer_stage(left, right, out):
    high = out.shape[2]

    def body(i, carry):
        at = rows_of(i * high, high, 128)
        out[i // 2, lax.rem(i, 2)] = tn(left[:, at], right[...]).astype(BF)
        return carry

    lax.fori_loop(0, out.shape[0] * 2, body, 0)


def readout_kernel(
    nz, ndp, nrow, zero, one,
    sizes, patches, cot, rin_part, rout_part, bias_part, conv_in, conv_out, pack,
    tokens, agrad, s1, f2, early, rc1, rc2, rp2, keep_zero, keep_one, rim_zero, rim_one,
    mask_zero, mask_one, pool, hsum, rin, rout, bias, abst, abst_t, hid, mg, ag_send, ag_recv, s2, cmask, edge_zero, edge_one, send, recv, local,
):
    me = Place(nz, ndp, nrow)
    links = Links(send, recv)
    taps, gains, biases = [[pack.at[b, pl.ds(at, n)] for b in range(2)] for at, n in ((0, 16), (16, 8), (24, 8))]
    T, C = agrad.shape
    hw, ow = rout.shape[1], rout.shape[2]
    tall = nz * T
    np_ = 2 * me.nq
    strip = me.c * me.nq + me.q
    ra, rb = C // np_, hw // np_
    me.greet()

    own = [
        pltpu.make_async_copy(rin_part, rin.at[0], local.at[0]),
        pltpu.make_async_copy(rout_part.at[:, rows_of(me.k * ow, ow, 128)], rout.at[0], local.at[1]),
    ]
    convs = [
        pltpu.make_async_copy(part.at[b], s2.at[2 * b + i], local.at[2 + 2 * b + i])
        for b in range(2)
        for i, part in enumerate((conv_in, conv_out))
    ]
    given = pltpu.make_async_copy(patches, mg.at[0], local.at[6])
    convs[0].start()
    given.start()
    za, zb, zc = [[], []], [], []
    rh = ra // 2
    row_b = rows_of(strip * rb, rb, rb)
    for t in range(1, nz):
        there = lax.rem(me.k + nz - t, nz)
        for h in range(2):
            row_a = rows_of(strip * ra + h * rh, rh, rh)
            za[h].append(links.copy(rin_part.at[row_a], rin.at[t, row_a], me.at(k=there)))
        zc.append(links.copy(bias_part, bias.at[t], me.at(k=there)))
    start_all(za[0])
    start_all(zc)
    start_all(za[1])
    for t in range(1, nz):
        there = lax.rem(me.k + nz - t, nz)
        zb.append(links.copy(
            rout_part.at[row_b, rows_of(there * ow, ow, 128)], rout.at[t, row_b], me.at(k=there)))
    for copy in convs[1:] + own:
        copy.start()
    bias[0] = bias_part[...]
    column_masks(cmask, zero.width)
    live_stage(sizes, me.r, zero, one, mask_zero, mask_one, pool)

    def strips(weights, height, part, parts):
        wide = weights.shape[2]

        def strip(q, half):
            few = height // parts
            rows = rows_of((me.c * me.nq + q) * height + part * few, few, few)
            cols = pl.ds(0, wide) if half is None else pl.ds(half * (wide // 2), wide // 2)
            return weights.at[pl.ds(1, nz - 1), rows, cols]

        return Spread(me, links, strip)

    def between_cores(weights, height):
        half = rows_of(me.c * (me.nq * height), me.nq * height, height)
        part = weights.at[pl.ds(1, nz - 1), half]
        return start_all([links.copy(part, part, me.at(c=1 - me.c))])

    pa, pb = [strips(rin, ra, h, 2) for h in range(2)], strips(rout, rb, 0, 1)

    first = (1 - me.r).astype(F32)
    neighbour = me.at(q=me.x * nrow + (nrow - 1 - me.r))

    def masked(rows):
        x = (mg[0, rows].astype(F32) * mask_zero[rows]).astype(BF)
        mg[0, rows] = x
        return x

    convs[0].wait()
    given.wait()
    head_stage(zero, 1, masked, s2.at[0], gains[0], biases[0], mask_zero, hid.at[0], hid.at[1], edge_zero, first)
    rim0 = links.copy(edge_zero, rim_zero, neighbour)
    rim0.start()
    recv_all(za[0])
    pa[0].start()
    rim0.wait_recv()
    depth_stage(zero, hid.at[1], rim_zero, taps[0], cmask, hid.at[2], first, C)
    for copy in convs[1:]:
        copy.wait()

    def to_pooled(i, rows, out):
        mg[1, one.rows(i)] = nn(pool[i], out.astype(BF)).astype(BF)

    sent_all(za[0])
    sent_all(za[1])
    start_all(zb)
    recv_all(za[1])
    pa[1].start()
    pa[0].pass_on()
    tail_stage(zero, 1, mg.at[0], s2.at[1], gains[0], biases[0], mask_zero, hid.at[2], hid.at[3], to_pooled)
    kept_zero = pltpu.make_async_copy(hid, keep_zero, local.at[2])
    kept_zero.start()
    all_one = one.cells * one.count
    part = [mg.at[1 + i // 3, pl.ds((i % 3) * all_one, all_one)] for i in range(5)]
    pooled, pre_one, hidden, pre_two, pre_three = part
    head_stage(one, one.count, lambda rows: pooled[rows], s2.at[2], gains[1], biases[1], mask_one, pre_one, hidden, edge_one, first)
    rim1 = links.copy(edge_one, rim_one, neighbour)
    rim1.start()
    rim1.wait_recv()
    depth_stage(one, hidden, rim_one, taps[1], None, pre_two, first, C)
    here = rows_of(me.k * T, T, 16)

    def to_tokens(i, rows, out):
        abst[here] = nn(picked((T, all_one), 0, one.width), out.astype(BF)).astype(BF)

    tail_stage(one, one.count, pooled, s2.at[3], gains[1], biases[1], mask_one, pre_two, pre_three, to_tokens)
    kept_one = pltpu.make_async_copy(mg.at[pl.ds(1, 2)], keep_one, local.at[3])
    kept_one.start()
    def along(step, group, to):
        rows = rows_of(lax.rem(group + nz, nz) * T, T, 16)
        return links.copy(abst.at[rows], abst.at[rows], me.at(k=lax.rem(to + nz, nz)))

    up = [along(step, me.k - step, me.k + 1) for step in range(nz - 1)]
    down = [along(step, me.k + step, me.k - 1) for step in range(nz - 1)]
    more, less = me.k + 1 < nz, me.k > 0

    def hop(step):
        if step < nz - 1:
            pl.when(jnp.logical_and(more, me.k - step >= 0))(up[step].start)
            pl.when(jnp.logical_and(less, me.k + step < nz))(down[step].start)

    hop(0)
    pa[1].pass_on()
    recv_all(zb)
    pa[0].finish()
    pa[1].finish()
    pb.start()
    ca = between_cores(rin, ra)
    for copy in own + [kept_zero, kept_one]:
        copy.wait()
    recv_all(zc)
    recv_all(ca)

    hsum[...] = jnp.zeros_like(hsum)
    total = jnp.sum(cot[...].astype(F32), axis=0, keepdims=True)
    for j in range(nz):
        early[nz + j : nz + j + 1] = jnp.where(me.k == j, total, 0.0)
    ag = [None] + [
        links.copy(ag_send.at[t - 1], ag_recv.at[t - 1], me.at(k=me.deep(t))) for t in range(1, nz)
    ]
    NT = min(512, hw)

    def hidden_group(z):
        rows = rows_of(z * T, T, 16)

        def front(i, carry):
            u = i // (hw // NT)
            cols = rows_of(lax.rem(i, hw // NT) * NT, NT, 128)
            value, slope = gelu_pair(nn(abst[rows], rin[u, :, cols]) + bias[u, 0:1, cols])
            hid[u, rows, cols] = value.astype(BF)
            mg[u, rows, cols] = slope.astype(BF)
            return carry

        lax.fori_loop(0, nz * (hw // NT), front, 0)

    hidden_group(me.k)
    pb.pass_on()
    for step in range(nz - 1):
        from_less, from_more = me.k - 1 - step >= 0, me.k + 1 + step < nz
        pl.when(from_less)(up[step].wait_recv)
        pl.when(from_more)(down[step].wait_recv)
        hop(step + 1)
        lower = from_less.astype(jnp.int32)

        def arrived(i, carry):
            hidden_group(jnp.where(i < lower, me.k - 1 - step, me.k + 1 + step))
            return carry

        lax.fori_loop(0, lower + from_more.astype(jnp.int32), arrived, 0)
        if step == 0:
            pb.finish()
            cb = between_cores(rout, rb)

    HT = 256

    def g2(i, carry):
        u = i // (hw // HT)
        at = rows_of(lax.rem(i, hw // HT) * HT, HT, HT)
        s2[me.deep(u), at, :] = tn(hid[u, :, at], cot[...]).astype(BF)
        return carry

    lax.fori_loop(0, nz * (hw // HT), g2, 0)
    half = me.nq * rb
    theirs = rows_of((1 - me.c) * half, half, half)
    core2 = start_all([links.copy(s2.at[:, theirs], rc2, me.at(c=1 - me.c))])
    abst_t[...] = abst[...].T
    recv_all(cb)

    def unit(i, carry):
        u = i // (hw // 256)
        cols = rows_of(lax.rem(i, hw // 256) * 256, 256, 256)
        grad = (nt(cot[...], rout[u, cols, :]) * mg[u, :, cols].astype(F32)).astype(BF)
        mg[u, :, cols] = grad
        hsum[me.deep(u), 0:1, cols] += jnp.sum(grad.astype(F32), axis=0, keepdims=True)
        return carry

    lax.fori_loop(0, nz * (hw // 256), unit, 0)

    recv_all(core2)
    mine2 = me.c * half
    gather2 = Gather(
        me, links,
        lambda q, h: s2.at[pl.ds(h * (nz // 2), nz // 2), rows_of(mine2 + q * rb, rb, rb)],
        lambda i, h: rp2.at[i, pl.ds(h * (nz // 2), nz // 2)],
    )
    piece = 256
    parts = half // piece
    loads = [
        pltpu.make_async_copy(
            rc2.at[i // parts, pl.ds(i % parts * piece, piece)], ag_send.at[i % 2, pl.ds(0, piece)], local.at[i % 2]
        )
        for i in range(nz * parts)
    ]
    loads[0].start()
    for i in range(nz * parts):
        loads[i].wait()
        if i + 1 < nz * parts:
            loads[i + 1].start()
        j, where = i // parts, mine2 + i % parts * piece
        fold(
            lambda at, v, j=j, w=where: s2.__setitem__((j, rows_of(w + at.start, at.size, 16)), v.astype(BF)),
            [
                lambda at, j=j, w=where: s2[j, rows_of(w + at.start, at.size, 16)],
                lambda at, i=i: ag_send[i % 2, at],
            ],
            piece, 32,
        )
        if (i + 1) % (nz // 2 * parts) == 0:
            gather2.start(i // (nz // 2 * parts))

    def group_back(t):
        rows = rows_of(me.deep(t) * T, T, 16)

        def back(i, carry):
            at = rows_of(i * 256, 256, 256)
            total = nt(mg[0, rows, :], rin[0, at, :])
            for u in range(1, nz):
                total = total + nt(mg[u, rows, :], rin[u, at, :])
            if t == 0:
                agrad[:, at] = total
            else:
                ag_send[t - 1, :, at] = total.astype(BF)
            return carry

        lax.fori_loop(0, C // 256, back, 0)
        if t:
            ag[t].start()

    for t in (*range(1, nz), 0):
        group_back(t)


    sent_all(ca)
    for group in pa:
        group.sent()

    def g1(i, carry):
        u = i // (C // 256)
        at = rows_of(lax.rem(i, C // 256) * 256, 256, 256)
        rin[u, at, :] = nn(abst_t[at, :], mg[u]).astype(BF)
        return carry

    lax.fori_loop(0, nz * (C // 256), g1, 0)
    low = me.nq * ra
    core1 = links.copy(rin.at[:, rows_of((1 - me.c) * low, low, low)], rc1, me.at(c=1 - me.c))
    core1.start()

    for h in range(2):
        to = gather2.passing(h)
        block = range(h * (nz // 2), (h + 1) * (nz // 2))
        loads = [pltpu.make_async_copy(rp2.at[1, j], mg.at[j, pl.ds(0, rb)], local.at[j]) for j in block]
        for copy in loads:
            copy.start()
        for j, copy in zip(block, loads):
            copy.wait()
            where = mine2 + to * rb
            fold(
                lambda at, v, j=j, w=where: s2.__setitem__((j, rows_of(w + at.start, at.size, 16)), v.astype(BF)),
                [lambda at, j=j, w=where: s2[j, rows_of(w + at.start, at.size, 16)], lambda at, j=j: mg[j, at]],
                rb, min(rb, 32),
            )
        gather2.pass_on(h, gather2.chunk(to, h))

    for step in range(nz - 1):
        pl.when(jnp.logical_and(more, me.k - step >= 0))(up[step].wait_send)
        pl.when(jnp.logical_and(less, me.k + step < nz))(down[step].wait_send)

    def f2_body(i, carry):
        at = rows_of(i * 256, 256, 256)
        total = nn(hid[0], rout[0, :, at]) + bias_part[1:2, at]
        for u in range(1, nz):
            total = total + nn(hid[u], rout[u, :, at])
        abst[:, at] = total.astype(BF)
        return carry

    lax.fori_loop(0, ow // 256, f2_body, 0)
    out_tokens = pltpu.make_async_copy(abst, tokens, local.at[6])
    out_tokens.start()
    recv_all(ag[1:])
    fold(
        lambda at, v: agrad.__setitem__(at, v),
        [lambda at: agrad[at]] + [lambda at, t=t: ag_recv[t - 1, at] for t in range(1, nz)],
        T, 32,
    )
    core1.wait_recv()
    loads = [pltpu.make_async_copy(rc1.at[u], mg.at[u, pl.ds(0, low)], local.at[u]) for u in range(nz)]
    for copy in loads:
        copy.start()
    outs = []
    for u in range(nz):
        loads[u].wait()
        fold(
            lambda at, v, u=u: rin.__setitem__((u, rows_of(me.c * low + at.start, at.size, 16)), v.astype(BF)),
            [lambda at, u=u: rin[u, rows_of(me.c * low + at.start, at.size, 16)], lambda at, u=u: mg[u, at]],
            low, 32,
        )
        outs.append(pltpu.make_async_copy(rin.at[u, rows_of(me.c * low, low, low)], s1.at[u], local.at[u]))
        outs[-1].start()
    gather2.finish()
    for copy in outs:
        copy.wait()
    loads = [
        pltpu.make_async_copy(rp2.at[i], mg.at[pl.ds(0, nz), pl.ds(i * rb, rb)], local.at[i]) for i in (0, 2)
    ]
    for copy in loads:
        copy.start()
    for copy in loads:
        copy.wait()
    for j in range(nz):
        fold(
            lambda at, v, j=j: f2.__setitem__((j, at), v.astype(BF)),
            [lambda at, j=j: s2[j, rows_of(strip * rb + at.start, at.size, 16)]]
            + [lambda at, j=j, i=i: mg[j, rows_of(i * rb + at.start, at.size, 16)] for i in (0, 2)],
            rb, min(rb, 32),
        )
    for j in range(nz):
        early[j : j + 1] = hsum[j]
    out_tokens.wait()
    for group in (pb, gather2):
        group.sent()
    for group_of in (zb, zc, cb, core2, ag[1:], [rim0, rim1, core1]):
        sent_all(group_of)


def grads_kernel(
    nz, ndp, nrow, zero, one,
    sizes, s1, f2, agrad, patches, keep_zero, keep_one, rim_zero, rim_one, conv_in, conv_out, pack, early_in,
    out1, out2, out3, small_out, early, patch_grad, rp1,
    mask_zero, mask_one, pool, small, ec, ep, ez, xs, kept, keep, third, resid, weights, cmask, edge_zero, edge_one, got_zero, got_one,
    sent_on, f1, rz1, conv, rc3, rp3, f3, rz3, sc, sp, sz, send, recv, local,
):
    me = Place(nz, ndp, nrow)
    links = Links(send, recv)
    C, hw = out1.shape
    ow = f2.shape[2]
    np_ = 2 * me.nq
    strip = me.c * me.nq + me.q
    ra, rb = C // np_, hw // np_
    width = C // nrow
    R = out3.shape[2] // 2
    other = me.at(c=1 - me.c)
    first = (1 - me.r).astype(F32)
    neighbour = me.at(q=me.x * nrow + (nrow - 1 - me.r))
    me.greet()

    loads = [
        pltpu.make_async_copy(keep_one, keep, local.at[0]),
        pltpu.make_async_copy(conv_out.at[1], weights.at[1], local.at[1]),
        pltpu.make_async_copy(conv_in.at[1], weights.at[0], local.at[2]),
        pltpu.make_async_copy(keep_zero, kept, local.at[3]),
        pltpu.make_async_copy(patches, xs, local.at[4]),
    ]
    for copy in loads:
        copy.start()
    lead = nz // 2
    gather1 = Gather(
        me, links,
        lambda q, h: s1.at[pl.ds(h * lead, lead), rows_of(q * ra, ra, ra)],
        lambda i, h: rp1.at[i, pl.ds(h * lead, lead)],
    )
    gather1.start(0)
    gather1.start(1)
    row_b = rows_of(strip * rb, rb, rb)
    col_k = rows_of(me.k * ow, ow, 128)
    z2 = start_all([
        links.copy(f2.at[me.deep(t)], out2.at[row_b, col_k], me.at(k=me.deep(t))) for t in range(1, nz)
    ])
    own2 = pltpu.make_async_copy(f2.at[me.k], out2.at[row_b, col_k], local.at[5])
    own2.start()
    early_c = links.copy(early_in, ec, other)
    early_c.start()
    small[...] = jnp.zeros_like(small)
    column_masks(cmask, zero.width)
    live_stage(sizes, me.r, zero, one, mask_zero, mask_one, pool)
    taps, gains, biases = [[pack.at[b, pl.ds(at, n)] for b in range(2)] for at, n in ((0, 16), (16, 8), (24, 8))]

    def spread(b):
        core3[b].wait_recv()
        for m in range(2):
            for x in range(me.nx):
                fold(
                    lambda at, v, i=(b, m, x, me.c): conv.__setitem__((*i, at), v.astype(BF)),
                    [lambda at, i=(b, m, x, me.c): conv[(*i, at)], lambda at, i=(b, m, x): rc3[(*i, at)]],
                    nz * R, 32,
                )
        gather = Gather(
            me, links,
            lambda q, h: conv.at[b, h, q // nrow, me.c, :, rows_of(lax.rem(q, nrow) * width, width, 128)],
            lambda i, h: rp3.at[b, i, h],
        )
        gather.start(1)
        gather.start(0)
        return gather

    def spread_on(b):
        for h in (1, 0):
            to = p3[b].passing(h)
            cols = rows_of(lax.rem(to, nrow) * width, width, 128)
            x = to // nrow
            fold(
                lambda at, v: conv.__setitem__((b, h, x, me.c, at, cols), v.astype(BF)),
                [lambda at: conv[b, h, x, me.c, at, cols], lambda at: rp3[b, 1, h, at, :]],
                nz * R, 32,
            )
            p3[b].pass_on(h, p3[b].chunk(to, h))

    core3, p3 = [None, None], [None, None]

    all_one = one.cells * one.count
    pooled, pre_one, hidden, pre_two, pre_three, pooled_grad = [
        keep.at[i // 3, pl.ds((i % 3) * all_one, all_one)] for i in range(6)
    ]
    third_one, resid_one = third.at[pl.ds(0, all_one)], resid.at[pl.ds(0, all_one)]
    loads[0].wait()
    loads[1].wait()
    back_tail_stage(
        one, one.count, lambda i: nn(picked((all_one, agrad.shape[0]), 1, one.width), agrad[...].astype(BF)), pooled, weights.at[1], gains[1], biases[1], mask_one,
        pre_two, pre_three, resid_one, third_one, pre_three, pre_two, edge_one, first, small, 16,
    )
    rim1 = links.copy(edge_one, got_one, neighbour)
    rim1.start()
    early_c.wait_recv()
    early[...] = early_in[...] + ec[...]
    early_p = start_all([links.copy(early, ep.at[t - 1], me.at(q=me.chip(t))) for t in range(1, me.nq)])
    outer_stage(third_one, pre_three, conv.at[1, 1])
    rim1.wait_recv()
    back_depth_stage(one, pre_two, got_one, hidden, rim_one, taps[1], None, third_one, first, C, small, 16)
    loads[2].wait()

    def to_pooled_grad(i, rows, grad):
        pooled_grad[rows] = grad.astype(BF)

    back_head_stage(
        one, one.count, third_one, weights.at[0], gains[1], biases[1], mask_one, pre_one, resid_one, pre_three, to_pooled_grad, small, 16
    )
    again = [
        pltpu.make_async_copy(conv_out.at[0], weights.at[1], local.at[1]),
        pltpu.make_async_copy(conv_in.at[0], weights.at[0], local.at[2]),
    ]
    for copy in again:
        copy.start()
    outer_stage(pre_three, pooled, conv.at[1, 0])
    core3[1] = links.copy(conv.at[1, :, :, 1 - me.c], rc3.at[1], other)
    core3[1].start()

    temp = [keep.at[0, pl.ds(i * lead * ra, lead * ra)] for i in range(4)]

    def bring(sources):
        copies = [
            pltpu.make_async_copy(source.at[j], to.at[pl.ds(j * ra, ra)], local.at[6 + n * lead + j])
            for n, (source, to) in enumerate(sources)
            for j in range(lead)
        ]
        for copy in copies:
            copy.start()
        for copy in copies:
            copy.wait()

    for h in range(2):
        to = gather1.passing(h)
        bring([(gather1.chunk(to, h), temp[2 * h]), (gather1.slot(1, h), temp[2 * h + 1])])
        for j in range(lead):
            fold(
                lambda at, v: sent_on.__setitem__((h, j, at), v.astype(BF)),
                [lambda at, ref=ref: ref[rows_of(j * ra + at.start, at.size, 16)] for ref in temp[2 * h : 2 * h + 2]],
                ra, 32,
            )
        gather1.pass_on(h, sent_on.at[h])
    p3[1] = spread(1)
    sent_all(early_p)
    recv_all(early_p)
    for t in range(1, me.nq):
        early[...] += ep[t - 1]
    early_z = start_all([links.copy(early, ez.at[t - 1], me.at(k=me.deep(t))) for t in range(1, nz)])
    loads[3].wait()
    loads[4].wait()
    xs[...] = (xs[...].astype(F32) * mask_zero[...]).astype(BF)
    again[0].wait()
    back_tail_stage(
        zero, 1, lambda i: tn(pool[i], pooled_grad[one.rows(i)]), xs, weights.at[1], gains[0], biases[0], mask_zero,
        kept.at[2], kept.at[3], resid, third, kept.at[3], kept.at[2], edge_zero, first, small, 0,
    )
    rim0 = links.copy(edge_zero, got_zero, neighbour)
    rim0.start()
    outer_stage(third, kept.at[3], conv.at[0, 1])
    own2.wait()
    recv_all(z2)
    spread2 = Spread(me, links, lambda q, h: out2.at[
        rows_of((me.c * me.nq + q) * rb, rb, rb),
        pl.ds(0, nz * ow) if h is None else pl.ds(h * (nz * ow // 2), nz * ow // 2),
    ])
    spread2.start()
    rim0.wait_recv()
    back_depth_stage(zero, kept.at[2], got_zero, kept.at[1], rim_zero, taps[0], cmask, third, first, C, small, 0)
    spread_on(1)
    gather1.finish()
    for h in range(2):
        mine = [keep.at[0, pl.ds(i * lead * ra, lead * ra)] for i in range(3)]
        bring([(gather1.chunk(me.q, h), mine[0]), (gather1.slot(0, h), mine[1]), (gather1.slot(2, h), mine[2])])
        for j in range(lead):
            fold(
                lambda at, v: f1.__setitem__((h * lead + j, at), v.astype(BF)),
                [lambda at, ref=ref: ref[rows_of(j * ra + at.start, at.size, 16)] for ref in mine],
                ra, 32,
            )
    z1 = start_all([links.copy(f1.at[t], rz1.at[t - 1], me.at(k=me.deep(t))) for t in range(1, nz)])
    again[1].wait()

    def to_patches(i, rows, grad):
        resid[rows] = (grad * mask_zero[rows]).astype(BF)

    back_head_stage(
        zero, 1, third, weights.at[0], gains[0], biases[0], mask_zero, kept.at[0], resid, kept.at[3], to_patches, small, 0
    )
    out_patches = pltpu.make_async_copy(resid, patch_grad, local.at[0])
    out_patches.start()
    outer_stage(kept.at[3], xs, conv.at[0, 0])
    core3[0] = links.copy(conv.at[0, :, :, 1 - me.c], rc3.at[0], other)
    core3[0].start()
    sums = start_all([links.copy(small, sc, other)])
    z3 = [None, None]
    my_cols = rows_of(me.r * width, width, 128)

    def deepen(b):
        p3[b].finish()
        for m in range(2):
            for j in range(nz):
                rows = pl.ds(j * R, R)
                total = conv[b, m, me.x, me.c, rows, my_cols].astype(F32)
                for i in (0, 2):
                    total = total + rp3[b, i, m, rows, :].astype(F32)
                f3[b, j, pl.ds(m * R, R)] = total.astype(BF)
        z3[b] = start_all([
            links.copy(f3.at[b, me.deep(t)], rz3.at[b, t - 1], me.at(k=me.deep(t))) for t in range(1, nz)
        ])

    g3 = []

    def settle(b):
        recv_all(z3[b])
        total = f3[b, me.k].astype(F32)
        for t in range(1, nz):
            total = total + rz3[b, t - 1].astype(F32)
        out3[b, me.r] = total.astype(BF)
        g3.extend(start_all([
            links.copy(out3.at[b, me.r], out3.at[b, me.r], me.at(q=me.x * nrow + lax.rem(me.r + t, nrow)))
            for t in range(1, nrow)
        ]))

    p3[0] = spread(0)
    deepen(1)
    recv_all(z1)
    row_a = rows_of(strip * ra, ra, ra)
    fold(
        lambda at, v: out1.__setitem__(rows_of(strip * ra + at.start, at.size, 16), v.astype(BF)),
        [lambda at: f1[0, at]] + [lambda at, t=t: rz1[t - 1, at] for t in range(1, nz)],
        ra, 32,
    )
    spread1 = Spread(me, links, lambda q, h: out1.at[
        rows_of((me.c * me.nq + q) * ra, ra, ra), pl.ds(0, hw) if h is None else pl.ds(h * (hw // 2), hw // 2)
    ])
    spread1.start()
    recv_all(sums)
    sent_all(sums)
    small[...] += sc[...]
    few = C // ndp

    def columns(q):
        return rows_of((q // nrow * 2 + me.c) * few, few, 128)

    sums_p = start_all([
        links.copy(small.at[:, columns(me.chip(t))], sp.at[t - 1], me.at(q=me.chip(t))) for t in range(1, me.nq)
    ])
    spread_on(0)
    spread2.pass_on()
    spread1.pass_on()
    settle(1)
    recv_all(sums_p)
    total = small[:, columns(me.q)]
    for t in range(1, me.nq):
        total = total + sp[t - 1]
    small_out[...] = total
    sums_z = start_all([links.copy(small_out, sz.at[t - 1], me.at(k=me.deep(t))) for t in range(1, nz)])
    deepen(0)
    spread1.finish()
    half_a = rows_of(me.c * me.nq * ra, me.nq * ra, me.nq * ra)
    h1 = start_all([links.copy(out1.at[half_a], out1.at[half_a], other)])
    spread2.finish()
    half_b = rows_of(me.c * me.nq * rb, me.nq * rb, me.nq * rb)
    h2 = start_all([links.copy(out2.at[half_b], out2.at[half_b], other)])
    settle(0)
    sent_all(sums_z)
    recv_all(sums_z)
    sent_all(early_z)
    recv_all(early_z)
    for t in range(1, nz):
        small_out[...] += sz[t - 1]
        early[...] += ez[t - 1]
    recv_all(g3)
    recv_all(h1)
    recv_all(h2)
    out_patches.wait()
    for group_of in ([early_c], sums_p, core3, z2, z1, z3[0], z3[1], g3, h1, h2, [rim0, rim1]):
        sent_all(group_of)
    for group in (gather1, p3[0], p3[1], spread1, spread2):
        group.sent()


def spec(*kinds):
    return [pl.BlockSpec(memory_space=kind) for kind in kinds]


def run_readout(mesh, zero, one, sizes, patches, cot, read_in, read_out, read_bias, conv_in, conv_out, pack):
    nz, ndp, nrow = mesh.shape["wide"], mesh.shape["dp"], mesh.shape["row"]
    nq = ndp // 2 * nrow
    T, C = one.count * one.height * POOL, patches.shape[1]
    hw, ow = read_out.shape[0], cot.shape[1]
    tall = nz * T
    rb = hw // (2 * nq)
    copies = 7 * (nz - 1) + 28
    bias_part = jnp.pad(read_bias, ((0, 6), (0, 0)))
    ANY = pl.ANY
    return pl.pallas_call(
        functools.partial(readout_kernel, nz, ndp, nrow, zero, one),
        out_shape=[
            jax.ShapeDtypeStruct((tall, ow), BF),
            jax.ShapeDtypeStruct((T, C), F32),
            jax.ShapeDtypeStruct((nz, C // 2, hw), BF),
            jax.ShapeDtypeStruct((nz, rb, ow), BF),
            jax.ShapeDtypeStruct((2 * nz, C), F32),
            jax.ShapeDtypeStruct((nz, C // 2, hw), BF),
            jax.ShapeDtypeStruct((nz, nq * rb, ow), BF),
            jax.ShapeDtypeStruct((nq - 1, nz, rb, ow), BF),
            jax.ShapeDtypeStruct((4, tall, hw), BF),
            jax.ShapeDtypeStruct((2, tall, hw), BF),
            jax.ShapeDtypeStruct((zero.count, 32, C), BF),
            jax.ShapeDtypeStruct((one.count, 16, C), BF),
        ],
        in_specs=spec(pltpu.SMEM, ANY, VMEM, ANY, ANY, VMEM, ANY, ANY, VMEM),
        out_specs=spec(ANY, VMEM, ANY, VMEM, VMEM, ANY, ANY, ANY, ANY, ANY, VMEM, VMEM),
        scratch_shapes=[
            VMEM((tall, 1), F32),
            VMEM((one.count * one.cells, 1), F32),
            VMEM((zero.count, one.cells, zero.cells), BF),
            VMEM((nz, 1, hw), F32),
            VMEM((nz, C, hw), BF),
            VMEM((nz, hw, ow), BF),
            VMEM((nz, 8, hw), F32),
            VMEM((tall, C), BF),
            VMEM((C, tall), BF),
            VMEM((nz, tall, hw), BF),
            VMEM((nz, tall, hw), BF),
            VMEM((nz - 1, T, C), BF),
            VMEM((nz - 1, T, C), BF),
            VMEM((nz, hw, ow), BF),
            VMEM((2, zero.cells + 2 * zero.width, 128), F32),
            VMEM((zero.count, 32, C), BF),
            VMEM((one.count, 16, C), BF),
            pltpu.SemaphoreType.DMA((copies,)),
            pltpu.SemaphoreType.DMA((copies,)),
            pltpu.SemaphoreType.DMA((7,)),
        ],
        compiler_params=pltpu.CompilerParams(
            collective_id=0, has_side_effects=True, vmem_limit_bytes=LIMIT
        ),
        name="readout",
    )(sizes, patches, cot, read_in, read_out, bias_part, conv_in, conv_out, pack)


LIMIT = 62 * 1024 * 1024


def run_grads(mesh, zero, one, sizes, s1, f2, agrad, patches, keep_zero, keep_one, rim_zero, rim_one, conv_in, conv_out, pack, early):
    nz, ndp, nrow = mesh.shape["wide"], mesh.shape["dp"], mesh.shape["row"]
    nq = ndp // 2 * nrow
    nx = ndp // 2
    C, hw = s1.shape[1] * 2, s1.shape[2]
    _, rb, ow = f2.shape
    ra = C // (2 * nq)
    R = C // (ndp * nz)
    tall = patches.shape[0]
    S = 32
    copies = 7 * (nz - 1) + 40
    width = C // nrow
    ANY = pl.ANY
    return pl.pallas_call(
        functools.partial(grads_kernel, nz, ndp, nrow, zero, one),
        out_shape=[
            jax.ShapeDtypeStruct((C, hw), BF),
            jax.ShapeDtypeStruct((hw, nz * ow), BF),
            jax.ShapeDtypeStruct((2, nrow, 2 * R, width), BF),
            jax.ShapeDtypeStruct((S, C // ndp), F32),
            jax.ShapeDtypeStruct(early.shape, F32),
            jax.ShapeDtypeStruct((tall, C), BF),
            jax.ShapeDtypeStruct((nq - 1, nz, ra, hw), BF),
        ],
        in_specs=spec(pltpu.SMEM, ANY, VMEM, VMEM, ANY, ANY, ANY, VMEM, VMEM, ANY, ANY, VMEM, VMEM),
        out_specs=spec(VMEM, ANY, VMEM, VMEM, VMEM, ANY, ANY),
        scratch_shapes=[
            VMEM((tall, 1), F32),
            VMEM((one.count * one.cells, 1), F32),
            VMEM((zero.count, one.cells, zero.cells), BF),
            VMEM((S, C), F32),
            VMEM(early.shape, F32),
            VMEM((nq - 1, *early.shape), F32),
            VMEM((nz - 1, *early.shape), F32),
            VMEM((tall, C), BF),
            VMEM((4, tall, C), BF),
            VMEM((2, tall, C), BF),
            VMEM((tall, C), BF),
            VMEM((tall, C), BF),
            VMEM((2, C, C), BF),
            VMEM((2, zero.cells + 2 * zero.width, 128), F32),
            VMEM((zero.count, 32, C), BF),
            VMEM((one.count, 16, C), BF),
            VMEM((zero.count, 32, C), BF),
            VMEM((one.count, 16, C), BF),
            VMEM((2, nz // 2, ra, hw), BF),
            VMEM((nz, ra, hw), BF),
            VMEM((nz - 1, ra, hw), BF),
            VMEM((2, 2, nx, 2, nz * R, C), BF),
            VMEM((2, 2, nx, nz * R, C), BF),
            VMEM((2, nq - 1, 2, nz * R, width), BF),
            VMEM((2, nz, 2 * R, width), BF),
            VMEM((2, nz - 1, 2 * R, width), BF),
            VMEM((S, C), F32),
            VMEM((nq - 1, S, C // ndp), F32),
            VMEM((nz - 1, S, C // ndp), F32),
            pltpu.SemaphoreType.DMA((copies,)),
            pltpu.SemaphoreType.DMA((copies,)),
            pltpu.SemaphoreType.DMA((6 + nq * nz,)),
        ],
        compiler_params=pltpu.CompilerParams(
            collective_id=1, has_side_effects=True, vmem_limit_bytes=LIMIT
        ),
        name="grads",
    )(sizes, s1, f2, agrad, patches, keep_zero, keep_one, rim_zero, rim_one, conv_in, conv_out, pack, early)


POOL = 12


def widened(values):
    rows, columns = values.shape
    step = rows // 8

    def body(given, out):
        out[...] = given[...].astype(F32)

    block = pl.BlockSpec((step, columns), lambda i: (i, 0))
    return pl.pallas_call(
        body,
        grid=(8,),
        in_specs=[block],
        out_specs=block,
        out_shape=jax.ShapeDtypeStruct(values.shape, F32),
        name="widen",
    )(values)


eps_norm = 1e-06
exact_mode = lax.Precision.HIGHEST


def extended(cells, sides, width):
    for axis, dim in sides:
        count = lax.axis_size(axis)
        ends = count - 1
        head = lax.slice_in_dim(cells, 0, width, axis=dim)
        tail = lax.slice_in_dim(cells, cells.shape[dim] - width, cells.shape[dim], axis=dim)
        cells = jnp.concatenate(
            [
                lax.ppermute(tail, axis, [(i, (i + 1) % count) for i in range(ends)]),
                cells,
                lax.ppermute(head, axis, [((i + 1) % count, i) for i in range(ends)]),
            ],
            axis=dim,
        )
    return cells


def layer_norm(values, gain_row, bias_row):
    centre = jnp.mean(values, axis=-1, keepdims=True)
    centred = values - centre
    variance = jnp.mean(centred * centred, axis=-1, keepdims=True)
    return centred * lax.rsqrt(variance + eps_norm) * gain_row + bias_row


def head_piece(pre_values, gain_row, bias_row, live_mask):
    return jax.nn.silu(layer_norm(pre_values, gain_row, bias_row)) * live_mask


def tail_piece(source, third_pre, gain_row, bias_row, live_mask):
    return jax.nn.silu(source + layer_norm(third_pre, gain_row, bias_row)) * live_mask


def outer_sum(left_rows, right_rows):
    return lax.dot_general(
        left_rows, right_rows, (((0,), (0,)), ((), ())), preferred_element_type=jnp.float32
    )


def times_transposed(left_rows, weight):
    return lax.dot_general(
        left_rows, weight, (((1,), (1,)), ((), ())), preferred_element_type=jnp.float32
    )


def pad_columns(values):
    return jnp.pad(values, ((0, 0), (0, 0), (1, 1), (0, 0)))


def rows_forward(hidden_one):
    return extended(hidden_one, (("row", 1),), 1)


def rows_backward(second_low):
    return extended(second_low, (("row", 1),), 1)


def depth_apply(padded, tap_table, row_count, col_count):
    result = jnp.zeros((padded.shape[0], row_count, col_count, padded.shape[3]), jnp.float32)
    for offset in range(9):
        window = padded[
            :, offset // 3 : offset // 3 + row_count, offset % 3 : offset % 3 + col_count, :
        ]
        result = result + window.astype(jnp.float32) * tap_table[offset].astype(jnp.float32)
    return result


def block_forward(source, live_mask, weights):
    w_first, w_last, tap_table, gain_rows, bias_rows = weights
    grid_count, row_count, col_count, channels = source.shape
    flat_rows = source.astype(jnp.bfloat16).reshape(-1, channels)
    first_pre = jnp.dot(flat_rows, w_first, preferred_element_type=jnp.float32).reshape(
        source.shape
    )
    hidden_one = head_piece(first_pre, gain_rows[0], bias_rows[0], live_mask).astype(jnp.bfloat16)
    padded_one = pad_columns(rows_forward(hidden_one))
    second_pre = depth_apply(padded_one, tap_table, row_count, col_count)
    hidden_two = head_piece(second_pre, gain_rows[1], bias_rows[1], live_mask).astype(jnp.bfloat16)
    two_rows = hidden_two.reshape(-1, channels)
    third_pre = jnp.dot(two_rows, w_last, preferred_element_type=jnp.float32).reshape(source.shape)
    output = tail_piece(source, third_pre, gain_rows[2], bias_rows[2], live_mask)
    return (output, (flat_rows, first_pre, padded_one, second_pre, two_rows, third_pre))


def block_backward(output_grad, source, live_mask, weights, kept):
    w_first, w_last, tap_table, gain_rows, bias_rows = weights
    flat_rows, first_pre, padded_one, second_pre, two_rows, third_pre = kept
    grid_count, row_count, col_count, channels = source.shape
    _, tail_back = jax.vjp(
        functools.partial(tail_piece, live_mask=live_mask), source, third_pre, gain_rows[2], bias_rows[2]
    )
    residual_grad, third_grad, gain_three, bias_three = tail_back(output_grad)
    third_low = third_grad.astype(jnp.bfloat16).reshape(-1, channels)
    grad_last = outer_sum(two_rows, third_low)
    two_grad = times_transposed(third_low, w_last).reshape(source.shape)
    _, middle_back = jax.vjp(
        functools.partial(head_piece, live_mask=live_mask), second_pre, gain_rows[1], bias_rows[1]
    )
    second_grad, gain_two, bias_two = middle_back(two_grad)
    second_low = second_grad.astype(jnp.bfloat16)
    padded_grad = pad_columns(rows_backward(second_low))
    one_grad = depth_apply(padded_grad, tap_table[::-1], row_count, col_count)
    second_wide = second_low.astype(jnp.float32)
    tap_grads = []
    for offset in range(9):
        window = padded_one[
            :, offset // 3 : offset // 3 + row_count, offset % 3 : offset % 3 + col_count, :
        ]
        tap_grads.append(jnp.sum(second_wide * window.astype(jnp.float32), axis=(0, 1, 2)))
    _, first_back = jax.vjp(
        functools.partial(head_piece, live_mask=live_mask), first_pre, gain_rows[0], bias_rows[0]
    )
    first_grad, gain_one, bias_one = first_back(one_grad)
    first_low = first_grad.astype(jnp.bfloat16).reshape(-1, channels)
    grad_first = outer_sum(flat_rows, first_low)
    source_grad = residual_grad + times_transposed(first_low, w_first).reshape(source.shape)
    grads = (
        grad_first,
        grad_last,
        jnp.stack(tap_grads),
        jnp.stack([gain_one, gain_two, gain_three]),
        jnp.stack([bias_one, bias_two, bias_three]),
    )
    return (source_grad, grads)


def pool_weights(grid_side, row_shift, pooled_index, slot_index):
    place = slot_index - row_shift
    begin = pooled_index * grid_side // POOL
    finish = ((pooled_index + 1) * grid_side + POOL - 1) // POOL
    inside = (place >= begin) & (place < finish)
    return jnp.where(inside, 1.0, 0.0).astype(jnp.float32) / (finish - begin).astype(jnp.float32)


def plain(
    patches,
    grid_sizes,
    conv_in,
    conv_out,
    depth_taps,
    norm_gain,
    norm_bias,
    read_in,
    read_bias,
    read_out,
    cotangent,
):
    grid_count, local_rows, grid_width, channels = patches.shape
    row_place = lax.axis_index("row")
    slot_rows = row_place * local_rows + jnp.arange(local_rows, dtype=jnp.int32)
    column_index = jnp.arange(grid_width, dtype=jnp.int32)
    row_shift = (grid_width - grid_sizes) // 2
    row_live = (slot_rows[None, :] >= row_shift[:, None]) & (
        slot_rows[None, :] < (row_shift + grid_sizes)[:, None]
    )
    col_live = column_index[None, :] < grid_sizes[:, None]
    live_mask = (row_live[:, :, None] & col_live[:, None, :]).astype(jnp.float32)[..., None]
    weights_one = (conv_in[0], conv_out[0], depth_taps[0], norm_gain[0], norm_bias[0])
    weights_two = (conv_in[1], conv_out[1], depth_taps[1], norm_gain[1], norm_bias[1])
    source = patches.astype(jnp.float32) * live_mask
    encoded, kept_one = block_forward(source, live_mask, weights_one)
    pool_local = POOL // lax.axis_size("row")
    pooled_index = row_place * pool_local + jnp.arange(pool_local, dtype=jnp.int32)
    side_shaped = grid_sizes[:, None, None]
    row_pool = pool_weights(
        side_shaped, row_shift[:, None, None], pooled_index[None, :, None], slot_rows[None, None, :]
    )
    col_pool = pool_weights(
        side_shaped,
        0,
        jnp.arange(POOL, dtype=jnp.int32)[None, :, None],
        column_index[None, None, :],
    )
    pooled = jnp.einsum("gir,gjw,grwc->gijc", row_pool, col_pool, encoded, precision=exact_mode)
    all_live = jnp.ones((grid_count, pool_local, POOL, 1), jnp.float32)
    abstract, kept_two = block_forward(pooled, all_live, weights_two)
    token_rows = abstract.astype(jnp.bfloat16).reshape(-1, channels)
    gathered = lax.all_gather(token_rows, "wide", axis=0, tiled=True)
    gelu_exact = functools.partial(jax.nn.gelu, approximate=False)
    mixed_pre = jnp.dot(gathered, read_in, preferred_element_type=jnp.float32) + read_bias[0]
    hidden_wide, gelu_back = jax.vjp(gelu_exact, mixed_pre)
    hidden = hidden_wide.astype(jnp.bfloat16)
    partial_out = jnp.dot(hidden, read_out, preferred_element_type=jnp.float32)
    summed = (
        lax.psum_scatter(
            partial_out.astype(jnp.bfloat16), "wide", scatter_dimension=1, tiled=True
        ).astype(jnp.float32)
        + read_bias[1]
    )
    tokens = summed.astype(jnp.bfloat16).reshape(cotangent.shape)
    cot_local = cotangent.reshape(-1, cotangent.shape[-1])
    cot_all = lax.all_gather(cot_local, "wide", axis=1, tiled=True)
    hidden_grad = times_transposed(cot_all, read_out)
    mixed_grad = gelu_back(hidden_grad)[0].astype(jnp.bfloat16)
    grad_exit = outer_sum(hidden, cot_all)
    grad_entry = outer_sum(gathered, mixed_grad)
    bias_pair = jnp.stack(
        [
            jnp.sum(mixed_grad.astype(jnp.float32), axis=0),
            jnp.sum(cot_local.astype(jnp.float32), axis=0),
        ]
    )
    abstract_grad = lax.psum_scatter(
        times_transposed(mixed_grad, read_in).astype(jnp.bfloat16),
        "wide",
        scatter_dimension=0,
        tiled=True,
    ).astype(jnp.float32)
    grad_entry, bias_pair, grad_exit = (
        lax.psum(grad_entry.astype(jnp.bfloat16), ("dp", "row")).astype(jnp.float32),
        lax.psum(bias_pair.astype(jnp.bfloat16), ("dp", "row")).astype(jnp.float32),
        lax.psum(grad_exit.astype(jnp.bfloat16), ("dp", "row")).astype(jnp.float32),
    )
    pooled_grad, grads_two = block_backward(
        abstract_grad.reshape(abstract.shape), pooled, all_live, weights_two, kept_two
    )
    encoded_grad = jnp.einsum(
        "gir,gjw,gijc->grwc", row_pool, col_pool, pooled_grad, precision=exact_mode
    )
    source_grad, grads_one = block_backward(encoded_grad, source, live_mask, weights_one, kept_one)
    patch_grad = (source_grad * live_mask).astype(jnp.bfloat16)
    stacked = tuple((jnp.stack([grads_one[index], grads_two[index]]) for index in range(5)))
    totals = (
        lax.psum_scatter(stacked[0], ("dp", "wide"), scatter_dimension=2, tiled=True),
        lax.psum_scatter(stacked[1], ("dp", "wide"), scatter_dimension=2, tiled=True),
        lax.psum_scatter(stacked[2], ("dp", "wide"), scatter_dimension=2, tiled=True),
        lax.psum_scatter(stacked[3], ("dp", "wide"), scatter_dimension=2, tiled=True),
        lax.psum_scatter(stacked[4], ("dp", "wide"), scatter_dimension=2, tiled=True),
    )
    totals = (
        lax.psum(totals[0].astype(jnp.bfloat16), "row").astype(jnp.float32),
        lax.psum(totals[1].astype(jnp.bfloat16), "row").astype(jnp.float32),
        lax.psum(totals[2].astype(jnp.bfloat16), "row").astype(jnp.float32),
        lax.psum(totals[3].astype(jnp.bfloat16), "row").astype(jnp.float32),
        lax.psum(totals[4].astype(jnp.bfloat16), "row").astype(jnp.float32),
    )
    return (
        tokens,
        patch_grad,
        totals[0],
        totals[1],
        totals[2],
        totals[3],
        totals[4],
        grad_entry,
        bias_pair,
        grad_exit,
    )


def on_device(
    mesh,
    patches,
    grid_sizes,
    conv_in,
    conv_out,
    depth_taps,
    norm_gain,
    norm_bias,
    read_in,
    read_bias,
    read_out,
    cotangent,
):
    nz, ndp = mesh.shape["wide"], mesh.shape["dp"]
    grid_count, local_rows, grid_width, channels = patches.shape
    zero = Geometry(grid_count, local_rows, grid_width)
    one = Geometry(grid_count, POOL // mesh.shape["row"], 16)
    flat = patches.reshape(-1, channels)
    cot_local = cotangent.reshape(-1, cotangent.shape[-1])
    pack = jnp.concatenate(
        [
            jnp.pad(piece.astype(F32), ((0, 0), (0, height - piece.shape[1]), (0, 0)))
            for piece, height in ((depth_taps, 16), (norm_gain, 8), (norm_bias, 8))
        ],
        axis=1,
    )
    tokens, agrad, s1, f2, early, _, _, _, keep_zero, keep_one, rim_zero, rim_one = run_readout(
        mesh, zero, one, grid_sizes, flat, cot_local, read_in, read_out, read_bias, conv_in, conv_out, pack
    )
    tokens = tokens.reshape(cotangent.shape)
    out1, out2, out3, small, early, patch_grad, _ = run_grads(
        mesh, zero, one, grid_sizes, s1, f2, agrad, flat, keep_zero, keep_one, rim_zero, rim_one, conv_in, conv_out, pack, early
    )
    patch_grad = patch_grad.reshape(patches.shape)
    R = channels // (ndp * nz)
    out3 = out3.reshape(2, -1, 2, R, out3.shape[-1]).transpose(0, 2, 1, 4, 3).reshape(2, 2, channels, R).astype(F32)
    place = lax.axis_index("wide")
    own = lax.dynamic_slice_in_dim(small, place * R, R, axis=1).reshape(2, 16, R)
    taps, gains, biases = own[:, 0:9], own[:, 9:12], own[:, 12:15]
    bias_pair = lax.dynamic_slice_in_dim(early.reshape(2, nz, -1), place, 1, axis=1)[:, 0]
    return (
        tokens,
        patch_grad,
        out3[:, 0],
        out3[:, 1],
        taps,
        gains,
        biases,
        out1.astype(F32),
        bias_pair,
        widened(out2),
    )


def fits(mesh):
    return mesh.shape["wide"] == 4 and mesh.shape["dp"] % 2 == 0 and mesh.shape["row"] == 2


def solution(mesh):

    placed = (
        P(("dp", "wide"), "row", None, None),
        P(("dp", "wide")),
        P(),
        P(),
        P(),
        P(),
        P(),
        P(None, "wide"),
        P(None, "wide"),
        P("wide", None),
        P("dp", "row", None, "wide"),
    )
    return jax.shard_map(
        functools.partial(on_device, mesh) if fits(mesh) else plain,
        mesh=mesh,
        in_specs=placed,
        out_specs=(
            P("dp", "row", None, "wide"),
            P(("dp", "wide"), "row", None, None),
            P(None, None, ("dp", "wide")),
            P(None, None, ("dp", "wide")),
            P(None, None, ("dp", "wide")),
            P(None, None, ("dp", "wide")),
            P(None, None, ("dp", "wide")),
            P(None, "wide"),
            P(None, "wide"),
            P("wide", None),
        ),
        check_vma=False,
    )
```
